32 devices in a mesh: groups: 2 (over y), col: 4 (over z), row: 2 (over x), side: 2 (over core).
Axes of the slice: x: 2, y: 2, z: 4, core: 2. Of those that a mesh axis runs over, the one named last changes fastest.
Arguments:
- hidden_in: bfloat16 [256, 8192], P(('groups', 'col'), 'row'), parts along dimension 0, may hold values from -40 to 40
- norm_gain: bfloat16 [8192], P('row'), may hold values from 0.099609375 to 1.8984375
- qkv_weight: bfloat16 [8192, 10240], P('row', 'col'), may hold values from -0.0625 to 0.0625
- out_weight: bfloat16 [8192, 8192], P('row', 'col'), may hold values from -0.0625 to 0.0625
- key_cache: bfloat16 [256, 64, 1024], P(('groups', 'col'), None, 'row'), parts along dimension 0, may hold values from -320 to 320
- value_cache: bfloat16 [256, 64, 1024], P(('groups', 'col'), None, 'row'), parts along dimension 0, may hold values from -4 to 4
- cache_lengths: int32 [256], P(('groups', 'col')), parts along dimension 0, may hold values from 1 to 64, 4096 in all
- slot_request: int32 [256], P('groups'), parts along dimension 0, may hold values from 0 to 127, each once
Outputs:
- layer_rows: bfloat16 [2, 256, 8192], P('side', ('groups', 'col'), 'row'), parts along dimension 1
The draws below stay inside these ranges and needn't reach their ends.
There are 2 independent parts, one for each index of `groups`. The reference program is written for one: setup_inputs(seed, part) draws one part's arguments, and reference() takes and returns one part's arrays. A program takes and returns all parts, laid end to end along the dimension named above; an argument that names none is the same for every part. Nothing has to cross between parts.
Inputs may be any that keep to these rules, and one draw needn't show every extreme that they name: Slot s of cache_lengths, key_cache and value_cache belongs to request slot_request[s]; every request has exactly one slot. Positions from cache_lengths[s] on are not filled; some slot is full in every draw.
All inputs are finite; a program needn't handle non-finite values. No bound on the sum of `cache_lengths` on one device may be relied on, other than what follows from the above.
Results may differ from the reference program's by a relative error of at most 0.035.
Values may be sent and summed in bfloat16 or wider, within the bound.
No kernel may reach another device: no remote copies, remote signals or barrier semaphores. Data moves between devices by JAX's collectives and lax.ppermute only.
A program may use at most 128 MiB of HBM per device.

```python
import math
import jax
import jax.numpy as jnp
import numpy as np
from jax import lax

D = 8192
HEADS = 64
KV_HEADS = 8
HEAD_DIM = 128
CACHE = 64
QKV = 10240
REQUESTS = 128


def draw_hidden_in(key, part):
    noise_key, row_key, col_key = jax.random.split(key, 3)
    columns = jnp.arange(D, dtype=jnp.float32) / D
    noise_vals = jnp.clip(jax.random.normal(noise_key, (REQUESTS, D), jnp.float32), -3.0, 3.0)
    row_scale = jnp.exp(math.log(10.0) * (jax.random.uniform(row_key, (REQUESTS, 1), jnp.float32) - 0.5))
    col_trend = jnp.exp(math.log(3.0) * (columns - 0.5))
    jitter = jnp.exp(math.log(3.0) * (jax.random.uniform(col_key, (1, D), jnp.float32) - 0.5))
    return (noise_vals * row_scale * jitter * col_trend[None, :]).astype(jnp.bfloat16)


def draw_key_cache(key, part):
    noise_key = jax.random.fold_in(key, 0)
    values = jnp.clip(jax.random.normal(noise_key, (REQUESTS, CACHE, KV_HEADS * HEAD_DIM), jnp.float32), -4.0, 4.0)
    return values.astype(jnp.bfloat16)


def levels(own_key, extent, cuts, smallest, largest):
    def one(dim, parts):
        heights = jax.random.uniform(jax.random.fold_in(jax.random.fold_in(own_key, 6), dim), (parts,), jnp.float32, smallest / len(cuts), largest / len(cuts))
        return jnp.repeat(jnp.exp(heights), extent[dim] // parts).reshape((-1,) + (1,) * (len(extent) - dim - 1))

    factor_of = one(*cuts[0])
    for cut in cuts[1:]:
        factor_of = factor_of * one(*cut)
    return factor_of


def length_profile(number_of, total, reach, slope):
    loads = [(1 << 20) // math.isqrt(grade ** slope) + 1 for grade in range(2, number_of + 1)]
    surplus, counts = total - reach - (number_of - 1), [1] * (number_of - 1)
    while surplus > 0:
        free = [i for i in range(number_of - 1) if counts[i] < reach]
        mass, remaining = sum([loads[i] for i in free]), surplus
        for i in free:
            more = min(reach - counts[i], max(1, remaining * loads[i] // mass), surplus)
            counts[i] = counts[i] + more
            surplus = surplus - more
    return np.array([reach] + counts)


def uneven(own_key, number_of, total, reach, skew):
    if number_of == 2:
        one = jax.random.randint(own_key, (), max(1, total - reach), min(reach, total - 1) + 1)
        return jnp.stack([one, total - one])
    sizes = jnp.asarray(length_profile(number_of, total, reach, skew), jnp.int32)
    pairs = (number_of - 1) // 2
    giver, receiver = sizes[1:1 + 2 * pairs:2], sizes[2:2 + 2 * pairs:2]
    slack = jnp.minimum(giver - 1, reach - receiver)
    passed = jax.random.randint(jax.random.fold_in(own_key, 1), (pairs,), 0, 1 << 20) % (slack + 1)
    sizes = sizes.at[1:1 + 2 * pairs:2].set(giver - passed).at[2:2 + 2 * pairs:2].set(receiver + passed)
    return sizes[jax.random.permutation(jax.random.fold_in(own_key, 2), number_of)]


def bell_draw(rng, shape, spread, bound, cuts=(), kind=jnp.bfloat16):
    values = jax.random.normal(rng, shape, jnp.float32) * spread
    if len(cuts) > 0:
        values = levels(rng, shape, cuts, -0.22, 0.18) * values
    return jnp.clip(values, min=-bound, max=bound).astype(kind)


def setup_inputs(seed: int = 0, part: int = 0) -> dict:
    key_list = jax.random.split(jax.random.key(seed), 9)
    part_splits = jax.random.split(jax.random.fold_in(key_list[8], part), 9)
    hidden_in = draw_hidden_in(jax.random.fold_in(jax.random.fold_in(key_list[8], part), 71), part)
    norm_gain = jnp.clip(1.0 + 0.18 * jax.random.normal(key_list[1], (D,), jnp.float32), 0.099609375, 1.8984375).astype(jnp.bfloat16)
    qkv_weight = bell_draw(key_list[2], (D, QKV), D ** -0.5, 0.0625, ((0, 2), (1, 4)))
    out_weight = bell_draw(key_list[3], (D, D), D ** -0.5, 0.0625, ((0, 2), (1, 4)))
    key_cache = draw_key_cache(jax.random.fold_in(jax.random.fold_in(key_list[8], part), 71), part)
    value_cache = bell_draw(part_splits[5], (REQUESTS, CACHE, KV_HEADS * HEAD_DIM), 1.0, 4.0, ((0, 4), (2, 2)))
    cache_lengths = uneven(part_splits[6], REQUESTS, REQUESTS * CACHE // 2, CACHE, 2).astype(jnp.int32)
    slot_request = jax.random.permutation(part_splits[7], REQUESTS).astype(jnp.int32)
    return dict(hidden_in=hidden_in, norm_gain=norm_gain, qkv_weight=qkv_weight, out_weight=out_weight, key_cache=key_cache, value_cache=value_cache, cache_lengths=cache_lengths, slot_request=slot_request)


EPSILON = 1e-05
THETA = 500000.0

def rope_tables(lengths, head_dim):
    half_dim = head_dim // 2
    inv_freq = jnp.exp(-jnp.log(jnp.float32(THETA)) * jnp.arange(half_dim, dtype=jnp.float32) / half_dim)
    phases = lengths.astype(jnp.float32)[:, None] * inv_freq[None, :]
    return (jnp.cos(phases), jnp.sin(phases))

def rotate(vector, cos_vals, sine_vals):
    half_dim = vector.shape[-1] // 2
    front_half = vector[..., :half_dim]
    back_half = vector[..., half_dim:]
    return jnp.concatenate([front_half * cos_vals - back_half * sine_vals, back_half * cos_vals + front_half * sine_vals], axis=-1)

def reference(hidden_in, norm_gain, qkv_weight, out_weight, key_cache, value_cache, cache_lengths, slot_request):
    residual = hidden_in.astype(jnp.float32)
    mean_square = lax.optimization_barrier(jnp.mean(residual * residual, axis=1, keepdims=True))
    normed = (residual * lax.rsqrt(mean_square + EPSILON) * norm_gain.astype(jnp.float32)[None, :]).astype(jnp.bfloat16)
    projected_in = jnp.dot(normed, qkv_weight, preferred_element_type=jnp.float32).astype(jnp.bfloat16)
    slot_count = hidden_in.shape[0]
    per_group = HEADS // KV_HEADS
    grouped = jnp.take(projected_in, slot_request, axis=0).reshape(slot_count, KV_HEADS, per_group + 2, HEAD_DIM)
    cos_vals, sine_vals = rope_tables(cache_lengths, HEAD_DIM)
    queries = rotate(grouped[:, :, :per_group].astype(jnp.float32), cos_vals[:, None, None, :], sine_vals[:, None, None, :]).astype(jnp.bfloat16)
    new_keys = rotate(grouped[:, :, per_group].astype(jnp.float32), cos_vals[:, None, :], sine_vals[:, None, :]).astype(jnp.bfloat16)
    new_values = grouped[:, :, per_group + 1]
    cache_keys = key_cache.reshape(slot_count, CACHE, KV_HEADS, HEAD_DIM).astype(jnp.float32)
    cache_values = value_cache.reshape(slot_count, CACHE, KV_HEADS, HEAD_DIM).astype(jnp.float32)
    factor = HEAD_DIM ** (-0.5)
    cache_scores = jnp.einsum('sghd,slgd->sghl', queries.astype(jnp.float32), cache_keys) * factor
    own_scores = lax.optimization_barrier(jnp.sum(queries.astype(jnp.float32) * new_keys.astype(jnp.float32)[:, :, None, :], axis=-1)) * factor
    in_cache = lax.broadcasted_iota(jnp.int32, (slot_count, CACHE), 1) < cache_lengths[:, None]
    cache_scores = jnp.where(in_cache[:, None, None, :], cache_scores, -1e+30)
    row_max = jnp.maximum(lax.optimization_barrier(jnp.max(cache_scores, axis=-1)), own_scores)
    cache_exp = jnp.exp(cache_scores - row_max[..., None])
    own_exp = jnp.exp(own_scores - row_max)
    denominator = lax.optimization_barrier(jnp.sum(cache_exp, axis=-1)) + own_exp
    cache_weight = (cache_exp / denominator[..., None]).astype(jnp.bfloat16)
    own_weight = (own_exp / denominator).astype(jnp.bfloat16)
    combined = jnp.einsum('sghl,slgd->sghd', cache_weight.astype(jnp.float32), cache_values)
    combined = combined + own_weight.astype(jnp.float32)[..., None] * new_values.astype(jnp.float32)[:, :, None, :]
    attention = combined.astype(jnp.bfloat16).reshape(slot_count, HEADS * HEAD_DIM)
    inverse = jnp.argsort(slot_request).astype(jnp.int32)
    by_request = jnp.take(attention, inverse, axis=0)
    projected = jnp.dot(by_request, out_weight, preferred_element_type=jnp.float32)
    hidden = (residual + projected).astype(jnp.bfloat16)
    return jnp.stack([hidden, attention])
```

```python
import functools

import jax
import jax.numpy as jnp
from jax import lax
from jax.experimental import pallas as pl
from jax.experimental.pallas import tpu as pltpu
from jax.sharding import PartitionSpec as P

D = 8192
HEADS = 64
KV_HEADS = 8
HEAD_DIM = 128
QKV = 10240


EPSILON = 1e-05
THETA = 500000.0


def swapped(value, axis, bit):
    mask = 2**bit
    pairs = [(source, source ^ mask) for source in range(lax.axis_size(axis))]
    return lax.ppermute(value, axis, pairs)


def rope_tables(lengths, head_dim):
    half_dim = head_dim // 2
    inv_freq = jnp.exp(
        -jnp.log(jnp.float32(THETA)) * jnp.arange(half_dim, dtype=jnp.float32) / half_dim
    )
    phases = lengths.astype(jnp.float32)[:, None] * inv_freq[None, :]
    return (jnp.cos(phases), jnp.sin(phases))


def rotate(vector, cos_vals, sine_vals):
    half_dim = vector.shape[-1] // 2
    front_half = vector[..., :half_dim]
    back_half = vector[..., half_dim:]
    return jnp.concatenate(
        [
            front_half * cos_vals - back_half * sine_vals,
            back_half * cos_vals + front_half * sine_vals,
        ],
        axis=-1,
    )


def attend(packed, key_block, value_block, lengths):
    slot_count = packed.shape[0]
    cache_size = key_block.shape[1]
    groups = key_block.shape[2] // HEAD_DIM
    per_group = HEADS // KV_HEADS
    grouped = packed.reshape(slot_count, groups, per_group + 2, HEAD_DIM)
    cos_vals, sine_vals = rope_tables(lengths, HEAD_DIM)
    queries = rotate(
        grouped[:, :, :per_group].astype(jnp.float32),
        cos_vals[:, None, None, :],
        sine_vals[:, None, None, :],
    ).astype(jnp.bfloat16)
    new_keys = rotate(
        grouped[:, :, per_group].astype(jnp.float32), cos_vals[:, None, :], sine_vals[:, None, :]
    ).astype(jnp.bfloat16)
    new_values = grouped[:, :, per_group + 1]
    cache_keys = key_block.reshape(slot_count, cache_size, groups, HEAD_DIM)
    cache_values = value_block.reshape(slot_count, cache_size, groups, HEAD_DIM)
    factor = HEAD_DIM ** (-0.5)
    cache_scores = (
        jnp.einsum("sghd,slgd->sghl", queries, cache_keys, preferred_element_type=jnp.float32)
        * factor
    )
    own_scores = (
        jnp.einsum("sghd,sgd->sgh", queries, new_keys, preferred_element_type=jnp.float32) * factor
    )
    in_cache = lax.broadcasted_iota(jnp.int32, (slot_count, cache_size), 1) < lengths[:, None]
    cache_scores = jnp.where(in_cache[:, None, None, :], cache_scores, -1e30)
    row_max = jnp.maximum(jnp.max(cache_scores, axis=-1), own_scores)
    cache_exp = jnp.exp(cache_scores - row_max[..., None])
    own_exp = jnp.exp(own_scores - row_max)
    denominator = jnp.sum(cache_exp, axis=-1) + own_exp
    cache_weight = (cache_exp / denominator[..., None]).astype(jnp.bfloat16)
    own_weight = (own_exp / denominator).astype(jnp.bfloat16)
    combined = jnp.einsum(
        "sghl,slgd->sghd", cache_weight, cache_values, preferred_element_type=jnp.float32
    )
    combined = (
        combined
        + own_weight.astype(jnp.float32)[..., None] * new_values.astype(jnp.float32)[:, :, None, :]
    )
    return combined.astype(jnp.bfloat16).reshape(slot_count, groups * per_group * HEAD_DIM)


def general_plan(
    hidden_in,
    norm_gain,
    qkv_weight,
    out_weight,
    key_cache,
    value_cache,
    cache_lengths,
    slot_request,
):
    side_index = lax.axis_index("side")
    is_weight = side_index == 0
    col_count = lax.axis_size("col")
    row_count = lax.axis_size("row")
    group_cols = col_count // row_count
    in_half = qkv_weight.shape[1] // 2
    out_half = out_weight.shape[1] // 2
    residual = hidden_in.astype(jnp.float32)
    square_sums = lax.psum(jnp.sum(residual * residual, axis=1), "row")
    normed = (
        residual
        * lax.rsqrt(square_sums[:, None] / D + EPSILON)
        * norm_gain.astype(jnp.float32)[None, :]
    ).astype(jnp.bfloat16)
    in_weight = lax.dynamic_slice_in_dim(qkv_weight, side_index * in_half, in_half, 1)
    partial_in = jnp.dot(
        lax.all_gather(normed, "col", axis=0, tiled=True),
        in_weight,
        preferred_element_type=jnp.float32,
    )
    in_slots = jnp.take(partial_in, slot_request, axis=0)
    own_width = QKV // row_count
    summed = lax.psum(in_slots.astype(jnp.bfloat16), "row")
    spread = lax.all_to_all(summed, "col", split_axis=0, concat_axis=1, tiled=True)
    own_columns = lax.dynamic_slice_in_dim(
        spread.reshape(spread.shape[0], col_count, in_half),
        lax.axis_index("row") * group_cols,
        group_cols,
        1,
    )
    slot_half = key_cache.shape[0] // 2
    halves = lax.all_to_all(
        own_columns[:, :, None, :], "side", split_axis=0, concat_axis=2, tiled=True
    )
    arrived = halves.reshape(slot_half, own_width)
    first_slot = side_index * slot_half
    key_part = lax.dynamic_slice_in_dim(key_cache, first_slot, slot_half, 0)
    value_part = lax.dynamic_slice_in_dim(value_cache, first_slot, slot_half, 0)
    length_part = lax.dynamic_slice_in_dim(cache_lengths, first_slot, slot_half, 0)
    attended = attend(arrived, key_part, value_part, length_part)
    out_cols = lax.dynamic_slice_in_dim(out_weight, side_index * out_half, out_half, 1)
    collected = lax.all_gather(attended, ("col", "side"), axis=0, tiled=True)
    out_slots = jnp.dot(collected, out_cols, preferred_element_type=jnp.float32)
    inverse = jnp.argsort(slot_request)
    out_requests = jnp.take(out_slots, inverse, axis=0)
    spread_out = lax.all_to_all(
        out_requests.astype(jnp.bfloat16), "col", split_axis=0, concat_axis=1, tiled=True
    ).astype(out_requests.dtype)
    out_view = spread_out.reshape(spread_out.shape[0], col_count, out_half)
    summed_out = lax.psum_scatter(
        out_view.astype(jnp.bfloat16), "row", scatter_dimension=1, tiled=True
    ).astype(jnp.float32)
    req_rows = hidden_in.shape[0]
    residual_view = residual.reshape(req_rows, group_cols, 2, out_half)
    residual_half = lax.dynamic_index_in_dim(residual_view, side_index, 2, keepdims=False)
    own_hidden = (residual_half + summed_out).astype(jnp.bfloat16)
    payload = jnp.where(is_weight, attended, own_hidden.reshape(attended.shape))
    received = swapped(payload, "side", 0)
    hidden = jnp.stack([own_hidden, received.reshape(own_hidden.shape)], axis=2).reshape(
        req_rows, residual.shape[1]
    )
    attention_rows = jnp.concatenate([received, attended], axis=0)
    result = jnp.where(is_weight, hidden, attention_rows)
    return result[None]


GROUP = HEADS // KV_HEADS
GROUP_WIDTH = (GROUP + 2) * HEAD_DIM
OUT_WIDTH = GROUP * HEAD_DIM
SLOTS = 8
VMEM = pl.BlockSpec(memory_space=pltpu.VMEM)
SMEM = pl.BlockSpec(memory_space=pltpu.SMEM)
HBM = pl.BlockSpec(memory_space=pl.ANY)
MIB = 2**20


def call(kernel, out_shape, in_specs, out_specs, flops, size, scratch=(), limit=16):
    return pl.pallas_call(
        kernel,
        out_shape=out_shape,
        in_specs=in_specs,
        out_specs=out_specs,
        scratch_shapes=list(scratch),
        compiler_params=pltpu.CompilerParams(vmem_limit_bytes=limit * MIB),
        cost_estimate=pl.CostEstimate(flops=flops, bytes_accessed=size, transcendentals=0),
    )


def in_vmem(value):
    return pltpu.with_memory_space_constraint(value, pltpu.VMEM)


def struct(shape, dtype=jnp.bfloat16):
    return jax.ShapeDtypeStruct(shape, dtype)


def moved(value, axis, mask):
    pairs = [(source, source ^ mask) for source in range(lax.axis_size(axis))]
    return lax.ppermute(value, axis, pairs)


def stage_in_kernel(place, weight, staged, sem):
    depth = staged.shape[0]
    first = pl.multiple_of(place[0] * depth, depth)
    copy = pltpu.make_async_copy(weight.at[pl.ds(first, depth), :], staged, sem)
    copy.start()
    copy.wait()


def stage_rest_kernel(place, weight, keys, values, staged, key_part, value_part, sems):
    pairs = staged.shape[0] // OUT_WIDTH
    copies = []
    for j in range(pairs):
        head = 2 * j + place[0]
        row = pl.multiple_of(head * OUT_WIDTH, OUT_WIDTH)
        lane = pl.multiple_of(head * HEAD_DIM, HEAD_DIM)
        for source, target in ((keys, key_part), (values, value_part)):
            copies.append(
                (
                    source.at[:, :, pl.ds(lane, HEAD_DIM)],
                    target.at[:, :, pl.ds(j * HEAD_DIM, HEAD_DIM)],
                )
            )
        copies.append(
            (weight.at[pl.ds(row, OUT_WIDTH), :], staged.at[pl.ds(j * OUT_WIDTH, OUT_WIDTH), :])
        )
    copies = [
        pltpu.make_async_copy(source, target, sems.at[i])
        for i, (source, target) in enumerate(copies)
    ]
    for copy in copies:
        copy.start()
    for copy in copies:
        copy.wait()


def square_kernel(hidden, total):
    values = hidden[...].astype(jnp.float32)
    sums = jnp.sum(values * values, axis=1, keepdims=True)
    total[...] = jnp.broadcast_to(sums, total.shape)


def one_hot(place, slots, request_axis_size):
    col = place[1]
    blocks, rows, _ = slots.shape
    lane = lax.broadcasted_iota(jnp.int32, (rows, request_axis_size), 1)
    request = (lax.div(lane, rows) ^ col) * rows + lax.rem(lane, rows)
    parts = [
        jnp.where(slots[col ^ block] == request, 1.0, 0.0) for block in range(blocks)
    ]
    return jnp.concatenate(parts, axis=0)


def dot_columns(rows, weight, first, out, width):
    def step(i, carry):
        start = pl.multiple_of(i * width, width)
        part = jnp.dot(
            rows,
            weight[:, pl.ds(pl.multiple_of(first + start, width), width)],
            preferred_element_type=jnp.float32,
        )
        out[:, pl.ds(start, width)] = part.astype(out.dtype)
        return carry

    lax.fori_loop(0, out.shape[1] // width, step, 0)


def project_kernel(count, transpose, scaled, place, slots, *refs):
    blocks = refs[:count]
    refs = refs[count:]
    if scaled:
        scales, gain, refs = refs[:count], refs[count], refs[count + 1 :]
    weight, give, permuted = refs
    side = place[0]
    rows, depth = blocks[0].shape
    parts = []
    for i, block in enumerate(blocks):
        value = block[...]
        if scaled:
            gains = gain[:, pl.ds(pl.multiple_of(side * depth, depth), depth)]
            value = (
                value.astype(jnp.float32) * scales[i][:, :1] * gains.astype(jnp.float32)
            ).astype(jnp.bfloat16)
        parts.append(value)
    gathered = jnp.concatenate(parts, axis=0)
    chosen = one_hot(place, slots, rows * count)
    chosen = (chosen.T if transpose else chosen).astype(jnp.bfloat16)
    order = jnp.dot(chosen, gathered, preferred_element_type=jnp.float32).astype(jnp.bfloat16)
    permuted[...] = order
    dot_columns(order, weight, (1 - side) * give.shape[1], give, 256)


def own_kernel(place, permuted, weight, own):
    dot_columns(permuted[...], weight, place[0] * own.shape[1], own, 256)


def project(place, slots, blocks, scales, gain, weight, transpose):
    count = len(blocks)
    rows, depth = blocks[0].shape
    rows = rows * count
    half = weight.shape[1] // 2
    flops = 2 * rows * depth * half
    scaled = scales is not None
    extra = [*scales, gain] if scaled else []
    give, permuted = call(
        functools.partial(project_kernel, count, transpose, scaled),
        [struct((rows, half)), struct((rows, depth))],
        [SMEM, VMEM] + [VMEM] * (count + len(extra) + 1),
        [VMEM, VMEM],
        flops,
        depth * half * 2,
    )(place, slots, *blocks, *extra, in_vmem(weight))
    received = moved(give, "side", 1)
    own = call(
        own_kernel,
        struct((rows, half), jnp.float32),
        [SMEM, VMEM, VMEM],
        VMEM,
        flops,
        depth * half * 2,
    )(place, permuted, in_vmem(weight))
    total = (own + received.astype(jnp.float32)).astype(jnp.bfloat16)
    return total.reshape(count, rows // count, half)


def rotated(vector, cosine, sine):
    return vector * cosine + pltpu.roll(vector, HEAD_DIM // 2, 1) * sine


def attend_all(count, place, cosine, sine, lengths, *refs):
    kept, (arrived, keys, values, out) = refs[:count], refs[count:]
    others, pairs, rows, _ = arrived.shape
    cache = keys.shape[1]
    base = place[2]
    low = place[1] % pairs
    factor = HEAD_DIM ** (-0.5)
    cosines, sines = cosine[...], sine[...]
    lane = lax.broadcasted_iota(jnp.int32, (SLOTS, SLOTS * cache), 1)
    slot = lax.broadcasted_iota(jnp.int32, (SLOTS, SLOTS * cache), 0)
    for pair in range(pairs):
        column = low ^ pair
        total = jnp.zeros(arrived.shape[2:], jnp.float32)
        for chunk in range(count // pairs):
            part = kept[chunk * pairs + pair][...].astype(jnp.float32)
            total = total + jnp.where(base == chunk, part, 0.0)
        for other in range(others):
            total = total + arrived[other, pair].astype(jnp.float32)
        total = total.astype(jnp.bfloat16).astype(jnp.float32)
        heads = [total[:, h * HEAD_DIM : (h + 1) * HEAD_DIM] for h in range(GROUP + 2)]
        queries = [
            rotated(head, cosines, sines).astype(jnp.bfloat16).astype(jnp.float32)
            for head in heads[:GROUP]
        ]
        new_key = rotated(heads[GROUP], cosines, sines).astype(jnp.bfloat16).astype(jnp.float32)
        new_value = heads[GROUP + 1]
        own = [jnp.sum(query * new_key, axis=1, keepdims=True) * factor for query in queries]
        lanes = pl.ds(pl.multiple_of(column * HEAD_DIM, HEAD_DIM), HEAD_DIM)
        results = []
        for start in range(0, rows, SLOTS):
            part = slice(start, start + SLOTS)
            query = jnp.concatenate([head[part] for head in queries], axis=0)
            key = keys[start : start + SLOTS, :, lanes].reshape(SLOTS * cache, HEAD_DIM)
            value = values[start : start + SLOTS, :, lanes].reshape(SLOTS * cache, HEAD_DIM)
            scores = (
                lax.dot_general(
                    query.astype(jnp.bfloat16),
                    key,
                    (((1,), (1,)), ((), ())),
                    preferred_element_type=jnp.float32,
                )
                * factor
            ).reshape(GROUP, SLOTS, SLOTS * cache)
            position = lane - slot * cache
            filled = (position >= 0) & (position < lengths[part])
            scores = jnp.where(filled[None], scores, -1e30)
            own_score = jnp.concatenate([head[part] for head in own], axis=0).reshape(
                GROUP, SLOTS, 1
            )
            highest = jnp.maximum(jnp.max(scores, axis=2, keepdims=True), own_score)
            weights = jnp.exp(scores - highest)
            own_weight = jnp.exp(own_score - highest)
            inverse = 1.0 / (jnp.sum(weights, axis=2, keepdims=True) + own_weight)
            probs = (weights * inverse).astype(jnp.bfloat16)
            own_prob = (own_weight * inverse).astype(jnp.bfloat16).astype(jnp.float32)
            mixed = jnp.dot(
                probs.reshape(GROUP * SLOTS, SLOTS * cache),
                value,
                preferred_element_type=jnp.float32,
            ).reshape(GROUP, SLOTS, HEAD_DIM)
            results.append(mixed + own_prob * new_value[part][None])
        for head in range(GROUP):
            joined = jnp.concatenate([result[head] for result in results], axis=0)
            at = pl.multiple_of(column * OUT_WIDTH + head * HEAD_DIM, HEAD_DIM)
            out[:, pl.ds(at, HEAD_DIM)] = joined.astype(jnp.bfloat16)


def finish_kernel(count, others, place, hidden, attended, given, *refs):
    kept, refs = refs[:count], refs[count:]
    near, refs = refs[0], refs[1:]
    same, cross, out = refs[:others], refs[others : 2 * others], refs[2 * others]
    pairs, _, width = near.shape
    base = place[2]
    low = place[1] % pairs

    @pl.when(place[0] == 0)
    def _():
        for pair in range(pairs):
            column = low ^ pair
            total = jnp.zeros(near.shape[1:], jnp.float32)
            for chunk in range(count // pairs):
                part = kept[chunk * pairs + pair][...].astype(jnp.float32)
                total = total + jnp.where(base == chunk, part, 0.0)
            for ref in same:
                total = total + ref[pair].astype(jnp.float32)
            first = pl.ds(pl.multiple_of(column * 2 * width, width), width)
            out[0, :, first] = (hidden[:, first].astype(jnp.float32) + total).astype(jnp.bfloat16)
            total = near[pair].astype(jnp.float32)
            for ref in cross:
                total = total + ref[pair].astype(jnp.float32)
            second = pl.ds(pl.multiple_of((column * 2 + 1) * width, width), width)
            out[0, :, second] = (hidden[:, second].astype(jnp.float32) + total).astype(
                jnp.bfloat16
            )

    @pl.when(place[0] != 0)
    def _():
        size = OUT_WIDTH
        for j in range(attended.shape[1] // size):
            out[0, :, 2 * j * size : (2 * j + 1) * size] = given[:, j * size : (j + 1) * size]
            out[0, :, (2 * j + 1) * size : (2 * j + 2) * size] = attended[
                :, j * size : (j + 1) * size
            ]


def chunk_of(blocks, pairs, index):
    chunks = [jnp.stack(blocks[i : i + pairs]) for i in range(0, len(blocks), pairs)]
    chosen = chunks[0]
    for i, chunk in enumerate(chunks[1:], 1):
        chosen = jnp.where(index == i, chunk, chosen)
    return chosen


def paired_plan(
    hidden_in, norm_gain, qkv_weight, out_weight, key_cache, value_cache, cache_lengths, slot_request
):
    col_count, row_count = lax.axis_size("col"), lax.axis_size("row")
    pairs = col_count // row_count
    side, col, row = (lax.axis_index(name) for name in ("side", "col", "row"))
    base = lax.div(col, pairs) ^ row
    place = jnp.stack([side, col, base]).astype(jnp.int32)
    rows, depth = hidden_in.shape
    half = depth // 2
    cache = key_cache.shape[1]
    slots = slot_request.reshape(col_count, rows, 1)

    own_part = lax.dynamic_slice_in_dim(hidden_in, side * half, half, 1)
    blocks = [own_part] + [moved(own_part, "col", mask) for mask in range(1, col_count)]
    squares = call(
        square_kernel, struct((rows, 128), jnp.float32), [VMEM], VMEM, rows * depth * 2, rows * depth * 2
    )(hidden_in)
    total = squares
    for mask in range(1, row_count):
        total = total + moved(squares, "row", mask)
    scale = lax.rsqrt(total / D + EPSILON)
    scales = [scale] + [moved(scale, "col", mask) for mask in range(1, col_count)]

    weight_in = call(
        stage_in_kernel,
        pltpu.VMEM((half, qkv_weight.shape[1]), jnp.bfloat16),
        [SMEM, HBM],
        VMEM,
        0,
        half * qkv_weight.shape[1] * 2,
        [pltpu.SemaphoreType.DMA],
    )(place, qkv_weight)
    weight_out, key_part, value_part = call(
        stage_rest_kernel,
        [
            pltpu.VMEM((half, out_weight.shape[1]), jnp.bfloat16),
            pltpu.VMEM((rows, cache, pairs * HEAD_DIM), jnp.bfloat16),
            pltpu.VMEM((rows, cache, pairs * HEAD_DIM), jnp.bfloat16),
        ],
        [SMEM, HBM, HBM, HBM],
        [VMEM, VMEM, VMEM],
        0,
        half * out_weight.shape[1] * 2 + 4 * rows * cache * pairs * HEAD_DIM,
        [pltpu.SemaphoreType.DMA((3 * pairs,))],
    )(place, out_weight, key_cache, value_cache)

    products = project(
        place, slots, blocks, scales, norm_gain.reshape(1, depth), weight_in, False
    )
    products = [products[0]] + [
        moved(products[mask], "col", mask) for mask in range(1, col_count)
    ]
    arrived = jnp.stack(
        [
            moved(chunk_of(products, pairs, base ^ mask), "row", mask)
            for mask in range(1, row_count)
        ]
    )

    cosine, sine = rope_tables(cache_lengths, HEAD_DIM)
    attended = call(
        functools.partial(attend_all, col_count),
        struct((rows, half)),
        [SMEM] + [VMEM] * (3 + col_count + 3),
        VMEM,
        4 * rows * half * cache,
        0,
    )(
        place,
        jnp.concatenate([cosine, cosine], axis=1),
        jnp.concatenate([-sine, sine], axis=1),
        cache_lengths.reshape(rows, 1),
        *products,
        arrived,
        in_vmem(key_part),
        in_vmem(value_part),
    )

    given = lax.ppermute(attended, "side", [(0, 1)])
    blocks = [attended] + [moved(attended, "col", mask) for mask in range(1, col_count)]
    products = project(place, slots, blocks, None, None, weight_out, True)
    products = [products[0]] + [
        moved(products[mask], "col", mask) for mask in range(1, col_count)
    ]
    near = lax.ppermute(chunk_of(products, pairs, base), "side", [(1, 0)])
    same, cross = [], []
    for mask in range(1, row_count):
        chunk = chunk_of(products, pairs, base ^ mask)
        for target, side_from in ((same, 0), (cross, 1)):
            target.append(
                lax.ppermute(
                    chunk,
                    ("row", "side"),
                    [(2 * r + side_from, 2 * (r ^ mask)) for r in range(row_count)],
                )
            )
    return call(
        functools.partial(finish_kernel, col_count, row_count - 1),
        struct((1, rows, depth)),
        [SMEM] + [VMEM] * (3 + col_count + 1 + 2 * (row_count - 1)),
        VMEM,
        rows * depth * 4,
        rows * depth * 8,
    )(place, hidden_in, attended, given, *products, near, *same, *cross)


def per_device(*args):
    hidden_in, _, qkv_weight, out_weight, key_cache = args[:5]
    col_count, row_count = lax.axis_size("col"), lax.axis_size("row")
    fits = (
        lax.axis_size("side") == 2
        and qkv_weight.shape[1] == 2 * GROUP_WIDTH
        and col_count % row_count == 0
        and col_count & (col_count - 1) == 0
        and hidden_in.shape[0] % 16 == 0
        and key_cache.shape[1] % 16 == 0
        and hidden_in.shape[1] == 2 * OUT_WIDTH * (col_count // row_count)
    )
    return paired_plan(*args) if fits else general_plan(*args)


def solution(mesh):
    placed = (
        P(("groups", "col"), "row"),
        P("row"),
        P("row", "col"),
        P("row", "col"),
        P(("groups", "col"), None, "row"),
        P(("groups", "col"), None, "row"),
        P(("groups", "col")),
        P("groups"),
    )
    return jax.shard_map(
        per_device,
        mesh=mesh,
        in_specs=placed,
        out_specs=P("side", ("groups", "col"), "row"),
        check_vma=False,
    )
```

```python
import functools

import jax
import jax.numpy as jnp
from jax import lax
from jax.experimental import pallas as pl
from jax.experimental.pallas import tpu as pltpu
from jax.sharding import PartitionSpec as P

D = 8192
HEADS = 64
KV_HEADS = 8
HEAD_DIM = 128
QKV = 10240


EPSILON = 1e-05
THETA = 500000.0


def swapped(value, axis, bit):
    mask = 2**bit
    pairs = [(source, source ^ mask) for source in range(lax.axis_size(axis))]
    return lax.ppermute(value, axis, pairs)


def rope_tables(lengths, head_dim):
    half_dim = head_dim // 2
    inv_freq = jnp.exp(
        -jnp.log(jnp.float32(THETA)) * jnp.arange(half_dim, dtype=jnp.float32) / half_dim
    )
    phases = lengths.astype(jnp.float32)[:, None] * inv_freq[None, :]
    return (jnp.cos(phases), jnp.sin(phases))


def rotate(vector, cos_vals, sine_vals):
    half_dim = vector.shape[-1] // 2
    front_half = vector[..., :half_dim]
    back_half = vector[..., half_dim:]
    return jnp.concatenate(
        [
            front_half * cos_vals - back_half * sine_vals,
            back_half * cos_vals + front_half * sine_vals,
        ],
        axis=-1,
    )


def attend(packed, key_block, value_block, lengths):
    slot_count = packed.shape[0]
    cache_size = key_block.shape[1]
    groups = key_block.shape[2] // HEAD_DIM
    per_group = HEADS // KV_HEADS
    grouped = packed.reshape(slot_count, groups, per_group + 2, HEAD_DIM)
    cos_vals, sine_vals = rope_tables(lengths, HEAD_DIM)
    queries = rotate(
        grouped[:, :, :per_group].astype(jnp.float32),
        cos_vals[:, None, None, :],
        sine_vals[:, None, None, :],
    ).astype(jnp.bfloat16)
    new_keys = rotate(
        grouped[:, :, per_group].astype(jnp.float32), cos_vals[:, None, :], sine_vals[:, None, :]
    ).astype(jnp.bfloat16)
    new_values = grouped[:, :, per_group + 1]
    cache_keys = key_block.reshape(slot_count, cache_size, groups, HEAD_DIM)
    cache_values = value_block.reshape(slot_count, cache_size, groups, HEAD_DIM)
    factor = HEAD_DIM ** (-0.5)
    cache_scores = (
        jnp.einsum("sghd,slgd->sghl", queries, cache_keys, preferred_element_type=jnp.float32)
        * factor
    )
    own_scores = (
        jnp.einsum("sghd,sgd->sgh", queries, new_keys, preferred_element_type=jnp.float32) * factor
    )
    in_cache = lax.broadcasted_iota(jnp.int32, (slot_count, cache_size), 1) < lengths[:, None]
    cache_scores = jnp.where(in_cache[:, None, None, :], cache_scores, -1e30)
    row_max = jnp.maximum(jnp.max(cache_scores, axis=-1), own_scores)
    cache_exp = jnp.exp(cache_scores - row_max[..., None])
    own_exp = jnp.exp(own_scores - row_max)
    denominator = jnp.sum(cache_exp, axis=-1) + own_exp
    cache_weight = (cache_exp / denominator[..., None]).astype(jnp.bfloat16)
    own_weight = (own_exp / denominator).astype(jnp.bfloat16)
    combined = jnp.einsum(
        "sghl,slgd->sghd", cache_weight, cache_values, preferred_element_type=jnp.float32
    )
    combined = (
        combined
        + own_weight.astype(jnp.float32)[..., None] * new_values.astype(jnp.float32)[:, :, None, :]
    )
    return combined.astype(jnp.bfloat16).reshape(slot_count, groups * per_group * HEAD_DIM)


def general_plan(
    hidden_in,
    norm_gain,
    qkv_weight,
    out_weight,
    key_cache,
    value_cache,
    cache_lengths,
    slot_request,
):
    side_index = lax.axis_index("side")
    is_weight = side_index == 0
    col_count = lax.axis_size("col")
    row_count = lax.axis_size("row")
    group_cols = col_count // row_count
    in_half = qkv_weight.shape[1] // 2
    out_half = out_weight.shape[1] // 2
    residual = hidden_in.astype(jnp.float32)
    square_sums = lax.psum(jnp.sum(residual * residual, axis=1), "row")
    normed = (
        residual
        * lax.rsqrt(square_sums[:, None] / D + EPSILON)
        * norm_gain.astype(jnp.float32)[None, :]
    ).astype(jnp.bfloat16)
    in_weight = lax.dynamic_slice_in_dim(qkv_weight, side_index * in_half, in_half, 1)
    partial_in = jnp.dot(
        lax.all_gather(normed, "col", axis=0, tiled=True),
        in_weight,
        preferred_element_type=jnp.float32,
    )
    in_slots = jnp.take(partial_in, slot_request, axis=0)
    own_width = QKV // row_count
    summed = lax.psum(in_slots.astype(jnp.bfloat16), "row")
    spread = lax.all_to_all(summed, "col", split_axis=0, concat_axis=1, tiled=True)
    own_columns = lax.dynamic_slice_in_dim(
        spread.reshape(spread.shape[0], col_count, in_half),
        lax.axis_index("row") * group_cols,
        group_cols,
        1,
    )
    slot_half = key_cache.shape[0] // 2
    halves = lax.all_to_all(
        own_columns[:, :, None, :], "side", split_axis=0, concat_axis=2, tiled=True
    )
    arrived = halves.reshape(slot_half, own_width)
    first_slot = side_index * slot_half
    key_part = lax.dynamic_slice_in_dim(key_cache, first_slot, slot_half, 0)
    value_part = lax.dynamic_slice_in_dim(value_cache, first_slot, slot_half, 0)
    length_part = lax.dynamic_slice_in_dim(cache_lengths, first_slot, slot_half, 0)
    attended = attend(arrived, key_part, value_part, length_part)
    out_cols = lax.dynamic_slice_in_dim(out_weight, side_index * out_half, out_half, 1)
    collected = lax.all_gather(attended, ("col", "side"), axis=0, tiled=True)
    out_slots = jnp.dot(collected, out_cols, preferred_element_type=jnp.float32)
    inverse = jnp.argsort(slot_request)
    out_requests = jnp.take(out_slots, inverse, axis=0)
    spread_out = lax.all_to_all(
        out_requests.astype(jnp.bfloat16), "col", split_axis=0, concat_axis=1, tiled=True
    ).astype(out_requests.dtype)
    out_view = spread_out.reshape(spread_out.shape[0], col_count, out_half)
    summed_out = lax.psum_scatter(
        out_view.astype(jnp.bfloat16), "row", scatter_dimension=1, tiled=True
    ).astype(jnp.float32)
    req_rows = hidden_in.shape[0]
    residual_view = residual.reshape(req_rows, group_cols, 2, out_half)
    residual_half = lax.dynamic_index_in_dim(residual_view, side_index, 2, keepdims=False)
    own_hidden = (residual_half + summed_out).astype(jnp.bfloat16)
    payload = jnp.where(is_weight, attended, own_hidden.reshape(attended.shape))
    received = swapped(payload, "side", 0)
    hidden = jnp.stack([own_hidden, received.reshape(own_hidden.shape)], axis=2).reshape(
        req_rows, residual.shape[1]
    )
    attention_rows = jnp.concatenate([received, attended], axis=0)
    result = jnp.where(is_weight, hidden, attention_rows)
    return result[None]


GROUP = HEADS // KV_HEADS
GROUP_WIDTH = (GROUP + 2) * HEAD_DIM
OUT_WIDTH = GROUP * HEAD_DIM
SLOTS = 8
VMEM = pl.BlockSpec(memory_space=pltpu.VMEM)
SMEM = pl.BlockSpec(memory_space=pltpu.SMEM)
HBM = pl.BlockSpec(memory_space=pl.ANY)
MIB = 2**20


def call(kernel, out_shape, in_specs, out_specs, flops, size, scratch=(), limit=16):
    return pl.pallas_call(
        kernel,
        out_shape=out_shape,
        in_specs=in_specs,
        out_specs=out_specs,
        scratch_shapes=list(scratch),
        compiler_params=pltpu.CompilerParams(vmem_limit_bytes=limit * MIB),
        cost_estimate=pl.CostEstimate(flops=flops, bytes_accessed=size, transcendentals=0),
    )


def in_vmem(value):
    return pltpu.with_memory_space_constraint(value, pltpu.VMEM)


def in_hbm(value):
    return pltpu.with_memory_space_constraint(value, pltpu.HBM)


def struct(shape, dtype=jnp.bfloat16):
    return jax.ShapeDtypeStruct(shape, dtype)


def moved(value, axis, mask):
    pairs = [(source, source ^ mask) for source in range(lax.axis_size(axis))]
    return lax.ppermute(value, axis, pairs)


def stage_in_kernel(place, weight, staged, sem):
    depth = staged.shape[0]
    first = pl.multiple_of(place[0] * depth, depth)
    copy = pltpu.make_async_copy(weight.at[pl.ds(first, depth), :], staged, sem)
    copy.start()
    copy.wait()


def stage_rest_kernel(place, weight, keys, values, staged, key_part, value_part, sems):
    pairs = staged.shape[0] // OUT_WIDTH
    copies = []
    for j in range(pairs):
        head = 2 * j + place[0]
        row = pl.multiple_of(head * OUT_WIDTH, OUT_WIDTH)
        lane = pl.multiple_of(head * HEAD_DIM, HEAD_DIM)
        for source, target in ((keys, key_part), (values, value_part)):
            copies.append(
                (
                    source.at[:, :, pl.ds(lane, HEAD_DIM)],
                    target.at[:, :, pl.ds(j * HEAD_DIM, HEAD_DIM)],
                )
            )
        copies.append(
            (weight.at[pl.ds(row, OUT_WIDTH), :], staged.at[pl.ds(j * OUT_WIDTH, OUT_WIDTH), :])
        )
    copies = [
        pltpu.make_async_copy(source, target, sems.at[i])
        for i, (source, target) in enumerate(copies)
    ]
    for copy in copies:
        copy.start()
    for copy in copies:
        copy.wait()


def one_hot(slots, slot_base, request_base):
    blocks, rows, _ = slots.shape
    lane = lax.broadcasted_iota(jnp.int32, (rows, blocks * rows), 1)
    request = (lax.div(lane, rows) ^ request_base) * rows + lax.rem(lane, rows)
    parts = [jnp.where(slots[slot_base ^ i] == request, 1.0, 0.0) for i in range(blocks)]
    return jnp.concatenate(parts, axis=0)


def pieces(sums):
    high = sums.astype(jnp.bfloat16).astype(jnp.float32)
    middle = (sums - high).astype(jnp.bfloat16).astype(jnp.float32)
    low = sums - high - middle
    lane = lax.broadcasted_iota(jnp.int32, (sums.shape[0], HEAD_DIM), 1)
    parts = jnp.where(lane == 0, high, jnp.where(lane == 1, middle, low))
    return jnp.where(lane < 3, parts, 0.0).astype(jnp.bfloat16)


def dot_columns(rows, weight, first, out, size, width):
    def step(i, carry):
        start = pl.multiple_of(i * width, width)
        part = jnp.dot(
            rows,
            weight[:, pl.ds(pl.multiple_of(first + start, width), width)],
            preferred_element_type=jnp.float32,
        )
        out[:, pl.ds(start, width)] = part.astype(out.dtype)
        return carry

    lax.fori_loop(0, size // width, step, 0)


def in_kernel(count, place, slots, *refs):
    blocks, (gain, weight, give, permuted) = refs[:count], refs[count:]
    side = place[0]
    depth = blocks[0].shape[1]
    half = weight.shape[1] // 2
    gains = gain[:, pl.ds(pl.multiple_of(side * depth, depth), depth)].astype(jnp.float32)
    values = jnp.concatenate([block[...].astype(jnp.float32) for block in blocks], axis=0)
    sums = pieces(jnp.sum(values * values, axis=1, keepdims=True))
    chosen = one_hot(slots, place[2], place[1]).astype(jnp.bfloat16)
    order = jnp.dot(
        chosen, (values * gains).astype(jnp.bfloat16), preferred_element_type=jnp.float32
    ).astype(jnp.bfloat16)
    permuted[...] = order
    give[:, half:] = jnp.dot(chosen, sums, preferred_element_type=jnp.float32).astype(jnp.bfloat16)
    dot_columns(order, weight, (1 - side) * half, give, half, 256)


def out_kernel(count, place, slots, *refs):
    blocks, (weight, give, permuted) = refs[:count], refs[count:]
    half = weight.shape[1] // 2
    values = jnp.concatenate([block[...] for block in blocks], axis=0)
    chosen = one_hot(slots, place[1], place[2]).T.astype(jnp.bfloat16)
    order = jnp.dot(chosen, values, preferred_element_type=jnp.float32).astype(jnp.bfloat16)
    permuted[...] = order
    dot_columns(order, weight, (1 - place[0]) * half, give, half, 256)


def own_kernel(place, permuted, weight, own):
    half = own.shape[1]
    dot_columns(permuted[...], weight, place[0] * half, own, half, 256)


def project(kernel, place, slots, blocks, extra, weight, more):
    count = len(blocks)
    rows, depth = blocks[0].shape
    rows = rows * count
    half = weight.shape[1] // 2
    flops = 2 * rows * depth * half
    give, permuted = call(
        functools.partial(kernel, count),
        [struct((rows, half + more)), struct((rows, depth))],
        [SMEM, VMEM] + [VMEM] * (count + len(extra) + 1),
        [VMEM, VMEM],
        flops,
        depth * half * 2,
    )(place, slots, *blocks, *extra, in_vmem(weight))
    received = moved(give, "side", 1)
    own = call(
        own_kernel,
        struct((rows, half), jnp.float32),
        [SMEM, VMEM, VMEM],
        VMEM,
        flops,
        depth * half * 2,
    )(place, permuted, in_vmem(weight))
    total = (own + received[:, :half].astype(jnp.float32)).astype(jnp.bfloat16)
    return total.reshape(count, rows // count, half), give, received


def gathered(value, axis):
    blocks = {0: value}
    mask = lax.axis_size(axis) // 2
    while mask:
        blocks |= {known | mask: moved(block, axis, mask) for known, block in blocks.items()}
        mask //= 2
    return [blocks[i] for i in sorted(blocks)]


def spread(products):
    col_count, row_count = lax.axis_size("col"), lax.axis_size("row")
    pairs = col_count // row_count
    return [
        lax.ppermute(
            products[j],
            ("col", "row"),
            [
                (
                    col * row_count + row,
                    ((row * pairs + col % pairs) ^ j) * row_count + col // pairs,
                )
                for col in range(col_count)
                for row in range(row_count)
            ],
        )
        for j in range(col_count)
    ]


def rotated(vector, cosine, sine):
    return vector * cosine + pltpu.roll(vector, HEAD_DIM // 2, 1) * sine


def attend_all(count, others, place, cosine, sine, lengths, *refs):
    blocks, sums, (keys, values, out) = refs[:count], refs[count : count + others], refs[-3:]
    pairs = keys.shape[2] // HEAD_DIM
    rows, cache = keys.shape[:2]
    low = place[1] % pairs
    squares = sums[0][...]
    for ref in sums[1:]:
        squares = squares + ref[...]
    scale = lax.rsqrt(jnp.sum(squares, axis=1, keepdims=True) / D + EPSILON)
    factor = HEAD_DIM ** (-0.5)
    cosines, sines = cosine[...], sine[...]
    lane = lax.broadcasted_iota(jnp.int32, (SLOTS, SLOTS * cache), 1)
    slot = lax.broadcasted_iota(jnp.int32, (SLOTS, SLOTS * cache), 0)
    for pair in range(pairs):
        column = low ^ pair
        total = blocks[pair][...].astype(jnp.float32)
        for i in range(pair + pairs, count, pairs):
            total = total + blocks[i][...].astype(jnp.float32)
        total = total * scale
        total = total.astype(jnp.bfloat16).astype(jnp.float32)
        heads = [total[:, h * HEAD_DIM : (h + 1) * HEAD_DIM] for h in range(GROUP + 2)]
        queries = [
            rotated(head, cosines, sines).astype(jnp.bfloat16).astype(jnp.float32)
            for head in heads[:GROUP]
        ]
        new_key = rotated(heads[GROUP], cosines, sines).astype(jnp.bfloat16).astype(jnp.float32)
        new_value = heads[GROUP + 1]
        own = [jnp.sum(query * new_key, axis=1, keepdims=True) * factor for query in queries]
        lanes = pl.ds(pl.multiple_of(column * HEAD_DIM, HEAD_DIM), HEAD_DIM)
        results = []
        for start in range(0, rows, SLOTS):
            part = slice(start, start + SLOTS)
            query = jnp.concatenate([head[part] for head in queries], axis=0)
            key = keys[start : start + SLOTS, :, lanes].reshape(SLOTS * cache, HEAD_DIM)
            value = values[start : start + SLOTS, :, lanes].reshape(SLOTS * cache, HEAD_DIM)
            scores = (
                lax.dot_general(
                    query.astype(jnp.bfloat16),
                    key,
                    (((1,), (1,)), ((), ())),
                    preferred_element_type=jnp.float32,
                )
                * factor
            ).reshape(GROUP, SLOTS, SLOTS * cache)
            position = lane - slot * cache
            filled = (position >= 0) & (position < lengths[part])
            scores = jnp.where(filled[None], scores, -1e30)
            own_score = jnp.concatenate([head[part] for head in own], axis=0).reshape(
                GROUP, SLOTS, 1
            )
            highest = jnp.maximum(jnp.max(scores, axis=2, keepdims=True), own_score)
            weights = jnp.exp(scores - highest)
            own_weight = jnp.exp(own_score - highest)
            inverse = 1.0 / (jnp.sum(weights, axis=2, keepdims=True) + own_weight)
            probs = (weights * inverse).astype(jnp.bfloat16)
            own_prob = (own_weight * inverse).astype(jnp.bfloat16).astype(jnp.float32)
            mixed = jnp.dot(
                probs.reshape(GROUP * SLOTS, SLOTS * cache),
                value,
                preferred_element_type=jnp.float32,
            ).reshape(GROUP, SLOTS, HEAD_DIM)
            results.append(mixed + own_prob * new_value[part][None])
        for head in range(GROUP):
            joined = jnp.concatenate([result[head] for result in results], axis=0)
            at = pl.multiple_of(column * OUT_WIDTH + head * HEAD_DIM, HEAD_DIM)
            out[:, pl.ds(at, HEAD_DIM)] = joined.astype(jnp.bfloat16)


def sum_kernel(count, place, hidden, attended, *refs):
    blocks, (keep, send) = refs[:count], refs[count:]
    rows, width = blocks[0].shape
    pairs = attended.shape[1] // width
    side = place[0]
    low = place[1] % pairs
    for pair in range(pairs):
        column = low ^ pair
        total = blocks[pair][...].astype(jnp.float32)
        for i in range(pair + pairs, count, pairs):
            total = total + blocks[i][...].astype(jnp.float32)
        at = pl.ds(pl.multiple_of((2 * column + side) * width, width), width)
        hidden_out = (hidden[:, at].astype(jnp.float32) + total).astype(jnp.bfloat16)
        at = pl.ds(pl.multiple_of(column * width, width), width)
        attention = attended[:, at]
        keep[:, at] = jnp.where(side == 0, hidden_out, attention)
        send[:, at] = jnp.where(side == 0, attention, hidden_out)


def join_kernel(place, keep, received, out):
    side = place[0]
    width = OUT_WIDTH
    for j in range(keep.shape[1] // width):
        part = slice(j * width, (j + 1) * width)
        out[0, :, pl.ds(pl.multiple_of((2 * j + side) * width, width), width)] = keep[:, part]
        out[0, :, pl.ds(pl.multiple_of((2 * j + 1 - side) * width, width), width)] = received[
            :, part
        ]


def paired_plan(
    hidden_in, norm_gain, qkv_weight, out_weight, key_cache, value_cache, cache_lengths, slot_request
):
    col_count, row_count = lax.axis_size("col"), lax.axis_size("row")
    pairs = col_count // row_count
    side, col, row = (lax.axis_index(name) for name in ("side", "col", "row"))
    run = row * pairs + lax.rem(col, pairs)
    place = jnp.stack([side, col, run]).astype(jnp.int32)
    rows, depth = hidden_in.shape
    half = depth // 2
    cache = key_cache.shape[1]
    slots = slot_request.reshape(col_count, rows, 1)

    blocks = gathered(lax.dynamic_slice_in_dim(hidden_in, side * half, half, 1), "col")

    weight_in = call(
        stage_in_kernel,
        pltpu.VMEM((half, qkv_weight.shape[1]), jnp.bfloat16),
        [SMEM, HBM],
        VMEM,
        0,
        half * qkv_weight.shape[1] * 2,
        [pltpu.SemaphoreType.DMA],
    )(place, in_hbm(qkv_weight))
    weight_out, key_part, value_part = call(
        stage_rest_kernel,
        [
            pltpu.VMEM((half, out_weight.shape[1]), jnp.bfloat16),
            pltpu.VMEM((rows, cache, pairs * HEAD_DIM), jnp.bfloat16),
            pltpu.VMEM((rows, cache, pairs * HEAD_DIM), jnp.bfloat16),
        ],
        [SMEM, HBM, HBM, HBM],
        [VMEM, VMEM, VMEM],
        0,
        half * out_weight.shape[1] * 2 + 4 * rows * cache * pairs * HEAD_DIM,
        [pltpu.SemaphoreType.DMA((3 * pairs,))],
    )(place, in_hbm(out_weight), in_hbm(key_cache), in_hbm(value_cache))

    gain = norm_gain.reshape(1, depth)
    products, given, received = project(
        in_kernel, place, slots, blocks, [gain], weight_in, HEAD_DIM
    )
    products = spread(products)
    sums = given[:, -HEAD_DIM:].astype(jnp.float32) + received[:, -HEAD_DIM:].astype(jnp.float32)
    own_sums = lax.dynamic_slice_in_dim(sums, (run ^ col) * rows, rows, 0)
    all_sums = [own_sums] + [moved(own_sums, "row", mask) for mask in range(1, row_count)]

    cosine, sine = rope_tables(cache_lengths, HEAD_DIM)
    attended = call(
        functools.partial(attend_all, col_count, row_count),
        struct((rows, half)),
        [SMEM] + [VMEM] * (3 + col_count + row_count + 2),
        VMEM,
        4 * rows * half * cache,
        0,
    )(
        place,
        jnp.concatenate([cosine, cosine], axis=1),
        jnp.concatenate([-sine, sine], axis=1),
        cache_lengths.reshape(rows, 1),
        *products,
        *all_sums,
        in_vmem(key_part),
        in_vmem(value_part),
    )

    products, _, _ = project(
        out_kernel, place, slots, gathered(attended, "col"), [], weight_out, 0
    )
    products = spread(products)
    keep, send = call(
        functools.partial(sum_kernel, col_count),
        [struct((rows, half)), struct((rows, half))],
        [SMEM] + [VMEM] * (2 + col_count),
        [VMEM, VMEM],
        rows * depth * 4,
        rows * depth * 8,
    )(place, hidden_in, attended, *products)
    return call(
        join_kernel,
        struct((1, rows, depth)),
        [SMEM, VMEM, VMEM],
        VMEM,
        0,
        rows * depth * 4,
    )(place, keep, moved(send, "side", 1))


def per_device(*args):
    hidden_in, _, qkv_weight, out_weight, key_cache = args[:5]
    col_count, row_count = lax.axis_size("col"), lax.axis_size("row")
    fits = (
        lax.axis_size("side") == 2
        and qkv_weight.shape[1] == 2 * GROUP_WIDTH
        and col_count % row_count == 0
        and col_count & (col_count - 1) == 0
        and hidden_in.shape[0] % 16 == 0
        and key_cache.shape[1] % 16 == 0
        and hidden_in.shape[1] == 2 * OUT_WIDTH * (col_count // row_count)
    )
    return paired_plan(*args) if fits else general_plan(*args)


def solution(mesh):
    placed = (
        P(("groups", "col"), "row"),
        P("row"),
        P("row", "col"),
        P("row", "col"),
        P(("groups", "col"), None, "row"),
        P(("groups", "col"), None, "row"),
        P(("groups", "col")),
        P("groups"),
    )
    return jax.shard_map(
        per_device,
        mesh=mesh,
        in_specs=placed,
        out_specs=P("side", ("groups", "col"), "row"),
        check_vma=False,
    )
```

```python
import functools

import jax
import jax.numpy as jnp
from jax import lax
from jax.experimental import pallas as pl
from jax.experimental.pallas import tpu as pltpu
from jax.sharding import PartitionSpec as P

D = 8192
HEADS = 64
KV_HEADS = 8
HEAD_DIM = 128
QKV = 10240


EPSILON = 1e-05
THETA = 500000.0


def swapped(value, axis, bit):
    mask = 2**bit
    pairs = [(source, source ^ mask) for source in range(lax.axis_size(axis))]
    return lax.ppermute(value, axis, pairs)


def rope_tables(lengths, head_dim):
    half_dim = head_dim // 2
    inv_freq = jnp.exp(
        -jnp.log(jnp.float32(THETA)) * jnp.arange(half_dim, dtype=jnp.float32) / half_dim
    )
    phases = lengths.astype(jnp.float32)[:, None] * inv_freq[None, :]
    return (jnp.cos(phases), jnp.sin(phases))


def rotate(vector, cos_vals, sine_vals):
    half_dim = vector.shape[-1] // 2
    front_half = vector[..., :half_dim]
    back_half = vector[..., half_dim:]
    return jnp.concatenate(
        [
            front_half * cos_vals - back_half * sine_vals,
            back_half * cos_vals + front_half * sine_vals,
        ],
        axis=-1,
    )


def attend(packed, key_block, value_block, lengths):
    slot_count = packed.shape[0]
    cache_size = key_block.shape[1]
    groups = key_block.shape[2] // HEAD_DIM
    per_group = HEADS // KV_HEADS
    grouped = packed.reshape(slot_count, groups, per_group + 2, HEAD_DIM)
    cos_vals, sine_vals = rope_tables(lengths, HEAD_DIM)
    queries = rotate(
        grouped[:, :, :per_group].astype(jnp.float32),
        cos_vals[:, None, None, :],
        sine_vals[:, None, None, :],
    ).astype(jnp.bfloat16)
    new_keys = rotate(
        grouped[:, :, per_group].astype(jnp.float32), cos_vals[:, None, :], sine_vals[:, None, :]
    ).astype(jnp.bfloat16)
    new_values = grouped[:, :, per_group + 1]
    cache_keys = key_block.reshape(slot_count, cache_size, groups, HEAD_DIM)
    cache_values = value_block.reshape(slot_count, cache_size, groups, HEAD_DIM)
    factor = HEAD_DIM ** (-0.5)
    cache_scores = (
        jnp.einsum("sghd,slgd->sghl", queries, cache_keys, preferred_element_type=jnp.float32)
        * factor
    )
    own_scores = (
        jnp.einsum("sghd,sgd->sgh", queries, new_keys, preferred_element_type=jnp.float32) * factor
    )
    in_cache = lax.broadcasted_iota(jnp.int32, (slot_count, cache_size), 1) < lengths[:, None]
    cache_scores = jnp.where(in_cache[:, None, None, :], cache_scores, -1e30)
    row_max = jnp.maximum(jnp.max(cache_scores, axis=-1), own_scores)
    cache_exp = jnp.exp(cache_scores - row_max[..., None])
    own_exp = jnp.exp(own_scores - row_max)
    denominator = jnp.sum(cache_exp, axis=-1) + own_exp
    cache_weight = (cache_exp / denominator[..., None]).astype(jnp.bfloat16)
    own_weight = (own_exp / denominator).astype(jnp.bfloat16)
    combined = jnp.einsum(
        "sghl,slgd->sghd", cache_weight, cache_values, preferred_element_type=jnp.float32
    )
    combined = (
        combined
        + own_weight.astype(jnp.float32)[..., None] * new_values.astype(jnp.float32)[:, :, None, :]
    )
    return combined.astype(jnp.bfloat16).reshape(slot_count, groups * per_group * HEAD_DIM)


def general_plan(
    hidden_in,
    norm_gain,
    qkv_weight,
    out_weight,
    key_cache,
    value_cache,
    cache_lengths,
    slot_request,
):
    side_index = lax.axis_index("side")
    is_weight = side_index == 0
    col_count = lax.axis_size("col")
    row_count = lax.axis_size("row")
    group_cols = col_count // row_count
    in_half = qkv_weight.shape[1] // 2
    out_half = out_weight.shape[1] // 2
    residual = hidden_in.astype(jnp.float32)
    square_sums = lax.psum(jnp.sum(residual * residual, axis=1), "row")
    normed = (
        residual
        * lax.rsqrt(square_sums[:, None] / D + EPSILON)
        * norm_gain.astype(jnp.float32)[None, :]
    ).astype(jnp.bfloat16)
    in_weight = lax.dynamic_slice_in_dim(qkv_weight, side_index * in_half, in_half, 1)
    partial_in = jnp.dot(
        lax.all_gather(normed, "col", axis=0, tiled=True),
        in_weight,
        preferred_element_type=jnp.float32,
    )
    in_slots = jnp.take(partial_in, slot_request, axis=0)
    own_width = QKV // row_count
    summed = lax.psum(in_slots.astype(jnp.bfloat16), "row")
    spread = lax.all_to_all(summed, "col", split_axis=0, concat_axis=1, tiled=True)
    own_columns = lax.dynamic_slice_in_dim(
        spread.reshape(spread.shape[0], col_count, in_half),
        lax.axis_index("row") * group_cols,
        group_cols,
        1,
    )
    slot_half = key_cache.shape[0] // 2
    halves = lax.all_to_all(
        own_columns[:, :, None, :], "side", split_axis=0, concat_axis=2, tiled=True
    )
    arrived = halves.reshape(slot_half, own_width)
    first_slot = side_index * slot_half
    key_part = lax.dynamic_slice_in_dim(key_cache, first_slot, slot_half, 0)
    value_part = lax.dynamic_slice_in_dim(value_cache, first_slot, slot_half, 0)
    length_part = lax.dynamic_slice_in_dim(cache_lengths, first_slot, slot_half, 0)
    attended = attend(arrived, key_part, value_part, length_part)
    out_cols = lax.dynamic_slice_in_dim(out_weight, side_index * out_half, out_half, 1)
    collected = lax.all_gather(attended, ("col", "side"), axis=0, tiled=True)
    out_slots = jnp.dot(collected, out_cols, preferred_element_type=jnp.float32)
    inverse = jnp.argsort(slot_request)
    out_requests = jnp.take(out_slots, inverse, axis=0)
    spread_out = lax.all_to_all(
        out_requests.astype(jnp.bfloat16), "col", split_axis=0, concat_axis=1, tiled=True
    ).astype(out_requests.dtype)
    out_view = spread_out.reshape(spread_out.shape[0], col_count, out_half)
    summed_out = lax.psum_scatter(
        out_view.astype(jnp.bfloat16), "row", scatter_dimension=1, tiled=True
    ).astype(jnp.float32)
    req_rows = hidden_in.shape[0]
    residual_view = residual.reshape(req_rows, group_cols, 2, out_half)
    residual_half = lax.dynamic_index_in_dim(residual_view, side_index, 2, keepdims=False)
    own_hidden = (residual_half + summed_out).astype(jnp.bfloat16)
    payload = jnp.where(is_weight, attended, own_hidden.reshape(attended.shape))
    received = swapped(payload, "side", 0)
    hidden = jnp.stack([own_hidden, received.reshape(own_hidden.shape)], axis=2).reshape(
        req_rows, residual.shape[1]
    )
    attention_rows = jnp.concatenate([received, attended], axis=0)
    result = jnp.where(is_weight, hidden, attention_rows)
    return result[None]


GROUP = HEADS // KV_HEADS
GROUP_WIDTH = (GROUP + 2) * HEAD_DIM
OUT_WIDTH = GROUP * HEAD_DIM
SLOTS = 8
VMEM = pl.BlockSpec(memory_space=pltpu.VMEM)
SMEM = pl.BlockSpec(memory_space=pltpu.SMEM)
HBM = pl.BlockSpec(memory_space=pl.ANY)
MIB = 2**20


def call(kernel, out_shape, in_specs, out_specs, flops, size, scratch=(), limit=16):
    return pl.pallas_call(
        kernel,
        out_shape=out_shape,
        in_specs=in_specs,
        out_specs=out_specs,
        scratch_shapes=list(scratch),
        compiler_params=pltpu.CompilerParams(vmem_limit_bytes=limit * MIB),
        cost_estimate=pl.CostEstimate(flops=flops, bytes_accessed=size, transcendentals=0),
    )


def in_vmem(value):
    return pltpu.with_memory_space_constraint(value, pltpu.VMEM)


def in_hbm(value):
    return pltpu.with_memory_space_constraint(value, pltpu.HBM)


def struct(shape, dtype=jnp.bfloat16):
    return jax.ShapeDtypeStruct(shape, dtype)


def moved(value, axis, mask):
    pairs = [(source, source ^ mask) for source in range(lax.axis_size(axis))]
    return lax.ppermute(value, axis, pairs)


def slice_kernel(place, source, part, sem):
    width = part.shape[1]
    columns = pl.ds(pl.multiple_of(place[0] * width, width), width)
    copy = pltpu.make_async_copy(source.at[:, columns], part, sem)
    copy.start()
    copy.wait()


def halves(place, weight, staged, row, target_row, size):
    width = staged[0].shape[1]
    copies = []
    for target, half in zip(staged, (1 - place[0], place[0])):
        columns = pl.ds(pl.multiple_of(half * width, width), width)
        copies.append(
            (weight.at[pl.ds(row, size), columns], target.at[pl.ds(target_row, size), :])
        )
    return copies


def run_copies(copies, sems):
    copies = [
        pltpu.make_async_copy(source, target, sems.at[i])
        for i, (source, target) in enumerate(copies)
    ]
    for copy in copies:
        copy.start()
    for copy in copies:
        copy.wait()


def stage_in_kernel(place, weight, *refs):
    give_part, own_part, sems = refs[-3:]
    depth = own_part.shape[0]
    first = pl.multiple_of(place[0] * depth, depth)
    run_copies(halves(place, weight, (give_part, own_part), first, 0, depth), sems)


def stage_rest_kernel(
    place, weight, keys, values, give_part, own_part, key_part, value_part, sems
):
    copies = []
    for j in range(own_part.shape[0] // OUT_WIDTH):
        head = 2 * j + place[0]
        row = pl.multiple_of(head * OUT_WIDTH, OUT_WIDTH)
        lane = pl.multiple_of(head * HEAD_DIM, HEAD_DIM)
        for source, target in ((keys, key_part), (values, value_part)):
            copies.append(
                (
                    source.at[:, :, pl.ds(lane, HEAD_DIM)],
                    target.at[:, :, pl.ds(j * HEAD_DIM, HEAD_DIM)],
                )
            )
        copies += halves(
            place, weight, (give_part, own_part), row, j * OUT_WIDTH, OUT_WIDTH
        )
    run_copies(copies, sems)


def one_hot(slots, slot_base, request_base):
    blocks, rows, _ = slots.shape
    lane = lax.broadcasted_iota(jnp.int32, (rows, blocks * rows), 1)
    request = (lax.div(lane, rows) ^ request_base) * rows + lax.rem(lane, rows)
    parts = [jnp.where(slots[slot_base ^ i] == request, 1.0, 0.0) for i in range(blocks)]
    return jnp.concatenate(parts, axis=0)


def pieces(sums):
    high = sums.astype(jnp.bfloat16).astype(jnp.float32)
    middle = (sums - high).astype(jnp.bfloat16).astype(jnp.float32)
    low = sums - high - middle
    lane = lax.broadcasted_iota(jnp.int32, (sums.shape[0], HEAD_DIM), 1)
    parts = jnp.where(lane == 0, high, jnp.where(lane == 1, middle, low))
    return jnp.where(lane < 3, parts, 0.0).astype(jnp.bfloat16)


def dot_columns(rows, weight, out):
    size, width = weight.shape[1], 512
    for start in range(0, size, width):
        part = slice(start, min(start + width, size))
        product = jnp.dot(rows, weight[:, part], preferred_element_type=jnp.float32)
        out[:, part] = product.astype(out.dtype)


def in_kernel(count, place, slots, *refs):
    blocks, (gain, weight, give, permuted) = refs[:count], refs[count:]
    side = place[0]
    depth = blocks[0].shape[1]
    half = weight.shape[1]
    gains = gain[:, pl.ds(pl.multiple_of(side * depth, depth), depth)].astype(jnp.float32)
    values = jnp.concatenate([block[...].astype(jnp.float32) for block in blocks], axis=0)
    sums = pieces(jnp.sum(values * values, axis=1, keepdims=True))
    chosen = one_hot(slots, place[2], place[1]).astype(jnp.bfloat16)
    order = jnp.dot(
        chosen, (values * gains).astype(jnp.bfloat16), preferred_element_type=jnp.float32
    ).astype(jnp.bfloat16)
    permuted[...] = order
    give[:, half:] = jnp.dot(chosen, sums, preferred_element_type=jnp.float32).astype(jnp.bfloat16)
    dot_columns(order, weight, give)


def out_kernel(count, place, slots, *refs):
    blocks, (weight, give, permuted) = refs[:count], refs[count:]
    values = jnp.concatenate([block[...] for block in blocks], axis=0)
    chosen = one_hot(slots, place[1], place[2]).T.astype(jnp.bfloat16)
    order = jnp.dot(chosen, values, preferred_element_type=jnp.float32).astype(jnp.bfloat16)
    permuted[...] = order
    dot_columns(order, weight, give)


def merge_kernel(own, given, received, *outs):
    rows = outs[0].shape[0]
    half = own.shape[1]
    more = given.shape[1] - half
    for i, out in enumerate(outs):
        part = slice(i * rows, (i + 1) * rows)
        total = own[part, :] + received[part, :half].astype(jnp.float32)
        out[:, :half] = total.astype(jnp.bfloat16)
        if out.shape[1] > half:
            out[:, half:] = jnp.concatenate(
                [given[part, half : half + more // 2], received[part, half : half + more // 2]],
                axis=1,
            )


def own_kernel(permuted, weight, own):
    dot_columns(permuted[...], weight, own)


def project(kernel, place, slots, blocks, extra, weights, more, pairs):
    count = len(blocks)
    rows, depth = blocks[0].shape
    rows = rows * count
    half = weights[0].shape[1]
    flops = 2 * rows * depth * half
    give, permuted = call(
        functools.partial(kernel, count),
        [struct((rows, half + more)), struct((rows, depth))],
        [SMEM, VMEM] + [VMEM] * (count + len(extra) + 1),
        [VMEM, VMEM],
        flops,
        depth * half * 2,
    )(place, slots, *blocks, *extra, in_vmem(weights[0]))
    received = moved(give, "side", 1)
    own = call(
        own_kernel,
        struct((rows, half), jnp.float32),
        [VMEM, VMEM],
        VMEM,
        flops,
        depth * half * 2,
    )(permuted, in_vmem(weights[1]))
    return call(
        merge_kernel,
        [
            struct((rows // count, half + (0 if i % pairs else more))) for i in range(count)
        ],
        [VMEM] * 3,
        [VMEM] * count,
        rows * half,
        rows * half * 8,
    )(own, give, received)


def gathered(value, axis):
    blocks = {0: value}
    mask = lax.axis_size(axis) // 2
    while mask:
        blocks |= {known | mask: moved(block, axis, mask) for known, block in blocks.items()}
        mask //= 2
    return [blocks[i] for i in sorted(blocks)]


def spread(products):
    col_count, row_count = lax.axis_size("col"), lax.axis_size("row")
    pairs = col_count // row_count
    return [
        lax.ppermute(
            products[j],
            ("col", "row"),
            [
                (
                    col * row_count + row,
                    ((row * pairs + col % pairs) ^ j) * row_count + col // pairs,
                )
                for col in range(col_count)
                for row in range(row_count)
            ],
        )
        for j in range(col_count)
    ]


def rotated(vector, cosine, sine):
    return vector * cosine + pltpu.roll(vector, HEAD_DIM // 2, 1) * sine


def attend_all(count, place, cosine, sine, lengths, *refs):
    blocks, (keys, values, out, scores_of, probs_of) = refs[:count], refs[count:]
    pairs = keys.shape[2] // HEAD_DIM
    rows, cache = keys.shape[:2]
    low = place[1] % pairs
    width = GROUP_WIDTH
    squares = blocks[0][:, width:].astype(jnp.float32)
    for i in range(pairs, count, pairs):
        squares = squares + blocks[i][:, width:].astype(jnp.float32)
    scale = lax.rsqrt(jnp.sum(squares, axis=1, keepdims=True) / D + EPSILON)
    factor = HEAD_DIM ** (-0.5)
    cosines, sines = cosine[...], sine[...]
    lane = lax.broadcasted_iota(jnp.int32, (SLOTS, SLOTS * cache), 1)
    slot = lax.broadcasted_iota(jnp.int32, (SLOTS, SLOTS * cache), 0)
    position = lane - slot * cache
    runs = [slice(start, start + SLOTS) for start in range(0, rows, SLOTS)]
    filled = [(position >= 0) & (position < lengths[part]) for part in runs]
    own, new_values, own_probs = [], [], []
    for pair in range(pairs):
        total = blocks[pair][:, :width].astype(jnp.float32)
        for i in range(pair + pairs, count, pairs):
            total = total + blocks[i][:, :width].astype(jnp.float32)
        total = (total * scale).astype(jnp.bfloat16).astype(jnp.float32)
        heads = [total[:, h * HEAD_DIM : (h + 1) * HEAD_DIM] for h in range(GROUP + 2)]
        queries = [
            rotated(head, cosines, sines).astype(jnp.bfloat16).astype(jnp.float32)
            for head in heads[:GROUP]
        ]
        new_key = rotated(heads[GROUP], cosines, sines).astype(jnp.bfloat16).astype(jnp.float32)
        new_values.append(heads[GROUP + 1])
        own.append([jnp.sum(query * new_key, axis=1, keepdims=True) * factor for query in queries])
        lanes = pl.ds(pl.multiple_of((low ^ pair) * HEAD_DIM, HEAD_DIM), HEAD_DIM)
        for run, part in enumerate(runs):
            query = jnp.concatenate([head[part] for head in queries], axis=0)
            key = keys[part, :, lanes].reshape(SLOTS * cache, HEAD_DIM)
            scores_of[pair, run] = lax.dot_general(
                query.astype(jnp.bfloat16),
                key,
                (((1,), (1,)), ((), ())),
                preferred_element_type=jnp.float32,
            )
    for pair in range(pairs):
        for run, part in enumerate(runs):
            scores = (scores_of[pair, run] * factor).reshape(GROUP, SLOTS, SLOTS * cache)
            scores = jnp.where(filled[run][None], scores, -1e30)
            own_score = jnp.concatenate([head[part] for head in own[pair]], axis=0).reshape(
                GROUP, SLOTS, 1
            )
            highest = jnp.maximum(jnp.max(scores, axis=2, keepdims=True), own_score)
            weights = jnp.exp(scores - highest)
            own_weight = jnp.exp(own_score - highest)
            inverse = 1.0 / (jnp.sum(weights, axis=2, keepdims=True) + own_weight)
            probs = (weights * inverse).astype(jnp.bfloat16)
            probs_of[pair, run] = probs.reshape(GROUP * SLOTS, SLOTS * cache)
            own_probs.append((own_weight * inverse).astype(jnp.bfloat16).astype(jnp.float32))
    for pair in range(pairs):
        lanes = pl.ds(pl.multiple_of((low ^ pair) * HEAD_DIM, HEAD_DIM), HEAD_DIM)
        results = []
        for run, part in enumerate(runs):
            value = values[part, :, lanes].reshape(SLOTS * cache, HEAD_DIM)
            mixed = jnp.dot(probs_of[pair, run], value, preferred_element_type=jnp.float32)
            own_prob = own_probs[pair * len(runs) + run]
            results.append(
                mixed.reshape(GROUP, SLOTS, HEAD_DIM) + own_prob * new_values[pair][part][None]
            )
        for head in range(GROUP):
            joined = jnp.concatenate([result[head] for result in results], axis=0)
            at = pl.multiple_of((low ^ pair) * OUT_WIDTH + head * HEAD_DIM, HEAD_DIM)
            out[:, pl.ds(at, HEAD_DIM)] = joined.astype(jnp.bfloat16)


def sum_kernel(count, place, hidden, attended, *refs):
    blocks, (keep, send) = refs[:count], refs[count:]
    rows, width = blocks[0].shape
    pairs = attended.shape[1] // width
    side = place[0]
    low = place[1] % pairs
    for pair in range(pairs):
        column = low ^ pair
        total = blocks[pair][...].astype(jnp.float32)
        for i in range(pair + pairs, count, pairs):
            total = total + blocks[i][...].astype(jnp.float32)
        at = pl.ds(pl.multiple_of((2 * column + side) * width, width), width)
        hidden_out = (hidden[:, at].astype(jnp.float32) + total).astype(jnp.bfloat16)
        at = pl.ds(pl.multiple_of(column * width, width), width)
        attention = attended[:, at]
        keep[:, at] = jnp.where(side == 0, hidden_out, attention)
        send[:, at] = jnp.where(side == 0, attention, hidden_out)


def join_kernel(place, keep, received, out):
    side = place[0]
    width = OUT_WIDTH
    for j in range(keep.shape[1] // width):
        part = slice(j * width, (j + 1) * width)
        out[0, :, pl.ds(pl.multiple_of((2 * j + side) * width, width), width)] = keep[:, part]
        out[0, :, pl.ds(pl.multiple_of((2 * j + 1 - side) * width, width), width)] = received[
            :, part
        ]


def paired_plan(
    hidden_in, norm_gain, qkv_weight, out_weight, key_cache, value_cache, cache_lengths, slot_request
):
    col_count, row_count = lax.axis_size("col"), lax.axis_size("row")
    pairs = col_count // row_count
    side, col, row = (lax.axis_index(name) for name in ("side", "col", "row"))
    run = row * pairs + lax.rem(col, pairs)
    place = jnp.stack([side, col, run]).astype(jnp.int32)
    rows, depth = hidden_in.shape
    half = depth // 2
    cache = key_cache.shape[1]
    slots = slot_request.reshape(col_count, rows, 1)

    own_part = call(
        slice_kernel,
        struct((rows, half)),
        [SMEM, HBM],
        VMEM,
        0,
        rows * depth * 2,
        [pltpu.SemaphoreType.DMA],
    )(place, in_hbm(hidden_in))
    blocks = gathered(own_part, "col")

    gain = norm_gain.reshape(1, depth)
    cosine, sine = rope_tables(cache_lengths, HEAD_DIM)
    tables = [
        jnp.concatenate([cosine, cosine], axis=1),
        jnp.concatenate([-sine, sine], axis=1),
        cache_lengths.reshape(rows, 1),
    ]
    ready = [slots, gain, *tables]
    half_in, half_out = qkv_weight.shape[1] // 2, out_weight.shape[1] // 2
    weights_in = call(
        stage_in_kernel,
        [pltpu.VMEM((half, half_in), jnp.bfloat16)] * 2,
        [SMEM, HBM] + [HBM] * len(ready),
        [VMEM] * 2,
        0,
        half * half_in * 4,
        [pltpu.SemaphoreType.DMA((2,))],
    )(place, in_hbm(qkv_weight), *ready)
    *weights_out, key_part, value_part = call(
        stage_rest_kernel,
        [pltpu.VMEM((half, half_out), jnp.bfloat16)] * 2
        + [pltpu.VMEM((rows, cache, pairs * HEAD_DIM), jnp.bfloat16)] * 2,
        [SMEM, HBM, HBM, HBM],
        [VMEM] * 4,
        0,
        half * half_out * 4 + 4 * rows * cache * pairs * HEAD_DIM,
        [pltpu.SemaphoreType.DMA((4 * pairs,))],
    )(place, in_hbm(out_weight), in_hbm(key_cache), in_hbm(value_cache))

    products = spread(
        project(in_kernel, place, slots, blocks, [gain], weights_in, HEAD_DIM, pairs)
    )

    attended = call(
        functools.partial(attend_all, col_count),
        struct((rows, half)),
        [SMEM] + [VMEM] * (3 + col_count + 2),
        VMEM,
        4 * rows * half * cache,
        0,
        [
            pltpu.VMEM((pairs, rows // SLOTS, GROUP * SLOTS, SLOTS * cache), jnp.float32),
            pltpu.VMEM((pairs, rows // SLOTS, GROUP * SLOTS, SLOTS * cache), jnp.bfloat16),
        ],
    )(
        place,
        *tables,
        *products,
        in_vmem(key_part),
        in_vmem(value_part),
    )

    products = spread(
        project(out_kernel, place, slots, gathered(attended, "col"), [], weights_out, 0, pairs)
    )
    keep, send = call(
        functools.partial(sum_kernel, col_count),
        [struct((rows, half)), struct((rows, half))],
        [SMEM] + [VMEM] * (2 + col_count),
        [VMEM, VMEM],
        rows * depth * 4,
        rows * depth * 8,
    )(place, hidden_in, attended, *products)
    return call(
        join_kernel,
        struct((1, rows, depth)),
        [SMEM, VMEM, VMEM],
        VMEM,
        0,
        rows * depth * 4,
    )(place, keep, moved(send, "side", 1))


def per_device(*args):
    hidden_in, _, qkv_weight, out_weight, key_cache = args[:5]
    col_count, row_count = lax.axis_size("col"), lax.axis_size("row")
    fits = (
        lax.axis_size("side") == 2
        and qkv_weight.shape[1] == 2 * GROUP_WIDTH
        and col_count % row_count == 0
        and col_count & (col_count - 1) == 0
        and hidden_in.shape[0] % 16 == 0
        and key_cache.shape[1] % 16 == 0
        and hidden_in.shape[1] == 2 * OUT_WIDTH * (col_count // row_count)
    )
    return paired_plan(*args) if fits else general_plan(*args)


def solution(mesh):
    placed = (
        P(("groups", "col"), "row"),
        P("row"),
        P("row", "col"),
        P("row", "col"),
        P(("groups", "col"), None, "row"),
        P(("groups", "col"), None, "row"),
        P(("groups", "col")),
        P("groups"),
    )
    return jax.shard_map(
        per_device,
        mesh=mesh,
        in_specs=placed,
        out_specs=P("side", ("groups", "col"), "row"),
        check_vma=False,
    )
```

```python
import functools
import math

import jax
import jax.numpy as jnp
from jax import lax
from jax.experimental import pallas as pl
from jax.experimental.pallas import tpu as pltpu
from jax.sharding import PartitionSpec as P

D = 8192
HEADS = 64
KV_HEADS = 8
HEAD_DIM = 128
QKV = 10240


EPSILON = 1e-05
THETA = 500000.0


def swapped(value, axis, bit):
    mask = 2**bit
    pairs = [(source, source ^ mask) for source in range(lax.axis_size(axis))]
    return lax.ppermute(value, axis, pairs)


def rope_tables(lengths, head_dim):
    half_dim = head_dim // 2
    inv_freq = jnp.exp(
        -jnp.log(jnp.float32(THETA)) * jnp.arange(half_dim, dtype=jnp.float32) / half_dim
    )
    phases = lengths.astype(jnp.float32)[:, None] * inv_freq[None, :]
    return (jnp.cos(phases), jnp.sin(phases))


def rotate(vector, cos_vals, sine_vals):
    half_dim = vector.shape[-1] // 2
    front_half = vector[..., :half_dim]
    back_half = vector[..., half_dim:]
    return jnp.concatenate(
        [
            front_half * cos_vals - back_half * sine_vals,
            back_half * cos_vals + front_half * sine_vals,
        ],
        axis=-1,
    )


def attend(packed, key_block, value_block, lengths):
    slot_count = packed.shape[0]
    cache_size = key_block.shape[1]
    groups = key_block.shape[2] // HEAD_DIM
    per_group = HEADS // KV_HEADS
    grouped = packed.reshape(slot_count, groups, per_group + 2, HEAD_DIM)
    cos_vals, sine_vals = rope_tables(lengths, HEAD_DIM)
    queries = rotate(
        grouped[:, :, :per_group].astype(jnp.float32),
        cos_vals[:, None, None, :],
        sine_vals[:, None, None, :],
    ).astype(jnp.bfloat16)
    new_keys = rotate(
        grouped[:, :, per_group].astype(jnp.float32), cos_vals[:, None, :], sine_vals[:, None, :]
    ).astype(jnp.bfloat16)
    new_values = grouped[:, :, per_group + 1]
    cache_keys = key_block.reshape(slot_count, cache_size, groups, HEAD_DIM)
    cache_values = value_block.reshape(slot_count, cache_size, groups, HEAD_DIM)
    factor = HEAD_DIM ** (-0.5)
    cache_scores = (
        jnp.einsum("sghd,slgd->sghl", queries, cache_keys, preferred_element_type=jnp.float32)
        * factor
    )
    own_scores = (
        jnp.einsum("sghd,sgd->sgh", queries, new_keys, preferred_element_type=jnp.float32) * factor
    )
    in_cache = lax.broadcasted_iota(jnp.int32, (slot_count, cache_size), 1) < lengths[:, None]
    cache_scores = jnp.where(in_cache[:, None, None, :], cache_scores, -1e30)
    row_max = jnp.maximum(jnp.max(cache_scores, axis=-1), own_scores)
    cache_exp = jnp.exp(cache_scores - row_max[..., None])
    own_exp = jnp.exp(own_scores - row_max)
    denominator = jnp.sum(cache_exp, axis=-1) + own_exp
    cache_weight = (cache_exp / denominator[..., None]).astype(jnp.bfloat16)
    own_weight = (own_exp / denominator).astype(jnp.bfloat16)
    combined = jnp.einsum(
        "sghl,slgd->sghd", cache_weight, cache_values, preferred_element_type=jnp.float32
    )
    combined = (
        combined
        + own_weight.astype(jnp.float32)[..., None] * new_values.astype(jnp.float32)[:, :, None, :]
    )
    return combined.astype(jnp.bfloat16).reshape(slot_count, groups * per_group * HEAD_DIM)


def general_plan(
    hidden_in,
    norm_gain,
    qkv_weight,
    out_weight,
    key_cache,
    value_cache,
    cache_lengths,
    slot_request,
):
    side_index = lax.axis_index("side")
    is_weight = side_index == 0
    col_count = lax.axis_size("col")
    row_count = lax.axis_size("row")
    group_cols = col_count // row_count
    in_half = qkv_weight.shape[1] // 2
    out_half = out_weight.shape[1] // 2
    residual = hidden_in.astype(jnp.float32)
    square_sums = lax.psum(jnp.sum(residual * residual, axis=1), "row")
    normed = (
        residual
        * lax.rsqrt(square_sums[:, None] / D + EPSILON)
        * norm_gain.astype(jnp.float32)[None, :]
    ).astype(jnp.bfloat16)
    in_weight = lax.dynamic_slice_in_dim(qkv_weight, side_index * in_half, in_half, 1)
    partial_in = jnp.dot(
        lax.all_gather(normed, "col", axis=0, tiled=True),
        in_weight,
        preferred_element_type=jnp.float32,
    )
    in_slots = jnp.take(partial_in, slot_request, axis=0)
    own_width = QKV // row_count
    summed = lax.psum(in_slots.astype(jnp.bfloat16), "row")
    spread = lax.all_to_all(summed, "col", split_axis=0, concat_axis=1, tiled=True)
    own_columns = lax.dynamic_slice_in_dim(
        spread.reshape(spread.shape[0], col_count, in_half),
        lax.axis_index("row") * group_cols,
        group_cols,
        1,
    )
    slot_half = key_cache.shape[0] // 2
    halves = lax.all_to_all(
        own_columns[:, :, None, :], "side", split_axis=0, concat_axis=2, tiled=True
    )
    arrived = halves.reshape(slot_half, own_width)
    first_slot = side_index * slot_half
    key_part = lax.dynamic_slice_in_dim(key_cache, first_slot, slot_half, 0)
    value_part = lax.dynamic_slice_in_dim(value_cache, first_slot, slot_half, 0)
    length_part = lax.dynamic_slice_in_dim(cache_lengths, first_slot, slot_half, 0)
    attended = attend(arrived, key_part, value_part, length_part)
    out_cols = lax.dynamic_slice_in_dim(out_weight, side_index * out_half, out_half, 1)
    collected = lax.all_gather(attended, ("col", "side"), axis=0, tiled=True)
    out_slots = jnp.dot(collected, out_cols, preferred_element_type=jnp.float32)
    inverse = jnp.argsort(slot_request)
    out_requests = jnp.take(out_slots, inverse, axis=0)
    spread_out = lax.all_to_all(
        out_requests.astype(jnp.bfloat16), "col", split_axis=0, concat_axis=1, tiled=True
    ).astype(out_requests.dtype)
    out_view = spread_out.reshape(spread_out.shape[0], col_count, out_half)
    summed_out = lax.psum_scatter(
        out_view.astype(jnp.bfloat16), "row", scatter_dimension=1, tiled=True
    ).astype(jnp.float32)
    req_rows = hidden_in.shape[0]
    residual_view = residual.reshape(req_rows, group_cols, 2, out_half)
    residual_half = lax.dynamic_index_in_dim(residual_view, side_index, 2, keepdims=False)
    own_hidden = (residual_half + summed_out).astype(jnp.bfloat16)
    payload = jnp.where(is_weight, attended, own_hidden.reshape(attended.shape))
    received = swapped(payload, "side", 0)
    hidden = jnp.stack([own_hidden, received.reshape(own_hidden.shape)], axis=2).reshape(
        req_rows, residual.shape[1]
    )
    attention_rows = jnp.concatenate([received, attended], axis=0)
    result = jnp.where(is_weight, hidden, attention_rows)
    return result[None]


GROUP = HEADS // KV_HEADS
GROUP_WIDTH = (GROUP + 2) * HEAD_DIM
OUT_WIDTH = GROUP * HEAD_DIM
SLOTS = 8
VMEM = pl.BlockSpec(memory_space=pltpu.VMEM)
SMEM = pl.BlockSpec(memory_space=pltpu.SMEM)
HBM = pl.BlockSpec(memory_space=pl.ANY)
MIB = 2**20


def call(kernel, out_shape, in_specs, out_specs, flops, size, scratch=(), limit=16):
    return pl.pallas_call(
        kernel,
        out_shape=out_shape,
        in_specs=in_specs,
        out_specs=out_specs,
        scratch_shapes=list(scratch),
        compiler_params=pltpu.CompilerParams(vmem_limit_bytes=limit * MIB),
        cost_estimate=pl.CostEstimate(flops=flops, bytes_accessed=size, transcendentals=0),
    )


def in_vmem(value):
    return pltpu.with_memory_space_constraint(value, pltpu.VMEM)


def in_hbm(value):
    return pltpu.with_memory_space_constraint(value, pltpu.HBM)


def struct(shape, dtype=jnp.bfloat16):
    return jax.ShapeDtypeStruct(shape, dtype)


def moved(value, axis, mask):
    pairs = [(source, source ^ mask) for source in range(lax.axis_size(axis))]
    return lax.ppermute(value, axis, pairs)


def hold_kernel(value, token, out):
    pass


def held(value, token):
    return pl.pallas_call(
        hold_kernel,
        out_shape=pltpu.VMEM(value.shape, value.dtype),
        in_specs=[VMEM, HBM],
        out_specs=VMEM,
        input_output_aliases={0: 0},
        compiler_params=pltpu.CompilerParams(vmem_limit_bytes=MIB),
    )(in_vmem(value), token)


def halves(place, weight, staged, row, target_row, size):
    width = staged[0].shape[1]
    copies = []
    for target, half in zip(staged, (1 - place[0], place[0])):
        columns = pl.ds(pl.multiple_of(half * width, width), width)
        copies.append(
            (weight.at[pl.ds(row, size), columns], target.at[pl.ds(target_row, size), :])
        )
    return copies


def run_copies(copies, sems):
    copies = [
        pltpu.make_async_copy(source, target, sems.at[i])
        for i, (source, target) in enumerate(copies)
    ]
    for copy in copies:
        copy.start()
    for copy in copies:
        copy.wait()


def stage_in_kernel(place, weight, *refs):
    give_part, own_part, token, sems = refs[-4:]
    token[...] = jnp.zeros(token.shape, token.dtype)
    depth = own_part.shape[0]
    first = pl.multiple_of(place[0] * depth, depth)
    run_copies(halves(place, weight, (give_part, own_part), first, 0, depth), sems)


def stage_rest_kernel(
    place, weight, keys, values, give_part, own_part, key_part, value_part, sems
):
    copies = []
    for j in range(own_part.shape[0] // OUT_WIDTH):
        head = 2 * j + place[0]
        row = pl.multiple_of(head * OUT_WIDTH, OUT_WIDTH)
        lane = pl.multiple_of(head * HEAD_DIM, HEAD_DIM)
        for source, target in ((keys, key_part), (values, value_part)):
            copies.append(
                (
                    source.at[:, :, pl.ds(lane, HEAD_DIM)],
                    target.at[:, :, pl.ds(j * HEAD_DIM, HEAD_DIM)],
                )
            )
        copies += halves(
            place, weight, (give_part, own_part), row, j * OUT_WIDTH, OUT_WIDTH
        )
    run_copies(copies, sems)


def one_hot(slots, scratch, blocks, slot_base, request_base):
    total = slots.shape[0]
    rows = total // blocks
    index = lax.broadcasted_iota(jnp.int32, (total, total), 0)
    request = (lax.div(index, rows) ^ request_base) * rows + lax.rem(index, rows)
    scratch[...] = jnp.where(slots[...].reshape(1, total) == request, 1.0, 0.0).T
    parts = [
        scratch[pl.ds(pl.multiple_of((slot_base ^ i) * rows, rows), rows), :]
        for i in range(blocks)
    ]
    return jnp.concatenate(parts, axis=0)


def pieces(sums):
    high = sums.astype(jnp.bfloat16).astype(jnp.float32)
    middle = (sums - high).astype(jnp.bfloat16).astype(jnp.float32)
    low = sums - high - middle
    lane = lax.broadcasted_iota(jnp.int32, (sums.shape[0], HEAD_DIM), 1)
    parts = jnp.where(lane == 0, high, jnp.where(lane == 1, middle, low))
    return jnp.where(lane < 3, parts, 0.0).astype(jnp.bfloat16)


def dot_columns(rows, weight, out):
    size, width = weight.shape[1], 512
    for start in range(0, size, width):
        part = slice(start, min(start + width, size))
        product = jnp.dot(rows, weight[:, part], preferred_element_type=jnp.float32)
        out[:, part] = product.astype(out.dtype)


def in_kernel(count, blocks, place, slots, *refs):
    pieces_in, (gain, weight, give, permuted, scratch) = refs[:count], refs[count:]
    side = place[0]
    depth = pieces_in[0].shape[1]
    half = weight.shape[1]
    gains = gain[:, pl.ds(pl.multiple_of(side * depth, depth), depth)].astype(jnp.float32)
    values = jnp.concatenate([piece[...].astype(jnp.float32) for piece in pieces_in], axis=0)
    sums = pieces(jnp.sum(values * values, axis=1, keepdims=True))
    chosen = one_hot(slots, scratch, blocks, place[2], place[1]).astype(jnp.bfloat16)
    order = jnp.dot(
        chosen, (values * gains).astype(jnp.bfloat16), preferred_element_type=jnp.float32
    ).astype(jnp.bfloat16)
    permuted[...] = order
    give[:, half:] = jnp.dot(chosen, sums, preferred_element_type=jnp.float32).astype(jnp.bfloat16)
    dot_columns(order, weight, give)


def out_kernel(count, blocks, place, slots, *refs):
    pieces_in, (weight, give, permuted, scratch) = refs[:count], refs[count:]
    values = jnp.concatenate([piece[...] for piece in pieces_in], axis=0)
    chosen = one_hot(slots, scratch, blocks, place[1], place[2]).T.astype(jnp.bfloat16)
    order = jnp.dot(chosen, values, preferred_element_type=jnp.float32).astype(jnp.bfloat16)
    permuted[...] = order
    dot_columns(order, weight, give)


def merge_kernel(own, given, received, *outs):
    rows = outs[0].shape[0]
    half = own.shape[1]
    more = given.shape[1] - half
    for i, out in enumerate(outs):
        part = slice(i * rows, (i + 1) * rows)
        total = own[part, :] + received[part, :half].astype(jnp.float32)
        out[:, :half] = total.astype(jnp.bfloat16)
        if out.shape[1] > half:
            out[:, half:] = jnp.concatenate(
                [given[part, half : half + more // 2], received[part, half : half + more // 2]],
                axis=1,
            )


def own_kernel(permuted, weight, own):
    dot_columns(permuted[...], weight, own)


def project(kernel, place, slots, pieces_in, extra, weights, more, pairs):
    count = lax.axis_size("col")
    parts = len(pieces_in)
    rows, depth = pieces_in[0].shape
    rows = rows * parts
    half = weights[0].shape[1]
    flops = 2 * rows * depth * half
    give, permuted = call(
        functools.partial(kernel, parts, count),
        [struct((rows, half + more)), struct((rows, depth))],
        [SMEM, VMEM] + [VMEM] * (parts + len(extra) + 1),
        [VMEM, VMEM],
        flops,
        depth * half * 2,
        [pltpu.VMEM((rows, rows), jnp.float32)],
    )(place, slots, *pieces_in, *extra, in_vmem(weights[0]))
    received = moved(give, "side", 1)
    own = call(
        own_kernel,
        struct((rows, half), jnp.float32),
        [VMEM, VMEM],
        VMEM,
        flops,
        depth * half * 2,
    )(permuted, in_vmem(weights[1]))
    return call(
        merge_kernel,
        [
            struct((rows // count, half + (0 if i % pairs else more))) for i in range(count)
        ],
        [VMEM] * 3,
        [VMEM] * count,
        rows * half,
        rows * half * 8,
    )(own, give, received)


def gathered(parts, axis, token=None):
    blocks = {0: parts}
    mask = lax.axis_size(axis) // 2
    while mask:
        blocks |= {
            known | mask: [moved(part, axis, mask) for part in block]
            for known, block in blocks.items()
        }
        if token is not None and mask > 1:
            blocks = {
                known: [held(part, token) for part in block] if known else block
                for known, block in blocks.items()
            }
        mask //= 2
    return [part for i in sorted(blocks) for part in blocks[i]]


def spread(products):
    col_count, row_count = lax.axis_size("col"), lax.axis_size("row")
    pairs = col_count // row_count
    return [
        lax.ppermute(
            products[j],
            ("col", "row"),
            [
                (
                    col * row_count + row,
                    ((row * pairs + col % pairs) ^ j) * row_count + col // pairs,
                )
                for col in range(col_count)
                for row in range(row_count)
            ],
        )
        for j in range(col_count)
    ]


def rotated(vector, cosine, sine):
    return vector * cosine + pltpu.roll(vector, HEAD_DIM // 2, 1) * sine


def rope(lengths, first, rows):
    slot = lax.broadcasted_iota(jnp.int32, (rows, HEAD_DIM), 0)
    length_of = jnp.zeros((rows, HEAD_DIM), jnp.int32)
    for i in range(rows):
        length_of = jnp.where(slot == i, lengths[first + i], length_of)
    lane = lax.broadcasted_iota(jnp.int32, (rows, HEAD_DIM), 1)
    half = HEAD_DIM // 2
    step = lax.rem(lane, half).astype(jnp.float32)
    phases = length_of.astype(jnp.float32) * jnp.exp(-math.log(THETA) * step / half)
    sine = jnp.sin(phases)
    return jnp.cos(phases), jnp.where(lane < half, -sine, sine), length_of[:, :1]


def attend_all(count, first, place, lengths, *refs):
    blocks, (keys, values, out, scores_of, probs_of) = refs[:count], refs[count:]
    pairs = keys.shape[2] // HEAD_DIM
    cache = keys.shape[1]
    rows = out.shape[0]
    here = slice(first, first + rows)
    low = place[1] % pairs
    width = GROUP_WIDTH
    squares = blocks[0][here, width:].astype(jnp.float32)
    for i in range(pairs, count, pairs):
        squares = squares + blocks[i][here, width:].astype(jnp.float32)
    scale = lax.rsqrt(jnp.sum(squares, axis=1, keepdims=True) / D + EPSILON)
    factor = HEAD_DIM ** (-0.5)
    cosines, sines, length_of = rope(lengths, first, rows)
    lane = lax.broadcasted_iota(jnp.int32, (SLOTS, SLOTS * cache), 1)
    slot = lax.broadcasted_iota(jnp.int32, (SLOTS, SLOTS * cache), 0)
    position = lane - slot * cache
    runs = [slice(start, start + SLOTS) for start in range(0, rows, SLOTS)]
    filled = [(position >= 0) & (position < length_of[part]) for part in runs]
    own, new_values, own_probs = [], [], []
    for pair in range(pairs):
        total = blocks[pair][here, :width].astype(jnp.float32)
        for i in range(pair + pairs, count, pairs):
            total = total + blocks[i][here, :width].astype(jnp.float32)
        total = (total * scale).astype(jnp.bfloat16).astype(jnp.float32)
        heads = [total[:, h * HEAD_DIM : (h + 1) * HEAD_DIM] for h in range(GROUP + 2)]
        queries = [
            rotated(head, cosines, sines).astype(jnp.bfloat16).astype(jnp.float32)
            for head in heads[:GROUP]
        ]
        new_key = rotated(heads[GROUP], cosines, sines).astype(jnp.bfloat16).astype(jnp.float32)
        new_values.append(heads[GROUP + 1])
        own.append([jnp.sum(query * new_key, axis=1, keepdims=True) * factor for query in queries])
        lanes = pl.ds(pl.multiple_of((low ^ pair) * HEAD_DIM, HEAD_DIM), HEAD_DIM)
        for run, part in enumerate(runs):
            query = jnp.concatenate([head[part] for head in queries], axis=0)
            key = keys[first + part.start : first + part.stop, :, lanes].reshape(SLOTS * cache, HEAD_DIM)
            scores_of[pair, run] = lax.dot_general(
                query.astype(jnp.bfloat16),
                key,
                (((1,), (1,)), ((), ())),
                preferred_element_type=jnp.float32,
            )
    for pair in range(pairs):
        for run, part in enumerate(runs):
            scores = (scores_of[pair, run] * factor).reshape(GROUP, SLOTS, SLOTS * cache)
            scores = jnp.where(filled[run][None], scores, -1e30)
            own_score = jnp.concatenate([head[part] for head in own[pair]], axis=0).reshape(
                GROUP, SLOTS, 1
            )
            highest = jnp.maximum(jnp.max(scores, axis=2, keepdims=True), own_score)
            weights = jnp.exp(scores - highest)
            own_weight = jnp.exp(own_score - highest)
            inverse = 1.0 / (jnp.sum(weights, axis=2, keepdims=True) + own_weight)
            probs = (weights * inverse).astype(jnp.bfloat16)
            probs_of[pair, run] = probs.reshape(GROUP * SLOTS, SLOTS * cache)
            own_probs.append((own_weight * inverse).astype(jnp.bfloat16).astype(jnp.float32))
    for pair in range(pairs):
        lanes = pl.ds(pl.multiple_of((low ^ pair) * HEAD_DIM, HEAD_DIM), HEAD_DIM)
        results = []
        for run, part in enumerate(runs):
            value = values[first + part.start : first + part.stop, :, lanes].reshape(SLOTS * cache, HEAD_DIM)
            mixed = jnp.dot(probs_of[pair, run], value, preferred_element_type=jnp.float32)
            own_prob = own_probs[pair * len(runs) + run]
            results.append(
                mixed.reshape(GROUP, SLOTS, HEAD_DIM) + own_prob * new_values[pair][part][None]
            )
        for head in range(GROUP):
            joined = jnp.concatenate([result[head] for result in results], axis=0)
            at = pl.multiple_of((low ^ pair) * OUT_WIDTH + head * HEAD_DIM, HEAD_DIM)
            out[:, pl.ds(at, HEAD_DIM)] = joined.astype(jnp.bfloat16)


def sum_kernel(count, parts, place, hidden, *refs):
    attended, blocks, (keep, send) = refs[:parts], refs[parts : parts + count], refs[parts + count :]
    rows, width = blocks[0].shape
    pairs = keep.shape[1] // width
    side = place[0]
    low = place[1] % pairs
    for pair in range(pairs):
        column = low ^ pair
        total = blocks[pair][...].astype(jnp.float32)
        for i in range(pair + pairs, count, pairs):
            total = total + blocks[i][...].astype(jnp.float32)
        at = pl.ds(pl.multiple_of((2 * column + side) * width, width), width)
        hidden_out = (hidden[:, at].astype(jnp.float32) + total).astype(jnp.bfloat16)
        at = pl.ds(pl.multiple_of(column * width, width), width)
        attention = jnp.concatenate([part[:, at] for part in attended], axis=0)
        keep[:, at] = jnp.where(side == 0, hidden_out, attention)
        send[:, at] = jnp.where(side == 0, attention, hidden_out)


def join_kernel(place, keep, received, out):
    side = place[0]
    width = OUT_WIDTH
    for j in range(keep.shape[1] // width):
        part = slice(j * width, (j + 1) * width)
        out[0, :, pl.ds(pl.multiple_of((2 * j + side) * width, width), width)] = keep[:, part]
        out[0, :, pl.ds(pl.multiple_of((2 * j + 1 - side) * width, width), width)] = received[
            :, part
        ]


def paired_plan(
    hidden_in, norm_gain, qkv_weight, out_weight, key_cache, value_cache, cache_lengths, slot_request
):
    col_count, row_count = lax.axis_size("col"), lax.axis_size("row")
    pairs = col_count // row_count
    side, col, row = (lax.axis_index(name) for name in ("side", "col", "row"))
    run = row * pairs + lax.rem(col, pairs)
    place = jnp.stack([side, col, run]).astype(jnp.int32)
    rows, depth = hidden_in.shape
    half = depth // 2
    cache = key_cache.shape[1]
    parts = 2
    piece = rows // parts

    own_part = lax.dynamic_slice_in_dim(hidden_in, side * half, half, 1)
    gain = norm_gain.reshape(1, depth)
    half_in, half_out = qkv_weight.shape[1] // 2, out_weight.shape[1] // 2
    *weights_in, token = call(
        stage_in_kernel,
        [pltpu.VMEM((half, half_in), jnp.bfloat16)] * 2 + [struct((8, 128), jnp.float32)],
        [SMEM, HBM, HBM],
        [VMEM] * 3,
        0,
        half * half_in * 4,
        [pltpu.SemaphoreType.DMA((2,))],
    )(place, in_hbm(qkv_weight), gain)
    blocks = gathered(
        [own_part[i * piece : (i + 1) * piece] for i in range(parts)], "col", token
    )
    *weights_out, key_part, value_part = call(
        stage_rest_kernel,
        [pltpu.VMEM((half, half_out), jnp.bfloat16)] * 2
        + [pltpu.VMEM((rows, cache, pairs * HEAD_DIM), jnp.bfloat16)] * 2,
        [SMEM, HBM, HBM, HBM],
        [VMEM] * 4,
        0,
        half * half_out * 4 + 4 * rows * cache * pairs * HEAD_DIM,
        [pltpu.SemaphoreType.DMA((4 * pairs,))],
    )(place, in_hbm(out_weight), in_hbm(key_cache), in_hbm(value_cache))

    products = spread(
        project(in_kernel, place, slot_request, blocks, [gain], weights_in, HEAD_DIM, pairs)
    )

    key_part, value_part = in_vmem(key_part), in_vmem(value_part)
    runs = (pairs, piece // SLOTS, GROUP * SLOTS, SLOTS * cache)
    attended = [
        call(
            functools.partial(attend_all, col_count, first),
            struct((piece, half)),
            [SMEM, SMEM] + [VMEM] * (col_count + 2),
            VMEM,
            4 * piece * half * cache,
            0,
            [pltpu.VMEM(runs, jnp.float32), pltpu.VMEM(runs, jnp.bfloat16)],
        )(place, cache_lengths, *products, key_part, value_part)
        for first in range(0, rows, piece)
    ]

    products = spread(
        project(
            out_kernel, place, slot_request, gathered(attended, "col"), [], weights_out, 0, pairs
        )
    )
    keep, send = call(
        functools.partial(sum_kernel, col_count, parts),
        [struct((rows, half)), struct((rows, half))],
        [SMEM] + [VMEM] * (1 + parts + col_count),
        [VMEM, VMEM],
        rows * depth * 4,
        rows * depth * 8,
    )(place, hidden_in, *attended, *products)
    return call(
        join_kernel,
        struct((1, rows, depth)),
        [SMEM, VMEM, VMEM],
        VMEM,
        0,
        rows * depth * 4,
    )(place, keep, moved(send, "side", 1))


def per_device(*args):
    hidden_in, _, qkv_weight, out_weight, key_cache = args[:5]
    col_count, row_count = lax.axis_size("col"), lax.axis_size("row")
    fits = (
        lax.axis_size("side") == 2
        and qkv_weight.shape[1] == 2 * GROUP_WIDTH
        and col_count % row_count == 0
        and col_count & (col_count - 1) == 0
        and hidden_in.shape[0] % 32 == 0
        and key_cache.shape[1] % 16 == 0
        and hidden_in.shape[1] == 2 * OUT_WIDTH * (col_count // row_count)
    )
    return paired_plan(*args) if fits else general_plan(*args)


def solution(mesh):
    placed = (
        P(("groups", "col"), "row"),
        P("row"),
        P("row", "col"),
        P("row", "col"),
        P(("groups", "col"), None, "row"),
        P(("groups", "col"), None, "row"),
        P(("groups", "col")),
        P("groups"),
    )
    return jax.shard_map(
        per_device,
        mesh=mesh,
        in_specs=placed,
        out_specs=P("side", ("groups", "col"), "row"),
        check_vma=False,
    )
```

```python
import functools
import math

import jax
import jax.numpy as jnp
from jax import lax
from jax.experimental import pallas as pl
from jax.experimental.pallas import tpu as pltpu
from jax.sharding import PartitionSpec as P

D = 8192
HEADS = 64
KV_HEADS = 8
HEAD_DIM = 128
QKV = 10240


EPSILON = 1e-05
THETA = 500000.0


def swapped(value, axis, bit):
    mask = 2**bit
    pairs = [(source, source ^ mask) for source in range(lax.axis_size(axis))]
    return lax.ppermute(value, axis, pairs)


def rope_tables(lengths, head_dim):
    half_dim = head_dim // 2
    inv_freq = jnp.exp(
        -jnp.log(jnp.float32(THETA)) * jnp.arange(half_dim, dtype=jnp.float32) / half_dim
    )
    phases = lengths.astype(jnp.float32)[:, None] * inv_freq[None, :]
    return (jnp.cos(phases), jnp.sin(phases))


def rotate(vector, cos_vals, sine_vals):
    half_dim = vector.shape[-1] // 2
    front_half = vector[..., :half_dim]
    back_half = vector[..., half_dim:]
    return jnp.concatenate(
        [
            front_half * cos_vals - back_half * sine_vals,
            back_half * cos_vals + front_half * sine_vals,
        ],
        axis=-1,
    )


def attend(packed, key_block, value_block, lengths):
    slot_count = packed.shape[0]
    cache_size = key_block.shape[1]
    groups = key_block.shape[2] // HEAD_DIM
    per_group = HEADS // KV_HEADS
    grouped = packed.reshape(slot_count, groups, per_group + 2, HEAD_DIM)
    cos_vals, sine_vals = rope_tables(lengths, HEAD_DIM)
    queries = rotate(
        grouped[:, :, :per_group].astype(jnp.float32),
        cos_vals[:, None, None, :],
        sine_vals[:, None, None, :],
    ).astype(jnp.bfloat16)
    new_keys = rotate(
        grouped[:, :, per_group].astype(jnp.float32), cos_vals[:, None, :], sine_vals[:, None, :]
    ).astype(jnp.bfloat16)
    new_values = grouped[:, :, per_group + 1]
    cache_keys = key_block.reshape(slot_count, cache_size, groups, HEAD_DIM)
    cache_values = value_block.reshape(slot_count, cache_size, groups, HEAD_DIM)
    factor = HEAD_DIM ** (-0.5)
    cache_scores = (
        jnp.einsum("sghd,slgd->sghl", queries, cache_keys, preferred_element_type=jnp.float32)
        * factor
    )
    own_scores = (
        jnp.einsum("sghd,sgd->sgh", queries, new_keys, preferred_element_type=jnp.float32) * factor
    )
    in_cache = lax.broadcasted_iota(jnp.int32, (slot_count, cache_size), 1) < lengths[:, None]
    cache_scores = jnp.where(in_cache[:, None, None, :], cache_scores, -1e30)
    row_max = jnp.maximum(jnp.max(cache_scores, axis=-1), own_scores)
    cache_exp = jnp.exp(cache_scores - row_max[..., None])
    own_exp = jnp.exp(own_scores - row_max)
    denominator = jnp.sum(cache_exp, axis=-1) + own_exp
    cache_weight = (cache_exp / denominator[..., None]).astype(jnp.bfloat16)
    own_weight = (own_exp / denominator).astype(jnp.bfloat16)
    combined = jnp.einsum(
        "sghl,slgd->sghd", cache_weight, cache_values, preferred_element_type=jnp.float32
    )
    combined = (
        combined
        + own_weight.astype(jnp.float32)[..., None] * new_values.astype(jnp.float32)[:, :, None, :]
    )
    return combined.astype(jnp.bfloat16).reshape(slot_count, groups * per_group * HEAD_DIM)


def general_plan(
    hidden_in,
    norm_gain,
    qkv_weight,
    out_weight,
    key_cache,
    value_cache,
    cache_lengths,
    slot_request,
):
    side_index = lax.axis_index("side")
    is_weight = side_index == 0
    col_count = lax.axis_size("col")
    row_count = lax.axis_size("row")
    group_cols = col_count // row_count
    in_half = qkv_weight.shape[1] // 2
    out_half = out_weight.shape[1] // 2
    residual = hidden_in.astype(jnp.float32)
    square_sums = lax.psum(jnp.sum(residual * residual, axis=1), "row")
    normed = (
        residual
        * lax.rsqrt(square_sums[:, None] / D + EPSILON)
        * norm_gain.astype(jnp.float32)[None, :]
    ).astype(jnp.bfloat16)
    in_weight = lax.dynamic_slice_in_dim(qkv_weight, side_index * in_half, in_half, 1)
    partial_in = jnp.dot(
        lax.all_gather(normed, "col", axis=0, tiled=True),
        in_weight,
        preferred_element_type=jnp.float32,
    )
    in_slots = jnp.take(partial_in, slot_request, axis=0)
    own_width = QKV // row_count
    summed = lax.psum(in_slots.astype(jnp.bfloat16), "row")
    spread = lax.all_to_all(summed, "col", split_axis=0, concat_axis=1, tiled=True)
    own_columns = lax.dynamic_slice_in_dim(
        spread.reshape(spread.shape[0], col_count, in_half),
        lax.axis_index("row") * group_cols,
        group_cols,
        1,
    )
    slot_half = key_cache.shape[0] // 2
    halves = lax.all_to_all(
        own_columns[:, :, None, :], "side", split_axis=0, concat_axis=2, tiled=True
    )
    arrived = halves.reshape(slot_half, own_width)
    first_slot = side_index * slot_half
    key_part = lax.dynamic_slice_in_dim(key_cache, first_slot, slot_half, 0)
    value_part = lax.dynamic_slice_in_dim(value_cache, first_slot, slot_half, 0)
    length_part = lax.dynamic_slice_in_dim(cache_lengths, first_slot, slot_half, 0)
    attended = attend(arrived, key_part, value_part, length_part)
    out_cols = lax.dynamic_slice_in_dim(out_weight, side_index * out_half, out_half, 1)
    collected = lax.all_gather(attended, ("col", "side"), axis=0, tiled=True)
    out_slots = jnp.dot(collected, out_cols, preferred_element_type=jnp.float32)
    inverse = jnp.argsort(slot_request)
    out_requests = jnp.take(out_slots, inverse, axis=0)
    spread_out = lax.all_to_all(
        out_requests.astype(jnp.bfloat16), "col", split_axis=0, concat_axis=1, tiled=True
    ).astype(out_requests.dtype)
    out_view = spread_out.reshape(spread_out.shape[0], col_count, out_half)
    summed_out = lax.psum_scatter(
        out_view.astype(jnp.bfloat16), "row", scatter_dimension=1, tiled=True
    ).astype(jnp.float32)
    req_rows = hidden_in.shape[0]
    residual_view = residual.reshape(req_rows, group_cols, 2, out_half)
    residual_half = lax.dynamic_index_in_dim(residual_view, side_index, 2, keepdims=False)
    own_hidden = (residual_half + summed_out).astype(jnp.bfloat16)
    payload = jnp.where(is_weight, attended, own_hidden.reshape(attended.shape))
    received = swapped(payload, "side", 0)
    hidden = jnp.stack([own_hidden, received.reshape(own_hidden.shape)], axis=2).reshape(
        req_rows, residual.shape[1]
    )
    attention_rows = jnp.concatenate([received, attended], axis=0)
    result = jnp.where(is_weight, hidden, attention_rows)
    return result[None]


GROUP = HEADS // KV_HEADS
GROUP_WIDTH = (GROUP + 2) * HEAD_DIM
OUT_WIDTH = GROUP * HEAD_DIM
SLOTS = 8
VMEM = pl.BlockSpec(memory_space=pltpu.VMEM)
SMEM = pl.BlockSpec(memory_space=pltpu.SMEM)
HBM = pl.BlockSpec(memory_space=pl.ANY)
MIB = 2**20


def call(kernel, out_shape, in_specs, out_specs, flops, size, scratch=(), limit=16):
    return pl.pallas_call(
        kernel,
        out_shape=out_shape,
        in_specs=in_specs,
        out_specs=out_specs,
        scratch_shapes=list(scratch),
        compiler_params=pltpu.CompilerParams(vmem_limit_bytes=limit * MIB),
        cost_estimate=pl.CostEstimate(flops=flops, bytes_accessed=size, transcendentals=0),
    )


def in_vmem(value):
    return pltpu.with_memory_space_constraint(value, pltpu.VMEM)


def in_hbm(value):
    return pltpu.with_memory_space_constraint(value, pltpu.HBM)


def struct(shape, dtype=jnp.bfloat16):
    return jax.ShapeDtypeStruct(shape, dtype)


def moved(value, axis, mask):
    pairs = [(source, source ^ mask) for source in range(lax.axis_size(axis))]
    return lax.ppermute(value, axis, pairs)


def halves(place, weight, staged, row, target_row, size):
    width = staged[0].shape[1]
    copies = []
    for target, half in zip(staged, (1 - place[0], place[0])):
        columns = pl.ds(pl.multiple_of(half * width, width), width)
        copies.append(
            (weight.at[pl.ds(row, size), columns], target.at[pl.ds(target_row, size), :])
        )
    return copies


def started(copies, sems):
    copies = [
        pltpu.make_async_copy(source, target, sems.at[i])
        for i, (source, target) in enumerate(copies)
    ]
    for copy in copies:
        copy.start()
    return copies


def run_copies(copies, sems):
    for copy in started(copies, sems):
        copy.wait()


def rows_of(place, weight, half, target, chunks=4):
    depth, width = target.shape
    size = depth // chunks
    columns = pl.ds(pl.multiple_of(half * width, width), width)
    return [
        (
            weight.at[pl.ds(pl.multiple_of(place[0] * depth + i * size, size), size), columns],
            target.at[i * size : (i + 1) * size, :],
        )
        for i in range(chunks)
    ]


def stage_in_kernel(place, weight, gain, give_part, sems):
    run_copies(rows_of(place, weight, 1 - place[0], give_part), sems)


def stage_rest_kernel(
    place, weight, keys, values, give_part, own_part, key_part, value_part, sems
):
    copies = []
    for j in range(own_part.shape[0] // OUT_WIDTH):
        head = 2 * j + place[0]
        row = pl.multiple_of(head * OUT_WIDTH, OUT_WIDTH)
        lane = pl.multiple_of(head * HEAD_DIM, HEAD_DIM)
        for source, target in ((keys, key_part), (values, value_part)):
            copies.append(
                (
                    source.at[:, :, pl.ds(lane, HEAD_DIM)],
                    target.at[:, :, pl.ds(j * HEAD_DIM, HEAD_DIM)],
                )
            )
        copies += halves(
            place, weight, (give_part, own_part), row, j * OUT_WIDTH, OUT_WIDTH
        )
    run_copies(copies, sems)


def one_hot(slots, scratch, blocks, slot_base, request_base):
    total = slots.shape[0]
    rows = total // blocks
    index = lax.broadcasted_iota(jnp.int32, (total, total), 0)
    request = (lax.div(index, rows) ^ request_base) * rows + lax.rem(index, rows)
    scratch[...] = jnp.where(slots[...].reshape(1, total) == request, 1.0, 0.0).T
    parts = [
        scratch[pl.ds(pl.multiple_of((slot_base ^ i) * rows, rows), rows), :]
        for i in range(blocks)
    ]
    return jnp.concatenate(parts, axis=0)


def pieces(sums):
    high = sums.astype(jnp.bfloat16).astype(jnp.float32)
    middle = (sums - high).astype(jnp.bfloat16).astype(jnp.float32)
    low = sums - high - middle
    lane = lax.broadcasted_iota(jnp.int32, (sums.shape[0], HEAD_DIM), 1)
    parts = jnp.where(lane == 0, high, jnp.where(lane == 1, middle, low))
    return jnp.where(lane < 3, parts, 0.0).astype(jnp.bfloat16)


def dot_columns(rows, weight, out):
    size, width = weight.shape[1], 512
    for start in range(0, size, width):
        part = slice(start, min(start + width, size))
        product = jnp.dot(rows, weight[:, part], preferred_element_type=jnp.float32)
        out[:, part] = product.astype(out.dtype)


def in_kernel(count, blocks, place, slots, *refs):
    pieces_in, refs = refs[:count], refs[count:]
    gain, whole, weight, give, permuted, own_part, scratch, sems = refs
    side = place[0]
    copies = started(rows_of(place, whole, side, own_part), sems)
    depth = pieces_in[0].shape[1]
    half = weight.shape[1]
    gains = gain[:, pl.ds(pl.multiple_of(side * depth, depth), depth)].astype(jnp.float32)
    values = jnp.concatenate([piece[...].astype(jnp.float32) for piece in pieces_in], axis=0)
    sums = pieces(jnp.sum(values * values, axis=1, keepdims=True))
    chosen = one_hot(slots, scratch, blocks, place[2], place[1]).astype(jnp.bfloat16)
    order = jnp.dot(
        chosen, (values * gains).astype(jnp.bfloat16), preferred_element_type=jnp.float32
    ).astype(jnp.bfloat16)
    permuted[...] = order
    give[:, half:] = jnp.dot(chosen, sums, preferred_element_type=jnp.float32).astype(jnp.bfloat16)
    dot_columns(order, weight, give)
    for copy in copies:
        copy.wait()


def out_kernel(count, blocks, place, slots, *refs):
    pieces_in, (weight, give, permuted, scratch) = refs[:count], refs[count:]
    values = jnp.concatenate([piece[...] for piece in pieces_in], axis=0)
    chosen = one_hot(slots, scratch, blocks, place[1], place[2]).T.astype(jnp.bfloat16)
    order = jnp.dot(chosen, values, preferred_element_type=jnp.float32).astype(jnp.bfloat16)
    permuted[...] = order
    dot_columns(order, weight, give)


def merge_kernel(own, given, received, *outs):
    rows = outs[0].shape[0]
    half = own.shape[1]
    more = given.shape[1] - half
    for i, out in enumerate(outs):
        part = slice(i * rows, (i + 1) * rows)
        total = own[part, :] + received[part, :half].astype(jnp.float32)
        out[:, :half] = total.astype(jnp.bfloat16)
        if out.shape[1] > half:
            out[:, half:] = jnp.concatenate(
                [given[part, half : half + more // 2], received[part, half : half + more // 2]],
                axis=1,
            )


def own_kernel(permuted, weight, own):
    dot_columns(permuted[...], weight, own)


def project(kernel, place, slots, pieces_in, extra, weight, own_weight, more, pairs):
    count = lax.axis_size("col")
    parts = len(pieces_in)
    rows, depth = pieces_in[0].shape
    rows = rows * parts
    half = weight.shape[1]
    flops = 2 * rows * depth * half
    staged = own_weight is None
    give, permuted, *rest = call(
        functools.partial(kernel, parts, count),
        [struct((rows, half + more)), struct((rows, depth))]
        + [pltpu.VMEM(weight.shape, weight.dtype)] * staged,
        [SMEM, VMEM]
        + [VMEM] * parts
        + ([VMEM, HBM] if staged else [])
        + [VMEM],
        [VMEM] * (2 + staged),
        flops,
        depth * half * 2,
        [pltpu.VMEM((rows, rows), jnp.float32)] + [pltpu.SemaphoreType.DMA((4,))] * staged,
    )(place, slots, *pieces_in, *extra, in_vmem(weight))
    if staged:
        (own_weight,) = rest
    received = moved(give, "side", 1)
    own = call(
        own_kernel,
        struct((rows, half), jnp.float32),
        [VMEM, VMEM],
        VMEM,
        flops,
        depth * half * 2,
    )(permuted, in_vmem(own_weight))
    return call(
        merge_kernel,
        [
            struct((rows // count, half + (0 if i % pairs else more))) for i in range(count)
        ],
        [VMEM] * 3,
        [VMEM] * count,
        rows * half,
        rows * half * 8,
    )(own, give, received)


def gathered(parts, axis):
    blocks = {0: parts}
    mask = lax.axis_size(axis) // 2
    while mask:
        blocks |= {
            known | mask: [moved(part, axis, mask) for part in block]
            for known, block in blocks.items()
        }
        mask //= 2
    return [part for i in sorted(blocks) for part in blocks[i]]


def spread(products):
    col_count, row_count = lax.axis_size("col"), lax.axis_size("row")
    pairs = col_count // row_count
    return [
        lax.ppermute(
            products[j],
            ("col", "row"),
            [
                (
                    col * row_count + row,
                    ((row * pairs + col % pairs) ^ j) * row_count + col // pairs,
                )
                for col in range(col_count)
                for row in range(row_count)
            ],
        )
        for j in range(col_count)
    ]


def rotated(vector, cosine, sine):
    return vector * cosine + pltpu.roll(vector, HEAD_DIM // 2, 1) * sine


def rope(lengths, first, rows):
    slot = lax.broadcasted_iota(jnp.int32, (rows, HEAD_DIM), 0)
    length_of = jnp.zeros((rows, HEAD_DIM), jnp.int32)
    for i in range(rows):
        length_of = jnp.where(slot == i, lengths[first + i], length_of)
    lane = lax.broadcasted_iota(jnp.int32, (rows, HEAD_DIM), 1)
    half = HEAD_DIM // 2
    step = lax.rem(lane, half).astype(jnp.float32)
    phases = length_of.astype(jnp.float32) * jnp.exp(-math.log(THETA) * step / half)
    sine = jnp.sin(phases)
    return jnp.cos(phases), jnp.where(lane < half, -sine, sine), length_of[:, :1]


def attend_all(count, first, place, lengths, *refs):
    blocks, (keys, values, out, scores_of, probs_of) = refs[:count], refs[count:]
    pairs = keys.shape[2] // HEAD_DIM
    cache = keys.shape[1]
    rows = out.shape[0]
    here = slice(first, first + rows)
    low = place[1] % pairs
    width = GROUP_WIDTH
    squares = blocks[0][here, width:].astype(jnp.float32)
    for i in range(pairs, count, pairs):
        squares = squares + blocks[i][here, width:].astype(jnp.float32)
    scale = lax.rsqrt(jnp.sum(squares, axis=1, keepdims=True) / D + EPSILON)
    factor = HEAD_DIM ** (-0.5)
    cosines, sines, length_of = rope(lengths, first, rows)
    lane = lax.broadcasted_iota(jnp.int32, (SLOTS, SLOTS * cache), 1)
    slot = lax.broadcasted_iota(jnp.int32, (SLOTS, SLOTS * cache), 0)
    position = lane - slot * cache
    runs = [slice(start, start + SLOTS) for start in range(0, rows, SLOTS)]
    filled = [(position >= 0) & (position < length_of[part]) for part in runs]
    own, new_values, own_probs = [], [], []
    for pair in range(pairs):
        total = blocks[pair][here, :width].astype(jnp.float32)
        for i in range(pair + pairs, count, pairs):
            total = total + blocks[i][here, :width].astype(jnp.float32)
        total = (total * scale).astype(jnp.bfloat16).astype(jnp.float32)
        heads = [total[:, h * HEAD_DIM : (h + 1) * HEAD_DIM] for h in range(GROUP + 2)]
        queries = [
            rotated(head, cosines, sines).astype(jnp.bfloat16).astype(jnp.float32)
            for head in heads[:GROUP]
        ]
        new_key = rotated(heads[GROUP], cosines, sines).astype(jnp.bfloat16).astype(jnp.float32)
        new_values.append(heads[GROUP + 1])
        own.append([jnp.sum(query * new_key, axis=1, keepdims=True) * factor for query in queries])
        lanes = pl.ds(pl.multiple_of((low ^ pair) * HEAD_DIM, HEAD_DIM), HEAD_DIM)
        for run, part in enumerate(runs):
            query = jnp.concatenate([head[part] for head in queries], axis=0)
            key = keys[first + part.start : first + part.stop, :, lanes].reshape(SLOTS * cache, HEAD_DIM)
            scores_of[pair, run] = lax.dot_general(
                query.astype(jnp.bfloat16),
                key,
                (((1,), (1,)), ((), ())),
                preferred_element_type=jnp.float32,
            )
    for pair in range(pairs):
        for run, part in enumerate(runs):
            scores = (scores_of[pair, run] * factor).reshape(GROUP, SLOTS, SLOTS * cache)
            scores = jnp.where(filled[run][None], scores, -1e30)
            own_score = jnp.concatenate([head[part] for head in own[pair]], axis=0).reshape(
                GROUP, SLOTS, 1
            )
            highest = jnp.maximum(jnp.max(scores, axis=2, keepdims=True), own_score)
            weights = jnp.exp(scores - highest)
            own_weight = jnp.exp(own_score - highest)
            inverse = 1.0 / (jnp.sum(weights, axis=2, keepdims=True) + own_weight)
            probs = (weights * inverse).astype(jnp.bfloat16)
            probs_of[pair, run] = probs.reshape(GROUP * SLOTS, SLOTS * cache)
            own_probs.append((own_weight * inverse).astype(jnp.bfloat16).astype(jnp.float32))
    for pair in range(pairs):
        lanes = pl.ds(pl.multiple_of((low ^ pair) * HEAD_DIM, HEAD_DIM), HEAD_DIM)
        results = []
        for run, part in enumerate(runs):
            value = values[first + part.start : first + part.stop, :, lanes].reshape(SLOTS * cache, HEAD_DIM)
            mixed = jnp.dot(probs_of[pair, run], value, preferred_element_type=jnp.float32)
            own_prob = own_probs[pair * len(runs) + run]
            results.append(
                mixed.reshape(GROUP, SLOTS, HEAD_DIM) + own_prob * new_values[pair][part][None]
            )
        for head in range(GROUP):
            joined = jnp.concatenate([result[head] for result in results], axis=0)
            at = pl.multiple_of((low ^ pair) * OUT_WIDTH + head * HEAD_DIM, HEAD_DIM)
            out[:, pl.ds(at, HEAD_DIM)] = joined.astype(jnp.bfloat16)


def sum_kernel(count, parts, place, hidden, *refs):
    attended, blocks, (keep, send) = refs[:parts], refs[parts : parts + count], refs[parts + count :]
    rows, width = blocks[0].shape
    pairs = keep.shape[1] // width
    side = place[0]
    low = place[1] % pairs
    for pair in range(pairs):
        column = low ^ pair
        total = blocks[pair][...].astype(jnp.float32)
        for i in range(pair + pairs, count, pairs):
            total = total + blocks[i][...].astype(jnp.float32)
        at = pl.ds(pl.multiple_of((2 * column + side) * width, width), width)
        hidden_out = (hidden[:, at].astype(jnp.float32) + total).astype(jnp.bfloat16)
        at = pl.ds(pl.multiple_of(column * width, width), width)
        attention = jnp.concatenate([part[:, at] for part in attended], axis=0)
        keep[:, at] = jnp.where(side == 0, hidden_out, attention)
        send[:, at] = jnp.where(side == 0, attention, hidden_out)


def join_kernel(place, keep, received, out):
    side = place[0]
    width = OUT_WIDTH
    for j in range(keep.shape[1] // width):
        part = slice(j * width, (j + 1) * width)
        out[0, :, pl.ds(pl.multiple_of((2 * j + side) * width, width), width)] = keep[:, part]
        out[0, :, pl.ds(pl.multiple_of((2 * j + 1 - side) * width, width), width)] = received[
            :, part
        ]


def paired_plan(
    hidden_in, norm_gain, qkv_weight, out_weight, key_cache, value_cache, cache_lengths, slot_request
):
    col_count, row_count = lax.axis_size("col"), lax.axis_size("row")
    pairs = col_count // row_count
    side, col, row = (lax.axis_index(name) for name in ("side", "col", "row"))
    run = row * pairs + lax.rem(col, pairs)
    place = jnp.stack([side, col, run]).astype(jnp.int32)
    rows, depth = hidden_in.shape
    half = depth // 2
    cache = key_cache.shape[1]
    parts = 1
    piece = rows // parts

    own_part = lax.dynamic_slice_in_dim(hidden_in, side * half, half, 1)
    gain = norm_gain.reshape(1, depth)
    half_in, half_out = qkv_weight.shape[1] // 2, out_weight.shape[1] // 2
    weight_in = call(
        stage_in_kernel,
        pltpu.VMEM((half, half_in), jnp.bfloat16),
        [SMEM, HBM, HBM],
        VMEM,
        0,
        half * half_in * 2,
        [pltpu.SemaphoreType.DMA((4,))],
    )(place, in_hbm(qkv_weight), gain)
    blocks = gathered([own_part], "col")
    *weights_out, key_part, value_part = call(
        stage_rest_kernel,
        [pltpu.VMEM((half, half_out), jnp.bfloat16)] * 2
        + [pltpu.VMEM((rows, cache, pairs * HEAD_DIM), jnp.bfloat16)] * 2,
        [SMEM, HBM, HBM, HBM],
        [VMEM] * 4,
        0,
        half * half_out * 4 + 4 * rows * cache * pairs * HEAD_DIM,
        [pltpu.SemaphoreType.DMA((4 * pairs,))],
    )(place, in_hbm(out_weight), in_hbm(key_cache), in_hbm(value_cache))

    products = spread(
        project(
            in_kernel,
            place,
            slot_request,
            blocks,
            [gain, in_hbm(qkv_weight)],
            weight_in,
            None,
            HEAD_DIM,
            pairs,
        )
    )

    key_part, value_part = in_vmem(key_part), in_vmem(value_part)
    runs = (pairs, piece // SLOTS, GROUP * SLOTS, SLOTS * cache)
    attended = [
        call(
            functools.partial(attend_all, col_count, first),
            struct((piece, half)),
            [SMEM, SMEM] + [VMEM] * (col_count + 2),
            VMEM,
            4 * piece * half * cache,
            0,
            [pltpu.VMEM(runs, jnp.float32), pltpu.VMEM(runs, jnp.bfloat16)],
        )(place, cache_lengths, *products, key_part, value_part)
        for first in range(0, rows, piece)
    ]

    products = spread(
        project(
            out_kernel, place, slot_request, gathered(attended, "col"), [], *weights_out, 0, pairs
        )
    )
    keep, send = call(
        functools.partial(sum_kernel, col_count, parts),
        [struct((rows, half)), struct((rows, half))],
        [SMEM] + [VMEM] * (1 + parts + col_count),
        [VMEM, VMEM],
        rows * depth * 4,
        rows * depth * 8,
    )(place, hidden_in, *attended, *products)
    return call(
        join_kernel,
        struct((1, rows, depth)),
        [SMEM, VMEM, VMEM],
        VMEM,
        0,
        rows * depth * 4,
    )(place, keep, moved(send, "side", 1))


def per_device(*args):
    hidden_in, _, qkv_weight, out_weight, key_cache = args[:5]
    col_count, row_count = lax.axis_size("col"), lax.axis_size("row")
    fits = (
        lax.axis_size("side") == 2
        and qkv_weight.shape[1] == 2 * GROUP_WIDTH
        and col_count % row_count == 0
        and col_count & (col_count - 1) == 0
        and hidden_in.shape[0] % 32 == 0
        and key_cache.shape[1] % 16 == 0
        and hidden_in.shape[1] == 2 * OUT_WIDTH * (col_count // row_count)
    )
    return paired_plan(*args) if fits else general_plan(*args)


def solution(mesh):
    placed = (
        P(("groups", "col"), "row"),
        P("row"),
        P("row", "col"),
        P("row", "col"),
        P(("groups", "col"), None, "row"),
        P(("groups", "col"), None, "row"),
        P(("groups", "col")),
        P("groups"),
    )
    return jax.shard_map(
        per_device,
        mesh=mesh,
        in_specs=placed,
        out_specs=P("side", ("groups", "col"), "row"),
        check_vma=False,
    )
```

```python
import functools
import math

import jax
import jax.numpy as jnp
from jax import lax
from jax.experimental import pallas as pl
from jax.experimental.pallas import tpu as pltpu
from jax.sharding import PartitionSpec as P

D = 8192
HEADS = 64
KV_HEADS = 8
HEAD_DIM = 128
QKV = 10240


EPSILON = 1e-05
THETA = 500000.0


def swapped(value, axis, bit):
    mask = 2**bit
    pairs = [(source, source ^ mask) for source in range(lax.axis_size(axis))]
    return lax.ppermute(value, axis, pairs)


def rope_tables(lengths, head_dim):
    half_dim = head_dim // 2
    inv_freq = jnp.exp(
        -jnp.log(jnp.float32(THETA)) * jnp.arange(half_dim, dtype=jnp.float32) / half_dim
    )
    phases = lengths.astype(jnp.float32)[:, None] * inv_freq[None, :]
    return (jnp.cos(phases), jnp.sin(phases))


def rotate(vector, cos_vals, sine_vals):
    half_dim = vector.shape[-1] // 2
    front_half = vector[..., :half_dim]
    back_half = vector[..., half_dim:]
    return jnp.concatenate(
        [
            front_half * cos_vals - back_half * sine_vals,
            back_half * cos_vals + front_half * sine_vals,
        ],
        axis=-1,
    )


def attend(packed, key_block, value_block, lengths):
    slot_count = packed.shape[0]
    cache_size = key_block.shape[1]
    groups = key_block.shape[2] // HEAD_DIM
    per_group = HEADS // KV_HEADS
    grouped = packed.reshape(slot_count, groups, per_group + 2, HEAD_DIM)
    cos_vals, sine_vals = rope_tables(lengths, HEAD_DIM)
    queries = rotate(
        grouped[:, :, :per_group].astype(jnp.float32),
        cos_vals[:, None, None, :],
        sine_vals[:, None, None, :],
    ).astype(jnp.bfloat16)
    new_keys = rotate(
        grouped[:, :, per_group].astype(jnp.float32), cos_vals[:, None, :], sine_vals[:, None, :]
    ).astype(jnp.bfloat16)
    new_values = grouped[:, :, per_group + 1]
    cache_keys = key_block.reshape(slot_count, cache_size, groups, HEAD_DIM)
    cache_values = value_block.reshape(slot_count, cache_size, groups, HEAD_DIM)
    factor = HEAD_DIM ** (-0.5)
    cache_scores = (
        jnp.einsum("sghd,slgd->sghl", queries, cache_keys, preferred_element_type=jnp.float32)
        * factor
    )
    own_scores = (
        jnp.einsum("sghd,sgd->sgh", queries, new_keys, preferred_element_type=jnp.float32) * factor
    )
    in_cache = lax.broadcasted_iota(jnp.int32, (slot_count, cache_size), 1) < lengths[:, None]
    cache_scores = jnp.where(in_cache[:, None, None, :], cache_scores, -1e30)
    row_max = jnp.maximum(jnp.max(cache_scores, axis=-1), own_scores)
    cache_exp = jnp.exp(cache_scores - row_max[..., None])
    own_exp = jnp.exp(own_scores - row_max)
    denominator = jnp.sum(cache_exp, axis=-1) + own_exp
    cache_weight = (cache_exp / denominator[..., None]).astype(jnp.bfloat16)
    own_weight = (own_exp / denominator).astype(jnp.bfloat16)
    combined = jnp.einsum(
        "sghl,slgd->sghd", cache_weight, cache_values, preferred_element_type=jnp.float32
    )
    combined = (
        combined
        + own_weight.astype(jnp.float32)[..., None] * new_values.astype(jnp.float32)[:, :, None, :]
    )
    return combined.astype(jnp.bfloat16).reshape(slot_count, groups * per_group * HEAD_DIM)


def general_plan(
    hidden_in,
    norm_gain,
    qkv_weight,
    out_weight,
    key_cache,
    value_cache,
    cache_lengths,
    slot_request,
):
    side_index = lax.axis_index("side")
    is_weight = side_index == 0
    col_count = lax.axis_size("col")
    row_count = lax.axis_size("row")
    group_cols = col_count // row_count
    in_half = qkv_weight.shape[1] // 2
    out_half = out_weight.shape[1] // 2
    residual = hidden_in.astype(jnp.float32)
    square_sums = lax.psum(jnp.sum(residual * residual, axis=1), "row")
    normed = (
        residual
        * lax.rsqrt(square_sums[:, None] / D + EPSILON)
        * norm_gain.astype(jnp.float32)[None, :]
    ).astype(jnp.bfloat16)
    in_weight = lax.dynamic_slice_in_dim(qkv_weight, side_index * in_half, in_half, 1)
    partial_in = jnp.dot(
        lax.all_gather(normed, "col", axis=0, tiled=True),
        in_weight,
        preferred_element_type=jnp.float32,
    )
    in_slots = jnp.take(partial_in, slot_request, axis=0)
    own_width = QKV // row_count
    summed = lax.psum(in_slots.astype(jnp.bfloat16), "row")
    spread = lax.all_to_all(summed, "col", split_axis=0, concat_axis=1, tiled=True)
    own_columns = lax.dynamic_slice_in_dim(
        spread.reshape(spread.shape[0], col_count, in_half),
        lax.axis_index("row") * group_cols,
        group_cols,
        1,
    )
    slot_half = key_cache.shape[0] // 2
    halves = lax.all_to_all(
        own_columns[:, :, None, :], "side", split_axis=0, concat_axis=2, tiled=True
    )
    arrived = halves.reshape(slot_half, own_width)
    first_slot = side_index * slot_half
    key_part = lax.dynamic_slice_in_dim(key_cache, first_slot, slot_half, 0)
    value_part = lax.dynamic_slice_in_dim(value_cache, first_slot, slot_half, 0)
    length_part = lax.dynamic_slice_in_dim(cache_lengths, first_slot, slot_half, 0)
    attended = attend(arrived, key_part, value_part, length_part)
    out_cols = lax.dynamic_slice_in_dim(out_weight, side_index * out_half, out_half, 1)
    collected = lax.all_gather(attended, ("col", "side"), axis=0, tiled=True)
    out_slots = jnp.dot(collected, out_cols, preferred_element_type=jnp.float32)
    inverse = jnp.argsort(slot_request)
    out_requests = jnp.take(out_slots, inverse, axis=0)
    spread_out = lax.all_to_all(
        out_requests.astype(jnp.bfloat16), "col", split_axis=0, concat_axis=1, tiled=True
    ).astype(out_requests.dtype)
    out_view = spread_out.reshape(spread_out.shape[0], col_count, out_half)
    summed_out = lax.psum_scatter(
        out_view.astype(jnp.bfloat16), "row", scatter_dimension=1, tiled=True
    ).astype(jnp.float32)
    req_rows = hidden_in.shape[0]
    residual_view = residual.reshape(req_rows, group_cols, 2, out_half)
    residual_half = lax.dynamic_index_in_dim(residual_view, side_index, 2, keepdims=False)
    own_hidden = (residual_half + summed_out).astype(jnp.bfloat16)
    payload = jnp.where(is_weight, attended, own_hidden.reshape(attended.shape))
    received = swapped(payload, "side", 0)
    hidden = jnp.stack([own_hidden, received.reshape(own_hidden.shape)], axis=2).reshape(
        req_rows, residual.shape[1]
    )
    attention_rows = jnp.concatenate([received, attended], axis=0)
    result = jnp.where(is_weight, hidden, attention_rows)
    return result[None]


GROUP = HEADS // KV_HEADS
GROUP_WIDTH = (GROUP + 2) * HEAD_DIM
OUT_WIDTH = GROUP * HEAD_DIM
SLOTS = 8
VMEM = pl.BlockSpec(memory_space=pltpu.VMEM)
SMEM = pl.BlockSpec(memory_space=pltpu.SMEM)
HBM = pl.BlockSpec(memory_space=pl.ANY)
MIB = 2**20


def call(kernel, out_shape, in_specs, out_specs, flops, size, scratch=(), limit=16):
    return pl.pallas_call(
        kernel,
        out_shape=out_shape,
        in_specs=in_specs,
        out_specs=out_specs,
        scratch_shapes=list(scratch),
        compiler_params=pltpu.CompilerParams(vmem_limit_bytes=limit * MIB),
        cost_estimate=pl.CostEstimate(flops=flops, bytes_accessed=size, transcendentals=0),
    )


def in_vmem(value):
    return pltpu.with_memory_space_constraint(value, pltpu.VMEM)


def in_hbm(value):
    return pltpu.with_memory_space_constraint(value, pltpu.HBM)


def struct(shape, dtype=jnp.bfloat16):
    return jax.ShapeDtypeStruct(shape, dtype)


def moved(value, axis, mask):
    pairs = [(source, source ^ mask) for source in range(lax.axis_size(axis))]
    return lax.ppermute(value, axis, pairs)


def run_copies(copies, sems):
    copies = [
        pltpu.make_async_copy(source, target, sems.at[i])
        for i, (source, target) in enumerate(copies)
    ]
    for copy in copies:
        copy.start()
    for copy in copies:
        copy.wait()


def stage_in_kernel(place, weight, gain, give_part, own_part, sems):
    depth, width = own_part.shape
    rows = pl.ds(pl.multiple_of(place[0] * depth, depth), depth)
    copies = []
    for target, half in ((give_part, 1 - place[0]), (own_part, place[0])):
        columns = pl.ds(pl.multiple_of(half * width, width), width)
        copies.append((weight.at[rows, columns], target))
    run_copies(copies, sems)


def stage_out_kernel(give, place, weight, *refs):
    sems = refs[-1]
    target = refs[2] if give else refs[1]
    width = target.shape[1]
    half = 1 - place[0] if give else place[0]
    columns = pl.ds(pl.multiple_of(half * width, width), width)
    copies = []
    for j in range(target.shape[0] // OUT_WIDTH):
        head = 2 * j + place[0]
        row = pl.multiple_of(head * OUT_WIDTH, OUT_WIDTH)
        if give:
            keys, values, _, key_part, value_part, _ = refs
            lane = pl.multiple_of(head * HEAD_DIM, HEAD_DIM)
            for cache, part in ((keys, key_part), (values, value_part)):
                copies.append(
                    (
                        cache.at[:, :, pl.ds(lane, HEAD_DIM)],
                        part.at[:, :, pl.ds(j * HEAD_DIM, HEAD_DIM)],
                    )
                )
        copies.append(
            (
                weight.at[pl.ds(row, OUT_WIDTH), columns],
                target.at[pl.ds(j * OUT_WIDTH, OUT_WIDTH), :],
            )
        )
    run_copies(copies, sems)


def one_hot(slots, scratch, blocks, slot_base, request_base):
    total = slots.shape[0]
    rows = total // blocks
    index = lax.broadcasted_iota(jnp.int32, (total, total), 0)
    request = (lax.div(index, rows) ^ request_base) * rows + lax.rem(index, rows)
    scratch[...] = jnp.where(slots[...].reshape(1, total) == request, 1.0, 0.0).T
    parts = [
        scratch[pl.ds(pl.multiple_of((slot_base ^ i) * rows, rows), rows), :]
        for i in range(blocks)
    ]
    return jnp.concatenate(parts, axis=0)


def pieces(sums):
    high = sums.astype(jnp.bfloat16).astype(jnp.float32)
    middle = (sums - high).astype(jnp.bfloat16).astype(jnp.float32)
    low = sums - high - middle
    lane = lax.broadcasted_iota(jnp.int32, (sums.shape[0], HEAD_DIM), 1)
    parts = jnp.where(lane == 0, high, jnp.where(lane == 1, middle, low))
    return jnp.where(lane < 3, parts, 0.0).astype(jnp.bfloat16)


def dot_columns(rows, weight, out):
    size, width = weight.shape[1], 512
    for start in range(0, size, width):
        part = slice(start, min(start + width, size))
        product = jnp.dot(rows, weight[:, part], preferred_element_type=jnp.float32)
        out[:, part] = product.astype(out.dtype)


def in_kernel(count, blocks, place, slots, *refs):
    pieces_in, (gain, weight, give, permuted, scratch) = refs[:count], refs[count:]
    side = place[0]
    depth = pieces_in[0].shape[1]
    half = weight.shape[1]
    gains = gain[:, pl.ds(pl.multiple_of(side * depth, depth), depth)].astype(jnp.float32)
    values = jnp.concatenate([piece[...].astype(jnp.float32) for piece in pieces_in], axis=0)
    sums = pieces(jnp.sum(values * values, axis=1, keepdims=True))
    chosen = one_hot(slots, scratch, blocks, place[2], place[1]).astype(jnp.bfloat16)
    order = jnp.dot(
        chosen, (values * gains).astype(jnp.bfloat16), preferred_element_type=jnp.float32
    ).astype(jnp.bfloat16)
    permuted[...] = order
    give[:, half:] = jnp.dot(chosen, sums, preferred_element_type=jnp.float32).astype(jnp.bfloat16)
    dot_columns(order, weight, give)


def out_kernel(count, blocks, place, slots, *refs):
    pieces_in, (_, weight, give, permuted, scratch) = refs[:count], refs[count:]
    values = jnp.concatenate([piece[...] for piece in pieces_in], axis=0)
    chosen = one_hot(slots, scratch, blocks, place[1], place[2]).T.astype(jnp.bfloat16)
    order = jnp.dot(chosen, values, preferred_element_type=jnp.float32).astype(jnp.bfloat16)
    permuted[...] = order
    dot_columns(order, weight, give)


def merge_kernel(own, given, received, *outs):
    rows = outs[0].shape[0]
    half = own.shape[1]
    more = given.shape[1] - half
    for i, out in enumerate(outs):
        part = slice(i * rows, (i + 1) * rows)
        total = own[part, :] + received[part, :half].astype(jnp.float32)
        out[:, :half] = total.astype(jnp.bfloat16)
        if out.shape[1] > half:
            out[:, half:] = jnp.concatenate(
                [given[part, half : half + more // 2], received[part, half : half + more // 2]],
                axis=1,
            )


def own_kernel(permuted, weight, own):
    dot_columns(permuted[...], weight, own)


def project(kernel, place, slots, pieces_in, extra, weights, more, pairs):
    count = lax.axis_size("col")
    parts = len(pieces_in)
    rows, depth = pieces_in[0].shape
    rows = rows * parts
    half = weights[0].shape[1]
    flops = 2 * rows * depth * half
    give, permuted = call(
        functools.partial(kernel, parts, count),
        [struct((rows, half + more)), struct((rows, depth))],
        [SMEM, VMEM] + [VMEM] * (parts + len(extra) + 1),
        [VMEM, VMEM],
        flops,
        depth * half * 2,
        [pltpu.VMEM((rows, rows), jnp.float32)],
    )(place, slots, *pieces_in, *extra, in_vmem(weights[0]))
    received = moved(give, "side", 1)
    own = call(
        own_kernel,
        struct((rows, half), jnp.float32),
        [VMEM, VMEM],
        VMEM,
        flops,
        depth * half * 2,
    )(permuted, in_vmem(weights[1]))
    return call(
        merge_kernel,
        [
            struct((rows // count, half + (more if i % pairs == pairs - 1 else 0)))
            for i in range(count)
        ],
        [VMEM] * 3,
        [VMEM] * count,
        rows * half,
        rows * half * 8,
    )(own, give, received)


def gathered(parts, axis):
    blocks = {0: parts}
    mask = lax.axis_size(axis) // 2
    while mask:
        blocks |= {
            known | mask: [moved(part, axis, mask) for part in block]
            for known, block in blocks.items()
        }
        mask //= 2
    return [part for i in sorted(blocks) for part in blocks[i]]


def spread(products):
    col_count, row_count = lax.axis_size("col"), lax.axis_size("row")
    pairs = col_count // row_count
    order = sorted(range(col_count), key=lambda j: (-(j % pairs), -j))
    sent = {
        j: lax.ppermute(
            products[j],
            ("col", "row"),
            [
                (
                    col * row_count + row,
                    ((row * pairs + col % pairs) ^ j) * row_count + col // pairs,
                )
                for col in range(col_count)
                for row in range(row_count)
            ],
        )
        for j in order
    }
    return [sent[j] for j in range(col_count)]


def rotated(vector, cosine, sine):
    return vector * cosine + pltpu.roll(vector, HEAD_DIM // 2, 1) * sine


def rope(lengths, rows):
    slot = lax.broadcasted_iota(jnp.int32, (rows, HEAD_DIM), 0)
    length_of = jnp.zeros((rows, HEAD_DIM), jnp.int32)
    for i in range(rows):
        length_of = jnp.where(slot == i, lengths[i], length_of)
    lane = lax.broadcasted_iota(jnp.int32, (rows, HEAD_DIM), 1)
    half = HEAD_DIM // 2
    step = lax.rem(lane, half).astype(jnp.float32)
    phases = length_of.astype(jnp.float32) * jnp.exp(-math.log(THETA) * step / half)
    sine = jnp.sin(phases)
    return jnp.cos(phases), jnp.where(lane < half, -sine, sine), length_of[:, :1]


def attend_all(count, parts, place, lengths, *refs):
    blocks, (keys, values), refs = refs[:count], refs[count : count + 2], refs[count + 2 :]
    outs, (scores_of, probs_of) = refs[:parts], refs[parts:]
    pairs = keys.shape[2] // HEAD_DIM
    rows, cache = keys.shape[:2]
    low = place[1] % pairs
    width = GROUP_WIDTH
    squares = blocks[pairs - 1][:, width:].astype(jnp.float32)
    for i in range(2 * pairs - 1, count, pairs):
        squares = squares + blocks[i][:, width:].astype(jnp.float32)
    scale = lax.rsqrt(jnp.sum(squares, axis=1, keepdims=True) / D + EPSILON)
    factor = HEAD_DIM ** (-0.5)
    cosines, sines, length_of = rope(lengths, rows)
    lane = lax.broadcasted_iota(jnp.int32, (SLOTS, SLOTS * cache), 1)
    slot = lax.broadcasted_iota(jnp.int32, (SLOTS, SLOTS * cache), 0)
    position = lane - slot * cache
    runs = [slice(start, start + SLOTS) for start in range(0, rows, SLOTS)]
    filled = [(position >= 0) & (position < length_of[part]) for part in runs]
    own, new_values, own_probs = [], [], []
    for pair in range(pairs):
        total = blocks[pair][:, :width].astype(jnp.float32)
        for i in range(pair + pairs, count, pairs):
            total = total + blocks[i][:, :width].astype(jnp.float32)
        total = (total * scale).astype(jnp.bfloat16).astype(jnp.float32)
        heads = [total[:, h * HEAD_DIM : (h + 1) * HEAD_DIM] for h in range(GROUP + 2)]
        queries = [
            rotated(head, cosines, sines).astype(jnp.bfloat16).astype(jnp.float32)
            for head in heads[:GROUP]
        ]
        new_key = rotated(heads[GROUP], cosines, sines).astype(jnp.bfloat16).astype(jnp.float32)
        new_values.append(heads[GROUP + 1])
        own.append([jnp.sum(query * new_key, axis=1, keepdims=True) * factor for query in queries])
        lanes = pl.ds(pl.multiple_of((low ^ pair) * HEAD_DIM, HEAD_DIM), HEAD_DIM)
        for run, part in enumerate(runs):
            query = jnp.concatenate([head[part] for head in queries], axis=0)
            key = keys[part, :, lanes].reshape(SLOTS * cache, HEAD_DIM)
            scores_of[pair, run] = lax.dot_general(
                query.astype(jnp.bfloat16),
                key,
                (((1,), (1,)), ((), ())),
                preferred_element_type=jnp.float32,
            )
    for pair in range(pairs):
        for run, part in enumerate(runs):
            scores = (scores_of[pair, run] * factor).reshape(GROUP, SLOTS, SLOTS * cache)
            scores = jnp.where(filled[run][None], scores, -1e30)
            own_score = jnp.concatenate([head[part] for head in own[pair]], axis=0).reshape(
                GROUP, SLOTS, 1
            )
            highest = jnp.maximum(jnp.max(scores, axis=2, keepdims=True), own_score)
            weights = jnp.exp(scores - highest)
            own_weight = jnp.exp(own_score - highest)
            inverse = 1.0 / (jnp.sum(weights, axis=2, keepdims=True) + own_weight)
            probs = (weights * inverse).astype(jnp.bfloat16)
            probs_of[pair, run] = probs.reshape(GROUP * SLOTS, SLOTS * cache)
            own_probs.append((own_weight * inverse).astype(jnp.bfloat16).astype(jnp.float32))
    for pair in range(pairs):
        lanes = pl.ds(pl.multiple_of((low ^ pair) * HEAD_DIM, HEAD_DIM), HEAD_DIM)
        results = []
        for run, part in enumerate(runs):
            value = values[part, :, lanes].reshape(SLOTS * cache, HEAD_DIM)
            mixed = jnp.dot(probs_of[pair, run], value, preferred_element_type=jnp.float32)
            own_prob = own_probs[pair * len(runs) + run]
            results.append(
                mixed.reshape(GROUP, SLOTS, HEAD_DIM) + own_prob * new_values[pair][part][None]
            )
        for head in range(GROUP):
            at = pl.multiple_of((low ^ pair) * OUT_WIDTH + head * HEAD_DIM, HEAD_DIM)
            size = len(results) // parts
            for i, out in enumerate(outs):
                joined = jnp.concatenate(
                    [result[head] for result in results[i * size : (i + 1) * size]], axis=0
                )
                out[:, pl.ds(at, HEAD_DIM)] = joined.astype(jnp.bfloat16)


def sum_kernel(count, parts, place, hidden, *refs):
    attended, blocks, (keep, send) = refs[:parts], refs[parts : parts + count], refs[parts + count :]
    rows, width = blocks[0].shape
    pairs = keep.shape[1] // width
    side = place[0]
    low = place[1] % pairs
    for pair in range(pairs):
        column = low ^ pair
        total = blocks[pair][...].astype(jnp.float32)
        for i in range(pair + pairs, count, pairs):
            total = total + blocks[i][...].astype(jnp.float32)
        at = pl.ds(pl.multiple_of((2 * column + side) * width, width), width)
        hidden_out = (hidden[:, at].astype(jnp.float32) + total).astype(jnp.bfloat16)
        at = pl.ds(pl.multiple_of(column * width, width), width)
        attention = jnp.concatenate([part[:, at] for part in attended], axis=0)
        keep[:, at] = jnp.where(side == 0, hidden_out, attention)
        send[:, at] = jnp.where(side == 0, attention, hidden_out)


def join_kernel(place, keep, received, out):
    side = place[0]
    width = OUT_WIDTH
    for j in range(keep.shape[1] // width):
        part = slice(j * width, (j + 1) * width)
        out[0, :, pl.ds(pl.multiple_of((2 * j + side) * width, width), width)] = keep[:, part]
        out[0, :, pl.ds(pl.multiple_of((2 * j + 1 - side) * width, width), width)] = received[
            :, part
        ]


def paired_plan(
    hidden_in, norm_gain, qkv_weight, out_weight, key_cache, value_cache, cache_lengths, slot_request
):
    col_count, row_count = lax.axis_size("col"), lax.axis_size("row")
    pairs = col_count // row_count
    side, col, row = (lax.axis_index(name) for name in ("side", "col", "row"))
    run = row * pairs + lax.rem(col, pairs)
    place = jnp.stack([side, col, run]).astype(jnp.int32)
    rows, depth = hidden_in.shape
    half = depth // 2
    cache = key_cache.shape[1]
    parts = 2
    piece = rows // parts

    own_part = lax.dynamic_slice_in_dim(hidden_in, side * half, half, 1)
    gain = norm_gain.reshape(1, depth)
    half_in, half_out = qkv_weight.shape[1] // 2, out_weight.shape[1] // 2
    weights_in = call(
        stage_in_kernel,
        [pltpu.VMEM((half, half_in), jnp.bfloat16)] * 2,
        [SMEM, HBM, HBM],
        [VMEM] * 2,
        0,
        half * half_in * 4,
        [pltpu.SemaphoreType.DMA((2,))],
    )(place, in_hbm(qkv_weight), gain)
    blocks = gathered(
        [own_part[i * piece : (i + 1) * piece] for i in range(parts)], "col"
    )
    out_give, key_part, value_part = call(
        functools.partial(stage_out_kernel, True),
        [pltpu.VMEM((half, half_out), jnp.bfloat16)]
        + [pltpu.VMEM((rows, cache, pairs * HEAD_DIM), jnp.bfloat16)] * 2,
        [SMEM, HBM, HBM, HBM],
        [VMEM] * 3,
        0,
        half * half_out * 2 + 4 * rows * cache * pairs * HEAD_DIM,
        [pltpu.SemaphoreType.DMA((3 * pairs,))],
    )(place, in_hbm(out_weight), in_hbm(key_cache), in_hbm(value_cache))

    products = spread(
        project(in_kernel, place, slot_request, blocks, [gain], weights_in, HEAD_DIM, pairs)
    )

    key_part, value_part = in_vmem(key_part), in_vmem(value_part)
    runs = (pairs, rows // SLOTS, GROUP * SLOTS, SLOTS * cache)
    attended = call(
        functools.partial(attend_all, col_count, parts),
        [struct((piece, half))] * parts,
        [SMEM, SMEM] + [VMEM] * (col_count + 2),
        [VMEM] * parts,
        4 * rows * half * cache,
        0,
        [pltpu.VMEM(runs, jnp.float32), pltpu.VMEM(runs, jnp.bfloat16)],
    )(place, cache_lengths, *products, key_part, value_part)

    out_own = call(
        functools.partial(stage_out_kernel, False),
        pltpu.VMEM((half, half_out), jnp.bfloat16),
        [SMEM, HBM, HBM],
        VMEM,
        0,
        half * half_out * 2,
        [pltpu.SemaphoreType.DMA((pairs,))],
    )(place, in_hbm(out_weight), attended[-1])
    products = spread(
        project(
            out_kernel,
            place,
            slot_request,
            gathered(attended, "col"),
            [in_vmem(out_own)],
            [out_give, out_own],
            0,
            pairs,
        )
    )
    keep, send = call(
        functools.partial(sum_kernel, col_count, parts),
        [struct((rows, half)), struct((rows, half))],
        [SMEM] + [VMEM] * (1 + parts + col_count),
        [VMEM, VMEM],
        rows * depth * 4,
        rows * depth * 8,
    )(place, hidden_in, *attended, *products)
    return call(
        join_kernel,
        struct((1, rows, depth)),
        [SMEM, VMEM, VMEM],
        VMEM,
        0,
        rows * depth * 4,
    )(place, keep, moved(send, "side", 1))


def per_device(*args):
    hidden_in, _, qkv_weight, out_weight, key_cache = args[:5]
    col_count, row_count = lax.axis_size("col"), lax.axis_size("row")
    fits = (
        lax.axis_size("side") == 2
        and qkv_weight.shape[1] == 2 * GROUP_WIDTH
        and col_count % row_count == 0
        and col_count & (col_count - 1) == 0
        and hidden_in.shape[0] % 32 == 0
        and key_cache.shape[1] % 16 == 0
        and hidden_in.shape[1] == 2 * OUT_WIDTH * (col_count // row_count)
    )
    return paired_plan(*args) if fits else general_plan(*args)


def solution(mesh):
    placed = (
        P(("groups", "col"), "row"),
        P("row"),
        P("row", "col"),
        P("row", "col"),
        P(("groups", "col"), None, "row"),
        P(("groups", "col"), None, "row"),
        P(("groups", "col")),
        P("groups"),
    )
    return jax.shard_map(
        per_device,
        mesh=mesh,
        in_specs=placed,
        out_specs=P("side", ("groups", "col"), "row"),
        check_vma=False,
    )
```

```python
import functools
import math

import jax
import jax.numpy as jnp
from jax import lax
from jax.experimental import pallas as pl
from jax.experimental.pallas import tpu as pltpu
from jax.sharding import PartitionSpec as P

D = 8192
HEADS = 64
KV_HEADS = 8
HEAD_DIM = 128
QKV = 10240


EPSILON = 1e-05
THETA = 500000.0


def swapped(value, axis, bit):
    mask = 2**bit
    pairs = [(source, source ^ mask) for source in range(lax.axis_size(axis))]
    return lax.ppermute(value, axis, pairs)


def rope_tables(lengths, head_dim):
    half_dim = head_dim // 2
    inv_freq = jnp.exp(
        -jnp.log(jnp.float32(THETA)) * jnp.arange(half_dim, dtype=jnp.float32) / half_dim
    )
    phases = lengths.astype(jnp.float32)[:, None] * inv_freq[None, :]
    return (jnp.cos(phases), jnp.sin(phases))


def rotate(vector, cos_vals, sine_vals):
    half_dim = vector.shape[-1] // 2
    front_half = vector[..., :half_dim]
    back_half = vector[..., half_dim:]
    return jnp.concatenate(
        [
            front_half * cos_vals - back_half * sine_vals,
            back_half * cos_vals + front_half * sine_vals,
        ],
        axis=-1,
    )


def attend(packed, key_block, value_block, lengths):
    slot_count = packed.shape[0]
    cache_size = key_block.shape[1]
    groups = key_block.shape[2] // HEAD_DIM
    per_group = HEADS // KV_HEADS
    grouped = packed.reshape(slot_count, groups, per_group + 2, HEAD_DIM)
    cos_vals, sine_vals = rope_tables(lengths, HEAD_DIM)
    queries = rotate(
        grouped[:, :, :per_group].astype(jnp.float32),
        cos_vals[:, None, None, :],
        sine_vals[:, None, None, :],
    ).astype(jnp.bfloat16)
    new_keys = rotate(
        grouped[:, :, per_group].astype(jnp.float32), cos_vals[:, None, :], sine_vals[:, None, :]
    ).astype(jnp.bfloat16)
    new_values = grouped[:, :, per_group + 1]
    cache_keys = key_block.reshape(slot_count, cache_size, groups, HEAD_DIM)
    cache_values = value_block.reshape(slot_count, cache_size, groups, HEAD_DIM)
    factor = HEAD_DIM ** (-0.5)
    cache_scores = (
        jnp.einsum("sghd,slgd->sghl", queries, cache_keys, preferred_element_type=jnp.float32)
        * factor
    )
    own_scores = (
        jnp.einsum("sghd,sgd->sgh", queries, new_keys, preferred_element_type=jnp.float32) * factor
    )
    in_cache = lax.broadcasted_iota(jnp.int32, (slot_count, cache_size), 1) < lengths[:, None]
    cache_scores = jnp.where(in_cache[:, None, None, :], cache_scores, -1e30)
    row_max = jnp.maximum(jnp.max(cache_scores, axis=-1), own_scores)
    cache_exp = jnp.exp(cache_scores - row_max[..., None])
    own_exp = jnp.exp(own_scores - row_max)
    denominator = jnp.sum(cache_exp, axis=-1) + own_exp
    cache_weight = (cache_exp / denominator[..., None]).astype(jnp.bfloat16)
    own_weight = (own_exp / denominator).astype(jnp.bfloat16)
    combined = jnp.einsum(
        "sghl,slgd->sghd", cache_weight, cache_values, preferred_element_type=jnp.float32
    )
    combined = (
        combined
        + own_weight.astype(jnp.float32)[..., None] * new_values.astype(jnp.float32)[:, :, None, :]
    )
    return combined.astype(jnp.bfloat16).reshape(slot_count, groups * per_group * HEAD_DIM)


def general_plan(
    hidden_in,
    norm_gain,
    qkv_weight,
    out_weight,
    key_cache,
    value_cache,
    cache_lengths,
    slot_request,
):
    side_index = lax.axis_index("side")
    is_weight = side_index == 0
    col_count = lax.axis_size("col")
    row_count = lax.axis_size("row")
    group_cols = col_count // row_count
    in_half = qkv_weight.shape[1] // 2
    out_half = out_weight.shape[1] // 2
    residual = hidden_in.astype(jnp.float32)
    square_sums = lax.psum(jnp.sum(residual * residual, axis=1), "row")
    normed = (
        residual
        * lax.rsqrt(square_sums[:, None] / D + EPSILON)
        * norm_gain.astype(jnp.float32)[None, :]
    ).astype(jnp.bfloat16)
    in_weight = lax.dynamic_slice_in_dim(qkv_weight, side_index * in_half, in_half, 1)
    partial_in = jnp.dot(
        lax.all_gather(normed, "col", axis=0, tiled=True),
        in_weight,
        preferred_element_type=jnp.float32,
    )
    in_slots = jnp.take(partial_in, slot_request, axis=0)
    own_width = QKV // row_count
    summed = lax.psum(in_slots.astype(jnp.bfloat16), "row")
    spread = lax.all_to_all(summed, "col", split_axis=0, concat_axis=1, tiled=True)
    own_columns = lax.dynamic_slice_in_dim(
        spread.reshape(spread.shape[0], col_count, in_half),
        lax.axis_index("row") * group_cols,
        group_cols,
        1,
    )
    slot_half = key_cache.shape[0] // 2
    halves = lax.all_to_all(
        own_columns[:, :, None, :], "side", split_axis=0, concat_axis=2, tiled=True
    )
    arrived = halves.reshape(slot_half, own_width)
    first_slot = side_index * slot_half
    key_part = lax.dynamic_slice_in_dim(key_cache, first_slot, slot_half, 0)
    value_part = lax.dynamic_slice_in_dim(value_cache, first_slot, slot_half, 0)
    length_part = lax.dynamic_slice_in_dim(cache_lengths, first_slot, slot_half, 0)
    attended = attend(arrived, key_part, value_part, length_part)
    out_cols = lax.dynamic_slice_in_dim(out_weight, side_index * out_half, out_half, 1)
    collected = lax.all_gather(attended, ("col", "side"), axis=0, tiled=True)
    out_slots = jnp.dot(collected, out_cols, preferred_element_type=jnp.float32)
    inverse = jnp.argsort(slot_request)
    out_requests = jnp.take(out_slots, inverse, axis=0)
    spread_out = lax.all_to_all(
        out_requests.astype(jnp.bfloat16), "col", split_axis=0, concat_axis=1, tiled=True
    ).astype(out_requests.dtype)
    out_view = spread_out.reshape(spread_out.shape[0], col_count, out_half)
    summed_out = lax.psum_scatter(
        out_view.astype(jnp.bfloat16), "row", scatter_dimension=1, tiled=True
    ).astype(jnp.float32)
    req_rows = hidden_in.shape[0]
    residual_view = residual.reshape(req_rows, group_cols, 2, out_half)
    residual_half = lax.dynamic_index_in_dim(residual_view, side_index, 2, keepdims=False)
    own_hidden = (residual_half + summed_out).astype(jnp.bfloat16)
    payload = jnp.where(is_weight, attended, own_hidden.reshape(attended.shape))
    received = swapped(payload, "side", 0)
    hidden = jnp.stack([own_hidden, received.reshape(own_hidden.shape)], axis=2).reshape(
        req_rows, residual.shape[1]
    )
    attention_rows = jnp.concatenate([received, attended], axis=0)
    result = jnp.where(is_weight, hidden, attention_rows)
    return result[None]


GROUP = HEADS // KV_HEADS
GROUP_WIDTH = (GROUP + 2) * HEAD_DIM
OUT_WIDTH = GROUP * HEAD_DIM
SLOTS = 8
VMEM = pl.BlockSpec(memory_space=pltpu.VMEM)
SMEM = pl.BlockSpec(memory_space=pltpu.SMEM)
HBM = pl.BlockSpec(memory_space=pl.ANY)
MIB = 2**20


def call(kernel, out_shape, in_specs, out_specs, flops, size, scratch=(), limit=16):
    return pl.pallas_call(
        kernel,
        out_shape=out_shape,
        in_specs=in_specs,
        out_specs=out_specs,
        scratch_shapes=list(scratch),
        compiler_params=pltpu.CompilerParams(vmem_limit_bytes=limit * MIB),
        cost_estimate=pl.CostEstimate(flops=flops, bytes_accessed=size, transcendentals=0),
    )


def in_vmem(value):
    return pltpu.with_memory_space_constraint(value, pltpu.VMEM)


def in_hbm(value):
    return pltpu.with_memory_space_constraint(value, pltpu.HBM)


def struct(shape, dtype=jnp.bfloat16):
    return jax.ShapeDtypeStruct(shape, dtype)


def moved(value, axis, mask):
    pairs = [(source, source ^ mask) for source in range(lax.axis_size(axis))]
    return lax.ppermute(value, axis, pairs)


def run_copies(copies, sems):
    copies = [
        pltpu.make_async_copy(source, target, sems.at[i])
        for i, (source, target) in enumerate(copies)
    ]
    for copy in copies:
        copy.start()
    for copy in copies:
        copy.wait()


def stage_in_kernel(place, weight, gain, give_part, own_part, sems):
    depth, width = own_part.shape
    rows = pl.ds(pl.multiple_of(place[0] * depth, depth), depth)
    copies = []
    for target, half in ((give_part, 1 - place[0]), (own_part, place[0])):
        columns = pl.ds(pl.multiple_of(half * width, width), width)
        copies.append((weight.at[rows, columns], target))
    run_copies(copies, sems)


def stage_out_kernel(first, place, weight, *refs):
    sems = refs[-1]
    target = refs[2] if first else refs[1]
    width = target.shape[1]
    columns = pl.ds(0 if first else width, width)
    copies = []
    for j in range(target.shape[0] // OUT_WIDTH):
        head = 2 * j + place[0]
        row = pl.multiple_of(head * OUT_WIDTH, OUT_WIDTH)
        if first:
            keys, values, _, key_part, value_part, _ = refs
            lane = pl.multiple_of(head * HEAD_DIM, HEAD_DIM)
            for cache, part in ((keys, key_part), (values, value_part)):
                copies.append(
                    (
                        cache.at[:, :, pl.ds(lane, HEAD_DIM)],
                        part.at[:, :, pl.ds(j * HEAD_DIM, HEAD_DIM)],
                    )
                )
        copies.append(
            (
                weight.at[pl.ds(row, OUT_WIDTH), columns],
                target.at[pl.ds(j * OUT_WIDTH, OUT_WIDTH), :],
            )
        )
    run_copies(copies, sems)


def one_hot(slots, scratch, blocks, slot_base, request_base):
    total = slots.shape[0]
    rows = total // blocks
    index = lax.broadcasted_iota(jnp.int32, (total, total), 0)
    request = (lax.div(index, rows) ^ request_base) * rows + lax.rem(index, rows)
    scratch[...] = jnp.where(slots[...].reshape(1, total) == request, 1.0, 0.0).T
    parts = [
        scratch[pl.ds(pl.multiple_of((slot_base ^ i) * rows, rows), rows), :]
        for i in range(blocks)
    ]
    return jnp.concatenate(parts, axis=0)


def pieces(sums):
    high = sums.astype(jnp.bfloat16).astype(jnp.float32)
    middle = (sums - high).astype(jnp.bfloat16).astype(jnp.float32)
    low = sums - high - middle
    lane = lax.broadcasted_iota(jnp.int32, (sums.shape[0], HEAD_DIM), 1)
    parts = jnp.where(lane == 0, high, jnp.where(lane == 1, middle, low))
    return jnp.where(lane < 3, parts, 0.0).astype(jnp.bfloat16)


def dot_columns(rows, weight, out):
    size, width = weight.shape[1], 512
    for start in range(0, size, width):
        part = slice(start, min(start + width, size))
        product = jnp.dot(rows, weight[:, part], preferred_element_type=jnp.float32)
        out[:, part] = product.astype(out.dtype)


def in_kernel(count, blocks, place, slots, *refs):
    pieces_in, (gain, weight, give, permuted, scratch) = refs[:count], refs[count:]
    side = place[0]
    depth = pieces_in[0].shape[1]
    half = weight.shape[1]
    gains = gain[:, pl.ds(pl.multiple_of(side * depth, depth), depth)].astype(jnp.float32)
    values = jnp.concatenate([piece[...].astype(jnp.float32) for piece in pieces_in], axis=0)
    sums = pieces(jnp.sum(values * values, axis=1, keepdims=True))
    chosen = one_hot(slots, scratch, blocks, place[2], place[1]).astype(jnp.bfloat16)
    order = jnp.dot(
        chosen, (values * gains).astype(jnp.bfloat16), preferred_element_type=jnp.float32
    ).astype(jnp.bfloat16)
    permuted[...] = order
    give[:, half:] = jnp.dot(chosen, sums, preferred_element_type=jnp.float32).astype(jnp.bfloat16)
    dot_columns(order, weight, give)


def out_kernel(count, blocks, place, slots, *refs):
    pieces_in, (first, second, give, own, scratch) = refs[:count], refs[count:]
    half = first.shape[1]
    values = jnp.concatenate([piece[...] for piece in pieces_in], axis=0)
    chosen = one_hot(slots, scratch, blocks, place[1], place[1]).T.astype(jnp.bfloat16)
    order = jnp.dot(chosen, values, preferred_element_type=jnp.float32).astype(jnp.bfloat16)
    dot_columns(order, first, own.at[:, :half])
    dot_columns(order, second, own.at[:, half:])
    give[...] = own[...].astype(give.dtype)


def sum_kernel(own, received, *outs):
    rows = outs[0].shape[0]
    for i, out in enumerate(outs):
        part = slice(i * rows, (i + 1) * rows)
        out[...] = (own[part, :] + received[part, :].astype(jnp.float32)).astype(out.dtype)


def merge_kernel(own, given, received, *outs):
    rows = outs[0].shape[0]
    half = own.shape[1]
    more = given.shape[1] - half
    for i, out in enumerate(outs):
        part = slice(i * rows, (i + 1) * rows)
        total = own[part, :] + received[part, :half].astype(jnp.float32)
        out[:, :half] = total.astype(jnp.bfloat16)
        if out.shape[1] > half:
            out[:, half:] = jnp.concatenate(
                [given[part, half : half + more // 2], received[part, half : half + more // 2]],
                axis=1,
            )


def own_kernel(permuted, weight, own):
    dot_columns(permuted[...], weight, own)


def project(kernel, place, slots, pieces_in, extra, weights, more, pairs):
    count = lax.axis_size("col")
    parts = len(pieces_in)
    depth = pieces_in[0].shape[1]
    rows = sum(part.shape[0] for part in pieces_in)
    half = weights[0].shape[1]
    flops = 2 * rows * depth * half
    give, permuted = call(
        functools.partial(kernel, parts, count),
        [struct((rows, half + more)), struct((rows, depth))],
        [SMEM, VMEM] + [VMEM] * (parts + len(extra) + 1),
        [VMEM, VMEM],
        flops,
        depth * half * 2,
        [pltpu.VMEM((rows, rows), jnp.float32)],
    )(place, slots, *pieces_in, *extra, in_vmem(weights[0]))
    received = moved(give, "side", 1)
    own = call(
        own_kernel,
        struct((rows, half), jnp.float32),
        [VMEM, VMEM],
        VMEM,
        flops,
        depth * half * 2,
    )(permuted, in_vmem(weights[1]))
    return call(
        merge_kernel,
        [
            struct((rows // count, half + (more if i % pairs == pairs - 1 else 0)))
            for i in range(count)
        ],
        [VMEM] * 3,
        [VMEM] * count,
        rows * half,
        rows * half * 8,
    )(own, give, received)


def gathered(whole, parts, axis):
    blocks = {0: parts}
    mask = lax.axis_size(axis) // 2
    while mask:
        arrived = {}
        for known, block in blocks.items():
            sent = [whole] if mask == 1 and known == 0 else block
            arrived[known | mask] = [moved(part, axis, mask) for part in sent]
        blocks |= arrived
        mask //= 2
    blocks[0] = [whole]
    return [part for i in sorted(blocks) for part in blocks[i]]


def spread(products):
    col_count, row_count = lax.axis_size("col"), lax.axis_size("row")
    pairs = col_count // row_count
    order = sorted(range(col_count), key=lambda j: (-(j % pairs), -j))
    sent = {
        j: lax.ppermute(
            products[j],
            ("col", "row"),
            [
                (
                    col * row_count + row,
                    ((row * pairs + col % pairs) ^ j) * row_count + col // pairs,
                )
                for col in range(col_count)
                for row in range(row_count)
            ],
        )
        for j in order
    }
    return [sent[j] for j in range(col_count)]


def rotated(vector, cosine, sine):
    return vector * cosine + pltpu.roll(vector, HEAD_DIM // 2, 1) * sine


def rope(lengths, rows):
    slot = lax.broadcasted_iota(jnp.int32, (rows, HEAD_DIM), 0)
    length_of = jnp.zeros((rows, HEAD_DIM), jnp.int32)
    for i in range(rows):
        length_of = jnp.where(slot == i, lengths[i], length_of)
    lane = lax.broadcasted_iota(jnp.int32, (rows, HEAD_DIM), 1)
    half = HEAD_DIM // 2
    step = lax.rem(lane, half).astype(jnp.float32)
    phases = length_of.astype(jnp.float32) * jnp.exp(-math.log(THETA) * step / half)
    sine = jnp.sin(phases)
    return jnp.cos(phases), jnp.where(lane < half, -sine, sine), length_of[:, :1]


def attend_all(count, parts, place, lengths, *refs):
    blocks, (keys, values), refs = refs[:count], refs[count : count + 2], refs[count + 2 :]
    whole, outs, (scores_of, probs_of) = refs[0], refs[1 : parts + 1], refs[parts + 1 :]
    pairs = keys.shape[2] // HEAD_DIM
    rows, cache = keys.shape[:2]
    low = place[1] % pairs
    width = GROUP_WIDTH
    squares = blocks[pairs - 1][:, width:].astype(jnp.float32)
    for i in range(2 * pairs - 1, count, pairs):
        squares = squares + blocks[i][:, width:].astype(jnp.float32)
    scale = lax.rsqrt(jnp.sum(squares, axis=1, keepdims=True) / D + EPSILON)
    factor = HEAD_DIM ** (-0.5)
    cosines, sines, length_of = rope(lengths, rows)
    lane = lax.broadcasted_iota(jnp.int32, (SLOTS, SLOTS * cache), 1)
    slot = lax.broadcasted_iota(jnp.int32, (SLOTS, SLOTS * cache), 0)
    position = lane - slot * cache
    runs = [slice(start, start + SLOTS) for start in range(0, rows, SLOTS)]
    filled = [(position >= 0) & (position < length_of[part]) for part in runs]
    own, new_values, own_probs = [], [], []
    for pair in range(pairs):
        total = blocks[pair][:, :width].astype(jnp.float32)
        for i in range(pair + pairs, count, pairs):
            total = total + blocks[i][:, :width].astype(jnp.float32)
        total = (total * scale).astype(jnp.bfloat16).astype(jnp.float32)
        heads = [total[:, h * HEAD_DIM : (h + 1) * HEAD_DIM] for h in range(GROUP + 2)]
        queries = [
            rotated(head, cosines, sines).astype(jnp.bfloat16).astype(jnp.float32)
            for head in heads[:GROUP]
        ]
        new_key = rotated(heads[GROUP], cosines, sines).astype(jnp.bfloat16).astype(jnp.float32)
        new_values.append(heads[GROUP + 1])
        own.append([jnp.sum(query * new_key, axis=1, keepdims=True) * factor for query in queries])
        lanes = pl.ds(pl.multiple_of((low ^ pair) * HEAD_DIM, HEAD_DIM), HEAD_DIM)
        for run, part in enumerate(runs):
            query = jnp.concatenate([head[part] for head in queries], axis=0)
            key = keys[part, :, lanes].reshape(SLOTS * cache, HEAD_DIM)
            scores_of[pair, run] = lax.dot_general(
                query.astype(jnp.bfloat16),
                key,
                (((1,), (1,)), ((), ())),
                preferred_element_type=jnp.float32,
            )
    for pair in range(pairs):
        for run, part in enumerate(runs):
            scores = (scores_of[pair, run] * factor).reshape(GROUP, SLOTS, SLOTS * cache)
            scores = jnp.where(filled[run][None], scores, -1e30)
            own_score = jnp.concatenate([head[part] for head in own[pair]], axis=0).reshape(
                GROUP, SLOTS, 1
            )
            highest = jnp.maximum(jnp.max(scores, axis=2, keepdims=True), own_score)
            weights = jnp.exp(scores - highest)
            own_weight = jnp.exp(own_score - highest)
            inverse = 1.0 / (jnp.sum(weights, axis=2, keepdims=True) + own_weight)
            probs = (weights * inverse).astype(jnp.bfloat16)
            probs_of[pair, run] = probs.reshape(GROUP * SLOTS, SLOTS * cache)
            own_probs.append((own_weight * inverse).astype(jnp.bfloat16).astype(jnp.float32))
    for pair in range(pairs):
        lanes = pl.ds(pl.multiple_of((low ^ pair) * HEAD_DIM, HEAD_DIM), HEAD_DIM)
        results = []
        for run, part in enumerate(runs):
            value = values[part, :, lanes].reshape(SLOTS * cache, HEAD_DIM)
            mixed = jnp.dot(probs_of[pair, run], value, preferred_element_type=jnp.float32)
            own_prob = own_probs[pair * len(runs) + run]
            results.append(
                mixed.reshape(GROUP, SLOTS, HEAD_DIM) + own_prob * new_values[pair][part][None]
            )
        for head in range(GROUP):
            at = pl.multiple_of((low ^ pair) * OUT_WIDTH + head * HEAD_DIM, HEAD_DIM)
            size = len(results) // parts
            for i, out in enumerate(outs):
                joined = jnp.concatenate(
                    [result[head] for result in results[i * size : (i + 1) * size]], axis=0
                )
                joined = joined.astype(jnp.bfloat16)
                out[:, pl.ds(at, HEAD_DIM)] = joined
                run = slice(i * joined.shape[0], (i + 1) * joined.shape[0])
                whole[run, pl.ds(at, HEAD_DIM)] = joined


def choose_kernel(count, other, place, *refs):
    blocks, out = refs[:count], refs[count]
    pairs = out.shape[0]
    wanted = place[3] ^ other
    for chunk in range(count // pairs):

        @pl.when(wanted == chunk)
        def _():
            for pair in range(pairs):
                out[pair] = blocks[chunk * pairs + pair][...]


def finish_kernel(count, others, place, hidden, attended, given, *refs):
    blocks, arrived, out = refs[:count], refs[count : count + others], refs[-1]
    pairs, _, width = arrived[0].shape
    low = place[1] % pairs

    @pl.when(place[0] == 0)
    def _():
        for pair in range(pairs):
            total = jnp.zeros(arrived[0].shape[1:], jnp.float32)
            for chunk in range(count // pairs):
                part = blocks[chunk * pairs + pair][...].astype(jnp.float32)
                total = total + jnp.where(place[3] == chunk, part, 0.0)
            for ref in arrived:
                total = total + ref[pair].astype(jnp.float32)
            at = pl.ds(pl.multiple_of((low ^ pair) * width, width), width)
            out[0, :, at] = (hidden[:, at].astype(jnp.float32) + total).astype(jnp.bfloat16)

    @pl.when(place[0] != 0)
    def _():
        size = OUT_WIDTH
        for j in range(attended.shape[1] // size):
            part = slice(j * size, (j + 1) * size)
            out[0, :, 2 * j * size : (2 * j + 1) * size] = given[:, part]
            out[0, :, (2 * j + 1) * size : (2 * j + 2) * size] = attended[:, part]


def paired_plan(
    hidden_in, norm_gain, qkv_weight, out_weight, key_cache, value_cache, cache_lengths, slot_request
):
    col_count, row_count = lax.axis_size("col"), lax.axis_size("row")
    pairs = col_count // row_count
    side, col, row = (lax.axis_index(name) for name in ("side", "col", "row"))
    run = row * pairs + lax.rem(col, pairs)
    base = lax.div(col, pairs) ^ row
    place = jnp.stack([side, col, run, base]).astype(jnp.int32)
    rows, depth = hidden_in.shape
    half = depth // 2
    cache = key_cache.shape[1]
    parts = 2
    piece = rows // parts

    own_part = lax.dynamic_slice_in_dim(hidden_in, side * half, half, 1)
    gain = norm_gain.reshape(1, depth)
    half_in, half_out = qkv_weight.shape[1] // 2, out_weight.shape[1] // 2
    weights_in = call(
        stage_in_kernel,
        [pltpu.VMEM((half, half_in), jnp.bfloat16)] * 2,
        [SMEM, HBM, HBM],
        [VMEM] * 2,
        0,
        half * half_in * 4,
        [pltpu.SemaphoreType.DMA((2,))],
    )(place, in_hbm(qkv_weight), gain)
    blocks = gathered(
        own_part, [own_part[i * piece : (i + 1) * piece] for i in range(parts)], "col"
    )
    out_first, key_part, value_part = call(
        functools.partial(stage_out_kernel, True),
        [pltpu.VMEM((half, half_out), jnp.bfloat16)]
        + [pltpu.VMEM((rows, cache, pairs * HEAD_DIM), jnp.bfloat16)] * 2,
        [SMEM, HBM, HBM, HBM],
        [VMEM] * 3,
        0,
        half * half_out * 2 + 4 * rows * cache * pairs * HEAD_DIM,
        [pltpu.SemaphoreType.DMA((3 * pairs,))],
    )(place, in_hbm(out_weight), in_hbm(key_cache), in_hbm(value_cache))

    products = spread(
        project(in_kernel, place, slot_request, blocks, [gain], weights_in, HEAD_DIM, pairs)
    )

    key_part, value_part = in_vmem(key_part), in_vmem(value_part)
    runs = (pairs, rows // SLOTS, GROUP * SLOTS, SLOTS * cache)
    attended, *attended_parts = call(
        functools.partial(attend_all, col_count, parts),
        [struct((rows, half))] + [struct((piece, half))] * parts,
        [SMEM, SMEM] + [VMEM] * (col_count + 2),
        [VMEM] * (parts + 1),
        4 * rows * half * cache,
        0,
        [pltpu.VMEM(runs, jnp.float32), pltpu.VMEM(runs, jnp.bfloat16)],
    )(place, cache_lengths, *products, key_part, value_part)

    out_second = call(
        functools.partial(stage_out_kernel, False),
        pltpu.VMEM((half, half_out), jnp.bfloat16),
        [SMEM, HBM, HBM],
        VMEM,
        0,
        half * half_out * 2,
        [pltpu.SemaphoreType.DMA((pairs,))],
    )(place, in_hbm(out_weight), attended)
    given = lax.ppermute(attended, "side", [(0, 1)])
    pieces_in = gathered(attended, attended_parts, "col")
    total_rows = rows * col_count
    give, own = call(
        functools.partial(out_kernel, len(pieces_in), col_count),
        [struct((total_rows, 2 * half_out)), struct((total_rows, 2 * half_out), jnp.float32)],
        [SMEM] + [VMEM] * (len(pieces_in) + 3),
        [VMEM] * 2,
        4 * total_rows * half * half_out,
        half * half_out * 4,
        [pltpu.VMEM((total_rows, total_rows), jnp.float32)],
    )(place, slot_request, *pieces_in, in_vmem(out_first), in_vmem(out_second))
    received = lax.ppermute(give, "side", [(1, 0)])
    products = call(
        sum_kernel,
        [struct((rows, 2 * half_out))] * col_count,
        [VMEM] * 2,
        [VMEM] * col_count,
        2 * total_rows * half_out,
        total_rows * half_out * 16,
    )(own, received)
    products = [products[0]] + [
        lax.ppermute(
            products[mask], ("col", "side"), [(2 * c, 2 * (c ^ mask)) for c in range(col_count)]
        )
        for mask in range(1, col_count)
    ]
    arrived = [
        lax.ppermute(
            call(
                functools.partial(choose_kernel, col_count, mask),
                struct((pairs, rows, 2 * half_out)),
                [SMEM] + [VMEM] * col_count,
                VMEM,
                0,
                pairs * rows * half_out * 8,
            )(place, *products),
            ("row", "side"),
            [(2 * r, 2 * (r ^ mask)) for r in range(row_count)],
        )
        for mask in range(1, row_count)
    ]
    return call(
        functools.partial(finish_kernel, col_count, row_count - 1),
        struct((1, rows, depth)),
        [SMEM] + [VMEM] * (3 + col_count + row_count - 1),
        VMEM,
        rows * depth * 4,
        rows * depth * 8,
    )(place, hidden_in, attended, given, *products, *arrived)


def per_device(*args):
    hidden_in, _, qkv_weight, out_weight, key_cache = args[:5]
    col_count, row_count = lax.axis_size("col"), lax.axis_size("row")
    fits = (
        lax.axis_size("side") == 2
        and qkv_weight.shape[1] == 2 * GROUP_WIDTH
        and col_count % row_count == 0
        and row_count > 1
        and col_count & (col_count - 1) == 0
        and hidden_in.shape[0] % 32 == 0
        and key_cache.shape[1] % 16 == 0
        and hidden_in.shape[1] == 2 * OUT_WIDTH * (col_count // row_count)
    )
    return paired_plan(*args) if fits else general_plan(*args)


def solution(mesh):
    placed = (
        P(("groups", "col"), "row"),
        P("row"),
        P("row", "col"),
        P("row", "col"),
        P(("groups", "col"), None, "row"),
        P(("groups", "col"), None, "row"),
        P(("groups", "col")),
        P("groups"),
    )
    return jax.shard_map(
        per_device,
        mesh=mesh,
        in_specs=placed,
        out_specs=P("side", ("groups", "col"), "row"),
        check_vma=False,
    )
```

```python
import functools
import math

import jax
import jax.numpy as jnp
from jax import lax
from jax.experimental import pallas as pl
from jax.experimental.pallas import tpu as pltpu
from jax.sharding import PartitionSpec as P

D = 8192
HEADS = 64
KV_HEADS = 8
HEAD_DIM = 128
QKV = 10240


EPSILON = 1e-05
THETA = 500000.0


def swapped(value, axis, bit):
    mask = 2**bit
    pairs = [(source, source ^ mask) for source in range(lax.axis_size(axis))]
    return lax.ppermute(value, axis, pairs)


def rope_tables(lengths, head_dim):
    half_dim = head_dim // 2
    inv_freq = jnp.exp(
        -jnp.log(jnp.float32(THETA)) * jnp.arange(half_dim, dtype=jnp.float32) / half_dim
    )
    phases = lengths.astype(jnp.float32)[:, None] * inv_freq[None, :]
    return (jnp.cos(phases), jnp.sin(phases))


def rotate(vector, cos_vals, sine_vals):
    half_dim = vector.shape[-1] // 2
    front_half = vector[..., :half_dim]
    back_half = vector[..., half_dim:]
    return jnp.concatenate(
        [
            front_half * cos_vals - back_half * sine_vals,
            back_half * cos_vals + front_half * sine_vals,
        ],
        axis=-1,
    )


def attend(packed, key_block, value_block, lengths):
    slot_count = packed.shape[0]
    cache_size = key_block.shape[1]
    groups = key_block.shape[2] // HEAD_DIM
    per_group = HEADS // KV_HEADS
    grouped = packed.reshape(slot_count, groups, per_group + 2, HEAD_DIM)
    cos_vals, sine_vals = rope_tables(lengths, HEAD_DIM)
    queries = rotate(
        grouped[:, :, :per_group].astype(jnp.float32),
        cos_vals[:, None, None, :],
        sine_vals[:, None, None, :],
    ).astype(jnp.bfloat16)
    new_keys = rotate(
        grouped[:, :, per_group].astype(jnp.float32), cos_vals[:, None, :], sine_vals[:, None, :]
    ).astype(jnp.bfloat16)
    new_values = grouped[:, :, per_group + 1]
    cache_keys = key_block.reshape(slot_count, cache_size, groups, HEAD_DIM)
    cache_values = value_block.reshape(slot_count, cache_size, groups, HEAD_DIM)
    factor = HEAD_DIM ** (-0.5)
    cache_scores = (
        jnp.einsum("sghd,slgd->sghl", queries, cache_keys, preferred_element_type=jnp.float32)
        * factor
    )
    own_scores = (
        jnp.einsum("sghd,sgd->sgh", queries, new_keys, preferred_element_type=jnp.float32) * factor
    )
    in_cache = lax.broadcasted_iota(jnp.int32, (slot_count, cache_size), 1) < lengths[:, None]
    cache_scores = jnp.where(in_cache[:, None, None, :], cache_scores, -1e30)
    row_max = jnp.maximum(jnp.max(cache_scores, axis=-1), own_scores)
    cache_exp = jnp.exp(cache_scores - row_max[..., None])
    own_exp = jnp.exp(own_scores - row_max)
    denominator = jnp.sum(cache_exp, axis=-1) + own_exp
    cache_weight = (cache_exp / denominator[..., None]).astype(jnp.bfloat16)
    own_weight = (own_exp / denominator).astype(jnp.bfloat16)
    combined = jnp.einsum(
        "sghl,slgd->sghd", cache_weight, cache_values, preferred_element_type=jnp.float32
    )
    combined = (
        combined
        + own_weight.astype(jnp.float32)[..., None] * new_values.astype(jnp.float32)[:, :, None, :]
    )
    return combined.astype(jnp.bfloat16).reshape(slot_count, groups * per_group * HEAD_DIM)


def general_plan(
    hidden_in,
    norm_gain,
    qkv_weight,
    out_weight,
    key_cache,
    value_cache,
    cache_lengths,
    slot_request,
):
    side_index = lax.axis_index("side")
    is_weight = side_index == 0
    col_count = lax.axis_size("col")
    row_count = lax.axis_size("row")
    group_cols = col_count // row_count
    in_half = qkv_weight.shape[1] // 2
    out_half = out_weight.shape[1] // 2
    residual = hidden_in.astype(jnp.float32)
    square_sums = lax.psum(jnp.sum(residual * residual, axis=1), "row")
    normed = (
        residual
        * lax.rsqrt(square_sums[:, None] / D + EPSILON)
        * norm_gain.astype(jnp.float32)[None, :]
    ).astype(jnp.bfloat16)
    in_weight = lax.dynamic_slice_in_dim(qkv_weight, side_index * in_half, in_half, 1)
    partial_in = jnp.dot(
        lax.all_gather(normed, "col", axis=0, tiled=True),
        in_weight,
        preferred_element_type=jnp.float32,
    )
    in_slots = jnp.take(partial_in, slot_request, axis=0)
    own_width = QKV // row_count
    summed = lax.psum(in_slots.astype(jnp.bfloat16), "row")
    spread = lax.all_to_all(summed, "col", split_axis=0, concat_axis=1, tiled=True)
    own_columns = lax.dynamic_slice_in_dim(
        spread.reshape(spread.shape[0], col_count, in_half),
        lax.axis_index("row") * group_cols,
        group_cols,
        1,
    )
    slot_half = key_cache.shape[0] // 2
    halves = lax.all_to_all(
        own_columns[:, :, None, :], "side", split_axis=0, concat_axis=2, tiled=True
    )
    arrived = halves.reshape(slot_half, own_width)
    first_slot = side_index * slot_half
    key_part = lax.dynamic_slice_in_dim(key_cache, first_slot, slot_half, 0)
    value_part = lax.dynamic_slice_in_dim(value_cache, first_slot, slot_half, 0)
    length_part = lax.dynamic_slice_in_dim(cache_lengths, first_slot, slot_half, 0)
    attended = attend(arrived, key_part, value_part, length_part)
    out_cols = lax.dynamic_slice_in_dim(out_weight, side_index * out_half, out_half, 1)
    collected = lax.all_gather(attended, ("col", "side"), axis=0, tiled=True)
    out_slots = jnp.dot(collected, out_cols, preferred_element_type=jnp.float32)
    inverse = jnp.argsort(slot_request)
    out_requests = jnp.take(out_slots, inverse, axis=0)
    spread_out = lax.all_to_all(
        out_requests.astype(jnp.bfloat16), "col", split_axis=0, concat_axis=1, tiled=True
    ).astype(out_requests.dtype)
    out_view = spread_out.reshape(spread_out.shape[0], col_count, out_half)
    summed_out = lax.psum_scatter(
        out_view.astype(jnp.bfloat16), "row", scatter_dimension=1, tiled=True
    ).astype(jnp.float32)
    req_rows = hidden_in.shape[0]
    residual_view = residual.reshape(req_rows, group_cols, 2, out_half)
    residual_half = lax.dynamic_index_in_dim(residual_view, side_index, 2, keepdims=False)
    own_hidden = (residual_half + summed_out).astype(jnp.bfloat16)
    payload = jnp.where(is_weight, attended, own_hidden.reshape(attended.shape))
    received = swapped(payload, "side", 0)
    hidden = jnp.stack([own_hidden, received.reshape(own_hidden.shape)], axis=2).reshape(
        req_rows, residual.shape[1]
    )
    attention_rows = jnp.concatenate([received, attended], axis=0)
    result = jnp.where(is_weight, hidden, attention_rows)
    return result[None]


GROUP = HEADS // KV_HEADS
GROUP_WIDTH = (GROUP + 2) * HEAD_DIM
OUT_WIDTH = GROUP * HEAD_DIM
SLOTS = 8
VMEM = pl.BlockSpec(memory_space=pltpu.VMEM)
SMEM = pl.BlockSpec(memory_space=pltpu.SMEM)
HBM = pl.BlockSpec(memory_space=pl.ANY)
MIB = 2**20


def call(kernel, out_shape, in_specs, out_specs, flops, size, scratch=(), limit=16):
    return pl.pallas_call(
        kernel,
        out_shape=out_shape,
        in_specs=in_specs,
        out_specs=out_specs,
        scratch_shapes=list(scratch),
        compiler_params=pltpu.CompilerParams(vmem_limit_bytes=limit * MIB),
        cost_estimate=pl.CostEstimate(flops=flops, bytes_accessed=size, transcendentals=0),
    )


def in_vmem(value):
    return pltpu.with_memory_space_constraint(value, pltpu.VMEM)


def in_hbm(value):
    return pltpu.with_memory_space_constraint(value, pltpu.HBM)


def struct(shape, dtype=jnp.bfloat16):
    return jax.ShapeDtypeStruct(shape, dtype)


def moved(value, axis, mask):
    pairs = [(source, source ^ mask) for source in range(lax.axis_size(axis))]
    return lax.ppermute(value, axis, pairs)


def run_copies(copies, sems):
    copies = [
        pltpu.make_async_copy(source, target, sems.at[i])
        for i, (source, target) in enumerate(copies)
    ]
    for copy in copies:
        copy.start()
    for copy in copies:
        copy.wait()


def stage_in_kernel(place, weight, gain, give_part, own_part, sems):
    depth, width = own_part.shape
    rows = pl.ds(pl.multiple_of(place[0] * depth, depth), depth)
    copies = []
    for target, half in ((give_part, 1 - place[0]), (own_part, place[0])):
        columns = pl.ds(pl.multiple_of(half * width, width), width)
        copies.append((weight.at[rows, columns], target))
    run_copies(copies, sems)


def stage_out_kernel(give, place, weight, *refs):
    sems = refs[-1]
    target = refs[2] if give else refs[1]
    width = target.shape[1]
    half = 1 - place[0] if give else place[0]
    columns = pl.ds(pl.multiple_of(half * width, width), width)
    copies = []
    for j in range(target.shape[0] // OUT_WIDTH):
        head = 2 * j + place[0]
        row = pl.multiple_of(head * OUT_WIDTH, OUT_WIDTH)
        if give:
            keys, values, _, key_part, value_part, _ = refs
            lane = pl.multiple_of(head * HEAD_DIM, HEAD_DIM)
            for cache, part in ((keys, key_part), (values, value_part)):
                copies.append(
                    (
                        cache.at[:, :, pl.ds(lane, HEAD_DIM)],
                        part.at[:, :, pl.ds(j * HEAD_DIM, HEAD_DIM)],
                    )
                )
        copies.append(
            (
                weight.at[pl.ds(row, OUT_WIDTH), columns],
                target.at[pl.ds(j * OUT_WIDTH, OUT_WIDTH), :],
            )
        )
    run_copies(copies, sems)


def one_hot(slots, scratch, blocks, slot_base, request_base):
    total = slots.shape[0]
    rows = total // blocks
    index = lax.broadcasted_iota(jnp.int32, (total, total), 0)
    request = (lax.div(index, rows) ^ request_base) * rows + lax.rem(index, rows)
    scratch[...] = jnp.where(slots[...].reshape(1, total) == request, 1.0, 0.0).T
    parts = [
        scratch[pl.ds(pl.multiple_of((slot_base ^ i) * rows, rows), rows), :]
        for i in range(blocks)
    ]
    return jnp.concatenate(parts, axis=0)


def pieces(sums):
    high = sums.astype(jnp.bfloat16).astype(jnp.float32)
    middle = (sums - high).astype(jnp.bfloat16).astype(jnp.float32)
    low = sums - high - middle
    lane = lax.broadcasted_iota(jnp.int32, (sums.shape[0], HEAD_DIM), 1)
    parts = jnp.where(lane == 0, high, jnp.where(lane == 1, middle, low))
    return jnp.where(lane < 3, parts, 0.0).astype(jnp.bfloat16)


def dot_columns(rows, weight, out):
    size, width = weight.shape[1], 512
    for start in range(0, size, width):
        part = slice(start, min(start + width, size))
        product = jnp.dot(rows, weight[:, part], preferred_element_type=jnp.float32)
        out[:, part] = product.astype(out.dtype)


def in_kernel(count, blocks, place, slots, *refs):
    pieces_in, (gain, weight, give, permuted, scratch) = refs[:count], refs[count:]
    side = place[0]
    depth = pieces_in[0].shape[1]
    half = weight.shape[1]
    gains = gain[:, pl.ds(pl.multiple_of(side * depth, depth), depth)].astype(jnp.float32)
    values = jnp.concatenate([piece[...].astype(jnp.float32) for piece in pieces_in], axis=0)
    sums = pieces(jnp.sum(values * values, axis=1, keepdims=True))
    chosen = one_hot(slots, scratch, blocks, place[1], place[1]).astype(jnp.bfloat16)
    order = jnp.dot(
        chosen, (values * gains).astype(jnp.bfloat16), preferred_element_type=jnp.float32
    ).astype(jnp.bfloat16)
    permuted[...] = order
    give[:, half:] = jnp.dot(chosen, sums, preferred_element_type=jnp.float32).astype(jnp.bfloat16)
    dot_columns(order, weight, give)


def out_kernel(count, blocks, place, slots, *refs):
    pieces_in, (_, weight, give, permuted, scratch) = refs[:count], refs[count:]
    values = jnp.concatenate([piece[...] for piece in pieces_in], axis=0)
    chosen = one_hot(slots, scratch, blocks, place[1], place[1]).T.astype(jnp.bfloat16)
    order = jnp.dot(chosen, values, preferred_element_type=jnp.float32).astype(jnp.bfloat16)
    permuted[...] = order
    dot_columns(order, weight, give)


def merge_kernel(count, own, given, received, *outs):
    rows = outs[0].shape[0]
    half = own.shape[1]
    more = given.shape[1] - half
    for i, out in enumerate(outs[:count]):
        part = slice(i * rows, (i + 1) * rows)
        total = own[part, :] + received[part, :half].astype(jnp.float32)
        out[...] = total.astype(jnp.bfloat16)
    for out in outs[count:]:
        lanes = slice(half, half + more // 2)
        out[...] = jnp.concatenate([given[:rows, lanes], received[:rows, lanes]], axis=1)


def own_kernel(permuted, weight, own):
    dot_columns(permuted[...], weight, own)


def project(kernel, place, slots, pieces_in, extra, weights, more):
    count = lax.axis_size("col")
    parts = len(pieces_in)
    depth = pieces_in[0].shape[1]
    rows = sum(part.shape[0] for part in pieces_in)
    half = weights[0].shape[1]
    flops = 2 * rows * depth * half
    give, permuted = call(
        functools.partial(kernel, parts, count),
        [struct((rows, half + more)), struct((rows, depth))],
        [SMEM, VMEM] + [VMEM] * (parts + len(extra) + 1),
        [VMEM, VMEM],
        flops,
        depth * half * 2,
        [pltpu.VMEM((rows, rows), jnp.float32)],
    )(place, slots, *pieces_in, *extra, in_vmem(weights[0]))
    received = moved(give, "side", 1)
    own = call(
        own_kernel,
        struct((rows, half), jnp.float32),
        [VMEM, VMEM],
        VMEM,
        flops,
        depth * half * 2,
    )(permuted, in_vmem(weights[1]))
    outs = [struct((rows // count, half))] * count
    if more:
        outs = outs + [struct((rows // count, more))]
    merged = call(
        functools.partial(merge_kernel, count),
        outs,
        [VMEM] * 3,
        [VMEM] * len(outs),
        rows * half,
        rows * half * 8,
    )(own, give, received)
    return merged[:count], merged[count:]


def gathered(whole, parts, axis):
    blocks = {0: parts}
    mask = lax.axis_size(axis) // 2
    while mask:
        arrived = {}
        for known, block in blocks.items():
            sent = [whole] if mask == 1 and known == 0 else block
            arrived[known | mask] = [moved(part, axis, mask) for part in sent]
        blocks |= arrived
        mask //= 2
    blocks[0] = [whole]
    return [part for i in sorted(blocks) for part in blocks[i]]


def spread(products):
    return [products[0]] + [
        moved(products[mask], "col", mask) for mask in range(1, len(products))
    ]


def choose_kernel(count, other, place, *refs):
    blocks, sums, out = refs[:count], refs[count:-1], refs[-1]
    pairs = out.shape[0]
    width = blocks[0].shape[1]
    wanted = place[2] ^ other
    for chunk in range(count // pairs):

        @pl.when(wanted == chunk)
        def _():
            for pair in range(pairs):
                out[pair, :, :width] = blocks[chunk * pairs + pair][...]

    for ref in sums:
        for pair in range(pairs):
            out[pair, :, width:] = ref[...]


def exchanged(place, blocks, sums):
    row_count = lax.axis_size("row")
    pairs = len(blocks) // row_count
    rows, width = blocks[0].shape
    width = width + sum(part.shape[1] for part in sums)
    return [
        moved(
            call(
                functools.partial(choose_kernel, len(blocks), mask),
                struct((pairs, rows, width)),
                [SMEM] + [VMEM] * (len(blocks) + len(sums)),
                VMEM,
                0,
                pairs * rows * width * 4,
            )(place, *blocks, *sums),
            "row",
            mask,
        )
        for mask in range(1, row_count)
    ]


def total_of(place, blocks, arrived, pair):
    pairs, _, width = arrived[0].shape
    width = min(width, blocks[0].shape[1])
    total = jnp.zeros(blocks[0].shape, jnp.float32)
    for chunk in range(len(blocks) // pairs):
        part = blocks[chunk * pairs + pair][...].astype(jnp.float32)
        total = total + jnp.where(place[2] == chunk, part, 0.0)
    for ref in arrived:
        total = total + ref[pair, :, :width].astype(jnp.float32)
    return total


def rotated(vector, cosine, sine):
    return vector * cosine + pltpu.roll(vector, HEAD_DIM // 2, 1) * sine


def rope(lengths, rows):
    slot = lax.broadcasted_iota(jnp.int32, (rows, HEAD_DIM), 0)
    length_of = jnp.zeros((rows, HEAD_DIM), jnp.int32)
    for i in range(rows):
        length_of = jnp.where(slot == i, lengths[i], length_of)
    lane = lax.broadcasted_iota(jnp.int32, (rows, HEAD_DIM), 1)
    half = HEAD_DIM // 2
    step = lax.rem(lane, half).astype(jnp.float32)
    phases = length_of.astype(jnp.float32) * jnp.exp(-math.log(THETA) * step / half)
    sine = jnp.sin(phases)
    return jnp.cos(phases), jnp.where(lane < half, -sine, sine), length_of[:, :1]


def attend_all(count, others, parts, place, lengths, *refs):
    blocks, own_sums, arrived = refs[:count], refs[count], refs[count + 1 : count + 1 + others]
    keys, values, whole, *refs = refs[count + 1 + others :]
    outs, (scores_of, probs_of) = refs[:parts], refs[parts:]
    pairs = keys.shape[2] // HEAD_DIM
    rows, cache = keys.shape[:2]
    low = place[1] % pairs
    width = GROUP_WIDTH
    squares = own_sums[...].astype(jnp.float32)
    for ref in arrived:
        squares = squares + ref[0, :, width:].astype(jnp.float32)
    scale = lax.rsqrt(jnp.sum(squares, axis=1, keepdims=True) / D + EPSILON)
    factor = HEAD_DIM ** (-0.5)
    cosines, sines, length_of = rope(lengths, rows)
    lane = lax.broadcasted_iota(jnp.int32, (SLOTS, SLOTS * cache), 1)
    slot = lax.broadcasted_iota(jnp.int32, (SLOTS, SLOTS * cache), 0)
    position = lane - slot * cache
    runs = [slice(start, start + SLOTS) for start in range(0, rows, SLOTS)]
    filled = [(position >= 0) & (position < length_of[part]) for part in runs]
    own, new_values, own_probs = [], [], []
    for pair in range(pairs):
        total = total_of(place, blocks, arrived, pair)
        total = (total * scale).astype(jnp.bfloat16).astype(jnp.float32)
        heads = [total[:, h * HEAD_DIM : (h + 1) * HEAD_DIM] for h in range(GROUP + 2)]
        queries = [
            rotated(head, cosines, sines).astype(jnp.bfloat16).astype(jnp.float32)
            for head in heads[:GROUP]
        ]
        new_key = rotated(heads[GROUP], cosines, sines).astype(jnp.bfloat16).astype(jnp.float32)
        new_values.append(heads[GROUP + 1])
        own.append([jnp.sum(query * new_key, axis=1, keepdims=True) * factor for query in queries])
        lanes = pl.ds(pl.multiple_of((low ^ pair) * HEAD_DIM, HEAD_DIM), HEAD_DIM)
        for run, part in enumerate(runs):
            query = jnp.concatenate([head[part] for head in queries], axis=0)
            key = keys[part, :, lanes].reshape(SLOTS * cache, HEAD_DIM)
            scores_of[pair, run] = lax.dot_general(
                query.astype(jnp.bfloat16),
                key,
                (((1,), (1,)), ((), ())),
                preferred_element_type=jnp.float32,
            )
    for pair in range(pairs):
        for run, part in enumerate(runs):
            scores = (scores_of[pair, run] * factor).reshape(GROUP, SLOTS, SLOTS * cache)
            scores = jnp.where(filled[run][None], scores, -1e30)
            own_score = jnp.concatenate([head[part] for head in own[pair]], axis=0).reshape(
                GROUP, SLOTS, 1
            )
            highest = jnp.maximum(jnp.max(scores, axis=2, keepdims=True), own_score)
            weights = jnp.exp(scores - highest)
            own_weight = jnp.exp(own_score - highest)
            inverse = 1.0 / (jnp.sum(weights, axis=2, keepdims=True) + own_weight)
            probs = (weights * inverse).astype(jnp.bfloat16)
            probs_of[pair, run] = probs.reshape(GROUP * SLOTS, SLOTS * cache)
            own_probs.append((own_weight * inverse).astype(jnp.bfloat16).astype(jnp.float32))
    for pair in range(pairs):
        lanes = pl.ds(pl.multiple_of((low ^ pair) * HEAD_DIM, HEAD_DIM), HEAD_DIM)
        results = []
        for run, part in enumerate(runs):
            value = values[part, :, lanes].reshape(SLOTS * cache, HEAD_DIM)
            mixed = jnp.dot(probs_of[pair, run], value, preferred_element_type=jnp.float32)
            own_prob = own_probs[pair * len(runs) + run]
            results.append(
                mixed.reshape(GROUP, SLOTS, HEAD_DIM) + own_prob * new_values[pair][part][None]
            )
        for head in range(GROUP):
            at = pl.multiple_of((low ^ pair) * OUT_WIDTH + head * HEAD_DIM, HEAD_DIM)
            size = len(results) // parts
            for i, out in enumerate(outs):
                joined = jnp.concatenate(
                    [result[head] for result in results[i * size : (i + 1) * size]], axis=0
                )
                joined = joined.astype(jnp.bfloat16)
                out[:, pl.ds(at, HEAD_DIM)] = joined
                run = slice(i * joined.shape[0], (i + 1) * joined.shape[0])
                whole[run, pl.ds(at, HEAD_DIM)] = joined


def sum_kernel(count, others, place, hidden, attended, *refs):
    blocks, arrived, (keep, send) = refs[:count], refs[count : count + others], refs[-2:]
    pairs, _, width = arrived[0].shape
    side = place[0]
    low = place[1] % pairs
    for pair in range(pairs):
        column = low ^ pair
        total = total_of(place, blocks, arrived, pair)
        at = pl.ds(pl.multiple_of((2 * column + side) * width, width), width)
        hidden_out = (hidden[:, at].astype(jnp.float32) + total).astype(jnp.bfloat16)
        at = pl.ds(pl.multiple_of(column * width, width), width)
        attention = attended[:, at]
        keep[:, at] = jnp.where(side == 0, hidden_out, attention)
        send[:, at] = jnp.where(side == 0, attention, hidden_out)


def join_kernel(place, keep, received, out):
    side = place[0]
    width = OUT_WIDTH
    for j in range(keep.shape[1] // width):
        part = slice(j * width, (j + 1) * width)
        out[0, :, pl.ds(pl.multiple_of((2 * j + side) * width, width), width)] = keep[:, part]
        out[0, :, pl.ds(pl.multiple_of((2 * j + 1 - side) * width, width), width)] = received[
            :, part
        ]


def paired_plan(
    hidden_in, norm_gain, qkv_weight, out_weight, key_cache, value_cache, cache_lengths, slot_request
):
    col_count, row_count = lax.axis_size("col"), lax.axis_size("row")
    pairs = col_count // row_count
    side, col, row = (lax.axis_index(name) for name in ("side", "col", "row"))
    base = lax.div(col, pairs) ^ row
    place = jnp.stack([side, col, base]).astype(jnp.int32)
    rows, depth = hidden_in.shape
    half = depth // 2
    cache = key_cache.shape[1]
    parts = 2
    piece = rows // parts

    own_part = lax.dynamic_slice_in_dim(hidden_in, side * half, half, 1)
    gain = norm_gain.reshape(1, depth)
    half_in, half_out = qkv_weight.shape[1] // 2, out_weight.shape[1] // 2
    weights_in = call(
        stage_in_kernel,
        [pltpu.VMEM((half, half_in), jnp.bfloat16)] * 2,
        [SMEM, HBM, HBM],
        [VMEM] * 2,
        0,
        half * half_in * 4,
        [pltpu.SemaphoreType.DMA((2,))],
    )(place, in_hbm(qkv_weight), gain)
    blocks = gathered(
        own_part, [own_part[i * piece : (i + 1) * piece] for i in range(parts)], "col"
    )
    out_give, key_part, value_part = call(
        functools.partial(stage_out_kernel, True),
        [pltpu.VMEM((half, half_out), jnp.bfloat16)]
        + [pltpu.VMEM((rows, cache, pairs * HEAD_DIM), jnp.bfloat16)] * 2,
        [SMEM, HBM, HBM, HBM],
        [VMEM] * 3,
        0,
        half * half_out * 2 + 4 * rows * cache * pairs * HEAD_DIM,
        [pltpu.SemaphoreType.DMA((3 * pairs,))],
    )(place, in_hbm(out_weight), in_hbm(key_cache), in_hbm(value_cache))

    products, sums = project(
        in_kernel, place, slot_request, blocks, [gain], weights_in, HEAD_DIM
    )
    products = spread(products)
    arrived = exchanged(place, products, sums)

    key_part, value_part = in_vmem(key_part), in_vmem(value_part)
    runs = (pairs, rows // SLOTS, GROUP * SLOTS, SLOTS * cache)
    attended, *attended_parts = call(
        functools.partial(attend_all, col_count, row_count - 1, parts),
        [struct((rows, half))] + [struct((piece, half))] * parts,
        [SMEM, SMEM] + [VMEM] * (col_count + row_count + 2),
        [VMEM] * (parts + 1),
        4 * rows * half * cache,
        0,
        [pltpu.VMEM(runs, jnp.float32), pltpu.VMEM(runs, jnp.bfloat16)],
    )(place, cache_lengths, *products, *sums, *arrived, key_part, value_part)

    out_own = call(
        functools.partial(stage_out_kernel, False),
        pltpu.VMEM((half, half_out), jnp.bfloat16),
        [SMEM, HBM, HBM],
        VMEM,
        0,
        half * half_out * 2,
        [pltpu.SemaphoreType.DMA((pairs,))],
    )(place, in_hbm(out_weight), attended)
    products, _ = project(
        out_kernel,
        place,
        slot_request,
        gathered(attended, attended_parts, "col"),
        [in_vmem(out_own)],
        [out_give, out_own],
        0,
    )
    products = spread(products)
    arrived = exchanged(place, products, [])
    keep, send = call(
        functools.partial(sum_kernel, col_count, row_count - 1),
        [struct((rows, half)), struct((rows, half))],
        [SMEM] + [VMEM] * (2 + col_count + row_count - 1),
        [VMEM, VMEM],
        rows * depth * 4,
        rows * depth * 8,
    )(place, hidden_in, attended, *products, *arrived)
    return call(
        join_kernel,
        struct((1, rows, depth)),
        [SMEM, VMEM, VMEM],
        VMEM,
        0,
        rows * depth * 4,
    )(place, keep, moved(send, "side", 1))


def per_device(*args):
    hidden_in, _, qkv_weight, out_weight, key_cache = args[:5]
    col_count, row_count = lax.axis_size("col"), lax.axis_size("row")
    fits = (
        lax.axis_size("side") == 2
        and qkv_weight.shape[1] == 2 * GROUP_WIDTH
        and col_count % row_count == 0
        and row_count > 1
        and col_count & (col_count - 1) == 0
        and hidden_in.shape[0] % 32 == 0
        and key_cache.shape[1] % 16 == 0
        and hidden_in.shape[1] == 2 * OUT_WIDTH * (col_count // row_count)
    )
    return paired_plan(*args) if fits else general_plan(*args)


def solution(mesh):
    placed = (
        P(("groups", "col"), "row"),
        P("row"),
        P("row", "col"),
        P("row", "col"),
        P(("groups", "col"), None, "row"),
        P(("groups", "col"), None, "row"),
        P(("groups", "col")),
        P("groups"),
    )
    return jax.shard_map(
        per_device,
        mesh=mesh,
        in_specs=placed,
        out_specs=P("side", ("groups", "col"), "row"),
        check_vma=False,
    )
```

```python
import functools
import math

import jax
import jax.numpy as jnp
from jax import lax
from jax.experimental import pallas as pl
from jax.experimental.pallas import tpu as pltpu
from jax.sharding import PartitionSpec as P

D = 8192
HEADS = 64
KV_HEADS = 8
HEAD_DIM = 128
QKV = 10240


EPSILON = 1e-05
THETA = 500000.0


def swapped(value, axis, bit):
    mask = 2**bit
    pairs = [(source, source ^ mask) for source in range(lax.axis_size(axis))]
    return lax.ppermute(value, axis, pairs)


def rope_tables(lengths, head_dim):
    half_dim = head_dim // 2
    inv_freq = jnp.exp(
        -jnp.log(jnp.float32(THETA)) * jnp.arange(half_dim, dtype=jnp.float32) / half_dim
    )
    phases = lengths.astype(jnp.float32)[:, None] * inv_freq[None, :]
    return (jnp.cos(phases), jnp.sin(phases))


def rotate(vector, cos_vals, sine_vals):
    half_dim = vector.shape[-1] // 2
    front_half = vector[..., :half_dim]
    back_half = vector[..., half_dim:]
    return jnp.concatenate(
        [
            front_half * cos_vals - back_half * sine_vals,
            back_half * cos_vals + front_half * sine_vals,
        ],
        axis=-1,
    )


def attend(packed, key_block, value_block, lengths):
    slot_count = packed.shape[0]
    cache_size = key_block.shape[1]
    groups = key_block.shape[2] // HEAD_DIM
    per_group = HEADS // KV_HEADS
    grouped = packed.reshape(slot_count, groups, per_group + 2, HEAD_DIM)
    cos_vals, sine_vals = rope_tables(lengths, HEAD_DIM)
    queries = rotate(
        grouped[:, :, :per_group].astype(jnp.float32),
        cos_vals[:, None, None, :],
        sine_vals[:, None, None, :],
    ).astype(jnp.bfloat16)
    new_keys = rotate(
        grouped[:, :, per_group].astype(jnp.float32), cos_vals[:, None, :], sine_vals[:, None, :]
    ).astype(jnp.bfloat16)
    new_values = grouped[:, :, per_group + 1]
    cache_keys = key_block.reshape(slot_count, cache_size, groups, HEAD_DIM)
    cache_values = value_block.reshape(slot_count, cache_size, groups, HEAD_DIM)
    factor = HEAD_DIM ** (-0.5)
    cache_scores = (
        jnp.einsum("sghd,slgd->sghl", queries, cache_keys, preferred_element_type=jnp.float32)
        * factor
    )
    own_scores = (
        jnp.einsum("sghd,sgd->sgh", queries, new_keys, preferred_element_type=jnp.float32) * factor
    )
    in_cache = lax.broadcasted_iota(jnp.int32, (slot_count, cache_size), 1) < lengths[:, None]
    cache_scores = jnp.where(in_cache[:, None, None, :], cache_scores, -1e30)
    row_max = jnp.maximum(jnp.max(cache_scores, axis=-1), own_scores)
    cache_exp = jnp.exp(cache_scores - row_max[..., None])
    own_exp = jnp.exp(own_scores - row_max)
    denominator = jnp.sum(cache_exp, axis=-1) + own_exp
    cache_weight = (cache_exp / denominator[..., None]).astype(jnp.bfloat16)
    own_weight = (own_exp / denominator).astype(jnp.bfloat16)
    combined = jnp.einsum(
        "sghl,slgd->sghd", cache_weight, cache_values, preferred_element_type=jnp.float32
    )
    combined = (
        combined
        + own_weight.astype(jnp.float32)[..., None] * new_values.astype(jnp.float32)[:, :, None, :]
    )
    return combined.astype(jnp.bfloat16).reshape(slot_count, groups * per_group * HEAD_DIM)


def general_plan(
    hidden_in,
    norm_gain,
    qkv_weight,
    out_weight,
    key_cache,
    value_cache,
    cache_lengths,
    slot_request,
):
    side_index = lax.axis_index("side")
    is_weight = side_index == 0
    col_count = lax.axis_size("col")
    row_count = lax.axis_size("row")
    group_cols = col_count // row_count
    in_half = qkv_weight.shape[1] // 2
    out_half = out_weight.shape[1] // 2
    residual = hidden_in.astype(jnp.float32)
    square_sums = lax.psum(jnp.sum(residual * residual, axis=1), "row")
    normed = (
        residual
        * lax.rsqrt(square_sums[:, None] / D + EPSILON)
        * norm_gain.astype(jnp.float32)[None, :]
    ).astype(jnp.bfloat16)
    in_weight = lax.dynamic_slice_in_dim(qkv_weight, side_index * in_half, in_half, 1)
    partial_in = jnp.dot(
        lax.all_gather(normed, "col", axis=0, tiled=True),
        in_weight,
        preferred_element_type=jnp.float32,
    )
    in_slots = jnp.take(partial_in, slot_request, axis=0)
    own_width = QKV // row_count
    summed = lax.psum(in_slots.astype(jnp.bfloat16), "row")
    spread = lax.all_to_all(summed, "col", split_axis=0, concat_axis=1, tiled=True)
    own_columns = lax.dynamic_slice_in_dim(
        spread.reshape(spread.shape[0], col_count, in_half),
        lax.axis_index("row") * group_cols,
        group_cols,
        1,
    )
    slot_half = key_cache.shape[0] // 2
    halves = lax.all_to_all(
        own_columns[:, :, None, :], "side", split_axis=0, concat_axis=2, tiled=True
    )
    arrived = halves.reshape(slot_half, own_width)
    first_slot = side_index * slot_half
    key_part = lax.dynamic_slice_in_dim(key_cache, first_slot, slot_half, 0)
    value_part = lax.dynamic_slice_in_dim(value_cache, first_slot, slot_half, 0)
    length_part = lax.dynamic_slice_in_dim(cache_lengths, first_slot, slot_half, 0)
    attended = attend(arrived, key_part, value_part, length_part)
    out_cols = lax.dynamic_slice_in_dim(out_weight, side_index * out_half, out_half, 1)
    collected = lax.all_gather(attended, ("col", "side"), axis=0, tiled=True)
    out_slots = jnp.dot(collected, out_cols, preferred_element_type=jnp.float32)
    inverse = jnp.argsort(slot_request)
    out_requests = jnp.take(out_slots, inverse, axis=0)
    spread_out = lax.all_to_all(
        out_requests.astype(jnp.bfloat16), "col", split_axis=0, concat_axis=1, tiled=True
    ).astype(out_requests.dtype)
    out_view = spread_out.reshape(spread_out.shape[0], col_count, out_half)
    summed_out = lax.psum_scatter(
        out_view.astype(jnp.bfloat16), "row", scatter_dimension=1, tiled=True
    ).astype(jnp.float32)
    req_rows = hidden_in.shape[0]
    residual_view = residual.reshape(req_rows, group_cols, 2, out_half)
    residual_half = lax.dynamic_index_in_dim(residual_view, side_index, 2, keepdims=False)
    own_hidden = (residual_half + summed_out).astype(jnp.bfloat16)
    payload = jnp.where(is_weight, attended, own_hidden.reshape(attended.shape))
    received = swapped(payload, "side", 0)
    hidden = jnp.stack([own_hidden, received.reshape(own_hidden.shape)], axis=2).reshape(
        req_rows, residual.shape[1]
    )
    attention_rows = jnp.concatenate([received, attended], axis=0)
    result = jnp.where(is_weight, hidden, attention_rows)
    return result[None]


GROUP = HEADS // KV_HEADS
GROUP_WIDTH = (GROUP + 2) * HEAD_DIM
OUT_WIDTH = GROUP * HEAD_DIM
SLOTS = 8
VMEM = pl.BlockSpec(memory_space=pltpu.VMEM)
SMEM = pl.BlockSpec(memory_space=pltpu.SMEM)
HBM = pl.BlockSpec(memory_space=pl.ANY)
MIB = 2**20


def call(kernel, out_shape, in_specs, out_specs, flops, size, scratch=(), limit=16):
    return pl.pallas_call(
        kernel,
        out_shape=out_shape,
        in_specs=in_specs,
        out_specs=out_specs,
        scratch_shapes=list(scratch),
        compiler_params=pltpu.CompilerParams(vmem_limit_bytes=limit * MIB),
        cost_estimate=pl.CostEstimate(flops=flops, bytes_accessed=size, transcendentals=0),
    )


def in_vmem(value):
    return pltpu.with_memory_space_constraint(value, pltpu.VMEM)


def in_hbm(value):
    return pltpu.with_memory_space_constraint(value, pltpu.HBM)


def struct(shape, dtype=jnp.bfloat16):
    return jax.ShapeDtypeStruct(shape, dtype)


def moved(value, axis, mask):
    pairs = [(source, source ^ mask) for source in range(lax.axis_size(axis))]
    return lax.ppermute(value, axis, pairs)


def started(copies, sems):
    copies = [
        pltpu.make_async_copy(source, target, sems.at[i])
        for i, (source, target) in enumerate(copies)
    ]
    for copy in copies:
        copy.start()
    return copies


def run_copies(copies, sems):
    for copy in started(copies, sems):
        copy.wait()


def position():
    col = lax.axis_index("col")
    pairs = lax.axis_size("col") // lax.axis_size("row")
    return lax.axis_index("side"), col, lax.axis_index("row") * pairs + lax.rem(col, pairs)


def rows_copy(weight, target, half):
    depth, width = target.shape
    rows = pl.ds(pl.multiple_of(lax.axis_index("side") * depth, depth), depth)
    columns = pl.ds(pl.multiple_of(half * width, width), width)
    return weight.at[rows, columns], target


def stage_give_kernel(blocks, weight, slots, gain, give_part, chosen, scratch, sems):
    side, col, run = position()
    copies = started([rows_copy(weight, give_part, 1 - side)], sems)
    chosen[...] = one_hot(slots, scratch, blocks, run, col).astype(jnp.bfloat16)
    for copy in copies:
        copy.wait()


def stage_own_kernel(weight, own_part, sems):
    run_copies([rows_copy(weight, own_part, lax.axis_index("side"))], sems)


def head_copies(weight, target, half):
    width = target.shape[1]
    columns = pl.ds(pl.multiple_of(half * width, width), width)
    copies = []
    for j in range(target.shape[0] // OUT_WIDTH):
        row = pl.multiple_of((2 * j + lax.axis_index("side")) * OUT_WIDTH, OUT_WIDTH)
        copies.append(
            (
                weight.at[pl.ds(row, OUT_WIDTH), columns],
                target.at[pl.ds(j * OUT_WIDTH, OUT_WIDTH), :],
            )
        )
    return copies


def stage_rest_kernel(blocks, lengths, weight, keys, values, slots, *refs):
    target, key_part, value_part, cosine, sine, length_of, chosen, scratch, sems = refs
    side, col, run = position()
    copies = []
    for j in range(key_part.shape[2] // HEAD_DIM):
        lane = pl.multiple_of((2 * j + side) * HEAD_DIM, HEAD_DIM)
        for cache, part in ((keys, key_part), (values, value_part)):
            copies.append(
                (
                    cache.at[:, :, pl.ds(lane, HEAD_DIM)],
                    part.at[:, :, pl.ds(j * HEAD_DIM, HEAD_DIM)],
                )
            )
    copies = started(copies + head_copies(weight, target, 1 - side), sems)
    cosine[...], sine[...], length_of[...] = rope(lengths, cosine.shape[0])
    chosen[...] = one_hot(slots, scratch, blocks, col, run).T.astype(jnp.bfloat16)
    for copy in copies:
        copy.wait()


def stage_last_kernel(weight, attended, target, sems):
    run_copies(head_copies(weight, target, lax.axis_index("side")), sems)


def hold_kernel(value, token, out):
    pass


def held(value, token):
    return pl.pallas_call(
        hold_kernel,
        out_shape=pltpu.VMEM(value.shape, value.dtype),
        in_specs=[VMEM, HBM],
        out_specs=VMEM,
        input_output_aliases={0: 0},
        compiler_params=pltpu.CompilerParams(vmem_limit_bytes=MIB),
    )(in_vmem(value), token)


def one_hot(slots, scratch, blocks, slot_base, request_base):
    total = slots.shape[0]
    rows = total // blocks
    index = lax.broadcasted_iota(jnp.int32, (total, total), 0)
    request = (lax.div(index, rows) ^ request_base) * rows + lax.rem(index, rows)
    scratch[...] = jnp.where(slots[...].reshape(1, total) == request, 1.0, 0.0).T
    parts = [
        scratch[pl.ds(pl.multiple_of((slot_base ^ i) * rows, rows), rows), :]
        for i in range(blocks)
    ]
    return jnp.concatenate(parts, axis=0)


def pieces(sums):
    high = sums.astype(jnp.bfloat16).astype(jnp.float32)
    middle = (sums - high).astype(jnp.bfloat16).astype(jnp.float32)
    low = sums - high - middle
    lane = lax.broadcasted_iota(jnp.int32, (sums.shape[0], HEAD_DIM), 1)
    parts = jnp.where(lane == 0, high, jnp.where(lane == 1, middle, low))
    return jnp.where(lane < 3, parts, 0.0).astype(jnp.bfloat16)


def dot_columns(rows, weight, out):
    size, width = weight.shape[1], 512
    for start in range(0, size, width):
        part = slice(start, min(start + width, size))
        product = jnp.dot(rows, weight[:, part], preferred_element_type=jnp.float32)
        out[:, part] = product.astype(out.dtype)


def in_kernel(count, chosen, *refs):
    pieces_in, (_, gain, weight, give, permuted) = refs[:count], refs[count:]
    depth = pieces_in[0].shape[1]
    half = weight.shape[1]
    first = pl.multiple_of(lax.axis_index("side") * depth, depth)
    gains = gain[:, pl.ds(first, depth)].astype(jnp.float32)
    values = jnp.concatenate([piece[...].astype(jnp.float32) for piece in pieces_in], axis=0)
    sums = pieces(jnp.sum(values * values, axis=1, keepdims=True))
    order = jnp.dot(
        chosen[...], (values * gains).astype(jnp.bfloat16), preferred_element_type=jnp.float32
    ).astype(jnp.bfloat16)
    permuted[...] = order
    own_sums = jnp.dot(chosen[...], sums, preferred_element_type=jnp.float32)
    give[:, half:] = own_sums.astype(jnp.bfloat16)
    dot_columns(order, weight, give)


def out_kernel(count, chosen, *refs):
    pieces_in, (_, weight, give, permuted) = refs[:count], refs[count:]
    values = jnp.concatenate([piece[...] for piece in pieces_in], axis=0)
    order = jnp.dot(chosen[...], values, preferred_element_type=jnp.float32).astype(jnp.bfloat16)
    permuted[...] = order
    dot_columns(order, weight, give)


def merge_kernel(own, given, received, *outs):
    rows = outs[0].shape[0]
    half = own.shape[1]
    more = given.shape[1] - half
    for i, out in enumerate(outs):
        part = slice(i * rows, (i + 1) * rows)
        total = own[part, :] + received[part, :half].astype(jnp.float32)
        out[:, :half] = total.astype(jnp.bfloat16)
        if out.shape[1] > half:
            out[:, half:] = jnp.concatenate(
                [given[part, half : half + more // 2], received[part, half : half + more // 2]],
                axis=1,
            )


def own_kernel(permuted, weight, own):
    dot_columns(permuted[...], weight, own)


def project(kernel, chosen, pieces_in, extra, weights, more, pairs):
    count = lax.axis_size("col")
    parts = len(pieces_in)
    rows, depth = pieces_in[0].shape
    rows = rows * parts
    half = weights[0].shape[1]
    flops = 2 * rows * depth * half
    give, permuted = call(
        functools.partial(kernel, parts),
        [struct((rows, half + more)), struct((rows, depth))],
        [VMEM] * (parts + len(extra) + 3),
        [VMEM, VMEM],
        flops,
        depth * half * 2,
    )(chosen, *pieces_in, in_vmem(weights[1]), *extra, in_vmem(weights[0]))
    received = moved(give, "side", 1)
    own = call(
        own_kernel,
        struct((rows, half), jnp.float32),
        [VMEM, VMEM],
        VMEM,
        flops,
        depth * half * 2,
    )(permuted, in_vmem(weights[1]))
    return call(
        merge_kernel,
        [
            struct((rows // count, half + (more if i % pairs == pairs - 1 else 0)))
            for i in range(count)
        ],
        [VMEM] * 3,
        [VMEM] * count,
        rows * half,
        rows * half * 8,
    )(own, give, received)


def gathered(parts, axis, token=None):
    blocks = {0: parts}
    mask = lax.axis_size(axis) // 2
    while mask:
        blocks |= {
            known | mask: [moved(part, axis, mask) for part in block]
            for known, block in blocks.items()
        }
        mask //= 2
        if mask and token is not None:
            blocks = {
                known: [held(part, token) for part in block] if known else block
                for known, block in blocks.items()
            }
    return [part for i in sorted(blocks) for part in blocks[i]]


def spread(products):
    col_count, row_count = lax.axis_size("col"), lax.axis_size("row")
    pairs = col_count // row_count
    order = sorted(range(col_count), key=lambda j: (-(j % pairs), -j))
    sent = {
        j: lax.ppermute(
            products[j],
            ("col", "row"),
            [
                (
                    col * row_count + row,
                    ((row * pairs + col % pairs) ^ j) * row_count + col // pairs,
                )
                for col in range(col_count)
                for row in range(row_count)
            ],
        )
        for j in order
    }
    return [sent[j] for j in range(col_count)]


def rotated(vector, cosine, sine):
    return vector * cosine + pltpu.roll(vector, HEAD_DIM // 2, 1) * sine


def rope(lengths, rows):
    slot = lax.broadcasted_iota(jnp.int32, (rows, HEAD_DIM), 0)
    length_of = jnp.zeros((rows, HEAD_DIM), jnp.int32)
    for i in range(rows):
        length_of = jnp.where(slot == i, lengths[i], length_of)
    lane = lax.broadcasted_iota(jnp.int32, (rows, HEAD_DIM), 1)
    half = HEAD_DIM // 2
    step = lax.rem(lane, half).astype(jnp.float32)
    phases = length_of.astype(jnp.float32) * jnp.exp(-math.log(THETA) * step / half)
    sine = jnp.sin(phases)
    return jnp.cos(phases), jnp.where(lane < half, -sine, sine), length_of


def attend_all(count, parts, cosine, sine, lengths, *refs):
    blocks, (keys, values), refs = refs[:count], refs[count : count + 2], refs[count + 2 :]
    outs, (scores_of, probs_of) = refs[:parts], refs[parts:]
    pairs = keys.shape[2] // HEAD_DIM
    rows, cache = keys.shape[:2]
    low = lax.rem(lax.axis_index("col"), pairs)
    width = GROUP_WIDTH
    squares = blocks[pairs - 1][:, width:].astype(jnp.float32)
    for i in range(2 * pairs - 1, count, pairs):
        squares = squares + blocks[i][:, width:].astype(jnp.float32)
    scale = lax.rsqrt(jnp.sum(squares, axis=1, keepdims=True) / D + EPSILON)
    factor = HEAD_DIM ** (-0.5)
    cosines, sines, length_of = cosine[...], sine[...], lengths[:, :1]
    lane = lax.broadcasted_iota(jnp.int32, (SLOTS, SLOTS * cache), 1)
    slot = lax.broadcasted_iota(jnp.int32, (SLOTS, SLOTS * cache), 0)
    position = lane - slot * cache
    runs = [slice(start, start + SLOTS) for start in range(0, rows, SLOTS)]
    filled = [(position >= 0) & (position < length_of[part]) for part in runs]
    own, new_values, own_probs = [], [], []
    for pair in range(pairs):
        total = blocks[pair][:, :width].astype(jnp.float32)
        for i in range(pair + pairs, count, pairs):
            total = total + blocks[i][:, :width].astype(jnp.float32)
        total = (total * scale).astype(jnp.bfloat16).astype(jnp.float32)
        heads = [total[:, h * HEAD_DIM : (h + 1) * HEAD_DIM] for h in range(GROUP + 2)]
        queries = [
            rotated(head, cosines, sines).astype(jnp.bfloat16).astype(jnp.float32)
            for head in heads[:GROUP]
        ]
        new_key = rotated(heads[GROUP], cosines, sines).astype(jnp.bfloat16).astype(jnp.float32)
        new_values.append(heads[GROUP + 1])
        own.append([jnp.sum(query * new_key, axis=1, keepdims=True) * factor for query in queries])
        lanes = pl.ds(pl.multiple_of((low ^ pair) * HEAD_DIM, HEAD_DIM), HEAD_DIM)
        for run, part in enumerate(runs):
            query = jnp.concatenate([head[part] for head in queries], axis=0)
            key = keys[part, :, lanes].reshape(SLOTS * cache, HEAD_DIM)
            scores_of[pair, run] = lax.dot_general(
                query.astype(jnp.bfloat16),
                key,
                (((1,), (1,)), ((), ())),
                preferred_element_type=jnp.float32,
            )
    for pair in range(pairs):
        for run, part in enumerate(runs):
            scores = (scores_of[pair, run] * factor).reshape(GROUP, SLOTS, SLOTS * cache)
            scores = jnp.where(filled[run][None], scores, -1e30)
            own_score = jnp.concatenate([head[part] for head in own[pair]], axis=0).reshape(
                GROUP, SLOTS, 1
            )
            highest = jnp.maximum(jnp.max(scores, axis=2, keepdims=True), own_score)
            weights = jnp.exp(scores - highest)
            own_weight = jnp.exp(own_score - highest)
            inverse = 1.0 / (jnp.sum(weights, axis=2, keepdims=True) + own_weight)
            probs = (weights * inverse).astype(jnp.bfloat16)
            probs_of[pair, run] = probs.reshape(GROUP * SLOTS, SLOTS * cache)
            own_probs.append((own_weight * inverse).astype(jnp.bfloat16).astype(jnp.float32))
    for pair in range(pairs):
        lanes = pl.ds(pl.multiple_of((low ^ pair) * HEAD_DIM, HEAD_DIM), HEAD_DIM)
        results = []
        for run, part in enumerate(runs):
            value = values[part, :, lanes].reshape(SLOTS * cache, HEAD_DIM)
            mixed = jnp.dot(probs_of[pair, run], value, preferred_element_type=jnp.float32)
            own_prob = own_probs[pair * len(runs) + run]
            results.append(
                mixed.reshape(GROUP, SLOTS, HEAD_DIM) + own_prob * new_values[pair][part][None]
            )
        for head in range(GROUP):
            at = pl.multiple_of((low ^ pair) * OUT_WIDTH + head * HEAD_DIM, HEAD_DIM)
            size = len(results) // parts
            for i, out in enumerate(outs):
                joined = jnp.concatenate(
                    [result[head] for result in results[i * size : (i + 1) * size]], axis=0
                )
                out[:, pl.ds(at, HEAD_DIM)] = joined.astype(jnp.bfloat16)


def sum_kernel(count, parts, hidden, *refs):
    attended, blocks, (keep, send) = refs[:parts], refs[parts : parts + count], refs[parts + count :]
    rows, width = blocks[0].shape
    pairs = keep.shape[1] // width
    side = lax.axis_index("side")
    low = lax.rem(lax.axis_index("col"), pairs)
    for pair in range(pairs):
        column = low ^ pair
        total = blocks[pair][...].astype(jnp.float32)
        for i in range(pair + pairs, count, pairs):
            total = total + blocks[i][...].astype(jnp.float32)
        at = pl.ds(pl.multiple_of((2 * column + side) * width, width), width)
        hidden_out = (hidden[:, at].astype(jnp.float32) + total).astype(jnp.bfloat16)
        at = pl.ds(pl.multiple_of(column * width, width), width)
        attention = jnp.concatenate([part[:, at] for part in attended], axis=0)
        keep[:, at] = jnp.where(side == 0, hidden_out, attention)
        send[:, at] = jnp.where(side == 0, attention, hidden_out)


def join_kernel(keep, received, out, sems):
    side = lax.axis_index("side")
    width = OUT_WIDTH
    copies = []
    for j in range(keep.shape[1] // width):
        part = slice(j * width, (j + 1) * width)
        for ref, core in ((keep, side), (received, 1 - side)):
            at = pl.ds(pl.multiple_of((2 * j + core) * width, width), width)
            copies.append((ref.at[:, part], out.at[0, :, at]))
    run_copies(copies, sems)


def paired_plan(
    hidden_in, norm_gain, qkv_weight, out_weight, key_cache, value_cache, cache_lengths, slot_request
):
    col_count, row_count = lax.axis_size("col"), lax.axis_size("row")
    pairs = col_count // row_count
    side = lax.axis_index("side")
    rows, depth = hidden_in.shape
    half = depth // 2
    cache = key_cache.shape[1]
    parts = 2
    piece = rows // parts

    own_part = lax.dynamic_slice_in_dim(hidden_in, side * half, half, 1)
    gain = norm_gain.reshape(1, depth)
    half_in, half_out = qkv_weight.shape[1] // 2, out_weight.shape[1] // 2
    total = rows * col_count
    square = (total, total)
    give_in, chosen_in = call(
        functools.partial(stage_give_kernel, col_count),
        [pltpu.VMEM((half, half_in), jnp.bfloat16), struct(square)],
        [HBM, VMEM, HBM],
        [VMEM] * 2,
        0,
        half * half_in * 2,
        [pltpu.VMEM(square, jnp.float32), pltpu.SemaphoreType.DMA((1,))],
    )(in_hbm(qkv_weight), slot_request, gain)
    own_in = call(
        stage_own_kernel,
        pltpu.VMEM((half, half_in), jnp.bfloat16),
        [HBM],
        VMEM,
        0,
        half * half_in * 2,
        [pltpu.SemaphoreType.DMA((1,))],
    )(in_hbm(qkv_weight))
    blocks = gathered(
        [own_part[i * piece : (i + 1) * piece] for i in range(parts)], "col", chosen_in
    )
    products = spread(
        project(in_kernel, chosen_in, blocks, [gain], [give_in, own_in], HEAD_DIM, pairs)
    )

    table = struct((rows, HEAD_DIM), jnp.float32)
    give_out, key_part, value_part, *tables, chosen_out = call(
        functools.partial(stage_rest_kernel, col_count),
        [pltpu.VMEM((half, half_out), jnp.bfloat16)]
        + [pltpu.VMEM((rows, cache, pairs * HEAD_DIM), jnp.bfloat16)] * 2
        + [table, table, struct((rows, HEAD_DIM), jnp.int32), struct(square)],
        [SMEM, HBM, HBM, HBM, VMEM],
        [VMEM] * 7,
        0,
        half * half_out * 2 + 4 * rows * cache * pairs * HEAD_DIM,
        [pltpu.VMEM(square, jnp.float32), pltpu.SemaphoreType.DMA((3 * pairs,))],
    )(cache_lengths, in_hbm(out_weight), in_hbm(key_cache), in_hbm(value_cache), slot_request)
    runs = (pairs, rows // SLOTS, GROUP * SLOTS, SLOTS * cache)
    attended = call(
        functools.partial(attend_all, col_count, parts),
        [struct((piece, half))] * parts,
        [VMEM] * (col_count + 5),
        [VMEM] * parts,
        4 * rows * half * cache,
        0,
        [pltpu.VMEM(runs, jnp.float32), pltpu.VMEM(runs, jnp.bfloat16)],
    )(*tables, *products, in_vmem(key_part), in_vmem(value_part))

    own_out = call(
        stage_last_kernel,
        pltpu.VMEM((half, half_out), jnp.bfloat16),
        [HBM, HBM],
        VMEM,
        0,
        half * half_out * 2,
        [pltpu.SemaphoreType.DMA((pairs,))],
    )(in_hbm(out_weight), attended[-1])
    products = spread(
        project(
            out_kernel, chosen_out, gathered(attended, "col"), [], [give_out, own_out], 0, pairs
        )
    )
    keep, send = call(
        functools.partial(sum_kernel, col_count, parts),
        [struct((rows, half)), struct((rows, half))],
        [VMEM] * (1 + parts + col_count),
        [VMEM, VMEM],
        rows * depth * 4,
        rows * depth * 8,
    )(hidden_in, *attended, *products)
    return call(
        join_kernel,
        struct((1, rows, depth)),
        [VMEM, VMEM],
        HBM,
        0,
        rows * depth * 4,
        [pltpu.SemaphoreType.DMA((2 * pairs,))],
    )(keep, moved(send, "side", 1))


def per_device(*args):
    hidden_in, _, qkv_weight, out_weight, key_cache = args[:5]
    col_count, row_count = lax.axis_size("col"), lax.axis_size("row")
    fits = (
        lax.axis_size("side") == 2
        and qkv_weight.shape[1] == 2 * GROUP_WIDTH
        and col_count % row_count == 0
        and col_count & (col_count - 1) == 0
        and hidden_in.shape[0] % 32 == 0
        and key_cache.shape[1] % 16 == 0
        and hidden_in.shape[1] == 2 * OUT_WIDTH * (col_count // row_count)
    )
    return paired_plan(*args) if fits else general_plan(*args)


def solution(mesh):
    placed = (
        P(("groups", "col"), "row"),
        P("row"),
        P("row", "col"),
        P("row", "col"),
        P(("groups", "col"), None, "row"),
        P(("groups", "col"), None, "row"),
        P(("groups", "col")),
        P("groups"),
    )
    return jax.shard_map(
        per_device,
        mesh=mesh,
        in_specs=placed,
        out_specs=P("side", ("groups", "col"), "row"),
        check_vma=False,
    )
```

```python
import functools
import math

import jax
import jax.numpy as jnp
from jax import lax
from jax.experimental import pallas as pl
from jax.experimental.pallas import tpu as pltpu
from jax.sharding import PartitionSpec as P

D = 8192
HEADS = 64
KV_HEADS = 8
HEAD_DIM = 128
QKV = 10240


EPSILON = 1e-05
THETA = 500000.0


def swapped(value, axis, bit):
    mask = 2**bit
    pairs = [(source, source ^ mask) for source in range(lax.axis_size(axis))]
    return lax.ppermute(value, axis, pairs)


def rope_tables(lengths, head_dim):
    half_dim = head_dim // 2
    inv_freq = jnp.exp(
        -jnp.log(jnp.float32(THETA)) * jnp.arange(half_dim, dtype=jnp.float32) / half_dim
    )
    phases = lengths.astype(jnp.float32)[:, None] * inv_freq[None, :]
    return (jnp.cos(phases), jnp.sin(phases))


def rotate(vector, cos_vals, sine_vals):
    half_dim = vector.shape[-1] // 2
    front_half = vector[..., :half_dim]
    back_half = vector[..., half_dim:]
    return jnp.concatenate(
        [
            front_half * cos_vals - back_half * sine_vals,
            back_half * cos_vals + front_half * sine_vals,
        ],
        axis=-1,
    )


def attend(packed, key_block, value_block, lengths):
    slot_count = packed.shape[0]
    cache_size = key_block.shape[1]
    groups = key_block.shape[2] // HEAD_DIM
    per_group = HEADS // KV_HEADS
    grouped = packed.reshape(slot_count, groups, per_group + 2, HEAD_DIM)
    cos_vals, sine_vals = rope_tables(lengths, HEAD_DIM)
    queries = rotate(
        grouped[:, :, :per_group].astype(jnp.float32),
        cos_vals[:, None, None, :],
        sine_vals[:, None, None, :],
    ).astype(jnp.bfloat16)
    new_keys = rotate(
        grouped[:, :, per_group].astype(jnp.float32), cos_vals[:, None, :], sine_vals[:, None, :]
    ).astype(jnp.bfloat16)
    new_values = grouped[:, :, per_group + 1]
    cache_keys = key_block.reshape(slot_count, cache_size, groups, HEAD_DIM)
    cache_values = value_block.reshape(slot_count, cache_size, groups, HEAD_DIM)
    factor = HEAD_DIM ** (-0.5)
    cache_scores = (
        jnp.einsum("sghd,slgd->sghl", queries, cache_keys, preferred_element_type=jnp.float32)
        * factor
    )
    own_scores = (
        jnp.einsum("sghd,sgd->sgh", queries, new_keys, preferred_element_type=jnp.float32) * factor
    )
    in_cache = lax.broadcasted_iota(jnp.int32, (slot_count, cache_size), 1) < lengths[:, None]
    cache_scores = jnp.where(in_cache[:, None, None, :], cache_scores, -1e30)
    row_max = jnp.maximum(jnp.max(cache_scores, axis=-1), own_scores)
    cache_exp = jnp.exp(cache_scores - row_max[..., None])
    own_exp = jnp.exp(own_scores - row_max)
    denominator = jnp.sum(cache_exp, axis=-1) + own_exp
    cache_weight = (cache_exp / denominator[..., None]).astype(jnp.bfloat16)
    own_weight = (own_exp / denominator).astype(jnp.bfloat16)
    combined = jnp.einsum(
        "sghl,slgd->sghd", cache_weight, cache_values, preferred_element_type=jnp.float32
    )
    combined = (
        combined
        + own_weight.astype(jnp.float32)[..., None] * new_values.astype(jnp.float32)[:, :, None, :]
    )
    return combined.astype(jnp.bfloat16).reshape(slot_count, groups * per_group * HEAD_DIM)


def general_plan(
    hidden_in,
    norm_gain,
    qkv_weight,
    out_weight,
    key_cache,
    value_cache,
    cache_lengths,
    slot_request,
):
    side_index = lax.axis_index("side")
    is_weight = side_index == 0
    col_count = lax.axis_size("col")
    row_count = lax.axis_size("row")
    group_cols = col_count // row_count
    in_half = qkv_weight.shape[1] // 2
    out_half = out_weight.shape[1] // 2
    residual = hidden_in.astype(jnp.float32)
    square_sums = lax.psum(jnp.sum(residual * residual, axis=1), "row")
    normed = (
        residual
        * lax.rsqrt(square_sums[:, None] / D + EPSILON)
        * norm_gain.astype(jnp.float32)[None, :]
    ).astype(jnp.bfloat16)
    in_weight = lax.dynamic_slice_in_dim(qkv_weight, side_index * in_half, in_half, 1)
    partial_in = jnp.dot(
        lax.all_gather(normed, "col", axis=0, tiled=True),
        in_weight,
        preferred_element_type=jnp.float32,
    )
    in_slots = jnp.take(partial_in, slot_request, axis=0)
    own_width = QKV // row_count
    summed = lax.psum(in_slots.astype(jnp.bfloat16), "row")
    spread = lax.all_to_all(summed, "col", split_axis=0, concat_axis=1, tiled=True)
    own_columns = lax.dynamic_slice_in_dim(
        spread.reshape(spread.shape[0], col_count, in_half),
        lax.axis_index("row") * group_cols,
        group_cols,
        1,
    )
    slot_half = key_cache.shape[0] // 2
    halves = lax.all_to_all(
        own_columns[:, :, None, :], "side", split_axis=0, concat_axis=2, tiled=True
    )
    arrived = halves.reshape(slot_half, own_width)
    first_slot = side_index * slot_half
    key_part = lax.dynamic_slice_in_dim(key_cache, first_slot, slot_half, 0)
    value_part = lax.dynamic_slice_in_dim(value_cache, first_slot, slot_half, 0)
    length_part = lax.dynamic_slice_in_dim(cache_lengths, first_slot, slot_half, 0)
    attended = attend(arrived, key_part, value_part, length_part)
    out_cols = lax.dynamic_slice_in_dim(out_weight, side_index * out_half, out_half, 1)
    collected = lax.all_gather(attended, ("col", "side"), axis=0, tiled=True)
    out_slots = jnp.dot(collected, out_cols, preferred_element_type=jnp.float32)
    inverse = jnp.argsort(slot_request)
    out_requests = jnp.take(out_slots, inverse, axis=0)
    spread_out = lax.all_to_all(
        out_requests.astype(jnp.bfloat16), "col", split_axis=0, concat_axis=1, tiled=True
    ).astype(out_requests.dtype)
    out_view = spread_out.reshape(spread_out.shape[0], col_count, out_half)
    summed_out = lax.psum_scatter(
        out_view.astype(jnp.bfloat16), "row", scatter_dimension=1, tiled=True
    ).astype(jnp.float32)
    req_rows = hidden_in.shape[0]
    residual_view = residual.reshape(req_rows, group_cols, 2, out_half)
    residual_half = lax.dynamic_index_in_dim(residual_view, side_index, 2, keepdims=False)
    own_hidden = (residual_half + summed_out).astype(jnp.bfloat16)
    payload = jnp.where(is_weight, attended, own_hidden.reshape(attended.shape))
    received = swapped(payload, "side", 0)
    hidden = jnp.stack([own_hidden, received.reshape(own_hidden.shape)], axis=2).reshape(
        req_rows, residual.shape[1]
    )
    attention_rows = jnp.concatenate([received, attended], axis=0)
    result = jnp.where(is_weight, hidden, attention_rows)
    return result[None]


GROUP = HEADS // KV_HEADS
GROUP_WIDTH = (GROUP + 2) * HEAD_DIM
OUT_WIDTH = GROUP * HEAD_DIM
SLOTS = 8
VMEM = pl.BlockSpec(memory_space=pltpu.VMEM)
SMEM = pl.BlockSpec(memory_space=pltpu.SMEM)
HBM = pl.BlockSpec(memory_space=pl.ANY)
MIB = 2**20


def call(kernel, out_shape, in_specs, out_specs, flops, size, scratch=(), limit=16):
    return pl.pallas_call(
        kernel,
        out_shape=out_shape,
        in_specs=in_specs,
        out_specs=out_specs,
        scratch_shapes=list(scratch),
        compiler_params=pltpu.CompilerParams(vmem_limit_bytes=limit * MIB),
        cost_estimate=pl.CostEstimate(flops=flops, bytes_accessed=size, transcendentals=0),
    )


def in_vmem(value):
    return pltpu.with_memory_space_constraint(value, pltpu.VMEM)


def in_hbm(value):
    return pltpu.with_memory_space_constraint(value, pltpu.HBM)


def struct(shape, dtype=jnp.bfloat16):
    return jax.ShapeDtypeStruct(shape, dtype)


def moved(value, axis, mask):
    pairs = [(source, source ^ mask) for source in range(lax.axis_size(axis))]
    return lax.ppermute(value, axis, pairs)


def started(copies, sems):
    copies = [
        pltpu.make_async_copy(source, target, sems.at[i])
        for i, (source, target) in enumerate(copies)
    ]
    for copy in copies:
        copy.start()
    return copies


def run_copies(copies, sems):
    for copy in started(copies, sems):
        copy.wait()


def position():
    col = lax.axis_index("col")
    pairs = lax.axis_size("col") // lax.axis_size("row")
    return lax.axis_index("side"), col, lax.axis_index("row") * pairs + lax.rem(col, pairs)


def rows_copy(weight, target, half):
    depth, width = target.shape
    rows = pl.ds(pl.multiple_of(lax.axis_index("side") * depth, depth), depth)
    columns = pl.ds(pl.multiple_of(half * width, width), width)
    return weight.at[rows, columns], target


def stage_in_kernel(blocks, weight, slots, give_part, own_part, chosen, scratch, slot_part, sems):
    side, col, run = position()
    slots_copy, *copies = started(
        [
            (slots, slot_part),
            rows_copy(weight, give_part, 1 - side),
            rows_copy(weight, own_part, side),
        ],
        sems,
    )
    slots_copy.wait()
    chosen[...] = one_hot(slot_part, scratch, blocks, run, col).astype(jnp.bfloat16)
    for copy in copies:
        copy.wait()


def head_copies(weight, target, half):
    width = target.shape[1]
    columns = pl.ds(pl.multiple_of(half * width, width), width)
    copies = []
    for j in range(target.shape[0] // OUT_WIDTH):
        row = pl.multiple_of((2 * j + lax.axis_index("side")) * OUT_WIDTH, OUT_WIDTH)
        copies.append(
            (
                weight.at[pl.ds(row, OUT_WIDTH), columns],
                target.at[pl.ds(j * OUT_WIDTH, OUT_WIDTH), :],
            )
        )
    return copies


def stage_cache_kernel(blocks, lengths, keys, values, slots, *refs):
    key_part, value_part, cosine, sine, length_of, chosen, scratch, sems = refs
    side, col, run = position()
    copies = []
    for j in range(key_part.shape[2] // HEAD_DIM):
        lane = pl.multiple_of((2 * j + side) * HEAD_DIM, HEAD_DIM)
        for cache, part in ((keys, key_part), (values, value_part)):
            copies.append(
                (
                    cache.at[:, :, pl.ds(lane, HEAD_DIM)],
                    part.at[:, :, pl.ds(j * HEAD_DIM, HEAD_DIM)],
                )
            )
    copies = started(copies, sems)
    cosine[...], sine[...], length_of[...] = rope(lengths, cosine.shape[0])
    chosen[...] = one_hot(slots, scratch, blocks, col, run).T.astype(jnp.bfloat16)
    for copy in copies:
        copy.wait()


def stage_out_kernel(weight, attended, give_part, own_part, sems):
    side = lax.axis_index("side")
    copies = head_copies(weight, give_part, 1 - side) + head_copies(weight, own_part, side)
    run_copies(copies, sems)


def one_hot(slots, scratch, blocks, slot_base, request_base):
    total = slots.shape[0]
    rows = total // blocks
    index = lax.broadcasted_iota(jnp.int32, (total, total), 0)
    request = (lax.div(index, rows) ^ request_base) * rows + lax.rem(index, rows)
    scratch[...] = jnp.where(slots[...].reshape(1, total) == request, 1.0, 0.0).T
    parts = [
        scratch[pl.ds(pl.multiple_of((slot_base ^ i) * rows, rows), rows), :]
        for i in range(blocks)
    ]
    return jnp.concatenate(parts, axis=0)


def pieces(sums):
    high = sums.astype(jnp.bfloat16).astype(jnp.float32)
    middle = (sums - high).astype(jnp.bfloat16).astype(jnp.float32)
    low = sums - high - middle
    lane = lax.broadcasted_iota(jnp.int32, (sums.shape[0], HEAD_DIM), 1)
    parts = jnp.where(lane == 0, high, jnp.where(lane == 1, middle, low))
    return jnp.where(lane < 3, parts, 0.0).astype(jnp.bfloat16)


def dot_columns(rows, weight, out):
    size, width = weight.shape[1], 512
    for start in range(0, size, width):
        part = slice(start, min(start + width, size))
        product = jnp.dot(rows, weight[:, part], preferred_element_type=jnp.float32)
        out[:, part] = product.astype(out.dtype)


def in_kernel(count, chosen, *refs):
    pieces_in, (_, gain, weight, give, permuted) = refs[:count], refs[count:]
    depth = pieces_in[0].shape[1]
    half = weight.shape[1]
    runs = depth // HEAD_DIM
    first = pl.multiple_of(lax.axis_index("side") * runs, runs)
    gains = gain[pl.ds(first, runs), :].astype(jnp.float32)
    values = jnp.concatenate([piece[...].astype(jnp.float32) for piece in pieces_in], axis=0)
    scaled = jnp.concatenate(
        [
            values[:, i * HEAD_DIM : (i + 1) * HEAD_DIM] * gains[i : i + 1, :]
            for i in range(runs)
        ],
        axis=1,
    )
    sums = pieces(jnp.sum(values * values, axis=1, keepdims=True))
    order = jnp.dot(
        chosen[...], scaled.astype(jnp.bfloat16), preferred_element_type=jnp.float32
    ).astype(jnp.bfloat16)
    permuted[...] = order
    own_sums = jnp.dot(chosen[...], sums, preferred_element_type=jnp.float32)
    give[:, half:] = own_sums.astype(jnp.bfloat16)
    dot_columns(order, weight, give)


def out_kernel(count, chosen, *refs):
    pieces_in, (_, weight, give, permuted) = refs[:count], refs[count:]
    values = jnp.concatenate([piece[...] for piece in pieces_in], axis=0)
    order = jnp.dot(chosen[...], values, preferred_element_type=jnp.float32).astype(jnp.bfloat16)
    permuted[...] = order
    dot_columns(order, weight, give)


def carries(entry, pairs):
    return entry % pairs == (0 if entry // pairs % 2 else pairs - 1)


def arrival_order(count, pairs):
    return sorted(range(count), key=lambda i: (i == 0, not carries(i, pairs), i % pairs, -i))


def merge_kernel(own, given, received, *outs):
    rows = outs[0].shape[0]
    half = own.shape[1]
    more = given.shape[1] - half
    for i, out in enumerate(outs):
        part = slice(i * rows, (i + 1) * rows)
        total = own[part, :] + received[part, :half].astype(jnp.float32)
        out[:, :half] = total.astype(jnp.bfloat16)
        if out.shape[1] > half:
            out[:, half:] = jnp.concatenate(
                [given[part, half : half + more // 2], received[part, half : half + more // 2]],
                axis=1,
            )


def own_kernel(permuted, weight, own):
    dot_columns(permuted[...], weight, own)


def project(kernel, chosen, pieces_in, extra, weights, more, pairs):
    count = lax.axis_size("col")
    parts = len(pieces_in)
    rows, depth = pieces_in[0].shape
    rows = rows * parts
    half = weights[0].shape[1]
    flops = 2 * rows * depth * half
    give, permuted = call(
        functools.partial(kernel, parts),
        [struct((rows, half + more)), struct((rows, depth))],
        [VMEM] * (parts + len(extra) + 3),
        [VMEM, VMEM],
        flops,
        depth * half * 2,
    )(chosen, *pieces_in, in_vmem(weights[1]), *extra, in_vmem(weights[0]))
    received = moved(give, "side", 1)
    own = call(
        own_kernel,
        struct((rows, half), jnp.float32),
        [VMEM, VMEM],
        VMEM,
        flops,
        depth * half * 2,
    )(permuted, in_vmem(weights[1]))
    return call(
        merge_kernel,
        [
            struct((rows // count, half + (more if carries(i, pairs) else 0))) for i in range(count)
        ],
        [VMEM] * 3,
        [VMEM] * count,
        rows * half,
        rows * half * 8,
    )(own, give, received)


def gathered(parts, axis):
    blocks = {0: parts}
    mask = lax.axis_size(axis) // 2
    while mask:
        blocks |= {
            known | mask: [moved(part, axis, mask) for part in block]
            for known, block in blocks.items()
        }
        mask //= 2
    return [part for i in sorted(blocks) for part in blocks[i]]


def in_place(blocks, pairs):
    return [blocks[arrival_order(len(blocks), pairs).index(i)] for i in range(len(blocks))]


def spread(products):
    col_count, row_count = lax.axis_size("col"), lax.axis_size("row")
    pairs = col_count // row_count
    sent = {
        j: lax.ppermute(
            products[j],
            ("col", "row"),
            [
                (
                    col * row_count + row,
                    ((row * pairs + col % pairs) ^ j) * row_count + col // pairs,
                )
                for col in range(col_count)
                for row in range(row_count)
            ],
        )
        for j in range(col_count)
    }
    return [sent[j] for j in arrival_order(col_count, pairs)]


def rotated(vector, cosine, sine):
    return vector * cosine + pltpu.roll(vector, HEAD_DIM // 2, 1) * sine


def rope(lengths, rows):
    slot = lax.broadcasted_iota(jnp.int32, (rows, HEAD_DIM), 0)
    length_of = jnp.zeros((rows, HEAD_DIM), jnp.int32)
    for i in range(rows):
        length_of = jnp.where(slot == i, lengths[i], length_of)
    lane = lax.broadcasted_iota(jnp.int32, (rows, HEAD_DIM), 1)
    half = HEAD_DIM // 2
    step = lax.rem(lane, half).astype(jnp.float32)
    phases = length_of.astype(jnp.float32) * jnp.exp(-math.log(THETA) * step / half)
    sine = jnp.sin(phases)
    return jnp.cos(phases), jnp.where(lane < half, -sine, sine), length_of


def attend_all(count, parts, cosine, sine, lengths, *refs):
    blocks, (keys, values), refs = refs[:count], refs[count : count + 2], refs[count + 2 :]
    blocks = in_place(blocks, keys.shape[2] // HEAD_DIM)
    outs, (scores_of, probs_of) = refs[:parts], refs[parts:]
    pairs = keys.shape[2] // HEAD_DIM
    rows, cache = keys.shape[:2]
    low = lax.rem(lax.axis_index("col"), pairs)
    width = GROUP_WIDTH
    squares = sum(
        blocks[i][:, width:].astype(jnp.float32) for i in range(count) if carries(i, pairs)
    )
    scale = lax.rsqrt(jnp.sum(squares, axis=1, keepdims=True) / D + EPSILON)
    factor = HEAD_DIM ** (-0.5)
    cosines, sines, length_of = cosine[...], sine[...], lengths[:, :1]
    lane = lax.broadcasted_iota(jnp.int32, (SLOTS, SLOTS * cache), 1)
    slot = lax.broadcasted_iota(jnp.int32, (SLOTS, SLOTS * cache), 0)
    position = lane - slot * cache
    runs = [slice(start, start + SLOTS) for start in range(0, rows, SLOTS)]
    filled = [(position >= 0) & (position < length_of[part]) for part in runs]
    own, new_values, own_probs = [], [], []
    for pair in range(pairs):
        total = blocks[pair][:, :width].astype(jnp.float32)
        for i in range(pair + pairs, count, pairs):
            total = total + blocks[i][:, :width].astype(jnp.float32)
        total = (total * scale).astype(jnp.bfloat16).astype(jnp.float32)
        heads = [total[:, h * HEAD_DIM : (h + 1) * HEAD_DIM] for h in range(GROUP + 2)]
        queries = [
            rotated(head, cosines, sines).astype(jnp.bfloat16).astype(jnp.float32)
            for head in heads[:GROUP]
        ]
        new_key = rotated(heads[GROUP], cosines, sines).astype(jnp.bfloat16).astype(jnp.float32)
        new_values.append(heads[GROUP + 1])
        own.append([jnp.sum(query * new_key, axis=1, keepdims=True) * factor for query in queries])
        lanes = pl.ds(pl.multiple_of((low ^ pair) * HEAD_DIM, HEAD_DIM), HEAD_DIM)
        for run, part in enumerate(runs):
            query = jnp.concatenate([head[part] for head in queries], axis=0)
            key = keys[part, :, lanes].reshape(SLOTS * cache, HEAD_DIM)
            scores_of[pair, run] = lax.dot_general(
                query.astype(jnp.bfloat16),
                key,
                (((1,), (1,)), ((), ())),
                preferred_element_type=jnp.float32,
            )
    for pair in range(pairs):
        for run, part in enumerate(runs):
            scores = (scores_of[pair, run] * factor).reshape(GROUP, SLOTS, SLOTS * cache)
            scores = jnp.where(filled[run][None], scores, -1e30)
            own_score = jnp.concatenate([head[part] for head in own[pair]], axis=0).reshape(
                GROUP, SLOTS, 1
            )
            highest = jnp.maximum(jnp.max(scores, axis=2, keepdims=True), own_score)
            weights = jnp.exp(scores - highest)
            own_weight = jnp.exp(own_score - highest)
            inverse = 1.0 / (jnp.sum(weights, axis=2, keepdims=True) + own_weight)
            probs = (weights * inverse).astype(jnp.bfloat16)
            probs_of[pair, run] = probs.reshape(GROUP * SLOTS, SLOTS * cache)
            own_probs.append((own_weight * inverse).astype(jnp.bfloat16).astype(jnp.float32))
    for pair in range(pairs):
        lanes = pl.ds(pl.multiple_of((low ^ pair) * HEAD_DIM, HEAD_DIM), HEAD_DIM)
        results = []
        for run, part in enumerate(runs):
            value = values[part, :, lanes].reshape(SLOTS * cache, HEAD_DIM)
            mixed = jnp.dot(probs_of[pair, run], value, preferred_element_type=jnp.float32)
            own_prob = own_probs[pair * len(runs) + run]
            results.append(
                mixed.reshape(GROUP, SLOTS, HEAD_DIM) + own_prob * new_values[pair][part][None]
            )
        for head in range(GROUP):
            at = pl.multiple_of((low ^ pair) * OUT_WIDTH + head * HEAD_DIM, HEAD_DIM)
            size = len(results) // parts
            for i, out in enumerate(outs):
                joined = jnp.concatenate(
                    [result[head] for result in results[i * size : (i + 1) * size]], axis=0
                )
                out[:, pl.ds(at, HEAD_DIM)] = joined.astype(jnp.bfloat16)


def sum_kernel(count, parts, hidden, *refs):
    attended, blocks, (keep, send) = refs[:parts], refs[parts : parts + count], refs[parts + count :]
    rows, width = blocks[0].shape
    pairs = keep.shape[1] // width
    blocks = in_place(blocks, pairs)
    side = lax.axis_index("side")
    low = lax.rem(lax.axis_index("col"), pairs)
    for pair in range(pairs):
        column = low ^ pair
        total = blocks[pair][...].astype(jnp.float32)
        for i in range(pair + pairs, count, pairs):
            total = total + blocks[i][...].astype(jnp.float32)
        at = pl.ds(pl.multiple_of((2 * column + side) * width, width), width)
        hidden_out = (hidden[:, at].astype(jnp.float32) + total).astype(jnp.bfloat16)
        at = pl.ds(pl.multiple_of(column * width, width), width)
        attention = jnp.concatenate([part[:, at] for part in attended], axis=0)
        keep[:, at] = jnp.where(side == 0, hidden_out, attention)
        send[:, at] = jnp.where(side == 0, attention, hidden_out)


def join_kernel(keep, received, out, sems):
    side = lax.axis_index("side")
    width = OUT_WIDTH
    copies = []
    for j in range(keep.shape[1] // width):
        part = slice(j * width, (j + 1) * width)
        for ref, core in ((keep, side), (received, 1 - side)):
            at = pl.ds(pl.multiple_of((2 * j + core) * width, width), width)
            copies.append((ref.at[:, part], out.at[0, :, at]))
    run_copies(copies, sems)


def paired_plan(
    hidden_in, norm_gain, qkv_weight, out_weight, key_cache, value_cache, cache_lengths, slot_request
):
    col_count, row_count = lax.axis_size("col"), lax.axis_size("row")
    pairs = col_count // row_count
    side = lax.axis_index("side")
    rows, depth = hidden_in.shape
    half = depth // 2
    cache = key_cache.shape[1]
    parts = 2
    piece = rows // parts

    own_part = lax.dynamic_slice_in_dim(hidden_in, side * half, half, 1)
    gain = norm_gain.reshape(depth // HEAD_DIM, HEAD_DIM)
    half_in, half_out = qkv_weight.shape[1] // 2, out_weight.shape[1] // 2
    total = rows * col_count
    square = (total, total)
    give_in, own_in, chosen_in = call(
        functools.partial(stage_in_kernel, col_count),
        [pltpu.VMEM((half, half_in), jnp.bfloat16)] * 2 + [struct(square)],
        [HBM, HBM],
        [VMEM] * 3,
        0,
        half * half_in * 4,
        [
            pltpu.VMEM(square, jnp.float32),
            pltpu.VMEM((total,), jnp.int32),
            pltpu.SemaphoreType.DMA((3,)),
        ],
    )(in_hbm(qkv_weight), in_hbm(slot_request))
    blocks = gathered(
        [own_part[i * piece : (i + 1) * piece] for i in range(parts)], "col"
    )
    products = spread(
        project(in_kernel, chosen_in, blocks, [gain], [give_in, own_in], HEAD_DIM, pairs)
    )

    table = struct((rows, HEAD_DIM), jnp.float32)
    key_part, value_part, *tables, chosen_out = call(
        functools.partial(stage_cache_kernel, col_count),
        [pltpu.VMEM((rows, cache, pairs * HEAD_DIM), jnp.bfloat16)] * 2
        + [table, table, struct((rows, HEAD_DIM), jnp.int32), struct(square)],
        [SMEM, HBM, HBM, VMEM],
        [VMEM] * 6,
        0,
        4 * rows * cache * pairs * HEAD_DIM,
        [pltpu.VMEM(square, jnp.float32), pltpu.SemaphoreType.DMA((2 * pairs,))],
    )(cache_lengths, in_hbm(key_cache), in_hbm(value_cache), slot_request)
    runs = (pairs, rows // SLOTS, GROUP * SLOTS, SLOTS * cache)
    attended = call(
        functools.partial(attend_all, col_count, parts),
        [struct((piece, half))] * parts,
        [VMEM] * (col_count + 5),
        [VMEM] * parts,
        4 * rows * half * cache,
        0,
        [pltpu.VMEM(runs, jnp.float32), pltpu.VMEM(runs, jnp.bfloat16)],
    )(*tables, *products, in_vmem(key_part), in_vmem(value_part))

    give_out, own_out = call(
        stage_out_kernel,
        [pltpu.VMEM((half, half_out), jnp.bfloat16)] * 2,
        [HBM, HBM],
        [VMEM] * 2,
        0,
        half * half_out * 4,
        [pltpu.SemaphoreType.DMA((2 * pairs,))],
    )(in_hbm(out_weight), attended[-1])
    products = spread(
        project(
            out_kernel, chosen_out, gathered(attended, "col"), [], [give_out, own_out], 0, pairs
        )
    )
    keep, send = call(
        functools.partial(sum_kernel, col_count, parts),
        [struct((rows, half)), struct((rows, half))],
        [VMEM] * (1 + parts + col_count),
        [VMEM, VMEM],
        rows * depth * 4,
        rows * depth * 8,
    )(hidden_in, *attended, *products)
    return call(
        join_kernel,
        struct((1, rows, depth)),
        [VMEM, VMEM],
        HBM,
        0,
        rows * depth * 4,
        [pltpu.SemaphoreType.DMA((2 * pairs,))],
    )(keep, moved(send, "side", 1))


def per_device(*args):
    hidden_in, _, qkv_weight, out_weight, key_cache = args[:5]
    col_count, row_count = lax.axis_size("col"), lax.axis_size("row")
    fits = (
        lax.axis_size("side") == 2
        and qkv_weight.shape[1] == 2 * GROUP_WIDTH
        and col_count % row_count == 0
        and col_count & (col_count - 1) == 0
        and hidden_in.shape[0] % 32 == 0
        and key_cache.shape[1] % 16 == 0
        and hidden_in.shape[1] == 2 * OUT_WIDTH * (col_count // row_count)
    )
    return paired_plan(*args) if fits else general_plan(*args)


def solution(mesh):
    placed = (
        P(("groups", "col"), "row"),
        P("row"),
        P("row", "col"),
        P("row", "col"),
        P(("groups", "col"), None, "row"),
        P(("groups", "col"), None, "row"),
        P(("groups", "col")),
        P("groups"),
    )
    return jax.shard_map(
        per_device,
        mesh=mesh,
        in_specs=placed,
        out_specs=P("side", ("groups", "col"), "row"),
        check_vma=False,
    )
```

```python
import functools
import math

import jax
import jax.numpy as jnp
from jax import lax
from jax.experimental import pallas as pl
from jax.experimental.pallas import tpu as pltpu
from jax.sharding import PartitionSpec as P

D = 8192
HEADS = 64
KV_HEADS = 8
HEAD_DIM = 128
QKV = 10240


EPSILON = 1e-05
THETA = 500000.0


def swapped(value, axis, bit):
    mask = 2**bit
    pairs = [(source, source ^ mask) for source in range(lax.axis_size(axis))]
    return lax.ppermute(value, axis, pairs)


def rope_tables(lengths, head_dim):
    half_dim = head_dim // 2
    inv_freq = jnp.exp(
        -jnp.log(jnp.float32(THETA)) * jnp.arange(half_dim, dtype=jnp.float32) / half_dim
    )
    phases = lengths.astype(jnp.float32)[:, None] * inv_freq[None, :]
    return (jnp.cos(phases), jnp.sin(phases))


def rotate(vector, cos_vals, sine_vals):
    half_dim = vector.shape[-1] // 2
    front_half = vector[..., :half_dim]
    back_half = vector[..., half_dim:]
    return jnp.concatenate(
        [
            front_half * cos_vals - back_half * sine_vals,
            back_half * cos_vals + front_half * sine_vals,
        ],
        axis=-1,
    )


def attend(packed, key_block, value_block, lengths):
    slot_count = packed.shape[0]
    cache_size = key_block.shape[1]
    groups = key_block.shape[2] // HEAD_DIM
    per_group = HEADS // KV_HEADS
    grouped = packed.reshape(slot_count, groups, per_group + 2, HEAD_DIM)
    cos_vals, sine_vals = rope_tables(lengths, HEAD_DIM)
    queries = rotate(
        grouped[:, :, :per_group].astype(jnp.float32),
        cos_vals[:, None, None, :],
        sine_vals[:, None, None, :],
    ).astype(jnp.bfloat16)
    new_keys = rotate(
        grouped[:, :, per_group].astype(jnp.float32), cos_vals[:, None, :], sine_vals[:, None, :]
    ).astype(jnp.bfloat16)
    new_values = grouped[:, :, per_group + 1]
    cache_keys = key_block.reshape(slot_count, cache_size, groups, HEAD_DIM)
    cache_values = value_block.reshape(slot_count, cache_size, groups, HEAD_DIM)
    factor = HEAD_DIM ** (-0.5)
    cache_scores = (
        jnp.einsum("sghd,slgd->sghl", queries, cache_keys, preferred_element_type=jnp.float32)
        * factor
    )
    own_scores = (
        jnp.einsum("sghd,sgd->sgh", queries, new_keys, preferred_element_type=jnp.float32) * factor
    )
    in_cache = lax.broadcasted_iota(jnp.int32, (slot_count, cache_size), 1) < lengths[:, None]
    cache_scores = jnp.where(in_cache[:, None, None, :], cache_scores, -1e30)
    row_max = jnp.maximum(jnp.max(cache_scores, axis=-1), own_scores)
    cache_exp = jnp.exp(cache_scores - row_max[..., None])
    own_exp = jnp.exp(own_scores - row_max)
    denominator = jnp.sum(cache_exp, axis=-1) + own_exp
    cache_weight = (cache_exp / denominator[..., None]).astype(jnp.bfloat16)
    own_weight = (own_exp / denominator).astype(jnp.bfloat16)
    combined = jnp.einsum(
        "sghl,slgd->sghd", cache_weight, cache_values, preferred_element_type=jnp.float32
    )
    combined = (
        combined
        + own_weight.astype(jnp.float32)[..., None] * new_values.astype(jnp.float32)[:, :, None, :]
    )
    return combined.astype(jnp.bfloat16).reshape(slot_count, groups * per_group * HEAD_DIM)


def general_plan(
    hidden_in,
    norm_gain,
    qkv_weight,
    out_weight,
    key_cache,
    value_cache,
    cache_lengths,
    slot_request,
):
    side_index = lax.axis_index("side")
    is_weight = side_index == 0
    col_count = lax.axis_size("col")
    row_count = lax.axis_size("row")
    group_cols = col_count // row_count
    in_half = qkv_weight.shape[1] // 2
    out_half = out_weight.shape[1] // 2
    residual = hidden_in.astype(jnp.float32)
    square_sums = lax.psum(jnp.sum(residual * residual, axis=1), "row")
    normed = (
        residual
        * lax.rsqrt(square_sums[:, None] / D + EPSILON)
        * norm_gain.astype(jnp.float32)[None, :]
    ).astype(jnp.bfloat16)
    in_weight = lax.dynamic_slice_in_dim(qkv_weight, side_index * in_half, in_half, 1)
    partial_in = jnp.dot(
        lax.all_gather(normed, "col", axis=0, tiled=True),
        in_weight,
        preferred_element_type=jnp.float32,
    )
    in_slots = jnp.take(partial_in, slot_request, axis=0)
    own_width = QKV // row_count
    summed = lax.psum(in_slots.astype(jnp.bfloat16), "row")
    spread = lax.all_to_all(summed, "col", split_axis=0, concat_axis=1, tiled=True)
    own_columns = lax.dynamic_slice_in_dim(
        spread.reshape(spread.shape[0], col_count, in_half),
        lax.axis_index("row") * group_cols,
        group_cols,
        1,
    )
    slot_half = key_cache.shape[0] // 2
    halves = lax.all_to_all(
        own_columns[:, :, None, :], "side", split_axis=0, concat_axis=2, tiled=True
    )
    arrived = halves.reshape(slot_half, own_width)
    first_slot = side_index * slot_half
    key_part = lax.dynamic_slice_in_dim(key_cache, first_slot, slot_half, 0)
    value_part = lax.dynamic_slice_in_dim(value_cache, first_slot, slot_half, 0)
    length_part = lax.dynamic_slice_in_dim(cache_lengths, first_slot, slot_half, 0)
    attended = attend(arrived, key_part, value_part, length_part)
    out_cols = lax.dynamic_slice_in_dim(out_weight, side_index * out_half, out_half, 1)
    collected = lax.all_gather(attended, ("col", "side"), axis=0, tiled=True)
    out_slots = jnp.dot(collected, out_cols, preferred_element_type=jnp.float32)
    inverse = jnp.argsort(slot_request)
    out_requests = jnp.take(out_slots, inverse, axis=0)
    spread_out = lax.all_to_all(
        out_requests.astype(jnp.bfloat16), "col", split_axis=0, concat_axis=1, tiled=True
    ).astype(out_requests.dtype)
    out_view = spread_out.reshape(spread_out.shape[0], col_count, out_half)
    summed_out = lax.psum_scatter(
        out_view.astype(jnp.bfloat16), "row", scatter_dimension=1, tiled=True
    ).astype(jnp.float32)
    req_rows = hidden_in.shape[0]
    residual_view = residual.reshape(req_rows, group_cols, 2, out_half)
    residual_half = lax.dynamic_index_in_dim(residual_view, side_index, 2, keepdims=False)
    own_hidden = (residual_half + summed_out).astype(jnp.bfloat16)
    payload = jnp.where(is_weight, attended, own_hidden.reshape(attended.shape))
    received = swapped(payload, "side", 0)
    hidden = jnp.stack([own_hidden, received.reshape(own_hidden.shape)], axis=2).reshape(
        req_rows, residual.shape[1]
    )
    attention_rows = jnp.concatenate([received, attended], axis=0)
    result = jnp.where(is_weight, hidden, attention_rows)
    return result[None]


GROUP = HEADS // KV_HEADS
GROUP_WIDTH = (GROUP + 2) * HEAD_DIM
OUT_WIDTH = GROUP * HEAD_DIM
SLOTS = 8
VMEM = pl.BlockSpec(memory_space=pltpu.VMEM)
SMEM = pl.BlockSpec(memory_space=pltpu.SMEM)
HBM = pl.BlockSpec(memory_space=pl.ANY)
MIB = 2**20


def call(kernel, out_shape, in_specs, out_specs, flops, size, scratch=(), limit=16):
    return pl.pallas_call(
        kernel,
        out_shape=out_shape,
        in_specs=in_specs,
        out_specs=out_specs,
        scratch_shapes=list(scratch),
        compiler_params=pltpu.CompilerParams(vmem_limit_bytes=limit * MIB),
        cost_estimate=pl.CostEstimate(flops=flops, bytes_accessed=size, transcendentals=0),
    )


def in_vmem(value):
    return pltpu.with_memory_space_constraint(value, pltpu.VMEM)


def in_hbm(value):
    return pltpu.with_memory_space_constraint(value, pltpu.HBM)


def struct(shape, dtype=jnp.bfloat16):
    return jax.ShapeDtypeStruct(shape, dtype)


def moved(value, axis, mask):
    pairs = [(source, source ^ mask) for source in range(lax.axis_size(axis))]
    return lax.ppermute(value, axis, pairs)


def started(copies, sems):
    copies = [
        pltpu.make_async_copy(source, target, sems.at[i])
        for i, (source, target) in enumerate(copies)
    ]
    for copy in copies:
        copy.start()
    return copies


def run_copies(copies, sems):
    for copy in started(copies, sems):
        copy.wait()


def position():
    col = lax.axis_index("col")
    pairs = lax.axis_size("col") // lax.axis_size("row")
    return lax.axis_index("side"), col, lax.axis_index("row") * pairs + lax.rem(col, pairs)


def rows_copy(weight, target, half):
    depth, width = target.shape
    rows = pl.ds(pl.multiple_of(lax.axis_index("side") * depth, depth), depth)
    columns = pl.ds(pl.multiple_of(half * width, width), width)
    return weight.at[rows, columns], target


def stage_in_kernel(blocks, weight, slots, give_part, own_part, chosen, scratch, slot_part, sems):
    side, col, run = position()
    slots_copy, *copies = started(
        [
            (slots, slot_part),
            rows_copy(weight, give_part, 1 - side),
            rows_copy(weight, own_part, side),
        ],
        sems,
    )
    slots_copy.wait()
    chosen[...] = one_hot(slot_part, scratch, blocks, run, col).astype(jnp.bfloat16)
    for copy in copies:
        copy.wait()


def head_copies(weight, target, half):
    width = target.shape[1]
    columns = pl.ds(pl.multiple_of(half * width, width), width)
    copies = []
    for j in range(target.shape[0] // OUT_WIDTH):
        row = pl.multiple_of((2 * j + lax.axis_index("side")) * OUT_WIDTH, OUT_WIDTH)
        copies.append(
            (
                weight.at[pl.ds(row, OUT_WIDTH), columns],
                target.at[pl.ds(j * OUT_WIDTH, OUT_WIDTH), :],
            )
        )
    return copies


def stage_cache_kernel(blocks, lengths, keys, values, slots, *refs):
    key_part, value_part, cosine, sine, length_of, chosen, scratch, sems = refs
    side, col, run = position()
    copies = []
    for j in range(key_part.shape[2] // HEAD_DIM):
        lane = pl.multiple_of((2 * j + side) * HEAD_DIM, HEAD_DIM)
        for cache, part in ((keys, key_part), (values, value_part)):
            copies.append(
                (
                    cache.at[:, :, pl.ds(lane, HEAD_DIM)],
                    part.at[:, :, pl.ds(j * HEAD_DIM, HEAD_DIM)],
                )
            )
    copies = started(copies, sems)
    cosine[...], sine[...], length_of[...] = rope(lengths, cosine.shape[0])
    chosen[...] = one_hot(slots, scratch, blocks, col, run).T.astype(jnp.bfloat16)
    for copy in copies:
        copy.wait()


def stage_out_kernel(weight, attended, own_part, sems):
    run_copies(head_copies(weight, own_part, lax.axis_index("side")), sems)


def one_hot(slots, scratch, blocks, slot_base, request_base):
    total = slots.shape[0]
    rows = total // blocks
    index = lax.broadcasted_iota(jnp.int32, (total, total), 0)
    request = (lax.div(index, rows) ^ request_base) * rows + lax.rem(index, rows)
    scratch[...] = jnp.where(slots[...].reshape(1, total) == request, 1.0, 0.0).T
    parts = [
        scratch[pl.ds(pl.multiple_of((slot_base ^ i) * rows, rows), rows), :]
        for i in range(blocks)
    ]
    return jnp.concatenate(parts, axis=0)


def pieces(sums):
    high = sums.astype(jnp.bfloat16).astype(jnp.float32)
    middle = (sums - high).astype(jnp.bfloat16).astype(jnp.float32)
    low = sums - high - middle
    lane = lax.broadcasted_iota(jnp.int32, (sums.shape[0], HEAD_DIM), 1)
    parts = jnp.where(lane == 0, high, jnp.where(lane == 1, middle, low))
    return jnp.where(lane < 3, parts, 0.0).astype(jnp.bfloat16)


def dot_columns(rows, weight, out):
    size, width = weight.shape[1], 512
    for start in range(0, size, width):
        part = slice(start, min(start + width, size))
        product = jnp.dot(rows, weight[:, part], preferred_element_type=jnp.float32)
        out[:, part] = product.astype(out.dtype)


def in_kernel(count, chosen, *refs):
    pieces_in, (_, gain, weight, give, permuted) = refs[:count], refs[count:]
    depth = pieces_in[0].shape[1]
    half = weight.shape[1]
    runs = depth // HEAD_DIM
    first = pl.multiple_of(lax.axis_index("side") * runs, runs)
    gains = gain[pl.ds(first, runs), :].astype(jnp.float32)
    values = jnp.concatenate([piece[...].astype(jnp.float32) for piece in pieces_in], axis=0)
    scaled = jnp.concatenate(
        [
            values[:, i * HEAD_DIM : (i + 1) * HEAD_DIM] * gains[i : i + 1, :]
            for i in range(runs)
        ],
        axis=1,
    )
    sums = pieces(jnp.sum(values * values, axis=1, keepdims=True))
    order = jnp.dot(
        chosen[...], scaled.astype(jnp.bfloat16), preferred_element_type=jnp.float32
    ).astype(jnp.bfloat16)
    permuted[...] = order
    own_sums = jnp.dot(chosen[...], sums, preferred_element_type=jnp.float32)
    give[:, half:] = own_sums.astype(jnp.bfloat16)
    dot_columns(order, weight, give)


def out_kernel(count, chosen, *refs):
    pieces_in, (_, weight, give, permuted) = refs[:count], refs[count:]
    values = jnp.concatenate([piece[...] for piece in pieces_in], axis=0)
    order = jnp.dot(chosen[...], values, preferred_element_type=jnp.float32).astype(jnp.bfloat16)
    permuted[...] = order
    dot_columns(order, weight, give)


def carries(entry):
    return entry > 0


def sums_entry(run, pairs):
    return run * pairs + (pairs - 1 if run == 0 else 0)


def arrival_order(count, pairs):
    return sorted(range(count), key=lambda i: (i == 0, i % pairs, -i))


def merge_kernel(own, given, received, *outs):
    rows = outs[0].shape[0]
    half = own.shape[1]
    more = given.shape[1] - half
    for i, out in enumerate(outs):
        part = slice(i * rows, (i + 1) * rows)
        total = own[part, :] + received[part, :half].astype(jnp.float32)
        out[:, :half] = total.astype(jnp.bfloat16)
        if out.shape[1] > half:
            out[:, half:] = jnp.concatenate(
                [given[part, half : half + more // 2], received[part, half : half + more // 2]],
                axis=1,
            )


def own_kernel(permuted, weight, own):
    dot_columns(permuted[...], weight, own)


def project(kernel, chosen, pieces_in, extra, weights, more, pairs):
    count = lax.axis_size("col")
    parts = len(pieces_in)
    rows, depth = pieces_in[0].shape
    rows = rows * parts
    half = weights[0].shape[1]
    flops = 2 * rows * depth * half
    give, permuted = call(
        functools.partial(kernel, parts),
        [struct((rows, half + more)), struct((rows, depth))],
        [VMEM] * (parts + len(extra) + 3),
        [VMEM, VMEM],
        flops,
        depth * half * 2,
    )(chosen, *pieces_in, in_vmem(weights[1]), *extra, in_vmem(weights[0]))
    received = moved(give, "side", 1)
    own = call(
        own_kernel,
        struct((rows, half), jnp.float32),
        [VMEM, VMEM],
        VMEM,
        flops,
        depth * half * 2,
    )(permuted, in_vmem(weights[1]))
    return call(
        merge_kernel,
        [
            struct((rows // count, half + (more if carries(i) else 0))) for i in range(count)
        ],
        [VMEM] * 3,
        [VMEM] * count,
        rows * half,
        rows * half * 8,
    )(own, give, received)


def gathered(parts, axis):
    blocks = {0: parts}
    mask = lax.axis_size(axis) // 2
    while mask:
        blocks |= {
            known | mask: [moved(part, axis, mask) for part in block]
            for known, block in blocks.items()
        }
        mask //= 2
    return [part for i in sorted(blocks) for part in blocks[i]]


def in_place(blocks, pairs):
    return [blocks[arrival_order(len(blocks), pairs).index(i)] for i in range(len(blocks))]


def spread(products):
    col_count, row_count = lax.axis_size("col"), lax.axis_size("row")
    pairs = col_count // row_count
    sent = {
        j: lax.ppermute(
            products[j],
            ("col", "row"),
            [
                (
                    col * row_count + row,
                    ((row * pairs + col % pairs) ^ j) * row_count + col // pairs,
                )
                for col in range(col_count)
                for row in range(row_count)
            ],
        )
        for j in range(col_count)
    }
    return [sent[j] for j in arrival_order(col_count, pairs)]


def rotated(vector, cosine, sine):
    return vector * cosine + pltpu.roll(vector, HEAD_DIM // 2, 1) * sine


def rope(lengths, rows):
    slot = lax.broadcasted_iota(jnp.int32, (rows, HEAD_DIM), 0)
    length_of = jnp.zeros((rows, HEAD_DIM), jnp.int32)
    for i in range(rows):
        length_of = jnp.where(slot == i, lengths[i], length_of)
    lane = lax.broadcasted_iota(jnp.int32, (rows, HEAD_DIM), 1)
    half = HEAD_DIM // 2
    step = lax.rem(lane, half).astype(jnp.float32)
    phases = length_of.astype(jnp.float32) * jnp.exp(-math.log(THETA) * step / half)
    sine = jnp.sin(phases)
    return jnp.cos(phases), jnp.where(lane < half, -sine, sine), length_of


def attend_all(count, parts, cosine, sine, lengths, *refs):
    blocks, (keys, values, weight), refs = refs[:count], refs[count : count + 3], refs[count + 3 :]
    blocks = in_place(blocks, keys.shape[2] // HEAD_DIM)
    outs, (give_part, scores_of, probs_of, sems) = refs[:parts], refs[parts:]
    copies = started(head_copies(weight, give_part, 1 - lax.axis_index("side")), sems)
    pairs = keys.shape[2] // HEAD_DIM
    rows, cache = keys.shape[:2]
    low = lax.rem(lax.axis_index("col"), pairs)
    width = GROUP_WIDTH
    squares = sum(
        blocks[sums_entry(run, pairs)][:, width:].astype(jnp.float32)
        for run in range(count // pairs)
    )
    scale = lax.rsqrt(jnp.sum(squares, axis=1, keepdims=True) / D + EPSILON)
    factor = HEAD_DIM ** (-0.5)
    cosines, sines, length_of = cosine[...], sine[...], lengths[:, :1]
    lane = lax.broadcasted_iota(jnp.int32, (SLOTS, SLOTS * cache), 1)
    slot = lax.broadcasted_iota(jnp.int32, (SLOTS, SLOTS * cache), 0)
    position = lane - slot * cache
    runs = [slice(start, start + SLOTS) for start in range(0, rows, SLOTS)]
    filled = [(position >= 0) & (position < length_of[part]) for part in runs]
    own, new_values, own_probs = [], [], []
    for pair in range(pairs):
        total = blocks[pair][:, :width].astype(jnp.float32)
        for i in range(pair + pairs, count, pairs):
            total = total + blocks[i][:, :width].astype(jnp.float32)
        total = (total * scale).astype(jnp.bfloat16).astype(jnp.float32)
        heads = [total[:, h * HEAD_DIM : (h + 1) * HEAD_DIM] for h in range(GROUP + 2)]
        queries = [
            rotated(head, cosines, sines).astype(jnp.bfloat16).astype(jnp.float32)
            for head in heads[:GROUP]
        ]
        new_key = rotated(heads[GROUP], cosines, sines).astype(jnp.bfloat16).astype(jnp.float32)
        new_values.append(heads[GROUP + 1])
        own.append([jnp.sum(query * new_key, axis=1, keepdims=True) * factor for query in queries])
        lanes = pl.ds(pl.multiple_of((low ^ pair) * HEAD_DIM, HEAD_DIM), HEAD_DIM)
        for run, part in enumerate(runs):
            query = jnp.concatenate([head[part] for head in queries], axis=0)
            key = keys[part, :, lanes].reshape(SLOTS * cache, HEAD_DIM)
            scores_of[pair, run] = lax.dot_general(
                query.astype(jnp.bfloat16),
                key,
                (((1,), (1,)), ((), ())),
                preferred_element_type=jnp.float32,
            )
    for pair in range(pairs):
        for run, part in enumerate(runs):
            scores = (scores_of[pair, run] * factor).reshape(GROUP, SLOTS, SLOTS * cache)
            scores = jnp.where(filled[run][None], scores, -1e30)
            own_score = jnp.concatenate([head[part] for head in own[pair]], axis=0).reshape(
                GROUP, SLOTS, 1
            )
            highest = jnp.maximum(jnp.max(scores, axis=2, keepdims=True), own_score)
            weights = jnp.exp(scores - highest)
            own_weight = jnp.exp(own_score - highest)
            inverse = 1.0 / (jnp.sum(weights, axis=2, keepdims=True) + own_weight)
            probs = (weights * inverse).astype(jnp.bfloat16)
            probs_of[pair, run] = probs.reshape(GROUP * SLOTS, SLOTS * cache)
            own_probs.append((own_weight * inverse).astype(jnp.bfloat16).astype(jnp.float32))
    for pair in range(pairs):
        lanes = pl.ds(pl.multiple_of((low ^ pair) * HEAD_DIM, HEAD_DIM), HEAD_DIM)
        results = []
        for run, part in enumerate(runs):
            value = values[part, :, lanes].reshape(SLOTS * cache, HEAD_DIM)
            mixed = jnp.dot(probs_of[pair, run], value, preferred_element_type=jnp.float32)
            own_prob = own_probs[pair * len(runs) + run]
            results.append(
                mixed.reshape(GROUP, SLOTS, HEAD_DIM) + own_prob * new_values[pair][part][None]
            )
        for head in range(GROUP):
            at = pl.multiple_of((low ^ pair) * OUT_WIDTH + head * HEAD_DIM, HEAD_DIM)
            size = len(results) // parts
            for i, out in enumerate(outs):
                joined = jnp.concatenate(
                    [result[head] for result in results[i * size : (i + 1) * size]], axis=0
                )
                out[:, pl.ds(at, HEAD_DIM)] = joined.astype(jnp.bfloat16)
    for copy in copies:
        copy.wait()


def sum_kernel(count, parts, hidden, *refs):
    attended, blocks, (keep, send) = refs[:parts], refs[parts : parts + count], refs[parts + count :]
    rows, width = blocks[0].shape
    pairs = keep.shape[1] // width
    blocks = in_place(blocks, pairs)
    side = lax.axis_index("side")
    low = lax.rem(lax.axis_index("col"), pairs)
    for pair in range(pairs):
        column = low ^ pair
        total = blocks[pair][...].astype(jnp.float32)
        for i in range(pair + pairs, count, pairs):
            total = total + blocks[i][...].astype(jnp.float32)
        at = pl.ds(pl.multiple_of((2 * column + side) * width, width), width)
        hidden_out = (hidden[:, at].astype(jnp.float32) + total).astype(jnp.bfloat16)
        at = pl.ds(pl.multiple_of(column * width, width), width)
        attention = jnp.concatenate([part[:, at] for part in attended], axis=0)
        keep[:, at] = jnp.where(side == 0, hidden_out, attention)
        send[:, at] = jnp.where(side == 0, attention, hidden_out)


def join_kernel(keep, received, out, sems):
    side = lax.axis_index("side")
    width = OUT_WIDTH
    copies = []
    for j in range(keep.shape[1] // width):
        part = slice(j * width, (j + 1) * width)
        for ref, core in ((keep, side), (received, 1 - side)):
            at = pl.ds(pl.multiple_of((2 * j + core) * width, width), width)
            copies.append((ref.at[:, part], out.at[0, :, at]))
    run_copies(copies, sems)


def paired_plan(
    hidden_in, norm_gain, qkv_weight, out_weight, key_cache, value_cache, cache_lengths, slot_request
):
    col_count, row_count = lax.axis_size("col"), lax.axis_size("row")
    pairs = col_count // row_count
    side = lax.axis_index("side")
    rows, depth = hidden_in.shape
    half = depth // 2
    cache = key_cache.shape[1]
    parts = 2
    piece = rows // parts

    own_part = lax.dynamic_slice_in_dim(hidden_in, side * half, half, 1)
    gain = norm_gain.reshape(depth // HEAD_DIM, HEAD_DIM)
    half_in, half_out = qkv_weight.shape[1] // 2, out_weight.shape[1] // 2
    total = rows * col_count
    square = (total, total)
    give_in, own_in, chosen_in = call(
        functools.partial(stage_in_kernel, col_count),
        [pltpu.VMEM((half, half_in), jnp.bfloat16)] * 2 + [struct(square)],
        [HBM, HBM],
        [VMEM] * 3,
        0,
        half * half_in * 4,
        [
            pltpu.VMEM(square, jnp.float32),
            pltpu.VMEM((total,), jnp.int32),
            pltpu.SemaphoreType.DMA((3,)),
        ],
    )(in_hbm(qkv_weight), in_hbm(slot_request))
    blocks = gathered(
        [own_part[i * piece : (i + 1) * piece] for i in range(parts)], "col"
    )
    products = spread(
        project(in_kernel, chosen_in, blocks, [gain], [give_in, own_in], HEAD_DIM, pairs)
    )

    table = struct((rows, HEAD_DIM), jnp.float32)
    key_part, value_part, *tables, chosen_out = call(
        functools.partial(stage_cache_kernel, col_count),
        [pltpu.VMEM((rows, cache, pairs * HEAD_DIM), jnp.bfloat16)] * 2
        + [table, table, struct((rows, HEAD_DIM), jnp.int32), struct(square)],
        [SMEM, HBM, HBM, VMEM],
        [VMEM] * 6,
        0,
        4 * rows * cache * pairs * HEAD_DIM,
        [pltpu.VMEM(square, jnp.float32), pltpu.SemaphoreType.DMA((2 * pairs,))],
    )(cache_lengths, in_hbm(key_cache), in_hbm(value_cache), slot_request)
    runs = (pairs, rows // SLOTS, GROUP * SLOTS, SLOTS * cache)
    *attended, give_out = call(
        functools.partial(attend_all, col_count, parts),
        [struct((piece, half))] * parts + [pltpu.VMEM((half, half_out), jnp.bfloat16)],
        [VMEM] * (col_count + 5) + [HBM],
        [VMEM] * (parts + 1),
        4 * rows * half * cache,
        half * half_out * 2,
        [
            pltpu.VMEM(runs, jnp.float32),
            pltpu.VMEM(runs, jnp.bfloat16),
            pltpu.SemaphoreType.DMA((pairs,)),
        ],
    )(*tables, *products, in_vmem(key_part), in_vmem(value_part), in_hbm(out_weight))

    own_out = call(
        stage_out_kernel,
        pltpu.VMEM((half, half_out), jnp.bfloat16),
        [HBM, HBM],
        VMEM,
        0,
        half * half_out * 2,
        [pltpu.SemaphoreType.DMA((pairs,))],
    )(in_hbm(out_weight), attended[-1])
    products = spread(
        project(
            out_kernel, chosen_out, gathered(attended, "col"), [], [give_out, own_out], 0, pairs
        )
    )
    keep, send = call(
        functools.partial(sum_kernel, col_count, parts),
        [struct((rows, half)), struct((rows, half))],
        [VMEM] * (1 + parts + col_count),
        [VMEM, VMEM],
        rows * depth * 4,
        rows * depth * 8,
    )(hidden_in, *attended, *products)
    return call(
        join_kernel,
        struct((1, rows, depth)),
        [VMEM, VMEM],
        HBM,
        0,
        rows * depth * 4,
        [pltpu.SemaphoreType.DMA((2 * pairs,))],
    )(keep, moved(send, "side", 1))


def per_device(*args):
    hidden_in, _, qkv_weight, out_weight, key_cache = args[:5]
    col_count, row_count = lax.axis_size("col"), lax.axis_size("row")
    fits = (
        lax.axis_size("side") == 2
        and qkv_weight.shape[1] == 2 * GROUP_WIDTH
        and col_count % row_count == 0
        and col_count > row_count
        and col_count & (col_count - 1) == 0
        and hidden_in.shape[0] % 32 == 0
        and key_cache.shape[1] % 16 == 0
        and hidden_in.shape[1] == 2 * OUT_WIDTH * (col_count // row_count)
    )
    return paired_plan(*args) if fits else general_plan(*args)


def solution(mesh):
    placed = (
        P(("groups", "col"), "row"),
        P("row"),
        P("row", "col"),
        P("row", "col"),
        P(("groups", "col"), None, "row"),
        P(("groups", "col"), None, "row"),
        P(("groups", "col")),
        P("groups"),
    )
    return jax.shard_map(
        per_device,
        mesh=mesh,
        in_specs=placed,
        out_specs=P("side", ("groups", "col"), "row"),
        check_vma=False,
    )
```

```python
import functools
import math

import jax
import jax.numpy as jnp
from jax import lax
from jax.experimental import pallas as pl
from jax.experimental.pallas import tpu as pltpu
from jax.sharding import PartitionSpec as P

D = 8192
HEADS = 64
KV_HEADS = 8
HEAD_DIM = 128
QKV = 10240


EPSILON = 1e-05
THETA = 500000.0


def swapped(value, axis, bit):
    mask = 2**bit
    pairs = [(source, source ^ mask) for source in range(lax.axis_size(axis))]
    return lax.ppermute(value, axis, pairs)


def rope_tables(lengths, head_dim):
    half_dim = head_dim // 2
    inv_freq = jnp.exp(
        -jnp.log(jnp.float32(THETA)) * jnp.arange(half_dim, dtype=jnp.float32) / half_dim
    )
    phases = lengths.astype(jnp.float32)[:, None] * inv_freq[None, :]
    return (jnp.cos(phases), jnp.sin(phases))


def rotate(vector, cos_vals, sine_vals):
    half_dim = vector.shape[-1] // 2
    front_half = vector[..., :half_dim]
    back_half = vector[..., half_dim:]
    return jnp.concatenate(
        [
            front_half * cos_vals - back_half * sine_vals,
            back_half * cos_vals + front_half * sine_vals,
        ],
        axis=-1,
    )


def attend(packed, key_block, value_block, lengths):
    slot_count = packed.shape[0]
    cache_size = key_block.shape[1]
    groups = key_block.shape[2] // HEAD_DIM
    per_group = HEADS // KV_HEADS
    grouped = packed.reshape(slot_count, groups, per_group + 2, HEAD_DIM)
    cos_vals, sine_vals = rope_tables(lengths, HEAD_DIM)
    queries = rotate(
        grouped[:, :, :per_group].astype(jnp.float32),
        cos_vals[:, None, None, :],
        sine_vals[:, None, None, :],
    ).astype(jnp.bfloat16)
    new_keys = rotate(
        grouped[:, :, per_group].astype(jnp.float32), cos_vals[:, None, :], sine_vals[:, None, :]
    ).astype(jnp.bfloat16)
    new_values = grouped[:, :, per_group + 1]
    cache_keys = key_block.reshape(slot_count, cache_size, groups, HEAD_DIM)
    cache_values = value_block.reshape(slot_count, cache_size, groups, HEAD_DIM)
    factor = HEAD_DIM ** (-0.5)
    cache_scores = (
        jnp.einsum("sghd,slgd->sghl", queries, cache_keys, preferred_element_type=jnp.float32)
        * factor
    )
    own_scores = (
        jnp.einsum("sghd,sgd->sgh", queries, new_keys, preferred_element_type=jnp.float32) * factor
    )
    in_cache = lax.broadcasted_iota(jnp.int32, (slot_count, cache_size), 1) < lengths[:, None]
    cache_scores = jnp.where(in_cache[:, None, None, :], cache_scores, -1e30)
    row_max = jnp.maximum(jnp.max(cache_scores, axis=-1), own_scores)
    cache_exp = jnp.exp(cache_scores - row_max[..., None])
    own_exp = jnp.exp(own_scores - row_max)
    denominator = jnp.sum(cache_exp, axis=-1) + own_exp
    cache_weight = (cache_exp / denominator[..., None]).astype(jnp.bfloat16)
    own_weight = (own_exp / denominator).astype(jnp.bfloat16)
    combined = jnp.einsum(
        "sghl,slgd->sghd", cache_weight, cache_values, preferred_element_type=jnp.float32
    )
    combined = (
        combined
        + own_weight.astype(jnp.float32)[..., None] * new_values.astype(jnp.float32)[:, :, None, :]
    )
    return combined.astype(jnp.bfloat16).reshape(slot_count, groups * per_group * HEAD_DIM)


def general_plan(
    hidden_in,
    norm_gain,
    qkv_weight,
    out_weight,
    key_cache,
    value_cache,
    cache_lengths,
    slot_request,
):
    side_index = lax.axis_index("side")
    is_weight = side_index == 0
    col_count = lax.axis_size("col")
    row_count = lax.axis_size("row")
    group_cols = col_count // row_count
    in_half = qkv_weight.shape[1] // 2
    out_half = out_weight.shape[1] // 2
    residual = hidden_in.astype(jnp.float32)
    square_sums = lax.psum(jnp.sum(residual * residual, axis=1), "row")
    normed = (
        residual
        * lax.rsqrt(square_sums[:, None] / D + EPSILON)
        * norm_gain.astype(jnp.float32)[None, :]
    ).astype(jnp.bfloat16)
    in_weight = lax.dynamic_slice_in_dim(qkv_weight, side_index * in_half, in_half, 1)
    partial_in = jnp.dot(
        lax.all_gather(normed, "col", axis=0, tiled=True),
        in_weight,
        preferred_element_type=jnp.float32,
    )
    in_slots = jnp.take(partial_in, slot_request, axis=0)
    own_width = QKV // row_count
    summed = lax.psum(in_slots.astype(jnp.bfloat16), "row")
    spread = lax.all_to_all(summed, "col", split_axis=0, concat_axis=1, tiled=True)
    own_columns = lax.dynamic_slice_in_dim(
        spread.reshape(spread.shape[0], col_count, in_half),
        lax.axis_index("row") * group_cols,
        group_cols,
        1,
    )
    slot_half = key_cache.shape[0] // 2
    halves = lax.all_to_all(
        own_columns[:, :, None, :], "side", split_axis=0, concat_axis=2, tiled=True
    )
    arrived = halves.reshape(slot_half, own_width)
    first_slot = side_index * slot_half
    key_part = lax.dynamic_slice_in_dim(key_cache, first_slot, slot_half, 0)
    value_part = lax.dynamic_slice_in_dim(value_cache, first_slot, slot_half, 0)
    length_part = lax.dynamic_slice_in_dim(cache_lengths, first_slot, slot_half, 0)
    attended = attend(arrived, key_part, value_part, length_part)
    out_cols = lax.dynamic_slice_in_dim(out_weight, side_index * out_half, out_half, 1)
    collected = lax.all_gather(attended, ("col", "side"), axis=0, tiled=True)
    out_slots = jnp.dot(collected, out_cols, preferred_element_type=jnp.float32)
    inverse = jnp.argsort(slot_request)
    out_requests = jnp.take(out_slots, inverse, axis=0)
    spread_out = lax.all_to_all(
        out_requests.astype(jnp.bfloat16), "col", split_axis=0, concat_axis=1, tiled=True
    ).astype(out_requests.dtype)
    out_view = spread_out.reshape(spread_out.shape[0], col_count, out_half)
    summed_out = lax.psum_scatter(
        out_view.astype(jnp.bfloat16), "row", scatter_dimension=1, tiled=True
    ).astype(jnp.float32)
    req_rows = hidden_in.shape[0]
    residual_view = residual.reshape(req_rows, group_cols, 2, out_half)
    residual_half = lax.dynamic_index_in_dim(residual_view, side_index, 2, keepdims=False)
    own_hidden = (residual_half + summed_out).astype(jnp.bfloat16)
    payload = jnp.where(is_weight, attended, own_hidden.reshape(attended.shape))
    received = swapped(payload, "side", 0)
    hidden = jnp.stack([own_hidden, received.reshape(own_hidden.shape)], axis=2).reshape(
        req_rows, residual.shape[1]
    )
    attention_rows = jnp.concatenate([received, attended], axis=0)
    result = jnp.where(is_weight, hidden, attention_rows)
    return result[None]


GROUP = HEADS // KV_HEADS
GROUP_WIDTH = (GROUP + 2) * HEAD_DIM
OUT_WIDTH = GROUP * HEAD_DIM
SLOTS = 8
VMEM = pl.BlockSpec(memory_space=pltpu.VMEM)
SMEM = pl.BlockSpec(memory_space=pltpu.SMEM)
HBM = pl.BlockSpec(memory_space=pl.ANY)
MIB = 2**20


def call(kernel, out_shape, in_specs, out_specs, flops, size, scratch=(), limit=16):
    return pl.pallas_call(
        kernel,
        out_shape=out_shape,
        in_specs=in_specs,
        out_specs=out_specs,
        scratch_shapes=list(scratch),
        compiler_params=pltpu.CompilerParams(vmem_limit_bytes=limit * MIB),
        cost_estimate=pl.CostEstimate(flops=flops, bytes_accessed=size, transcendentals=0),
    )


def in_vmem(value):
    return pltpu.with_memory_space_constraint(value, pltpu.VMEM)


def in_hbm(value):
    return pltpu.with_memory_space_constraint(value, pltpu.HBM)


def struct(shape, dtype=jnp.bfloat16):
    return jax.ShapeDtypeStruct(shape, dtype)


def moved(value, axis, mask):
    pairs = [(source, source ^ mask) for source in range(lax.axis_size(axis))]
    return lax.ppermute(value, axis, pairs)


def started(copies, sems):
    copies = [
        pltpu.make_async_copy(source, target, sems.at[i])
        for i, (source, target) in enumerate(copies)
    ]
    for copy in copies:
        copy.start()
    return copies


def run_copies(copies, sems):
    for copy in started(copies, sems):
        copy.wait()


def position():
    col = lax.axis_index("col")
    pairs = lax.axis_size("col") // lax.axis_size("row")
    return lax.axis_index("side"), col, lax.axis_index("row") * pairs + lax.rem(col, pairs)


def rows_copy(weight, target, half):
    depth, width = target.shape
    rows = pl.ds(pl.multiple_of(lax.axis_index("side") * depth, depth), depth)
    columns = pl.ds(pl.multiple_of(half * width, width), width)
    return weight.at[rows, columns], target


def stage_in_kernel(blocks, weight, slots, give_part, own_part, chosen, scratch, slot_part, sems):
    side, col, run = position()
    slots_copy, *copies = started(
        [
            (slots, slot_part),
            rows_copy(weight, give_part, 1 - side),
            rows_copy(weight, own_part, side),
        ],
        sems,
    )
    slots_copy.wait()
    chosen[...] = one_hot(slot_part, scratch, blocks, run, col).astype(jnp.bfloat16)
    for copy in copies:
        copy.wait()


def head_copies(weight, target, half):
    width = target.shape[1]
    columns = pl.ds(pl.multiple_of(half * width, width), width)
    copies = []
    for j in range(target.shape[0] // OUT_WIDTH):
        row = pl.multiple_of((2 * j + lax.axis_index("side")) * OUT_WIDTH, OUT_WIDTH)
        copies.append(
            (
                weight.at[pl.ds(row, OUT_WIDTH), columns],
                target.at[pl.ds(j * OUT_WIDTH, OUT_WIDTH), :],
            )
        )
    return copies


def stage_rest_kernel(blocks, lengths, weight, keys, values, slots, *refs):
    target, key_part, value_part, cosine, sine, length_of, chosen, scratch, sems = refs
    side, col, run = position()
    copies = []
    for j in range(key_part.shape[2] // HEAD_DIM):
        lane = pl.multiple_of((2 * j + side) * HEAD_DIM, HEAD_DIM)
        for cache, part in ((keys, key_part), (values, value_part)):
            copies.append(
                (
                    cache.at[:, :, pl.ds(lane, HEAD_DIM)],
                    part.at[:, :, pl.ds(j * HEAD_DIM, HEAD_DIM)],
                )
            )
    copies = started(copies + head_copies(weight, target, 1 - side), sems)
    cosine[...], sine[...], length_of[...] = rope(lengths, cosine.shape[0])
    chosen[...] = one_hot(slots, scratch, blocks, col, run).T.astype(jnp.bfloat16)
    for copy in copies:
        copy.wait()


def stage_out_kernel(weight, attended, own_part, sems):
    run_copies(head_copies(weight, own_part, lax.axis_index("side")), sems)


def one_hot(slots, scratch, blocks, slot_base, request_base):
    total = slots.shape[0]
    rows = total // blocks
    index = lax.broadcasted_iota(jnp.int32, (total, total), 0)
    request = (lax.div(index, rows) ^ request_base) * rows + lax.rem(index, rows)
    scratch[...] = jnp.where(slots[...].reshape(1, total) == request, 1.0, 0.0).T
    parts = [
        scratch[pl.ds(pl.multiple_of((slot_base ^ i) * rows, rows), rows), :]
        for i in range(blocks)
    ]
    return jnp.concatenate(parts, axis=0)


def pieces(sums):
    high = sums.astype(jnp.bfloat16).astype(jnp.float32)
    middle = (sums - high).astype(jnp.bfloat16).astype(jnp.float32)
    low = sums - high - middle
    lane = lax.broadcasted_iota(jnp.int32, (sums.shape[0], HEAD_DIM), 1)
    parts = jnp.where(lane == 0, high, jnp.where(lane == 1, middle, low))
    return jnp.where(lane < 3, parts, 0.0).astype(jnp.bfloat16)


def dot_columns(rows, weight, out):
    size, width = weight.shape[1], 512
    for start in range(0, size, width):
        part = slice(start, min(start + width, size))
        product = jnp.dot(rows, weight[:, part], preferred_element_type=jnp.float32)
        out[:, part] = product.astype(out.dtype)


def in_kernel(count, chosen, *refs):
    pieces_in, (_, gain, weight, give, permuted) = refs[:count], refs[count:]
    depth = pieces_in[0].shape[1]
    half = weight.shape[1]
    runs = depth // HEAD_DIM
    first = pl.multiple_of(lax.axis_index("side") * runs, runs)
    gains = gain[pl.ds(first, runs), :].astype(jnp.float32)
    values = jnp.concatenate([piece[...].astype(jnp.float32) for piece in pieces_in], axis=0)
    scaled = jnp.concatenate(
        [
            values[:, i * HEAD_DIM : (i + 1) * HEAD_DIM] * gains[i : i + 1, :]
            for i in range(runs)
        ],
        axis=1,
    )
    sums = pieces(jnp.sum(values * values, axis=1, keepdims=True))
    order = jnp.dot(
        chosen[...], scaled.astype(jnp.bfloat16), preferred_element_type=jnp.float32
    ).astype(jnp.bfloat16)
    permuted[...] = order
    own_sums = jnp.dot(chosen[...], sums, preferred_element_type=jnp.float32)
    give[:, half:] = own_sums.astype(jnp.bfloat16)
    dot_columns(order, weight, give)


def out_kernel(count, chosen, *refs):
    pieces_in, (_, weight, give, permuted) = refs[:count], refs[count:]
    values = jnp.concatenate([piece[...] for piece in pieces_in], axis=0)
    order = jnp.dot(chosen[...], values, preferred_element_type=jnp.float32).astype(jnp.bfloat16)
    permuted[...] = order
    dot_columns(order, weight, give)


def carries(entry):
    return entry > 0


def sums_entry(run, pairs):
    return run * pairs + (pairs - 1 if run == 0 else 0)


def arrival_order(count, pairs):
    return sorted(range(count), key=lambda i: (i == 0, i % pairs, -i))


def merge_kernel(own, given, received, *outs):
    rows = outs[0].shape[0]
    half = own.shape[1]
    more = given.shape[1] - half
    for i, out in enumerate(outs):
        part = slice(i * rows, (i + 1) * rows)
        total = own[part, :] + received[part, :half].astype(jnp.float32)
        out[:, :half] = total.astype(jnp.bfloat16)
        if out.shape[1] > half:
            out[:, half:] = jnp.concatenate(
                [given[part, half : half + more // 2], received[part, half : half + more // 2]],
                axis=1,
            )


def own_kernel(permuted, weight, own):
    dot_columns(permuted[...], weight, own)


def project(kernel, chosen, pieces_in, extra, weights, more, pairs):
    count = lax.axis_size("col")
    parts = len(pieces_in)
    rows, depth = pieces_in[0].shape
    rows = rows * parts
    half = weights[0].shape[1]
    flops = 2 * rows * depth * half
    give, permuted = call(
        functools.partial(kernel, parts),
        [struct((rows, half + more)), struct((rows, depth))],
        [VMEM] * (parts + len(extra) + 3),
        [VMEM, VMEM],
        flops,
        depth * half * 2,
    )(chosen, *pieces_in, in_vmem(weights[1]), *extra, in_vmem(weights[0]))
    received = moved(give, "side", 1)
    own = call(
        own_kernel,
        struct((rows, half), jnp.float32),
        [VMEM, VMEM],
        VMEM,
        flops,
        depth * half * 2,
    )(permuted, in_vmem(weights[1]))
    return call(
        merge_kernel,
        [
            struct((rows // count, half + (more if carries(i) else 0))) for i in range(count)
        ],
        [VMEM] * 3,
        [VMEM] * count,
        rows * half,
        rows * half * 8,
    )(own, give, received)


def gathered(parts, axis):
    blocks = {0: parts}
    mask = lax.axis_size(axis) // 2
    while mask:
        blocks |= {
            known | mask: [moved(part, axis, mask) for part in block]
            for known, block in blocks.items()
        }
        mask //= 2
    return [part for i in sorted(blocks) for part in blocks[i]]


def in_place(blocks, pairs):
    return [blocks[arrival_order(len(blocks), pairs).index(i)] for i in range(len(blocks))]


def spread(products):
    col_count, row_count = lax.axis_size("col"), lax.axis_size("row")
    pairs = col_count // row_count
    sent = {
        j: lax.ppermute(
            products[j],
            ("col", "row"),
            [
                (
                    col * row_count + row,
                    ((row * pairs + col % pairs) ^ j) * row_count + col // pairs,
                )
                for col in range(col_count)
                for row in range(row_count)
            ],
        )
        for j in range(col_count)
    }
    return [sent[j] for j in arrival_order(col_count, pairs)]


def rotated(vector, cosine, sine):
    return vector * cosine + pltpu.roll(vector, HEAD_DIM // 2, 1) * sine


def rope(lengths, rows):
    slot = lax.broadcasted_iota(jnp.int32, (rows, HEAD_DIM), 0)
    length_of = jnp.zeros((rows, HEAD_DIM), jnp.int32)
    for i in range(rows):
        length_of = jnp.where(slot == i, lengths[i], length_of)
    lane = lax.broadcasted_iota(jnp.int32, (rows, HEAD_DIM), 1)
    half = HEAD_DIM // 2
    step = lax.rem(lane, half).astype(jnp.float32)
    phases = length_of.astype(jnp.float32) * jnp.exp(-math.log(THETA) * step / half)
    sine = jnp.sin(phases)
    return jnp.cos(phases), jnp.where(lane < half, -sine, sine), length_of


def attend_all(count, parts, cosine, sine, lengths, *refs):
    blocks, (keys, values), refs = refs[:count], refs[count : count + 2], refs[count + 2 :]
    blocks = in_place(blocks, keys.shape[2] // HEAD_DIM)
    outs, (scores_of, probs_of) = refs[:parts], refs[parts:]
    pairs = keys.shape[2] // HEAD_DIM
    rows, cache = keys.shape[:2]
    low = lax.rem(lax.axis_index("col"), pairs)
    width = GROUP_WIDTH
    squares = sum(
        blocks[sums_entry(run, pairs)][:, width:].astype(jnp.float32)
        for run in range(count // pairs)
    )
    scale = lax.rsqrt(jnp.sum(squares, axis=1, keepdims=True) / D + EPSILON)
    factor = HEAD_DIM ** (-0.5)
    cosines, sines, length_of = cosine[...], sine[...], lengths[:, :1]
    lane = lax.broadcasted_iota(jnp.int32, (SLOTS, SLOTS * cache), 1)
    slot = lax.broadcasted_iota(jnp.int32, (SLOTS, SLOTS * cache), 0)
    position = lane - slot * cache
    runs = [slice(start, start + SLOTS) for start in range(0, rows, SLOTS)]
    filled = [(position >= 0) & (position < length_of[part]) for part in runs]
    own, new_values, own_probs = [], [], []
    for pair in range(pairs):
        total = blocks[pair][:, :width].astype(jnp.float32)
        for i in range(pair + pairs, count, pairs):
            total = total + blocks[i][:, :width].astype(jnp.float32)
        total = (total * scale).astype(jnp.bfloat16).astype(jnp.float32)
        heads = [total[:, h * HEAD_DIM : (h + 1) * HEAD_DIM] for h in range(GROUP + 2)]
        queries = [
            rotated(head, cosines, sines).astype(jnp.bfloat16).astype(jnp.float32)
            for head in heads[:GROUP]
        ]
        new_key = rotated(heads[GROUP], cosines, sines).astype(jnp.bfloat16).astype(jnp.float32)
        new_values.append(heads[GROUP + 1])
        own.append([jnp.sum(query * new_key, axis=1, keepdims=True) * factor for query in queries])
        lanes = pl.ds(pl.multiple_of((low ^ pair) * HEAD_DIM, HEAD_DIM), HEAD_DIM)
        for run, part in enumerate(runs):
            query = jnp.concatenate([head[part] for head in queries], axis=0)
            key = keys[part, :, lanes].reshape(SLOTS * cache, HEAD_DIM)
            scores_of[pair, run] = lax.dot_general(
                query.astype(jnp.bfloat16),
                key,
                (((1,), (1,)), ((), ())),
                preferred_element_type=jnp.float32,
            )
    for pair in range(pairs):
        for run, part in enumerate(runs):
            scores = (scores_of[pair, run] * factor).reshape(GROUP, SLOTS, SLOTS * cache)
            scores = jnp.where(filled[run][None], scores, -1e30)
            own_score = jnp.concatenate([head[part] for head in own[pair]], axis=0).reshape(
                GROUP, SLOTS, 1
            )
            highest = jnp.maximum(jnp.max(scores, axis=2, keepdims=True), own_score)
            weights = jnp.exp(scores - highest)
            own_weight = jnp.exp(own_score - highest)
            inverse = 1.0 / (jnp.sum(weights, axis=2, keepdims=True) + own_weight)
            probs = (weights * inverse).astype(jnp.bfloat16)
            probs_of[pair, run] = probs.reshape(GROUP * SLOTS, SLOTS * cache)
            own_probs.append((own_weight * inverse).astype(jnp.bfloat16).astype(jnp.float32))
    for pair in range(pairs):
        lanes = pl.ds(pl.multiple_of((low ^ pair) * HEAD_DIM, HEAD_DIM), HEAD_DIM)
        results = []
        for run, part in enumerate(runs):
            value = values[part, :, lanes].reshape(SLOTS * cache, HEAD_DIM)
            mixed = jnp.dot(probs_of[pair, run], value, preferred_element_type=jnp.float32)
            own_prob = own_probs[pair * len(runs) + run]
            results.append(
                mixed.reshape(GROUP, SLOTS, HEAD_DIM) + own_prob * new_values[pair][part][None]
            )
        for head in range(GROUP):
            at = pl.multiple_of((low ^ pair) * OUT_WIDTH + head * HEAD_DIM, HEAD_DIM)
            size = len(results) // parts
            for i, out in enumerate(outs):
                joined = jnp.concatenate(
                    [result[head] for result in results[i * size : (i + 1) * size]], axis=0
                )
                out[:, pl.ds(at, HEAD_DIM)] = joined.astype(jnp.bfloat16)


def sum_kernel(count, parts, hidden, *refs):
    attended, blocks, (keep, send) = refs[:parts], refs[parts : parts + count], refs[parts + count :]
    rows, width = blocks[0].shape
    pairs = keep.shape[1] // width
    blocks = in_place(blocks, pairs)
    side = lax.axis_index("side")
    low = lax.rem(lax.axis_index("col"), pairs)
    for pair in range(pairs):
        column = low ^ pair
        total = blocks[pair][...].astype(jnp.float32)
        for i in range(pair + pairs, count, pairs):
            total = total + blocks[i][...].astype(jnp.float32)
        at = pl.ds(pl.multiple_of((2 * column + side) * width, width), width)
        hidden_out = (hidden[:, at].astype(jnp.float32) + total).astype(jnp.bfloat16)
        at = pl.ds(pl.multiple_of(column * width, width), width)
        attention = jnp.concatenate([part[:, at] for part in attended], axis=0)
        keep[:, at] = jnp.where(side == 0, hidden_out, attention)
        send[:, at] = jnp.where(side == 0, attention, hidden_out)


def join_kernel(keep, received, out, sems):
    side = lax.axis_index("side")
    width = OUT_WIDTH
    copies = []
    for j in range(keep.shape[1] // width):
        part = slice(j * width, (j + 1) * width)
        for ref, core in ((keep, side), (received, 1 - side)):
            at = pl.ds(pl.multiple_of((2 * j + core) * width, width), width)
            copies.append((ref.at[:, part], out.at[0, :, at]))
    run_copies(copies, sems)


def paired_plan(
    hidden_in, norm_gain, qkv_weight, out_weight, key_cache, value_cache, cache_lengths, slot_request
):
    col_count, row_count = lax.axis_size("col"), lax.axis_size("row")
    pairs = col_count // row_count
    side = lax.axis_index("side")
    rows, depth = hidden_in.shape
    half = depth // 2
    cache = key_cache.shape[1]
    parts = 2
    piece = rows // parts

    own_part = lax.dynamic_slice_in_dim(hidden_in, side * half, half, 1)
    gain = norm_gain.reshape(depth // HEAD_DIM, HEAD_DIM)
    half_in, half_out = qkv_weight.shape[1] // 2, out_weight.shape[1] // 2
    total = rows * col_count
    square = (total, total)
    give_in, own_in, chosen_in = call(
        functools.partial(stage_in_kernel, col_count),
        [pltpu.VMEM((half, half_in), jnp.bfloat16)] * 2 + [struct(square)],
        [HBM, HBM],
        [VMEM] * 3,
        0,
        half * half_in * 4,
        [
            pltpu.VMEM(square, jnp.float32),
            pltpu.VMEM((total,), jnp.int32),
            pltpu.SemaphoreType.DMA((3,)),
        ],
    )(in_hbm(qkv_weight), in_hbm(slot_request))
    blocks = gathered(
        [own_part[i * piece : (i + 1) * piece] for i in range(parts)], "col"
    )
    products = spread(
        project(in_kernel, chosen_in, blocks, [gain], [give_in, own_in], HEAD_DIM, pairs)
    )

    table = struct((rows, HEAD_DIM), jnp.float32)
    give_out, key_part, value_part, *tables, chosen_out = call(
        functools.partial(stage_rest_kernel, col_count),
        [pltpu.VMEM((half, half_out), jnp.bfloat16)]
        + [pltpu.VMEM((rows, cache, pairs * HEAD_DIM), jnp.bfloat16)] * 2
        + [table, table, struct((rows, HEAD_DIM), jnp.int32), struct(square)],
        [SMEM, HBM, HBM, HBM, VMEM],
        [VMEM] * 7,
        0,
        half * half_out * 2 + 4 * rows * cache * pairs * HEAD_DIM,
        [pltpu.VMEM(square, jnp.float32), pltpu.SemaphoreType.DMA((3 * pairs,))],
    )(cache_lengths, in_hbm(out_weight), in_hbm(key_cache), in_hbm(value_cache), slot_request)
    runs = (pairs, rows // SLOTS, GROUP * SLOTS, SLOTS * cache)
    attended = call(
        functools.partial(attend_all, col_count, parts),
        [struct((piece, half))] * parts,
        [VMEM] * (col_count + 5),
        [VMEM] * parts,
        4 * rows * half * cache,
        0,
        [pltpu.VMEM(runs, jnp.float32), pltpu.VMEM(runs, jnp.bfloat16)],
    )(*tables, *products, in_vmem(key_part), in_vmem(value_part))

    own_out = call(
        stage_out_kernel,
        pltpu.VMEM((half, half_out), jnp.bfloat16),
        [HBM, HBM],
        VMEM,
        0,
        half * half_out * 2,
        [pltpu.SemaphoreType.DMA((pairs,))],
    )(in_hbm(out_weight), attended[-1])
    products = spread(
        project(
            out_kernel, chosen_out, gathered(attended, "col"), [], [give_out, own_out], 0, pairs
        )
    )
    keep, send = call(
        functools.partial(sum_kernel, col_count, parts),
        [struct((rows, half)), struct((rows, half))],
        [VMEM] * (1 + parts + col_count),
        [VMEM, VMEM],
        rows * depth * 4,
        rows * depth * 8,
    )(hidden_in, *attended, *products)
    return call(
        join_kernel,
        struct((1, rows, depth)),
        [VMEM, VMEM],
        HBM,
        0,
        rows * depth * 4,
        [pltpu.SemaphoreType.DMA((2 * pairs,))],
    )(keep, moved(send, "side", 1))


def per_device(*args):
    hidden_in, _, qkv_weight, out_weight, key_cache = args[:5]
    col_count, row_count = lax.axis_size("col"), lax.axis_size("row")
    fits = (
        lax.axis_size("side") == 2
        and qkv_weight.shape[1] == 2 * GROUP_WIDTH
        and col_count % row_count == 0
        and col_count > row_count
        and col_count & (col_count - 1) == 0
        and hidden_in.shape[0] % 32 == 0
        and key_cache.shape[1] % 16 == 0
        and hidden_in.shape[1] == 2 * OUT_WIDTH * (col_count // row_count)
    )
    return paired_plan(*args) if fits else general_plan(*args)


def solution(mesh):
    placed = (
        P(("groups", "col"), "row"),
        P("row"),
        P("row", "col"),
        P("row", "col"),
        P(("groups", "col"), None, "row"),
        P(("groups", "col"), None, "row"),
        P(("groups", "col")),
        P("groups"),
    )
    return jax.shard_map(
        per_device,
        mesh=mesh,
        in_specs=placed,
        out_specs=P("side", ("groups", "col"), "row"),
        check_vma=False,
    )
```

```python
import functools
import math

import jax
import jax.numpy as jnp
from jax import lax
from jax.experimental import pallas as pl
from jax.experimental.pallas import tpu as pltpu
from jax.sharding import PartitionSpec as P

D = 8192
HEADS = 64
KV_HEADS = 8
HEAD_DIM = 128
QKV = 10240


EPSILON = 1e-05
THETA = 500000.0


def swapped(value, axis, bit):
    mask = 2**bit
    pairs = [(source, source ^ mask) for source in range(lax.axis_size(axis))]
    return lax.ppermute(value, axis, pairs)


def rope_tables(lengths, head_dim):
    half_dim = head_dim // 2
    inv_freq = jnp.exp(
        -jnp.log(jnp.float32(THETA)) * jnp.arange(half_dim, dtype=jnp.float32) / half_dim
    )
    phases = lengths.astype(jnp.float32)[:, None] * inv_freq[None, :]
    return (jnp.cos(phases), jnp.sin(phases))


def rotate(vector, cos_vals, sine_vals):
    half_dim = vector.shape[-1] // 2
    front_half = vector[..., :half_dim]
    back_half = vector[..., half_dim:]
    return jnp.concatenate(
        [
            front_half * cos_vals - back_half * sine_vals,
            back_half * cos_vals + front_half * sine_vals,
        ],
        axis=-1,
    )


def attend(packed, key_block, value_block, lengths):
    slot_count = packed.shape[0]
    cache_size = key_block.shape[1]
    groups = key_block.shape[2] // HEAD_DIM
    per_group = HEADS // KV_HEADS
    grouped = packed.reshape(slot_count, groups, per_group + 2, HEAD_DIM)
    cos_vals, sine_vals = rope_tables(lengths, HEAD_DIM)
    queries = rotate(
        grouped[:, :, :per_group].astype(jnp.float32),
        cos_vals[:, None, None, :],
        sine_vals[:, None, None, :],
    ).astype(jnp.bfloat16)
    new_keys = rotate(
        grouped[:, :, per_group].astype(jnp.float32), cos_vals[:, None, :], sine_vals[:, None, :]
    ).astype(jnp.bfloat16)
    new_values = grouped[:, :, per_group + 1]
    cache_keys = key_block.reshape(slot_count, cache_size, groups, HEAD_DIM)
    cache_values = value_block.reshape(slot_count, cache_size, groups, HEAD_DIM)
    factor = HEAD_DIM ** (-0.5)
    cache_scores = (
        jnp.einsum("sghd,slgd->sghl", queries, cache_keys, preferred_element_type=jnp.float32)
        * factor
    )
    own_scores = (
        jnp.einsum("sghd,sgd->sgh", queries, new_keys, preferred_element_type=jnp.float32) * factor
    )
    in_cache = lax.broadcasted_iota(jnp.int32, (slot_count, cache_size), 1) < lengths[:, None]
    cache_scores = jnp.where(in_cache[:, None, None, :], cache_scores, -1e30)
    row_max = jnp.maximum(jnp.max(cache_scores, axis=-1), own_scores)
    cache_exp = jnp.exp(cache_scores - row_max[..., None])
    own_exp = jnp.exp(own_scores - row_max)
    denominator = jnp.sum(cache_exp, axis=-1) + own_exp
    cache_weight = (cache_exp / denominator[..., None]).astype(jnp.bfloat16)
    own_weight = (own_exp / denominator).astype(jnp.bfloat16)
    combined = jnp.einsum(
        "sghl,slgd->sghd", cache_weight, cache_values, preferred_element_type=jnp.float32
    )
    combined = (
        combined
        + own_weight.astype(jnp.float32)[..., None] * new_values.astype(jnp.float32)[:, :, None, :]
    )
    return combined.astype(jnp.bfloat16).reshape(slot_count, groups * per_group * HEAD_DIM)


def general_plan(
    hidden_in,
    norm_gain,
    qkv_weight,
    out_weight,
    key_cache,
    value_cache,
    cache_lengths,
    slot_request,
):
    side_index = lax.axis_index("side")
    is_weight = side_index == 0
    col_count = lax.axis_size("col")
    row_count = lax.axis_size("row")
    group_cols = col_count // row_count
    in_half = qkv_weight.shape[1] // 2
    out_half = out_weight.shape[1] // 2
    residual = hidden_in.astype(jnp.float32)
    square_sums = lax.psum(jnp.sum(residual * residual, axis=1), "row")
    normed = (
        residual
        * lax.rsqrt(square_sums[:, None] / D + EPSILON)
        * norm_gain.astype(jnp.float32)[None, :]
    ).astype(jnp.bfloat16)
    in_weight = lax.dynamic_slice_in_dim(qkv_weight, side_index * in_half, in_half, 1)
    partial_in = jnp.dot(
        lax.all_gather(normed, "col", axis=0, tiled=True),
        in_weight,
        preferred_element_type=jnp.float32,
    )
    in_slots = jnp.take(partial_in, slot_request, axis=0)
    own_width = QKV // row_count
    summed = lax.psum(in_slots.astype(jnp.bfloat16), "row")
    spread = lax.all_to_all(summed, "col", split_axis=0, concat_axis=1, tiled=True)
    own_columns = lax.dynamic_slice_in_dim(
        spread.reshape(spread.shape[0], col_count, in_half),
        lax.axis_index("row") * group_cols,
        group_cols,
        1,
    )
    slot_half = key_cache.shape[0] // 2
    halves = lax.all_to_all(
        own_columns[:, :, None, :], "side", split_axis=0, concat_axis=2, tiled=True
    )
    arrived = halves.reshape(slot_half, own_width)
    first_slot = side_index * slot_half
    key_part = lax.dynamic_slice_in_dim(key_cache, first_slot, slot_half, 0)
    value_part = lax.dynamic_slice_in_dim(value_cache, first_slot, slot_half, 0)
    length_part = lax.dynamic_slice_in_dim(cache_lengths, first_slot, slot_half, 0)
    attended = attend(arrived, key_part, value_part, length_part)
    out_cols = lax.dynamic_slice_in_dim(out_weight, side_index * out_half, out_half, 1)
    collected = lax.all_gather(attended, ("col", "side"), axis=0, tiled=True)
    out_slots = jnp.dot(collected, out_cols, preferred_element_type=jnp.float32)
    inverse = jnp.argsort(slot_request)
    out_requests = jnp.take(out_slots, inverse, axis=0)
    spread_out = lax.all_to_all(
        out_requests.astype(jnp.bfloat16), "col", split_axis=0, concat_axis=1, tiled=True
    ).astype(out_requests.dtype)
    out_view = spread_out.reshape(spread_out.shape[0], col_count, out_half)
    summed_out = lax.psum_scatter(
        out_view.astype(jnp.bfloat16), "row", scatter_dimension=1, tiled=True
    ).astype(jnp.float32)
    req_rows = hidden_in.shape[0]
    residual_view = residual.reshape(req_rows, group_cols, 2, out_half)
    residual_half = lax.dynamic_index_in_dim(residual_view, side_index, 2, keepdims=False)
    own_hidden = (residual_half + summed_out).astype(jnp.bfloat16)
    payload = jnp.where(is_weight, attended, own_hidden.reshape(attended.shape))
    received = swapped(payload, "side", 0)
    hidden = jnp.stack([own_hidden, received.reshape(own_hidden.shape)], axis=2).reshape(
        req_rows, residual.shape[1]
    )
    attention_rows = jnp.concatenate([received, attended], axis=0)
    result = jnp.where(is_weight, hidden, attention_rows)
    return result[None]


GROUP = HEADS // KV_HEADS
GROUP_WIDTH = (GROUP + 2) * HEAD_DIM
OUT_WIDTH = GROUP * HEAD_DIM
SLOTS = 8
VMEM = pl.BlockSpec(memory_space=pltpu.VMEM)
SMEM = pl.BlockSpec(memory_space=pltpu.SMEM)
HBM = pl.BlockSpec(memory_space=pl.ANY)
MIB = 2**20


def call(kernel, out_shape, in_specs, out_specs, flops, size, scratch=(), limit=16):
    return pl.pallas_call(
        kernel,
        out_shape=out_shape,
        in_specs=in_specs,
        out_specs=out_specs,
        scratch_shapes=list(scratch),
        compiler_params=pltpu.CompilerParams(vmem_limit_bytes=limit * MIB),
        cost_estimate=pl.CostEstimate(flops=flops, bytes_accessed=size, transcendentals=0),
    )


def in_vmem(value):
    return pltpu.with_memory_space_constraint(value, pltpu.VMEM)


def in_hbm(value):
    return pltpu.with_memory_space_constraint(value, pltpu.HBM)


def struct(shape, dtype=jnp.bfloat16):
    return jax.ShapeDtypeStruct(shape, dtype)


def moved(value, axis, mask):
    pairs = [(source, source ^ mask) for source in range(lax.axis_size(axis))]
    return lax.ppermute(value, axis, pairs)


def started(copies, sems):
    copies = [
        pltpu.make_async_copy(source, target, sems.at[i])
        for i, (source, target) in enumerate(copies)
    ]
    for copy in copies:
        copy.start()
    return copies


def run_copies(copies, sems):
    for copy in started(copies, sems):
        copy.wait()


def position():
    col = lax.axis_index("col")
    pairs = lax.axis_size("col") // lax.axis_size("row")
    return lax.axis_index("side"), col, lax.axis_index("row") * pairs + lax.rem(col, pairs)


def rows_copy(weight, target, half):
    depth, width = target.shape
    rows = pl.ds(pl.multiple_of(lax.axis_index("side") * depth, depth), depth)
    columns = pl.ds(pl.multiple_of(half * width, width), width)
    return weight.at[rows, columns], target


def stage_in_kernel(blocks, weight, slots, give_part, own_part, chosen, scratch, slot_part, sems):
    side, col, run = position()
    slots_copy, *copies = started(
        [
            (slots, slot_part),
            rows_copy(weight, give_part, 1 - side),
            rows_copy(weight, own_part, side),
        ],
        sems,
    )
    slots_copy.wait()
    chosen[...] = one_hot(slot_part, scratch, blocks, run, col).astype(jnp.bfloat16)
    for copy in copies:
        copy.wait()


def head_copies(weight, target, half):
    width = target.shape[1]
    columns = pl.ds(pl.multiple_of(half * width, width), width)
    copies = []
    for j in range(target.shape[0] // OUT_WIDTH):
        row = pl.multiple_of((2 * j + lax.axis_index("side")) * OUT_WIDTH, OUT_WIDTH)
        copies.append(
            (
                weight.at[pl.ds(row, OUT_WIDTH), columns],
                target.at[pl.ds(j * OUT_WIDTH, OUT_WIDTH), :],
            )
        )
    return copies


def stage_rest_kernel(blocks, lengths, weight, keys, values, slots, *refs):
    target, key_part, value_part, cosine, sine, length_of, chosen, scratch, sems = refs
    side, col, run = position()
    copies = []
    for j in range(key_part.shape[2] // HEAD_DIM):
        lane = pl.multiple_of((2 * j + side) * HEAD_DIM, HEAD_DIM)
        for cache, part in ((keys, key_part), (values, value_part)):
            copies.append(
                (
                    cache.at[:, :, pl.ds(lane, HEAD_DIM)],
                    part.at[:, :, pl.ds(j * HEAD_DIM, HEAD_DIM)],
                )
            )
    copies = started(copies + head_copies(weight, target, 1 - side), sems)
    cosine[...], sine[...], length_of[...] = rope(lengths, cosine.shape[0])
    chosen[...] = one_hot(slots, scratch, blocks, col, run).T.astype(jnp.bfloat16)
    for copy in copies:
        copy.wait()


def stage_out_kernel(weight, attended, own_part, sems):
    run_copies(head_copies(weight, own_part, lax.axis_index("side")), sems)


def one_hot(slots, scratch, blocks, slot_base, request_base):
    total = slots.shape[0]
    rows = total // blocks
    index = lax.broadcasted_iota(jnp.int32, (total, total), 0)
    request = (lax.div(index, rows) ^ request_base) * rows + lax.rem(index, rows)
    scratch[...] = jnp.where(slots[...].reshape(1, total) == request, 1.0, 0.0).T
    parts = [
        scratch[pl.ds(pl.multiple_of((slot_base ^ i) * rows, rows), rows), :]
        for i in range(blocks)
    ]
    return jnp.concatenate(parts, axis=0)


def pieces(sums):
    high = sums.astype(jnp.bfloat16).astype(jnp.float32)
    middle = (sums - high).astype(jnp.bfloat16).astype(jnp.float32)
    low = sums - high - middle
    lane = lax.broadcasted_iota(jnp.int32, (sums.shape[0], HEAD_DIM), 1)
    parts = jnp.where(lane == 0, high, jnp.where(lane == 1, middle, low))
    return jnp.where(lane < 3, parts, 0.0).astype(jnp.bfloat16)


def dot_columns(rows, weight, out):
    size, width = weight.shape[1], 512
    for start in range(0, size, width):
        part = slice(start, min(start + width, size))
        product = jnp.dot(rows, weight[:, part], preferred_element_type=jnp.float32)
        out[:, part] = product.astype(out.dtype)


def in_kernel(count, chosen, *refs):
    pieces_in, (_, gain, weight, give, permuted) = refs[:count], refs[count:]
    depth = pieces_in[0].shape[1]
    half = weight.shape[1]
    runs = depth // HEAD_DIM
    first = pl.multiple_of(lax.axis_index("side") * runs, runs)
    gains = gain[pl.ds(first, runs), :].astype(jnp.float32)
    values = jnp.concatenate([piece[...].astype(jnp.float32) for piece in pieces_in], axis=0)
    scaled = jnp.concatenate(
        [
            values[:, i * HEAD_DIM : (i + 1) * HEAD_DIM] * gains[i : i + 1, :]
            for i in range(runs)
        ],
        axis=1,
    )
    sums = pieces(jnp.sum(values * values, axis=1, keepdims=True))
    order = jnp.dot(
        chosen[...], scaled.astype(jnp.bfloat16), preferred_element_type=jnp.float32
    ).astype(jnp.bfloat16)
    permuted[...] = order
    own_sums = jnp.dot(chosen[...], sums, preferred_element_type=jnp.float32)
    give[:, half:] = own_sums.astype(jnp.bfloat16)
    dot_columns(order, weight, give)


def out_kernel(count, chosen, *refs):
    pieces_in, (_, weight, give, permuted) = refs[:count], refs[count:]
    values = jnp.concatenate([piece[...] for piece in pieces_in], axis=0)
    order = jnp.dot(chosen[...], values, preferred_element_type=jnp.float32).astype(jnp.bfloat16)
    permuted[...] = order
    dot_columns(order, weight, give)


def carries(entry):
    return entry > 0


def sums_entry(run, pairs):
    return run * pairs + (pairs - 1 if run == 0 else 0)


def arrival_order(count, pairs):
    return sorted(range(count), key=lambda i: (i == 0, i % pairs, -i))


def merge_kernel(own, given, received, *outs):
    rows = outs[0].shape[0]
    half = own.shape[1]
    more = given.shape[1] - half
    for i, out in enumerate(outs):
        part = slice(i * rows, (i + 1) * rows)
        total = own[part, :] + received[part, :half].astype(jnp.float32)
        out[:, :half] = total.astype(jnp.bfloat16)
        if out.shape[1] > half:
            out[:, half:] = jnp.concatenate(
                [given[part, half : half + more // 2], received[part, half : half + more // 2]],
                axis=1,
            )


def own_kernel(permuted, weight, own):
    dot_columns(permuted[...], weight, own)


def project(kernel, chosen, pieces_in, extra, weights, more, pairs):
    count = lax.axis_size("col")
    parts = len(pieces_in)
    rows, depth = pieces_in[0].shape
    rows = rows * parts
    half = weights[0].shape[1]
    flops = 2 * rows * depth * half
    give, permuted = call(
        functools.partial(kernel, parts),
        [struct((rows, half + more)), struct((rows, depth))],
        [VMEM] * (parts + len(extra) + 3),
        [VMEM, VMEM],
        flops,
        depth * half * 2,
    )(chosen, *pieces_in, in_vmem(weights[1]), *extra, in_vmem(weights[0]))
    received = moved(give, "side", 1)
    own = call(
        own_kernel,
        struct((rows, half), jnp.float32),
        [VMEM, VMEM],
        VMEM,
        flops,
        depth * half * 2,
    )(permuted, in_vmem(weights[1]))
    return call(
        merge_kernel,
        [
            struct((rows // count, half + (more if carries(i) else 0))) for i in range(count)
        ],
        [VMEM] * 3,
        [VMEM] * count,
        rows * half,
        rows * half * 8,
    )(own, give, received)


def gathered(parts, axis):
    blocks = {0: parts}
    mask = lax.axis_size(axis) // 2
    while mask:
        blocks |= {
            known | mask: [moved(part, axis, mask) for part in block]
            for known, block in blocks.items()
        }
        mask //= 2
    return [part for i in sorted(blocks) for part in blocks[i]]


def in_place(blocks, pairs):
    return [blocks[arrival_order(len(blocks), pairs).index(i)] for i in range(len(blocks))]


def spread(products):
    col_count, row_count = lax.axis_size("col"), lax.axis_size("row")
    pairs = col_count // row_count
    def target(col, row, j):
        if j == 0 and row_count == 2:
            return (col ^ pairs) * row_count + (row ^ 1)
        return ((row * pairs + col % pairs) ^ j) * row_count + col // pairs

    sent = {
        j: lax.ppermute(
            products[j],
            ("col", "row"),
            [
                (col * row_count + row, target(col, row, j))
                for col in range(col_count)
                for row in range(row_count)
            ],
        )
        for j in range(col_count)
    }
    return [sent[j] for j in arrival_order(col_count, pairs)] + [products[0]]


def total_of(blocks, own, pairs, entry, width):
    first = blocks[entry][:, :width]
    if entry == 0:
        keeps = lax.axis_index("row") == lax.div(lax.axis_index("col"), pairs)
        first = jnp.where(keeps, own[...], first)
    total = first.astype(jnp.float32)
    for i in range(entry + pairs, len(blocks), pairs):
        total = total + blocks[i][:, :width].astype(jnp.float32)
    return total


def rotated(vector, cosine, sine):
    return vector * cosine + pltpu.roll(vector, HEAD_DIM // 2, 1) * sine


def rope(lengths, rows):
    slot = lax.broadcasted_iota(jnp.int32, (rows, HEAD_DIM), 0)
    length_of = jnp.zeros((rows, HEAD_DIM), jnp.int32)
    for i in range(rows):
        length_of = jnp.where(slot == i, lengths[i], length_of)
    lane = lax.broadcasted_iota(jnp.int32, (rows, HEAD_DIM), 1)
    half = HEAD_DIM // 2
    step = lax.rem(lane, half).astype(jnp.float32)
    phases = length_of.astype(jnp.float32) * jnp.exp(-math.log(THETA) * step / half)
    sine = jnp.sin(phases)
    return jnp.cos(phases), jnp.where(lane < half, -sine, sine), length_of


def attend_all(count, parts, cosine, sine, lengths, *refs):
    blocks, (own_block, keys, values), refs = refs[:count], refs[count : count + 3], refs[count + 3 :]
    blocks = in_place(blocks, keys.shape[2] // HEAD_DIM)
    outs, (scores_of, probs_of) = refs[:parts], refs[parts:]
    pairs = keys.shape[2] // HEAD_DIM
    rows, cache = keys.shape[:2]
    low = lax.rem(lax.axis_index("col"), pairs)
    width = GROUP_WIDTH
    squares = sum(
        blocks[sums_entry(run, pairs)][:, width:].astype(jnp.float32)
        for run in range(count // pairs)
    )
    scale = lax.rsqrt(jnp.sum(squares, axis=1, keepdims=True) / D + EPSILON)
    factor = HEAD_DIM ** (-0.5)
    cosines, sines, length_of = cosine[...], sine[...], lengths[:, :1]
    lane = lax.broadcasted_iota(jnp.int32, (SLOTS, SLOTS * cache), 1)
    slot = lax.broadcasted_iota(jnp.int32, (SLOTS, SLOTS * cache), 0)
    position = lane - slot * cache
    runs = [slice(start, start + SLOTS) for start in range(0, rows, SLOTS)]
    filled = [(position >= 0) & (position < length_of[part]) for part in runs]
    own, new_values, own_probs = [], [], []
    for pair in range(pairs):
        total = total_of(blocks, own_block, pairs, pair, width)
        total = (total * scale).astype(jnp.bfloat16).astype(jnp.float32)
        heads = [total[:, h * HEAD_DIM : (h + 1) * HEAD_DIM] for h in range(GROUP + 2)]
        queries = [
            rotated(head, cosines, sines).astype(jnp.bfloat16).astype(jnp.float32)
            for head in heads[:GROUP]
        ]
        new_key = rotated(heads[GROUP], cosines, sines).astype(jnp.bfloat16).astype(jnp.float32)
        new_values.append(heads[GROUP + 1])
        own.append([jnp.sum(query * new_key, axis=1, keepdims=True) * factor for query in queries])
        lanes = pl.ds(pl.multiple_of((low ^ pair) * HEAD_DIM, HEAD_DIM), HEAD_DIM)
        for run, part in enumerate(runs):
            query = jnp.concatenate([head[part] for head in queries], axis=0)
            key = keys[part, :, lanes].reshape(SLOTS * cache, HEAD_DIM)
            scores_of[pair, run] = lax.dot_general(
                query.astype(jnp.bfloat16),
                key,
                (((1,), (1,)), ((), ())),
                preferred_element_type=jnp.float32,
            )
    for pair in range(pairs):
        for run, part in enumerate(runs):
            scores = (scores_of[pair, run] * factor).reshape(GROUP, SLOTS, SLOTS * cache)
            scores = jnp.where(filled[run][None], scores, -1e30)
            own_score = jnp.concatenate([head[part] for head in own[pair]], axis=0).reshape(
                GROUP, SLOTS, 1
            )
            highest = jnp.maximum(jnp.max(scores, axis=2, keepdims=True), own_score)
            weights = jnp.exp(scores - highest)
            own_weight = jnp.exp(own_score - highest)
            inverse = 1.0 / (jnp.sum(weights, axis=2, keepdims=True) + own_weight)
            probs = (weights * inverse).astype(jnp.bfloat16)
            probs_of[pair, run] = probs.reshape(GROUP * SLOTS, SLOTS * cache)
            own_probs.append((own_weight * inverse).astype(jnp.bfloat16).astype(jnp.float32))
    for pair in range(pairs):
        lanes = pl.ds(pl.multiple_of((low ^ pair) * HEAD_DIM, HEAD_DIM), HEAD_DIM)
        results = []
        for run, part in enumerate(runs):
            value = values[part, :, lanes].reshape(SLOTS * cache, HEAD_DIM)
            mixed = jnp.dot(probs_of[pair, run], value, preferred_element_type=jnp.float32)
            own_prob = own_probs[pair * len(runs) + run]
            results.append(
                mixed.reshape(GROUP, SLOTS, HEAD_DIM) + own_prob * new_values[pair][part][None]
            )
        for head in range(GROUP):
            at = pl.multiple_of((low ^ pair) * OUT_WIDTH + head * HEAD_DIM, HEAD_DIM)
            size = len(results) // parts
            for i, out in enumerate(outs):
                joined = jnp.concatenate(
                    [result[head] for result in results[i * size : (i + 1) * size]], axis=0
                )
                out[:, pl.ds(at, HEAD_DIM)] = joined.astype(jnp.bfloat16)


def sum_kernel(count, parts, hidden, *refs):
    attended, blocks, (own_block, keep, send) = refs[:parts], refs[parts:-3], refs[-3:]
    rows, width = blocks[0].shape
    pairs = keep.shape[1] // width
    blocks = in_place(blocks, pairs)
    side = lax.axis_index("side")
    low = lax.rem(lax.axis_index("col"), pairs)
    for pair in range(pairs):
        column = low ^ pair
        total = total_of(blocks, own_block, pairs, pair, width)
        at = pl.ds(pl.multiple_of((2 * column + side) * width, width), width)
        hidden_out = (hidden[:, at].astype(jnp.float32) + total).astype(jnp.bfloat16)
        at = pl.ds(pl.multiple_of(column * width, width), width)
        attention = jnp.concatenate([part[:, at] for part in attended], axis=0)
        keep[:, at] = jnp.where(side == 0, hidden_out, attention)
        send[:, at] = jnp.where(side == 0, attention, hidden_out)


def join_kernel(keep, received, out, sems):
    side = lax.axis_index("side")
    width = OUT_WIDTH
    copies = []
    for j in range(keep.shape[1] // width):
        part = slice(j * width, (j + 1) * width)
        for ref, core in ((keep, side), (received, 1 - side)):
            at = pl.ds(pl.multiple_of((2 * j + core) * width, width), width)
            copies.append((ref.at[:, part], out.at[0, :, at]))
    run_copies(copies, sems)


def paired_plan(
    hidden_in, norm_gain, qkv_weight, out_weight, key_cache, value_cache, cache_lengths, slot_request
):
    col_count, row_count = lax.axis_size("col"), lax.axis_size("row")
    pairs = col_count // row_count
    side = lax.axis_index("side")
    rows, depth = hidden_in.shape
    half = depth // 2
    cache = key_cache.shape[1]
    parts = 2
    piece = rows // parts

    own_part = lax.dynamic_slice_in_dim(hidden_in, side * half, half, 1)
    gain = norm_gain.reshape(depth // HEAD_DIM, HEAD_DIM)
    half_in, half_out = qkv_weight.shape[1] // 2, out_weight.shape[1] // 2
    total = rows * col_count
    square = (total, total)
    give_in, own_in, chosen_in = call(
        functools.partial(stage_in_kernel, col_count),
        [pltpu.VMEM((half, half_in), jnp.bfloat16)] * 2 + [struct(square)],
        [HBM, HBM],
        [VMEM] * 3,
        0,
        half * half_in * 4,
        [
            pltpu.VMEM(square, jnp.float32),
            pltpu.VMEM((total,), jnp.int32),
            pltpu.SemaphoreType.DMA((3,)),
        ],
    )(in_hbm(qkv_weight), in_hbm(slot_request))
    blocks = gathered(
        [own_part[i * piece : (i + 1) * piece] for i in range(parts)], "col"
    )
    products = spread(
        project(in_kernel, chosen_in, blocks, [gain], [give_in, own_in], HEAD_DIM, pairs)
    )

    table = struct((rows, HEAD_DIM), jnp.float32)
    give_out, key_part, value_part, *tables, chosen_out = call(
        functools.partial(stage_rest_kernel, col_count),
        [pltpu.VMEM((half, half_out), jnp.bfloat16)]
        + [pltpu.VMEM((rows, cache, pairs * HEAD_DIM), jnp.bfloat16)] * 2
        + [table, table, struct((rows, HEAD_DIM), jnp.int32), struct(square)],
        [SMEM, HBM, HBM, HBM, VMEM],
        [VMEM] * 7,
        0,
        half * half_out * 2 + 4 * rows * cache * pairs * HEAD_DIM,
        [pltpu.VMEM(square, jnp.float32), pltpu.SemaphoreType.DMA((3 * pairs,))],
    )(cache_lengths, in_hbm(out_weight), in_hbm(key_cache), in_hbm(value_cache), slot_request)
    runs = (pairs, rows // SLOTS, GROUP * SLOTS, SLOTS * cache)
    attended = call(
        functools.partial(attend_all, col_count, parts),
        [struct((piece, half))] * parts,
        [VMEM] * (col_count + 6),
        [VMEM] * parts,
        4 * rows * half * cache,
        0,
        [pltpu.VMEM(runs, jnp.float32), pltpu.VMEM(runs, jnp.bfloat16)],
    )(*tables, *products, in_vmem(key_part), in_vmem(value_part))

    own_out = call(
        stage_out_kernel,
        pltpu.VMEM((half, half_out), jnp.bfloat16),
        [HBM, HBM],
        VMEM,
        0,
        half * half_out * 2,
        [pltpu.SemaphoreType.DMA((pairs,))],
    )(in_hbm(out_weight), attended[-1])
    products = spread(
        project(
            out_kernel, chosen_out, gathered(attended, "col"), [], [give_out, own_out], 0, pairs
        )
    )
    keep, send = call(
        functools.partial(sum_kernel, col_count, parts),
        [struct((rows, half)), struct((rows, half))],
        [VMEM] * (2 + parts + col_count),
        [VMEM, VMEM],
        rows * depth * 4,
        rows * depth * 8,
    )(hidden_in, *attended, *products)
    return call(
        join_kernel,
        struct((1, rows, depth)),
        [VMEM, VMEM],
        HBM,
        0,
        rows * depth * 4,
        [pltpu.SemaphoreType.DMA((2 * pairs,))],
    )(keep, moved(send, "side", 1))


def per_device(*args):
    hidden_in, _, qkv_weight, out_weight, key_cache = args[:5]
    col_count, row_count = lax.axis_size("col"), lax.axis_size("row")
    fits = (
        lax.axis_size("side") == 2
        and qkv_weight.shape[1] == 2 * GROUP_WIDTH
        and col_count % row_count == 0
        and col_count > row_count
        and col_count & (col_count - 1) == 0
        and hidden_in.shape[0] % 32 == 0
        and key_cache.shape[1] % 16 == 0
        and hidden_in.shape[1] == 2 * OUT_WIDTH * (col_count // row_count)
    )
    return paired_plan(*args) if fits else general_plan(*args)


def solution(mesh):
    placed = (
        P(("groups", "col"), "row"),
        P("row"),
        P("row", "col"),
        P("row", "col"),
        P(("groups", "col"), None, "row"),
        P(("groups", "col"), None, "row"),
        P(("groups", "col")),
        P("groups"),
    )
    return jax.shard_map(
        per_device,
        mesh=mesh,
        in_specs=placed,
        out_specs=P("side", ("groups", "col"), "row"),
        check_vma=False,
    )
```

```python
import functools
import math

import jax
import jax.numpy as jnp
from jax import lax
from jax.experimental import pallas as pl
from jax.experimental.pallas import tpu as pltpu
from jax.sharding import PartitionSpec as P

D = 8192
HEADS = 64
KV_HEADS = 8
HEAD_DIM = 128
QKV = 10240


EPSILON = 1e-05
THETA = 500000.0


def swapped(value, axis, bit):
    mask = 2**bit
    pairs = [(source, source ^ mask) for source in range(lax.axis_size(axis))]
    return lax.ppermute(value, axis, pairs)


def rope_tables(lengths, head_dim):
    half_dim = head_dim // 2
    inv_freq = jnp.exp(
        -jnp.log(jnp.float32(THETA)) * jnp.arange(half_dim, dtype=jnp.float32) / half_dim
    )
    phases = lengths.astype(jnp.float32)[:, None] * inv_freq[None, :]
    return (jnp.cos(phases), jnp.sin(phases))


def rotate(vector, cos_vals, sine_vals):
    half_dim = vector.shape[-1] // 2
    front_half = vector[..., :half_dim]
    back_half = vector[..., half_dim:]
    return jnp.concatenate(
        [
            front_half * cos_vals - back_half * sine_vals,
            back_half * cos_vals + front_half * sine_vals,
        ],
        axis=-1,
    )


def attend(packed, key_block, value_block, lengths):
    slot_count = packed.shape[0]
    cache_size = key_block.shape[1]
    groups = key_block.shape[2] // HEAD_DIM
    per_group = HEADS // KV_HEADS
    grouped = packed.reshape(slot_count, groups, per_group + 2, HEAD_DIM)
    cos_vals, sine_vals = rope_tables(lengths, HEAD_DIM)
    queries = rotate(
        grouped[:, :, :per_group].astype(jnp.float32),
        cos_vals[:, None, None, :],
        sine_vals[:, None, None, :],
    ).astype(jnp.bfloat16)
    new_keys = rotate(
        grouped[:, :, per_group].astype(jnp.float32), cos_vals[:, None, :], sine_vals[:, None, :]
    ).astype(jnp.bfloat16)
    new_values = grouped[:, :, per_group + 1]
    cache_keys = key_block.reshape(slot_count, cache_size, groups, HEAD_DIM)
    cache_values = value_block.reshape(slot_count, cache_size, groups, HEAD_DIM)
    factor = HEAD_DIM ** (-0.5)
    cache_scores = (
        jnp.einsum("sghd,slgd->sghl", queries, cache_keys, preferred_element_type=jnp.float32)
        * factor
    )
    own_scores = (
        jnp.einsum("sghd,sgd->sgh", queries, new_keys, preferred_element_type=jnp.float32) * factor
    )
    in_cache = lax.broadcasted_iota(jnp.int32, (slot_count, cache_size), 1) < lengths[:, None]
    cache_scores = jnp.where(in_cache[:, None, None, :], cache_scores, -1e30)
    row_max = jnp.maximum(jnp.max(cache_scores, axis=-1), own_scores)
    cache_exp = jnp.exp(cache_scores - row_max[..., None])
    own_exp = jnp.exp(own_scores - row_max)
    denominator = jnp.sum(cache_exp, axis=-1) + own_exp
    cache_weight = (cache_exp / denominator[..., None]).astype(jnp.bfloat16)
    own_weight = (own_exp / denominator).astype(jnp.bfloat16)
    combined = jnp.einsum(
        "sghl,slgd->sghd", cache_weight, cache_values, preferred_element_type=jnp.float32
    )
    combined = (
        combined
        + own_weight.astype(jnp.float32)[..., None] * new_values.astype(jnp.float32)[:, :, None, :]
    )
    return combined.astype(jnp.bfloat16).reshape(slot_count, groups * per_group * HEAD_DIM)


def general_plan(
    hidden_in,
    norm_gain,
    qkv_weight,
    out_weight,
    key_cache,
    value_cache,
    cache_lengths,
    slot_request,
):
    side_index = lax.axis_index("side")
    is_weight = side_index == 0
    col_count = lax.axis_size("col")
    row_count = lax.axis_size("row")
    group_cols = col_count // row_count
    in_half = qkv_weight.shape[1] // 2
    out_half = out_weight.shape[1] // 2
    residual = hidden_in.astype(jnp.float32)
    square_sums = lax.psum(jnp.sum(residual * residual, axis=1), "row")
    normed = (
        residual
        * lax.rsqrt(square_sums[:, None] / D + EPSILON)
        * norm_gain.astype(jnp.float32)[None, :]
    ).astype(jnp.bfloat16)
    in_weight = lax.dynamic_slice_in_dim(qkv_weight, side_index * in_half, in_half, 1)
    partial_in = jnp.dot(
        lax.all_gather(normed, "col", axis=0, tiled=True),
        in_weight,
        preferred_element_type=jnp.float32,
    )
    in_slots = jnp.take(partial_in, slot_request, axis=0)
    own_width = QKV // row_count
    summed = lax.psum(in_slots.astype(jnp.bfloat16), "row")
    spread = lax.all_to_all(summed, "col", split_axis=0, concat_axis=1, tiled=True)
    own_columns = lax.dynamic_slice_in_dim(
        spread.reshape(spread.shape[0], col_count, in_half),
        lax.axis_index("row") * group_cols,
        group_cols,
        1,
    )
    slot_half = key_cache.shape[0] // 2
    halves = lax.all_to_all(
        own_columns[:, :, None, :], "side", split_axis=0, concat_axis=2, tiled=True
    )
    arrived = halves.reshape(slot_half, own_width)
    first_slot = side_index * slot_half
    key_part = lax.dynamic_slice_in_dim(key_cache, first_slot, slot_half, 0)
    value_part = lax.dynamic_slice_in_dim(value_cache, first_slot, slot_half, 0)
    length_part = lax.dynamic_slice_in_dim(cache_lengths, first_slot, slot_half, 0)
    attended = attend(arrived, key_part, value_part, length_part)
    out_cols = lax.dynamic_slice_in_dim(out_weight, side_index * out_half, out_half, 1)
    collected = lax.all_gather(attended, ("col", "side"), axis=0, tiled=True)
    out_slots = jnp.dot(collected, out_cols, preferred_element_type=jnp.float32)
    inverse = jnp.argsort(slot_request)
    out_requests = jnp.take(out_slots, inverse, axis=0)
    spread_out = lax.all_to_all(
        out_requests.astype(jnp.bfloat16), "col", split_axis=0, concat_axis=1, tiled=True
    ).astype(out_requests.dtype)
    out_view = spread_out.reshape(spread_out.shape[0], col_count, out_half)
    summed_out = lax.psum_scatter(
        out_view.astype(jnp.bfloat16), "row", scatter_dimension=1, tiled=True
    ).astype(jnp.float32)
    req_rows = hidden_in.shape[0]
    residual_view = residual.reshape(req_rows, group_cols, 2, out_half)
    residual_half = lax.dynamic_index_in_dim(residual_view, side_index, 2, keepdims=False)
    own_hidden = (residual_half + summed_out).astype(jnp.bfloat16)
    payload = jnp.where(is_weight, attended, own_hidden.reshape(attended.shape))
    received = swapped(payload, "side", 0)
    hidden = jnp.stack([own_hidden, received.reshape(own_hidden.shape)], axis=2).reshape(
        req_rows, residual.shape[1]
    )
    attention_rows = jnp.concatenate([received, attended], axis=0)
    result = jnp.where(is_weight, hidden, attention_rows)
    return result[None]


GROUP = HEADS // KV_HEADS
GROUP_WIDTH = (GROUP + 2) * HEAD_DIM
OUT_WIDTH = GROUP * HEAD_DIM
SLOTS = 8
VMEM = pl.BlockSpec(memory_space=pltpu.VMEM)
SMEM = pl.BlockSpec(memory_space=pltpu.SMEM)
HBM = pl.BlockSpec(memory_space=pl.ANY)
MIB = 2**20


def call(kernel, out_shape, in_specs, out_specs, flops, size, scratch=(), limit=16):
    return pl.pallas_call(
        kernel,
        out_shape=out_shape,
        in_specs=in_specs,
        out_specs=out_specs,
        scratch_shapes=list(scratch),
        compiler_params=pltpu.CompilerParams(vmem_limit_bytes=limit * MIB),
        cost_estimate=pl.CostEstimate(flops=flops, bytes_accessed=size, transcendentals=0),
    )


def in_vmem(value):
    return pltpu.with_memory_space_constraint(value, pltpu.VMEM)


def in_hbm(value):
    return pltpu.with_memory_space_constraint(value, pltpu.HBM)


def struct(shape, dtype=jnp.bfloat16):
    return jax.ShapeDtypeStruct(shape, dtype)


def moved(value, axis, mask):
    pairs = [(source, source ^ mask) for source in range(lax.axis_size(axis))]
    return lax.ppermute(value, axis, pairs)


def started(copies, sems):
    copies = [
        pltpu.make_async_copy(source, target, sems.at[i])
        for i, (source, target) in enumerate(copies)
    ]
    for copy in copies:
        copy.start()
    return copies


def run_copies(copies, sems):
    for copy in started(copies, sems):
        copy.wait()


def position():
    col = lax.axis_index("col")
    pairs = lax.axis_size("col") // lax.axis_size("row")
    return lax.axis_index("side"), col, lax.axis_index("row") * pairs + lax.rem(col, pairs)


def rows_copy(weight, target, half):
    depth, width = target.shape
    rows = pl.ds(pl.multiple_of(lax.axis_index("side") * depth, depth), depth)
    columns = pl.ds(pl.multiple_of(half * width, width), width)
    return weight.at[rows, columns], target


def stage_in_kernel(blocks, weight, slots, give_part, own_part, chosen, scratch, slot_part, sems):
    side, col, run = position()
    slots_copy, *copies = started(
        [
            (slots, slot_part),
            rows_copy(weight, give_part, 1 - side),
            rows_copy(weight, own_part, side),
        ],
        sems,
    )
    slots_copy.wait()
    chosen[...] = one_hot(slot_part, scratch, blocks, run, col).astype(jnp.bfloat16)
    for copy in copies:
        copy.wait()


def head_copies(weight, target, half):
    width = target.shape[1]
    columns = pl.ds(pl.multiple_of(half * width, width), width)
    copies = []
    for j in range(target.shape[0] // OUT_WIDTH):
        row = pl.multiple_of((2 * j + lax.axis_index("side")) * OUT_WIDTH, OUT_WIDTH)
        copies.append(
            (
                weight.at[pl.ds(row, OUT_WIDTH), columns],
                target.at[pl.ds(j * OUT_WIDTH, OUT_WIDTH), :],
            )
        )
    return copies


def stage_rest_kernel(blocks, lengths, weight, keys, values, slots, *refs):
    target, key_part, value_part, cosine, sine, length_of, chosen, scratch, sems = refs
    side, col, run = position()
    copies = []
    for j in range(key_part.shape[2] // HEAD_DIM):
        lane = pl.multiple_of((2 * j + side) * HEAD_DIM, HEAD_DIM)
        for cache, part in ((keys, key_part), (values, value_part)):
            copies.append(
                (
                    cache.at[:, :, pl.ds(lane, HEAD_DIM)],
                    part.at[:, :, pl.ds(j * HEAD_DIM, HEAD_DIM)],
                )
            )
    copies = started(copies + head_copies(weight, target, 1 - side), sems)
    cosine[...], sine[...], length_of[...] = rope(lengths, cosine.shape[0])
    chosen[...] = one_hot(slots, scratch, blocks, col, run).T.astype(jnp.bfloat16)
    for copy in copies:
        copy.wait()


def stage_out_kernel(weight, attended, own_part, sems):
    run_copies(head_copies(weight, own_part, lax.axis_index("side")), sems)


def one_hot(slots, scratch, blocks, slot_base, request_base):
    total = slots.shape[0]
    rows = total // blocks
    index = lax.broadcasted_iota(jnp.int32, (total, total), 0)
    request = (lax.div(index, rows) ^ request_base) * rows + lax.rem(index, rows)
    scratch[...] = jnp.where(slots[...].reshape(1, total) == request, 1.0, 0.0).T
    parts = [
        scratch[pl.ds(pl.multiple_of((slot_base ^ i) * rows, rows), rows), :]
        for i in range(blocks)
    ]
    return jnp.concatenate(parts, axis=0)


def pieces(sums):
    high = sums.astype(jnp.bfloat16).astype(jnp.float32)
    middle = (sums - high).astype(jnp.bfloat16).astype(jnp.float32)
    low = sums - high - middle
    lane = lax.broadcasted_iota(jnp.int32, (sums.shape[0], HEAD_DIM), 1)
    parts = jnp.where(lane == 0, high, jnp.where(lane == 1, middle, low))
    return jnp.where(lane < 3, parts, 0.0).astype(jnp.bfloat16)


def dot_columns(rows, weight, out):
    size, width = weight.shape[1], 512
    for start in range(0, size, width):
        part = slice(start, min(start + width, size))
        product = jnp.dot(rows, weight[:, part], preferred_element_type=jnp.float32)
        out[:, part] = product.astype(out.dtype)


def in_kernel(count, chosen, *refs):
    pieces_in, (_, gain, weight, give, permuted) = refs[:count], refs[count:]
    depth = pieces_in[0].shape[1]
    half = weight.shape[1]
    runs = depth // HEAD_DIM
    first = pl.multiple_of(lax.axis_index("side") * runs, runs)
    gains = gain[pl.ds(first, runs), :].astype(jnp.float32)
    values = jnp.concatenate([piece[...].astype(jnp.float32) for piece in pieces_in], axis=0)
    scaled = jnp.concatenate(
        [
            values[:, i * HEAD_DIM : (i + 1) * HEAD_DIM] * gains[i : i + 1, :]
            for i in range(runs)
        ],
        axis=1,
    )
    sums = pieces(jnp.sum(values * values, axis=1, keepdims=True))
    order = jnp.dot(
        chosen[...], scaled.astype(jnp.bfloat16), preferred_element_type=jnp.float32
    ).astype(jnp.bfloat16)
    permuted[...] = order
    own_sums = jnp.dot(chosen[...], sums, preferred_element_type=jnp.float32)
    give[:, half:] = own_sums.astype(jnp.bfloat16)
    dot_columns(order, weight, give)


def out_kernel(count, chosen, *refs):
    pieces_in, (_, weight, give, permuted) = refs[:count], refs[count:]
    values = jnp.concatenate([piece[...] for piece in pieces_in], axis=0)
    order = jnp.dot(chosen[...], values, preferred_element_type=jnp.float32).astype(jnp.bfloat16)
    permuted[...] = order
    dot_columns(order, weight, give)


def carries(entry):
    return entry > 0


def sums_entry(run, pairs):
    return run * pairs + (pairs - 1 if run == 0 else 0)


def arrival_order(count, pairs):
    return sorted(range(count), key=lambda i: (i == 0, i % pairs, -i))


def merge_kernel(own, given, received, *outs):
    rows = outs[0].shape[0]
    half = own.shape[1]
    more = given.shape[1] - half
    for i, out in enumerate(outs):
        part = slice(i * rows, (i + 1) * rows)
        total = own[part, :] + received[part, :half].astype(jnp.float32)
        out[:, :half] = total.astype(jnp.bfloat16)
        if out.shape[1] > half:
            out[:, half:] = jnp.concatenate(
                [given[part, half : half + more // 2], received[part, half : half + more // 2]],
                axis=1,
            )


def own_kernel(permuted, weight, own):
    dot_columns(permuted[...], weight, own)


def project(kernel, chosen, pieces_in, extra, weights, more, pairs):
    count = lax.axis_size("col")
    parts = len(pieces_in)
    rows, depth = pieces_in[0].shape
    rows = rows * parts
    half = weights[0].shape[1]
    flops = 2 * rows * depth * half
    give, permuted = call(
        functools.partial(kernel, parts),
        [struct((rows, half + more)), struct((rows, depth))],
        [VMEM] * (parts + len(extra) + 3),
        [VMEM, VMEM],
        flops,
        depth * half * 2,
    )(chosen, *pieces_in, in_vmem(weights[1]), *extra, in_vmem(weights[0]))
    received = moved(give, "side", 1)
    own = call(
        own_kernel,
        struct((rows, half), jnp.float32),
        [VMEM, VMEM],
        VMEM,
        flops,
        depth * half * 2,
    )(permuted, in_vmem(weights[1]))
    return call(
        merge_kernel,
        [
            struct((rows // count, half + (more if carries(i) else 0))) for i in range(count)
        ],
        [VMEM] * 3,
        [VMEM] * count,
        rows * half,
        rows * half * 8,
    )(own, give, received)


def gathered(parts, axis):
    blocks = {0: parts}
    mask = lax.axis_size(axis) // 2
    while mask:
        blocks |= {
            known | mask: [moved(part, axis, mask) for part in block]
            for known, block in blocks.items()
        }
        mask //= 2
    return [part for i in sorted(blocks) for part in blocks[i]]


def in_place(blocks, pairs):
    return [blocks[arrival_order(len(blocks), pairs).index(i)] for i in range(len(blocks))]


def spread(products):
    col_count, row_count = lax.axis_size("col"), lax.axis_size("row")
    pairs = col_count // row_count
    groups = lax.axis_size("groups")

    def target(group, col, row, j):
        if j == 0 and col // pairs == row:
            group = (group + 1) % groups
        col, row = (row * pairs + col % pairs) ^ j, col // pairs
        return (group * col_count + col) * row_count + row

    sent = {
        j: lax.ppermute(
            products[j],
            ("groups", "col", "row"),
            [
                ((group * col_count + col) * row_count + row, target(group, col, row, j))
                for group in range(groups)
                for col in range(col_count)
                for row in range(row_count)
            ],
        )
        for j in range(col_count)
    }
    return [sent[j] for j in arrival_order(col_count, pairs)] + [products[0]]


def total_of(blocks, own, pairs, entry, width):
    first = blocks[entry][:, :width]
    if entry == 0:
        keeps = lax.axis_index("row") == lax.div(lax.axis_index("col"), pairs)
        first = jnp.where(keeps, own[...], first)
    total = first.astype(jnp.float32)
    for i in range(entry + pairs, len(blocks), pairs):
        total = total + blocks[i][:, :width].astype(jnp.float32)
    return total


def rotated(vector, cosine, sine):
    return vector * cosine + pltpu.roll(vector, HEAD_DIM // 2, 1) * sine


def rope(lengths, rows):
    slot = lax.broadcasted_iota(jnp.int32, (rows, HEAD_DIM), 0)
    length_of = jnp.zeros((rows, HEAD_DIM), jnp.int32)
    for i in range(rows):
        length_of = jnp.where(slot == i, lengths[i], length_of)
    lane = lax.broadcasted_iota(jnp.int32, (rows, HEAD_DIM), 1)
    half = HEAD_DIM // 2
    step = lax.rem(lane, half).astype(jnp.float32)
    phases = length_of.astype(jnp.float32) * jnp.exp(-math.log(THETA) * step / half)
    sine = jnp.sin(phases)
    return jnp.cos(phases), jnp.where(lane < half, -sine, sine), length_of


def attend_all(count, parts, cosine, sine, lengths, *refs):
    blocks, (own_block, keys, values), refs = refs[:count], refs[count : count + 3], refs[count + 3 :]
    blocks = in_place(blocks, keys.shape[2] // HEAD_DIM)
    outs, (scores_of, probs_of) = refs[:parts], refs[parts:]
    pairs = keys.shape[2] // HEAD_DIM
    rows, cache = keys.shape[:2]
    low = lax.rem(lax.axis_index("col"), pairs)
    width = GROUP_WIDTH
    squares = sum(
        blocks[sums_entry(run, pairs)][:, width:].astype(jnp.float32)
        for run in range(count // pairs)
    )
    scale = lax.rsqrt(jnp.sum(squares, axis=1, keepdims=True) / D + EPSILON)
    factor = HEAD_DIM ** (-0.5)
    cosines, sines, length_of = cosine[...], sine[...], lengths[:, :1]
    lane = lax.broadcasted_iota(jnp.int32, (SLOTS, SLOTS * cache), 1)
    slot = lax.broadcasted_iota(jnp.int32, (SLOTS, SLOTS * cache), 0)
    position = lane - slot * cache
    runs = [slice(start, start + SLOTS) for start in range(0, rows, SLOTS)]
    filled = [(position >= 0) & (position < length_of[part]) for part in runs]
    own, new_values, own_probs = [], [], []
    for pair in range(pairs):
        total = total_of(blocks, own_block, pairs, pair, width)
        total = (total * scale).astype(jnp.bfloat16).astype(jnp.float32)
        heads = [total[:, h * HEAD_DIM : (h + 1) * HEAD_DIM] for h in range(GROUP + 2)]
        queries = [
            rotated(head, cosines, sines).astype(jnp.bfloat16).astype(jnp.float32)
            for head in heads[:GROUP]
        ]
        new_key = rotated(heads[GROUP], cosines, sines).astype(jnp.bfloat16).astype(jnp.float32)
        new_values.append(heads[GROUP + 1])
        own.append([jnp.sum(query * new_key, axis=1, keepdims=True) * factor for query in queries])
        lanes = pl.ds(pl.multiple_of((low ^ pair) * HEAD_DIM, HEAD_DIM), HEAD_DIM)
        for run, part in enumerate(runs):
            query = jnp.concatenate([head[part] for head in queries], axis=0)
            key = keys[part, :, lanes].reshape(SLOTS * cache, HEAD_DIM)
            scores_of[pair, run] = lax.dot_general(
                query.astype(jnp.bfloat16),
                key,
                (((1,), (1,)), ((), ())),
                preferred_element_type=jnp.float32,
            )
    for pair in range(pairs):
        for run, part in enumerate(runs):
            scores = (scores_of[pair, run] * factor).reshape(GROUP, SLOTS, SLOTS * cache)
            scores = jnp.where(filled[run][None], scores, -1e30)
            own_score = jnp.concatenate([head[part] for head in own[pair]], axis=0).reshape(
                GROUP, SLOTS, 1
            )
            highest = jnp.maximum(jnp.max(scores, axis=2, keepdims=True), own_score)
            weights = jnp.exp(scores - highest)
            own_weight = jnp.exp(own_score - highest)
            inverse = 1.0 / (jnp.sum(weights, axis=2, keepdims=True) + own_weight)
            probs = (weights * inverse).astype(jnp.bfloat16)
            probs_of[pair, run] = probs.reshape(GROUP * SLOTS, SLOTS * cache)
            own_probs.append((own_weight * inverse).astype(jnp.bfloat16).astype(jnp.float32))
    for pair in range(pairs):
        lanes = pl.ds(pl.multiple_of((low ^ pair) * HEAD_DIM, HEAD_DIM), HEAD_DIM)
        results = []
        for run, part in enumerate(runs):
            value = values[part, :, lanes].reshape(SLOTS * cache, HEAD_DIM)
            mixed = jnp.dot(probs_of[pair, run], value, preferred_element_type=jnp.float32)
            own_prob = own_probs[pair * len(runs) + run]
            results.append(
                mixed.reshape(GROUP, SLOTS, HEAD_DIM) + own_prob * new_values[pair][part][None]
            )
        for head in range(GROUP):
            at = pl.multiple_of((low ^ pair) * OUT_WIDTH + head * HEAD_DIM, HEAD_DIM)
            size = len(results) // parts
            for i, out in enumerate(outs):
                joined = jnp.concatenate(
                    [result[head] for result in results[i * size : (i + 1) * size]], axis=0
                )
                out[:, pl.ds(at, HEAD_DIM)] = joined.astype(jnp.bfloat16)


def sum_kernel(count, parts, hidden, *refs):
    attended, blocks, (own_block, keep, send) = refs[:parts], refs[parts:-3], refs[-3:]
    rows, width = blocks[0].shape
    pairs = keep.shape[1] // width
    blocks = in_place(blocks, pairs)
    side = lax.axis_index("side")
    low = lax.rem(lax.axis_index("col"), pairs)
    for pair in range(pairs):
        column = low ^ pair
        total = total_of(blocks, own_block, pairs, pair, width)
        at = pl.ds(pl.multiple_of((2 * column + side) * width, width), width)
        hidden_out = (hidden[:, at].astype(jnp.float32) + total).astype(jnp.bfloat16)
        at = pl.ds(pl.multiple_of(column * width, width), width)
        attention = jnp.concatenate([part[:, at] for part in attended], axis=0)
        keep[:, at] = jnp.where(side == 0, hidden_out, attention)
        send[:, at] = jnp.where(side == 0, attention, hidden_out)


def join_kernel(keep, received, out, sems):
    side = lax.axis_index("side")
    width = OUT_WIDTH
    copies = []
    for j in range(keep.shape[1] // width):
        part = slice(j * width, (j + 1) * width)
        for ref, core in ((keep, side), (received, 1 - side)):
            at = pl.ds(pl.multiple_of((2 * j + core) * width, width), width)
            copies.append((ref.at[:, part], out.at[0, :, at]))
    run_copies(copies, sems)


def paired_plan(
    hidden_in, norm_gain, qkv_weight, out_weight, key_cache, value_cache, cache_lengths, slot_request
):
    col_count, row_count = lax.axis_size("col"), lax.axis_size("row")
    pairs = col_count // row_count
    side = lax.axis_index("side")
    rows, depth = hidden_in.shape
    half = depth // 2
    cache = key_cache.shape[1]
    parts = 2
    piece = rows // parts

    own_part = lax.dynamic_slice_in_dim(hidden_in, side * half, half, 1)
    gain = norm_gain.reshape(depth // HEAD_DIM, HEAD_DIM)
    half_in, half_out = qkv_weight.shape[1] // 2, out_weight.shape[1] // 2
    total = rows * col_count
    square = (total, total)
    give_in, own_in, chosen_in = call(
        functools.partial(stage_in_kernel, col_count),
        [pltpu.VMEM((half, half_in), jnp.bfloat16)] * 2 + [struct(square)],
        [HBM, HBM],
        [VMEM] * 3,
        0,
        half * half_in * 4,
        [
            pltpu.VMEM(square, jnp.float32),
            pltpu.VMEM((total,), jnp.int32),
            pltpu.SemaphoreType.DMA((3,)),
        ],
    )(in_hbm(qkv_weight), in_hbm(slot_request))
    blocks = gathered(
        [own_part[i * piece : (i + 1) * piece] for i in range(parts)], "col"
    )
    products = spread(
        project(in_kernel, chosen_in, blocks, [gain], [give_in, own_in], HEAD_DIM, pairs)
    )

    table = struct((rows, HEAD_DIM), jnp.float32)
    give_out, key_part, value_part, *tables, chosen_out = call(
        functools.partial(stage_rest_kernel, col_count),
        [pltpu.VMEM((half, half_out), jnp.bfloat16)]
        + [pltpu.VMEM((rows, cache, pairs * HEAD_DIM), jnp.bfloat16)] * 2
        + [table, table, struct((rows, HEAD_DIM), jnp.int32), struct(square)],
        [SMEM, HBM, HBM, HBM, VMEM],
        [VMEM] * 7,
        0,
        half * half_out * 2 + 4 * rows * cache * pairs * HEAD_DIM,
        [pltpu.VMEM(square, jnp.float32), pltpu.SemaphoreType.DMA((3 * pairs,))],
    )(cache_lengths, in_hbm(out_weight), in_hbm(key_cache), in_hbm(value_cache), slot_request)
    runs = (pairs, rows // SLOTS, GROUP * SLOTS, SLOTS * cache)
    attended = call(
        functools.partial(attend_all, col_count, parts),
        [struct((piece, half))] * parts,
        [VMEM] * (col_count + 6),
        [VMEM] * parts,
        4 * rows * half * cache,
        0,
        [pltpu.VMEM(runs, jnp.float32), pltpu.VMEM(runs, jnp.bfloat16)],
    )(*tables, *products, in_vmem(key_part), in_vmem(value_part))

    own_out = call(
        stage_out_kernel,
        pltpu.VMEM((half, half_out), jnp.bfloat16),
        [HBM, HBM],
        VMEM,
        0,
        half * half_out * 2,
        [pltpu.SemaphoreType.DMA((pairs,))],
    )(in_hbm(out_weight), attended[-1])
    products = spread(
        project(
            out_kernel, chosen_out, gathered(attended, "col"), [], [give_out, own_out], 0, pairs
        )
    )
    keep, send = call(
        functools.partial(sum_kernel, col_count, parts),
        [struct((rows, half)), struct((rows, half))],
        [VMEM] * (2 + parts + col_count),
        [VMEM, VMEM],
        rows * depth * 4,
        rows * depth * 8,
    )(hidden_in, *attended, *products)
    return call(
        join_kernel,
        struct((1, rows, depth)),
        [VMEM, VMEM],
        HBM,
        0,
        rows * depth * 4,
        [pltpu.SemaphoreType.DMA((2 * pairs,))],
    )(keep, moved(send, "side", 1))


def per_device(*args):
    hidden_in, _, qkv_weight, out_weight, key_cache = args[:5]
    col_count, row_count = lax.axis_size("col"), lax.axis_size("row")
    fits = (
        lax.axis_size("side") == 2
        and qkv_weight.shape[1] == 2 * GROUP_WIDTH
        and col_count % row_count == 0
        and col_count > row_count
        and col_count & (col_count - 1) == 0
        and hidden_in.shape[0] % 32 == 0
        and key_cache.shape[1] % 16 == 0
        and hidden_in.shape[1] == 2 * OUT_WIDTH * (col_count // row_count)
    )
    return paired_plan(*args) if fits else general_plan(*args)


def solution(mesh):
    placed = (
        P(("groups", "col"), "row"),
        P("row"),
        P("row", "col"),
        P("row", "col"),
        P(("groups", "col"), None, "row"),
        P(("groups", "col"), None, "row"),
        P(("groups", "col")),
        P("groups"),
    )
    return jax.shard_map(
        per_device,
        mesh=mesh,
        in_specs=placed,
        out_specs=P("side", ("groups", "col"), "row"),
        check_vma=False,
    )
```

```python
import functools
import math

import jax
import jax.numpy as jnp
from jax import lax
from jax.experimental import pallas as pl
from jax.experimental.pallas import tpu as pltpu
from jax.sharding import PartitionSpec as P

D = 8192
HEADS = 64
KV_HEADS = 8
HEAD_DIM = 128
QKV = 10240


EPSILON = 1e-05
THETA = 500000.0


def swapped(value, axis, bit):
    mask = 2**bit
    pairs = [(source, source ^ mask) for source in range(lax.axis_size(axis))]
    return lax.ppermute(value, axis, pairs)


def rope_tables(lengths, head_dim):
    half_dim = head_dim // 2
    inv_freq = jnp.exp(
        -jnp.log(jnp.float32(THETA)) * jnp.arange(half_dim, dtype=jnp.float32) / half_dim
    )
    phases = lengths.astype(jnp.float32)[:, None] * inv_freq[None, :]
    return (jnp.cos(phases), jnp.sin(phases))


def rotate(vector, cos_vals, sine_vals):
    half_dim = vector.shape[-1] // 2
    front_half = vector[..., :half_dim]
    back_half = vector[..., half_dim:]
    return jnp.concatenate(
        [
            front_half * cos_vals - back_half * sine_vals,
            back_half * cos_vals + front_half * sine_vals,
        ],
        axis=-1,
    )


def attend(packed, key_block, value_block, lengths):
    slot_count = packed.shape[0]
    cache_size = key_block.shape[1]
    groups = key_block.shape[2] // HEAD_DIM
    per_group = HEADS // KV_HEADS
    grouped = packed.reshape(slot_count, groups, per_group + 2, HEAD_DIM)
    cos_vals, sine_vals = rope_tables(lengths, HEAD_DIM)
    queries = rotate(
        grouped[:, :, :per_group].astype(jnp.float32),
        cos_vals[:, None, None, :],
        sine_vals[:, None, None, :],
    ).astype(jnp.bfloat16)
    new_keys = rotate(
        grouped[:, :, per_group].astype(jnp.float32), cos_vals[:, None, :], sine_vals[:, None, :]
    ).astype(jnp.bfloat16)
    new_values = grouped[:, :, per_group + 1]
    cache_keys = key_block.reshape(slot_count, cache_size, groups, HEAD_DIM)
    cache_values = value_block.reshape(slot_count, cache_size, groups, HEAD_DIM)
    factor = HEAD_DIM ** (-0.5)
    cache_scores = (
        jnp.einsum("sghd,slgd->sghl", queries, cache_keys, preferred_element_type=jnp.float32)
        * factor
    )
    own_scores = (
        jnp.einsum("sghd,sgd->sgh", queries, new_keys, preferred_element_type=jnp.float32) * factor
    )
    in_cache = lax.broadcasted_iota(jnp.int32, (slot_count, cache_size), 1) < lengths[:, None]
    cache_scores = jnp.where(in_cache[:, None, None, :], cache_scores, -1e30)
    row_max = jnp.maximum(jnp.max(cache_scores, axis=-1), own_scores)
    cache_exp = jnp.exp(cache_scores - row_max[..., None])
    own_exp = jnp.exp(own_scores - row_max)
    denominator = jnp.sum(cache_exp, axis=-1) + own_exp
    cache_weight = (cache_exp / denominator[..., None]).astype(jnp.bfloat16)
    own_weight = (own_exp / denominator).astype(jnp.bfloat16)
    combined = jnp.einsum(
        "sghl,slgd->sghd", cache_weight, cache_values, preferred_element_type=jnp.float32
    )
    combined = (
        combined
        + own_weight.astype(jnp.float32)[..., None] * new_values.astype(jnp.float32)[:, :, None, :]
    )
    return combined.astype(jnp.bfloat16).reshape(slot_count, groups * per_group * HEAD_DIM)


def general_plan(
    hidden_in,
    norm_gain,
    qkv_weight,
    out_weight,
    key_cache,
    value_cache,
    cache_lengths,
    slot_request,
):
    side_index = lax.axis_index("side")
    is_weight = side_index == 0
    col_count = lax.axis_size("col")
    row_count = lax.axis_size("row")
    group_cols = col_count // row_count
    in_half = qkv_weight.shape[1] // 2
    out_half = out_weight.shape[1] // 2
    residual = hidden_in.astype(jnp.float32)
    square_sums = lax.psum(jnp.sum(residual * residual, axis=1), "row")
    normed = (
        residual
        * lax.rsqrt(square_sums[:, None] / D + EPSILON)
        * norm_gain.astype(jnp.float32)[None, :]
    ).astype(jnp.bfloat16)
    in_weight = lax.dynamic_slice_in_dim(qkv_weight, side_index * in_half, in_half, 1)
    partial_in = jnp.dot(
        lax.all_gather(normed, "col", axis=0, tiled=True),
        in_weight,
        preferred_element_type=jnp.float32,
    )
    in_slots = jnp.take(partial_in, slot_request, axis=0)
    own_width = QKV // row_count
    summed = lax.psum(in_slots.astype(jnp.bfloat16), "row")
    spread = lax.all_to_all(summed, "col", split_axis=0, concat_axis=1, tiled=True)
    own_columns = lax.dynamic_slice_in_dim(
        spread.reshape(spread.shape[0], col_count, in_half),
        lax.axis_index("row") * group_cols,
        group_cols,
        1,
    )
    slot_half = key_cache.shape[0] // 2
    halves = lax.all_to_all(
        own_columns[:, :, None, :], "side", split_axis=0, concat_axis=2, tiled=True
    )
    arrived = halves.reshape(slot_half, own_width)
    first_slot = side_index * slot_half
    key_part = lax.dynamic_slice_in_dim(key_cache, first_slot, slot_half, 0)
    value_part = lax.dynamic_slice_in_dim(value_cache, first_slot, slot_half, 0)
    length_part = lax.dynamic_slice_in_dim(cache_lengths, first_slot, slot_half, 0)
    attended = attend(arrived, key_part, value_part, length_part)
    out_cols = lax.dynamic_slice_in_dim(out_weight, side_index * out_half, out_half, 1)
    collected = lax.all_gather(attended, ("col", "side"), axis=0, tiled=True)
    out_slots = jnp.dot(collected, out_cols, preferred_element_type=jnp.float32)
    inverse = jnp.argsort(slot_request)
    out_requests = jnp.take(out_slots, inverse, axis=0)
    spread_out = lax.all_to_all(
        out_requests.astype(jnp.bfloat16), "col", split_axis=0, concat_axis=1, tiled=True
    ).astype(out_requests.dtype)
    out_view = spread_out.reshape(spread_out.shape[0], col_count, out_half)
    summed_out = lax.psum_scatter(
        out_view.astype(jnp.bfloat16), "row", scatter_dimension=1, tiled=True
    ).astype(jnp.float32)
    req_rows = hidden_in.shape[0]
    residual_view = residual.reshape(req_rows, group_cols, 2, out_half)
    residual_half = lax.dynamic_index_in_dim(residual_view, side_index, 2, keepdims=False)
    own_hidden = (residual_half + summed_out).astype(jnp.bfloat16)
    payload = jnp.where(is_weight, attended, own_hidden.reshape(attended.shape))
    received = swapped(payload, "side", 0)
    hidden = jnp.stack([own_hidden, received.reshape(own_hidden.shape)], axis=2).reshape(
        req_rows, residual.shape[1]
    )
    attention_rows = jnp.concatenate([received, attended], axis=0)
    result = jnp.where(is_weight, hidden, attention_rows)
    return result[None]


GROUP = HEADS // KV_HEADS
GROUP_WIDTH = (GROUP + 2) * HEAD_DIM
OUT_WIDTH = GROUP * HEAD_DIM
SLOTS = 8
VMEM = pl.BlockSpec(memory_space=pltpu.VMEM)
SMEM = pl.BlockSpec(memory_space=pltpu.SMEM)
HBM = pl.BlockSpec(memory_space=pl.ANY)
MIB = 2**20


def call(kernel, out_shape, in_specs, out_specs, flops, size, scratch=(), limit=16):
    return pl.pallas_call(
        kernel,
        out_shape=out_shape,
        in_specs=in_specs,
        out_specs=out_specs,
        scratch_shapes=list(scratch),
        compiler_params=pltpu.CompilerParams(vmem_limit_bytes=limit * MIB),
        cost_estimate=pl.CostEstimate(flops=flops, bytes_accessed=size, transcendentals=0),
    )


def in_vmem(value):
    return pltpu.with_memory_space_constraint(value, pltpu.VMEM)


def in_hbm(value):
    return pltpu.with_memory_space_constraint(value, pltpu.HBM)


def struct(shape, dtype=jnp.bfloat16):
    return jax.ShapeDtypeStruct(shape, dtype)


def moved(value, axis, mask):
    pairs = [(source, source ^ mask) for source in range(lax.axis_size(axis))]
    return lax.ppermute(value, axis, pairs)


def started(copies, sems):
    copies = [
        pltpu.make_async_copy(source, target, sems.at[i])
        for i, (source, target) in enumerate(copies)
    ]
    for copy in copies:
        copy.start()
    return copies


def run_copies(copies, sems):
    for copy in started(copies, sems):
        copy.wait()


def position():
    return lax.axis_index("side"), lax.axis_index("col")


def run_base():
    pairs = lax.axis_size("col") // lax.axis_size("row")
    return lax.div(lax.axis_index("col"), pairs) ^ lax.axis_index("row")


def rows_copy(weight, target, half):
    depth, width = target.shape
    rows = pl.ds(pl.multiple_of(lax.axis_index("side") * depth, depth), depth)
    columns = pl.ds(pl.multiple_of(half * width, width), width)
    return weight.at[rows, columns], target


def stage_in_kernel(blocks, weight, slots, give_part, own_part, chosen, scratch, slot_part, sems):
    side, col = position()
    slots_copy, *copies = started(
        [
            (slots, slot_part),
            rows_copy(weight, give_part, 1 - side),
            rows_copy(weight, own_part, side),
        ],
        sems,
    )
    slots_copy.wait()
    chosen[...] = one_hot(slot_part, scratch, blocks, col, col).astype(jnp.bfloat16)
    for copy in copies:
        copy.wait()


def head_copies(weight, target, half):
    width = target.shape[1]
    columns = pl.ds(pl.multiple_of(half * width, width), width)
    copies = []
    for j in range(target.shape[0] // OUT_WIDTH):
        row = pl.multiple_of((2 * j + lax.axis_index("side")) * OUT_WIDTH, OUT_WIDTH)
        copies.append(
            (
                weight.at[pl.ds(row, OUT_WIDTH), columns],
                target.at[pl.ds(j * OUT_WIDTH, OUT_WIDTH), :],
            )
        )
    return copies


def stage_rest_kernel(blocks, lengths, weight, keys, values, slots, *refs):
    target, key_part, value_part, cosine, sine, length_of, chosen, scratch, sems = refs
    side, col = position()
    copies = []
    for j in range(key_part.shape[2] // HEAD_DIM):
        lane = pl.multiple_of((2 * j + side) * HEAD_DIM, HEAD_DIM)
        for cache, part in ((keys, key_part), (values, value_part)):
            copies.append(
                (
                    cache.at[:, :, pl.ds(lane, HEAD_DIM)],
                    part.at[:, :, pl.ds(j * HEAD_DIM, HEAD_DIM)],
                )
            )
    copies = started(copies + head_copies(weight, target, 1 - side), sems)
    cosine[...], sine[...], length_of[...] = rope(lengths, cosine.shape[0])
    chosen[...] = one_hot(slots, scratch, blocks, col, col).T.astype(jnp.bfloat16)
    for copy in copies:
        copy.wait()


def stage_out_kernel(weight, attended, own_part, sems):
    run_copies(head_copies(weight, own_part, lax.axis_index("side")), sems)


def one_hot(slots, scratch, blocks, slot_base, request_base):
    total = slots.shape[0]
    rows = total // blocks
    index = lax.broadcasted_iota(jnp.int32, (total, total), 0)
    request = (lax.div(index, rows) ^ request_base) * rows + lax.rem(index, rows)
    scratch[...] = jnp.where(slots[...].reshape(1, total) == request, 1.0, 0.0).T
    parts = [
        scratch[pl.ds(pl.multiple_of((slot_base ^ i) * rows, rows), rows), :]
        for i in range(blocks)
    ]
    return jnp.concatenate(parts, axis=0)


def pieces(sums):
    high = sums.astype(jnp.bfloat16).astype(jnp.float32)
    middle = (sums - high).astype(jnp.bfloat16).astype(jnp.float32)
    low = sums - high - middle
    lane = lax.broadcasted_iota(jnp.int32, (sums.shape[0], HEAD_DIM), 1)
    parts = jnp.where(lane == 0, high, jnp.where(lane == 1, middle, low))
    return jnp.where(lane < 3, parts, 0.0).astype(jnp.bfloat16)


def dot_columns(rows, weight, out):
    size, width = weight.shape[1], 512
    for start in range(0, size, width):
        part = slice(start, min(start + width, size))
        product = jnp.dot(rows, weight[:, part], preferred_element_type=jnp.float32)
        out[:, part] = product.astype(out.dtype)


def in_kernel(count, chosen, *refs):
    pieces_in, (_, gain, weight, give, permuted) = refs[:count], refs[count:]
    depth = pieces_in[0].shape[1]
    half = weight.shape[1]
    runs = depth // HEAD_DIM
    first = pl.multiple_of(lax.axis_index("side") * runs, runs)
    gains = gain[pl.ds(first, runs), :].astype(jnp.float32)
    values = jnp.concatenate([piece[...].astype(jnp.float32) for piece in pieces_in], axis=0)
    scaled = jnp.concatenate(
        [
            values[:, i * HEAD_DIM : (i + 1) * HEAD_DIM] * gains[i : i + 1, :]
            for i in range(runs)
        ],
        axis=1,
    )
    sums = pieces(jnp.sum(values * values, axis=1, keepdims=True))
    order = jnp.dot(
        chosen[...], scaled.astype(jnp.bfloat16), preferred_element_type=jnp.float32
    ).astype(jnp.bfloat16)
    permuted[...] = order
    own_sums = jnp.dot(chosen[...], sums, preferred_element_type=jnp.float32)
    give[:, half:] = own_sums.astype(jnp.bfloat16)
    dot_columns(order, weight, give)


def out_kernel(count, chosen, *refs):
    pieces_in, (_, weight, give, permuted) = refs[:count], refs[count:]
    values = jnp.concatenate([piece[...] for piece in pieces_in], axis=0)
    order = jnp.dot(chosen[...], values, preferred_element_type=jnp.float32).astype(jnp.bfloat16)
    permuted[...] = order
    dot_columns(order, weight, give)


def merge_kernel(count, own, given, received, *outs):
    rows = outs[0].shape[0]
    half = own.shape[1]
    more = given.shape[1] - half
    for i, out in enumerate(outs[:count]):
        part = slice(i * rows, (i + 1) * rows)
        total = own[part, :] + received[part, :half].astype(jnp.float32)
        out[...] = total.astype(jnp.bfloat16)
    for out in outs[count:]:
        lanes = slice(half, half + more // 2)
        out[...] = jnp.concatenate([given[:rows, lanes], received[:rows, lanes]], axis=1)


def own_kernel(permuted, weight, own):
    dot_columns(permuted[...], weight, own)


def project(kernel, chosen, pieces_in, extra, weights, more):
    count = lax.axis_size("col")
    parts = len(pieces_in)
    rows, depth = pieces_in[0].shape
    rows = rows * parts
    half = weights[0].shape[1]
    flops = 2 * rows * depth * half
    give, permuted = call(
        functools.partial(kernel, parts),
        [struct((rows, half + more)), struct((rows, depth))],
        [VMEM] * (parts + len(extra) + 3),
        [VMEM, VMEM],
        flops,
        depth * half * 2,
    )(chosen, *pieces_in, in_vmem(weights[1]), *extra, in_vmem(weights[0]))
    received = moved(give, "side", 1)
    own = call(
        own_kernel,
        struct((rows, half), jnp.float32),
        [VMEM, VMEM],
        VMEM,
        flops,
        depth * half * 2,
    )(permuted, in_vmem(weights[1]))
    outs = [struct((rows // count, half))] * count
    if more:
        outs = outs + [struct((rows // count, more))]
    merged = call(
        functools.partial(merge_kernel, count),
        outs,
        [VMEM] * 3,
        [VMEM] * len(outs),
        rows * half,
        rows * half * 8,
    )(own, give, received)
    return merged[:count], merged[count:]


def gathered(parts, axis):
    blocks = {0: parts}
    mask = lax.axis_size(axis) // 2
    while mask:
        blocks |= {
            known | mask: [moved(part, axis, mask) for part in block]
            for known, block in blocks.items()
        }
        mask //= 2
    return [part for i in sorted(blocks) for part in blocks[i]]


def choose_kernel(count, other, *refs):
    blocks, sums, out = refs[:count], refs[count:-1], refs[-1]
    width = blocks[0].shape[1]
    wanted = run_base() ^ other
    chosen = blocks[0][...]
    for run, block in enumerate(blocks[1:], 1):
        chosen = jnp.where(wanted == run, block[...], chosen)
    out[:, :width] = chosen
    for ref in sums:
        out[:, width:] = ref[...]


def spread(products, sums):
    col_count, row_count = lax.axis_size("col"), lax.axis_size("row")
    pairs = col_count // row_count
    blocks = {0: products[0]}
    for mask in [*range(pairs, col_count), *range(1, pairs)]:
        blocks[mask] = moved(products[mask], "col", mask)
    arrived = []
    for pair in range(pairs):
        runs = [blocks[run * pairs + pair] for run in range(row_count)]
        beside = sums if pair == 0 else []
        width = sum(part.shape[1] for part in [runs[0], *beside])
        for mask in range(1, row_count):
            chosen = call(
                functools.partial(choose_kernel, row_count, mask),
                struct((runs[0].shape[0], width)),
                [VMEM] * (row_count + len(beside)),
                VMEM,
                0,
                width * runs[0].shape[0] * 4,
            )(*runs, *beside)
            arrived.append(moved(chosen, "row", mask))
    return [blocks[i] for i in range(col_count)] + arrived


def total_of(blocks, arrived, pair):
    others = lax.axis_size("row") - 1
    pairs = len(blocks) // (others + 1)
    rows, width = blocks[0].shape
    base = run_base()
    kept = blocks[pair][...]
    for run in range(1, others + 1):
        kept = jnp.where(base == run, blocks[run * pairs + pair][...], kept)
    total = kept.astype(jnp.float32)
    for ref in arrived[pair * others : (pair + 1) * others]:
        total = total + ref[:, :width].astype(jnp.float32)
    return total


def rotated(vector, cosine, sine):
    return vector * cosine + pltpu.roll(vector, HEAD_DIM // 2, 1) * sine


def rope(lengths, rows):
    slot = lax.broadcasted_iota(jnp.int32, (rows, HEAD_DIM), 0)
    length_of = jnp.zeros((rows, HEAD_DIM), jnp.int32)
    for i in range(rows):
        length_of = jnp.where(slot == i, lengths[i], length_of)
    lane = lax.broadcasted_iota(jnp.int32, (rows, HEAD_DIM), 1)
    half = HEAD_DIM // 2
    step = lax.rem(lane, half).astype(jnp.float32)
    phases = length_of.astype(jnp.float32) * jnp.exp(-math.log(THETA) * step / half)
    sine = jnp.sin(phases)
    return jnp.cos(phases), jnp.where(lane < half, -sine, sine), length_of


def attend_all(count, parts, cosine, sine, lengths, *refs):
    others = lax.axis_size("row") - 1
    pairs = count // (others + 1)
    blocks, refs = refs[:count], refs[count:]
    arrived, refs = refs[: pairs * others], refs[pairs * others :]
    (sums, keys, values), refs = refs[:3], refs[3:]
    outs, (scores_of, probs_of) = refs[:parts], refs[parts:]
    rows, cache = keys.shape[:2]
    low = lax.rem(lax.axis_index("col"), pairs)
    width = GROUP_WIDTH
    squares = sums[...].astype(jnp.float32)
    for ref in arrived[:others]:
        squares = squares + ref[:, width:].astype(jnp.float32)
    scale = lax.rsqrt(jnp.sum(squares, axis=1, keepdims=True) / D + EPSILON)
    factor = HEAD_DIM ** (-0.5)
    cosines, sines, length_of = cosine[...], sine[...], lengths[:, :1]
    lane = lax.broadcasted_iota(jnp.int32, (SLOTS, SLOTS * cache), 1)
    slot = lax.broadcasted_iota(jnp.int32, (SLOTS, SLOTS * cache), 0)
    position = lane - slot * cache
    runs = [slice(start, start + SLOTS) for start in range(0, rows, SLOTS)]
    filled = [(position >= 0) & (position < length_of[part]) for part in runs]
    own, new_values, own_probs = [], [], []
    for pair in range(pairs):
        total = total_of(blocks, arrived, pair)
        total = (total * scale).astype(jnp.bfloat16).astype(jnp.float32)
        heads = [total[:, h * HEAD_DIM : (h + 1) * HEAD_DIM] for h in range(GROUP + 2)]
        queries = [
            rotated(head, cosines, sines).astype(jnp.bfloat16).astype(jnp.float32)
            for head in heads[:GROUP]
        ]
        new_key = rotated(heads[GROUP], cosines, sines).astype(jnp.bfloat16).astype(jnp.float32)
        new_values.append(heads[GROUP + 1])
        own.append([jnp.sum(query * new_key, axis=1, keepdims=True) * factor for query in queries])
        lanes = pl.ds(pl.multiple_of((low ^ pair) * HEAD_DIM, HEAD_DIM), HEAD_DIM)
        for run, part in enumerate(runs):
            query = jnp.concatenate([head[part] for head in queries], axis=0)
            key = keys[part, :, lanes].reshape(SLOTS * cache, HEAD_DIM)
            scores_of[pair, run] = lax.dot_general(
                query.astype(jnp.bfloat16),
                key,
                (((1,), (1,)), ((), ())),
                preferred_element_type=jnp.float32,
            )
    for pair in range(pairs):
        for run, part in enumerate(runs):
            scores = (scores_of[pair, run] * factor).reshape(GROUP, SLOTS, SLOTS * cache)
            scores = jnp.where(filled[run][None], scores, -1e30)
            own_score = jnp.concatenate([head[part] for head in own[pair]], axis=0).reshape(
                GROUP, SLOTS, 1
            )
            highest = jnp.maximum(jnp.max(scores, axis=2, keepdims=True), own_score)
            weights = jnp.exp(scores - highest)
            own_weight = jnp.exp(own_score - highest)
            inverse = 1.0 / (jnp.sum(weights, axis=2, keepdims=True) + own_weight)
            probs = (weights * inverse).astype(jnp.bfloat16)
            probs_of[pair, run] = probs.reshape(GROUP * SLOTS, SLOTS * cache)
            own_probs.append((own_weight * inverse).astype(jnp.bfloat16).astype(jnp.float32))
    for pair in range(pairs):
        lanes = pl.ds(pl.multiple_of((low ^ pair) * HEAD_DIM, HEAD_DIM), HEAD_DIM)
        results = []
        for run, part in enumerate(runs):
            value = values[part, :, lanes].reshape(SLOTS * cache, HEAD_DIM)
            mixed = jnp.dot(probs_of[pair, run], value, preferred_element_type=jnp.float32)
            own_prob = own_probs[pair * len(runs) + run]
            results.append(
                mixed.reshape(GROUP, SLOTS, HEAD_DIM) + own_prob * new_values[pair][part][None]
            )
        for head in range(GROUP):
            at = pl.multiple_of((low ^ pair) * OUT_WIDTH + head * HEAD_DIM, HEAD_DIM)
            size = len(results) // parts
            for i, out in enumerate(outs):
                joined = jnp.concatenate(
                    [result[head] for result in results[i * size : (i + 1) * size]], axis=0
                )
                out[:, pl.ds(at, HEAD_DIM)] = joined.astype(jnp.bfloat16)


def sum_kernel(count, parts, hidden, *refs):
    attended, blocks, arrived = refs[:parts], refs[parts : parts + count], refs[parts + count : -2]
    keep, send = refs[-2:]
    rows, width = blocks[0].shape
    pairs = keep.shape[1] // width
    side = lax.axis_index("side")
    low = lax.rem(lax.axis_index("col"), pairs)
    for pair in range(pairs):
        column = low ^ pair
        total = total_of(blocks, arrived, pair)
        at = pl.ds(pl.multiple_of((2 * column + side) * width, width), width)
        hidden_out = (hidden[:, at].astype(jnp.float32) + total).astype(jnp.bfloat16)
        at = pl.ds(pl.multiple_of(column * width, width), width)
        attention = jnp.concatenate([part[:, at] for part in attended], axis=0)
        keep[:, at] = jnp.where(side == 0, hidden_out, attention)
        send[:, at] = jnp.where(side == 0, attention, hidden_out)


def join_kernel(keep, received, out, sems):
    side = lax.axis_index("side")
    width = OUT_WIDTH
    copies = []
    for j in range(keep.shape[1] // width):
        part = slice(j * width, (j + 1) * width)
        for ref, core in ((keep, side), (received, 1 - side)):
            at = pl.ds(pl.multiple_of((2 * j + core) * width, width), width)
            copies.append((ref.at[:, part], out.at[0, :, at]))
    run_copies(copies, sems)


def paired_plan(
    hidden_in, norm_gain, qkv_weight, out_weight, key_cache, value_cache, cache_lengths, slot_request
):
    col_count, row_count = lax.axis_size("col"), lax.axis_size("row")
    pairs = col_count // row_count
    side = lax.axis_index("side")
    rows, depth = hidden_in.shape
    half = depth // 2
    cache = key_cache.shape[1]
    parts = 2
    piece = rows // parts

    own_part = lax.dynamic_slice_in_dim(hidden_in, side * half, half, 1)
    gain = norm_gain.reshape(depth // HEAD_DIM, HEAD_DIM)
    half_in, half_out = qkv_weight.shape[1] // 2, out_weight.shape[1] // 2
    total = rows * col_count
    square = (total, total)
    give_in, own_in, chosen_in = call(
        functools.partial(stage_in_kernel, col_count),
        [pltpu.VMEM((half, half_in), jnp.bfloat16)] * 2 + [struct(square)],
        [HBM, HBM],
        [VMEM] * 3,
        0,
        half * half_in * 4,
        [
            pltpu.VMEM(square, jnp.float32),
            pltpu.VMEM((total,), jnp.int32),
            pltpu.SemaphoreType.DMA((3,)),
        ],
    )(in_hbm(qkv_weight), in_hbm(slot_request))
    blocks = gathered(
        [own_part[i * piece : (i + 1) * piece] for i in range(parts)], "col"
    )
    products, sums = project(in_kernel, chosen_in, blocks, [gain], [give_in, own_in], HEAD_DIM)
    products = spread(products, sums)

    table = struct((rows, HEAD_DIM), jnp.float32)
    give_out, key_part, value_part, *tables, chosen_out = call(
        functools.partial(stage_rest_kernel, col_count),
        [pltpu.VMEM((half, half_out), jnp.bfloat16)]
        + [pltpu.VMEM((rows, cache, pairs * HEAD_DIM), jnp.bfloat16)] * 2
        + [table, table, struct((rows, HEAD_DIM), jnp.int32), struct(square)],
        [SMEM, HBM, HBM, HBM, VMEM],
        [VMEM] * 7,
        0,
        half * half_out * 2 + 4 * rows * cache * pairs * HEAD_DIM,
        [pltpu.VMEM(square, jnp.float32), pltpu.SemaphoreType.DMA((3 * pairs,))],
    )(cache_lengths, in_hbm(out_weight), in_hbm(key_cache), in_hbm(value_cache), slot_request)
    runs = (pairs, rows // SLOTS, GROUP * SLOTS, SLOTS * cache)
    attended = call(
        functools.partial(attend_all, col_count, parts),
        [struct((piece, half))] * parts,
        [VMEM] * (len(products) + 6),
        [VMEM] * parts,
        4 * rows * half * cache,
        0,
        [pltpu.VMEM(runs, jnp.float32), pltpu.VMEM(runs, jnp.bfloat16)],
    )(*tables, *products, *sums, in_vmem(key_part), in_vmem(value_part))

    own_out = call(
        stage_out_kernel,
        pltpu.VMEM((half, half_out), jnp.bfloat16),
        [HBM, HBM],
        VMEM,
        0,
        half * half_out * 2,
        [pltpu.SemaphoreType.DMA((pairs,))],
    )(in_hbm(out_weight), attended[-1])
    products, _ = project(
        out_kernel, chosen_out, gathered(attended, "col"), [], [give_out, own_out], 0
    )
    products = spread(products, [])
    keep, send = call(
        functools.partial(sum_kernel, col_count, parts),
        [struct((rows, half)), struct((rows, half))],
        [VMEM] * (1 + parts + len(products)),
        [VMEM, VMEM],
        rows * depth * 4,
        rows * depth * 8,
    )(hidden_in, *attended, *products)
    return call(
        join_kernel,
        struct((1, rows, depth)),
        [VMEM, VMEM],
        HBM,
        0,
        rows * depth * 4,
        [pltpu.SemaphoreType.DMA((2 * pairs,))],
    )(keep, moved(send, "side", 1))


def per_device(*args):
    hidden_in, _, qkv_weight, out_weight, key_cache = args[:5]
    col_count, row_count = lax.axis_size("col"), lax.axis_size("row")
    fits = (
        lax.axis_size("side") == 2
        and qkv_weight.shape[1] == 2 * GROUP_WIDTH
        and col_count % row_count == 0
        and col_count > row_count
        and col_count & (col_count - 1) == 0
        and hidden_in.shape[0] % 32 == 0
        and key_cache.shape[1] % 16 == 0
        and hidden_in.shape[1] == 2 * OUT_WIDTH * (col_count // row_count)
    )
    return paired_plan(*args) if fits else general_plan(*args)


def solution(mesh):
    placed = (
        P(("groups", "col"), "row"),
        P("row"),
        P("row", "col"),
        P("row", "col"),
        P(("groups", "col"), None, "row"),
        P(("groups", "col"), None, "row"),
        P(("groups", "col")),
        P("groups"),
    )
    return jax.shard_map(
        per_device,
        mesh=mesh,
        in_specs=placed,
        out_specs=P("side", ("groups", "col"), "row"),
        check_vma=False,
    )
```

```python
import functools
import math

import jax
import jax.numpy as jnp
from jax import lax
from jax.experimental import pallas as pl
from jax.experimental.pallas import tpu as pltpu
from jax.sharding import PartitionSpec as P

D = 8192
HEADS = 64
KV_HEADS = 8
HEAD_DIM = 128
QKV = 10240


EPSILON = 1e-05
THETA = 500000.0


def swapped(value, axis, bit):
    mask = 2**bit
    pairs = [(source, source ^ mask) for source in range(lax.axis_size(axis))]
    return lax.ppermute(value, axis, pairs)


def rope_tables(lengths, head_dim):
    half_dim = head_dim // 2
    inv_freq = jnp.exp(
        -jnp.log(jnp.float32(THETA)) * jnp.arange(half_dim, dtype=jnp.float32) / half_dim
    )
    phases = lengths.astype(jnp.float32)[:, None] * inv_freq[None, :]
    return (jnp.cos(phases), jnp.sin(phases))


def rotate(vector, cos_vals, sine_vals):
    half_dim = vector.shape[-1] // 2
    front_half = vector[..., :half_dim]
    back_half = vector[..., half_dim:]
    return jnp.concatenate(
        [
            front_half * cos_vals - back_half * sine_vals,
            back_half * cos_vals + front_half * sine_vals,
        ],
        axis=-1,
    )


def attend(packed, key_block, value_block, lengths):
    slot_count = packed.shape[0]
    cache_size = key_block.shape[1]
    groups = key_block.shape[2] // HEAD_DIM
    per_group = HEADS // KV_HEADS
    grouped = packed.reshape(slot_count, groups, per_group + 2, HEAD_DIM)
    cos_vals, sine_vals = rope_tables(lengths, HEAD_DIM)
    queries = rotate(
        grouped[:, :, :per_group].astype(jnp.float32),
        cos_vals[:, None, None, :],
        sine_vals[:, None, None, :],
    ).astype(jnp.bfloat16)
    new_keys = rotate(
        grouped[:, :, per_group].astype(jnp.float32), cos_vals[:, None, :], sine_vals[:, None, :]
    ).astype(jnp.bfloat16)
    new_values = grouped[:, :, per_group + 1]
    cache_keys = key_block.reshape(slot_count, cache_size, groups, HEAD_DIM)
    cache_values = value_block.reshape(slot_count, cache_size, groups, HEAD_DIM)
    factor = HEAD_DIM ** (-0.5)
    cache_scores = (
        jnp.einsum("sghd,slgd->sghl", queries, cache_keys, preferred_element_type=jnp.float32)
        * factor
    )
    own_scores = (
        jnp.einsum("sghd,sgd->sgh", queries, new_keys, preferred_element_type=jnp.float32) * factor
    )
    in_cache = lax.broadcasted_iota(jnp.int32, (slot_count, cache_size), 1) < lengths[:, None]
    cache_scores = jnp.where(in_cache[:, None, None, :], cache_scores, -1e30)
    row_max = jnp.maximum(jnp.max(cache_scores, axis=-1), own_scores)
    cache_exp = jnp.exp(cache_scores - row_max[..., None])
    own_exp = jnp.exp(own_scores - row_max)
    denominator = jnp.sum(cache_exp, axis=-1) + own_exp
    cache_weight = (cache_exp / denominator[..., None]).astype(jnp.bfloat16)
    own_weight = (own_exp / denominator).astype(jnp.bfloat16)
    combined = jnp.einsum(
        "sghl,slgd->sghd", cache_weight, cache_values, preferred_element_type=jnp.float32
    )
    combined = (
        combined
        + own_weight.astype(jnp.float32)[..., None] * new_values.astype(jnp.float32)[:, :, None, :]
    )
    return combined.astype(jnp.bfloat16).reshape(slot_count, groups * per_group * HEAD_DIM)


def general_plan(
    hidden_in,
    norm_gain,
    qkv_weight,
    out_weight,
    key_cache,
    value_cache,
    cache_lengths,
    slot_request,
):
    side_index = lax.axis_index("side")
    is_weight = side_index == 0
    col_count = lax.axis_size("col")
    row_count = lax.axis_size("row")
    group_cols = col_count // row_count
    in_half = qkv_weight.shape[1] // 2
    out_half = out_weight.shape[1] // 2
    residual = hidden_in.astype(jnp.float32)
    square_sums = lax.psum(jnp.sum(residual * residual, axis=1), "row")
    normed = (
        residual
        * lax.rsqrt(square_sums[:, None] / D + EPSILON)
        * norm_gain.astype(jnp.float32)[None, :]
    ).astype(jnp.bfloat16)
    in_weight = lax.dynamic_slice_in_dim(qkv_weight, side_index * in_half, in_half, 1)
    partial_in = jnp.dot(
        lax.all_gather(normed, "col", axis=0, tiled=True),
        in_weight,
        preferred_element_type=jnp.float32,
    )
    in_slots = jnp.take(partial_in, slot_request, axis=0)
    own_width = QKV // row_count
    summed = lax.psum(in_slots.astype(jnp.bfloat16), "row")
    spread = lax.all_to_all(summed, "col", split_axis=0, concat_axis=1, tiled=True)
    own_columns = lax.dynamic_slice_in_dim(
        spread.reshape(spread.shape[0], col_count, in_half),
        lax.axis_index("row") * group_cols,
        group_cols,
        1,
    )
    slot_half = key_cache.shape[0] // 2
    halves = lax.all_to_all(
        own_columns[:, :, None, :], "side", split_axis=0, concat_axis=2, tiled=True
    )
    arrived = halves.reshape(slot_half, own_width)
    first_slot = side_index * slot_half
    key_part = lax.dynamic_slice_in_dim(key_cache, first_slot, slot_half, 0)
    value_part = lax.dynamic_slice_in_dim(value_cache, first_slot, slot_half, 0)
    length_part = lax.dynamic_slice_in_dim(cache_lengths, first_slot, slot_half, 0)
    attended = attend(arrived, key_part, value_part, length_part)
    out_cols = lax.dynamic_slice_in_dim(out_weight, side_index * out_half, out_half, 1)
    collected = lax.all_gather(attended, ("col", "side"), axis=0, tiled=True)
    out_slots = jnp.dot(collected, out_cols, preferred_element_type=jnp.float32)
    inverse = jnp.argsort(slot_request)
    out_requests = jnp.take(out_slots, inverse, axis=0)
    spread_out = lax.all_to_all(
        out_requests.astype(jnp.bfloat16), "col", split_axis=0, concat_axis=1, tiled=True
    ).astype(out_requests.dtype)
    out_view = spread_out.reshape(spread_out.shape[0], col_count, out_half)
    summed_out = lax.psum_scatter(
        out_view.astype(jnp.bfloat16), "row", scatter_dimension=1, tiled=True
    ).astype(jnp.float32)
    req_rows = hidden_in.shape[0]
    residual_view = residual.reshape(req_rows, group_cols, 2, out_half)
    residual_half = lax.dynamic_index_in_dim(residual_view, side_index, 2, keepdims=False)
    own_hidden = (residual_half + summed_out).astype(jnp.bfloat16)
    payload = jnp.where(is_weight, attended, own_hidden.reshape(attended.shape))
    received = swapped(payload, "side", 0)
    hidden = jnp.stack([own_hidden, received.reshape(own_hidden.shape)], axis=2).reshape(
        req_rows, residual.shape[1]
    )
    attention_rows = jnp.concatenate([received, attended], axis=0)
    result = jnp.where(is_weight, hidden, attention_rows)
    return result[None]


GROUP = HEADS // KV_HEADS
GROUP_WIDTH = (GROUP + 2) * HEAD_DIM
OUT_WIDTH = GROUP * HEAD_DIM
SLOTS = 8
VMEM = pl.BlockSpec(memory_space=pltpu.VMEM)
SMEM = pl.BlockSpec(memory_space=pltpu.SMEM)
HBM = pl.BlockSpec(memory_space=pl.ANY)
MIB = 2**20


def call(kernel, out_shape, in_specs, out_specs, flops, size, scratch=(), limit=16):
    return pl.pallas_call(
        kernel,
        out_shape=out_shape,
        in_specs=in_specs,
        out_specs=out_specs,
        scratch_shapes=list(scratch),
        compiler_params=pltpu.CompilerParams(vmem_limit_bytes=limit * MIB),
        cost_estimate=pl.CostEstimate(flops=flops, bytes_accessed=size, transcendentals=0),
    )


def in_vmem(value):
    return pltpu.with_memory_space_constraint(value, pltpu.VMEM)


def in_hbm(value):
    return pltpu.with_memory_space_constraint(value, pltpu.HBM)


def struct(shape, dtype=jnp.bfloat16):
    return jax.ShapeDtypeStruct(shape, dtype)


def moved(value, axis, mask):
    pairs = [(source, source ^ mask) for source in range(lax.axis_size(axis))]
    return lax.ppermute(value, axis, pairs)


def started(copies, sems):
    copies = [
        pltpu.make_async_copy(source, target, sems.at[i])
        for i, (source, target) in enumerate(copies)
    ]
    for copy in copies:
        copy.start()
    return copies


def run_copies(copies, sems):
    for copy in started(copies, sems):
        copy.wait()


def position():
    return lax.axis_index("side"), lax.axis_index("col")


def rows_copy(weight, target, half):
    depth, width = target.shape
    rows = pl.ds(pl.multiple_of(lax.axis_index("side") * depth, depth), depth)
    columns = pl.ds(pl.multiple_of(half * width, width), width)
    return weight.at[rows, columns], target


def stage_in_kernel(blocks, weight, slots, give_part, own_part, chosen, scratch, slot_part, sems):
    side, col = position()
    slots_copy, *copies = started(
        [
            (slots, slot_part),
            rows_copy(weight, give_part, 1 - side),
            rows_copy(weight, own_part, side),
        ],
        sems,
    )
    slots_copy.wait()
    chosen[...] = one_hot(slot_part, scratch, blocks, col, col).astype(jnp.bfloat16)
    for copy in copies:
        copy.wait()


def head_copies(weight, target, half):
    width = target.shape[1]
    columns = pl.ds(pl.multiple_of(half * width, width), width)
    copies = []
    for j in range(target.shape[0] // OUT_WIDTH):
        row = pl.multiple_of((2 * j + lax.axis_index("side")) * OUT_WIDTH, OUT_WIDTH)
        copies.append(
            (
                weight.at[pl.ds(row, OUT_WIDTH), columns],
                target.at[pl.ds(j * OUT_WIDTH, OUT_WIDTH), :],
            )
        )
    return copies


def stage_rest_kernel(blocks, lengths, weight, keys, values, slots, *refs):
    target, key_part, value_part, cosine, sine, length_of, chosen, scratch, sems = refs
    side, col = position()
    copies = []
    for j in range(key_part.shape[2] // HEAD_DIM):
        lane = pl.multiple_of((2 * j + side) * HEAD_DIM, HEAD_DIM)
        for cache, part in ((keys, key_part), (values, value_part)):
            copies.append(
                (
                    cache.at[:, :, pl.ds(lane, HEAD_DIM)],
                    part.at[:, :, pl.ds(j * HEAD_DIM, HEAD_DIM)],
                )
            )
    copies = started(copies + head_copies(weight, target, 1 - side), sems)
    cosine[...], sine[...], length_of[...] = rope(lengths, cosine.shape[0])
    chosen[...] = one_hot(slots, scratch, blocks, col, col).T.astype(jnp.bfloat16)
    for copy in copies:
        copy.wait()


def stage_out_kernel(weight, attended, own_part, sems):
    run_copies(head_copies(weight, own_part, lax.axis_index("side")), sems)


def one_hot(slots, scratch, blocks, slot_base, request_base):
    total = slots.shape[0]
    rows = total // blocks
    index = lax.broadcasted_iota(jnp.int32, (total, total), 0)
    request = (lax.div(index, rows) ^ request_base) * rows + lax.rem(index, rows)
    scratch[...] = jnp.where(slots[...].reshape(1, total) == request, 1.0, 0.0).T
    parts = [
        scratch[pl.ds(pl.multiple_of((slot_base ^ i) * rows, rows), rows), :]
        for i in range(blocks)
    ]
    return jnp.concatenate(parts, axis=0)


def pieces(sums):
    high = sums.astype(jnp.bfloat16).astype(jnp.float32)
    middle = (sums - high).astype(jnp.bfloat16).astype(jnp.float32)
    low = sums - high - middle
    lane = lax.broadcasted_iota(jnp.int32, (sums.shape[0], HEAD_DIM), 1)
    parts = jnp.where(lane == 0, high, jnp.where(lane == 1, middle, low))
    return jnp.where(lane < 3, parts, 0.0).astype(jnp.bfloat16)


def dot_columns(rows, weight, out):
    size, width = weight.shape[1], 512
    for start in range(0, size, width):
        part = slice(start, min(start + width, size))
        product = jnp.dot(rows, weight[:, part], preferred_element_type=jnp.float32)
        out[:, part] = product.astype(out.dtype)


def in_kernel(count, chosen, *refs):
    pieces_in, (_, gain, weight, give, permuted) = refs[:count], refs[count:]
    depth = pieces_in[0].shape[1]
    half = weight.shape[1]
    runs = depth // HEAD_DIM
    first = pl.multiple_of(lax.axis_index("side") * runs, runs)
    gains = gain[pl.ds(first, runs), :].astype(jnp.float32)
    values = jnp.concatenate([piece[...].astype(jnp.float32) for piece in pieces_in], axis=0)
    scaled = jnp.concatenate(
        [
            values[:, i * HEAD_DIM : (i + 1) * HEAD_DIM] * gains[i : i + 1, :]
            for i in range(runs)
        ],
        axis=1,
    )
    sums = pieces(jnp.sum(values * values, axis=1, keepdims=True))
    order = jnp.dot(
        chosen[...], scaled.astype(jnp.bfloat16), preferred_element_type=jnp.float32
    ).astype(jnp.bfloat16)
    permuted[...] = order
    own_sums = jnp.dot(chosen[...], sums, preferred_element_type=jnp.float32)
    give[:, half:] = own_sums.astype(jnp.bfloat16)
    dot_columns(order, weight, give)


def out_kernel(count, chosen, *refs):
    pieces_in, (_, weight, give, permuted) = refs[:count], refs[count:]
    values = jnp.concatenate([piece[...] for piece in pieces_in], axis=0)
    order = jnp.dot(chosen[...], values, preferred_element_type=jnp.float32).astype(jnp.bfloat16)
    permuted[...] = order
    dot_columns(order, weight, give)


def at_home():
    pairs = lax.axis_size("col") // lax.axis_size("row")
    return lax.axis_index("row") == lax.div(lax.axis_index("col"), pairs)


def merge_kernel(count, own, given, received, *outs):
    rows = outs[0].shape[0]
    half = own.shape[1]
    more = given.shape[1] - half
    pairs = count // 2

    def write(out, first):
        first = first if isinstance(first, int) else pl.multiple_of(first, rows)
        part = pl.ds(first, rows)
        total = own[part, :] + received[part, :half].astype(jnp.float32)
        out[:, :half] = total.astype(jnp.bfloat16)
        if out.shape[1] > half:
            out[:, half:] = squares(part)

    def squares(part):
        lanes = slice(half, half + more // 2)
        return jnp.concatenate([given[part, lanes], received[part, lanes]], axis=1)

    write(outs[0], 0)
    write(outs[1], pairs * rows)
    home = at_home()
    for pair in range(1, pairs):
        write(outs[2 * pair], jnp.where(home, pairs + pair, pair) * rows)
        write(outs[2 * pair + 1], jnp.where(home, pair, pairs + pair) * rows)
    for out in outs[count:]:
        out[...] = squares(pl.ds(0, rows))


def own_kernel(permuted, weight, own):
    dot_columns(permuted[...], weight, own)


def project(kernel, chosen, pieces_in, extra, weights, more):
    count = lax.axis_size("col")
    parts = len(pieces_in)
    rows, depth = pieces_in[0].shape
    rows = rows * parts
    half = weights[0].shape[1]
    flops = 2 * rows * depth * half
    give, permuted = call(
        functools.partial(kernel, parts),
        [struct((rows, half + more)), struct((rows, depth))],
        [VMEM] * (parts + len(extra) + 3),
        [VMEM, VMEM],
        flops,
        depth * half * 2,
    )(chosen, *pieces_in, in_vmem(weights[1]), *extra, in_vmem(weights[0]))
    received = moved(give, "side", 1)
    own = call(
        own_kernel,
        struct((rows, half), jnp.float32),
        [VMEM, VMEM],
        VMEM,
        flops,
        depth * half * 2,
    )(permuted, in_vmem(weights[1]))
    outs = [struct((rows // count, half + (more if i > 1 else 0))) for i in range(count)]
    if more:
        outs = outs + [struct((rows // count, more))]
    merged = call(
        functools.partial(merge_kernel, count),
        outs,
        [VMEM] * 3,
        [VMEM] * len(outs),
        rows * half,
        rows * half * 8,
    )(own, give, received)
    return merged[:count], merged[count:]


def gathered(parts, axis):
    blocks = {0: parts}
    mask = lax.axis_size(axis) // 2
    while mask:
        blocks |= {
            known | mask: [moved(part, axis, mask) for part in block]
            for known, block in blocks.items()
        }
        mask //= 2
    return [part for i in sorted(blocks) for part in blocks[i]]


def choose_kernel(own, passed, out):
    out[...] = jnp.where(at_home(), passed[...], own[...])


def direct(value, far, pair):
    pairs = lax.axis_size("col") // 2
    moves = []
    for col in range(2 * pairs):
        for row in range(2):
            home = row == col // pairs
            target = col ^ pair ^ (pairs if home == far else 0)
            moves.append((2 * col + row, 2 * target + (row if home else 1 - row)))
    return lax.ppermute(value, ("col", "row"), moves)


def spread(products):
    own, passed, *rest = products
    pairs = len(products) // 2
    passed = moved(passed, "col", pairs)
    blocks = []
    for pair in range(1, pairs):
        blocks += [
            direct(rest[2 * pair - 2], True, pair),
            direct(rest[2 * pair - 1], False, pair),
        ]
    crossing = call(
        choose_kernel, struct(own.shape), [VMEM] * 2, VMEM, 0, own.size * 4
    )(own, passed)
    return [passed, *blocks, own, moved(crossing, "row", 1)]


def total_of(blocks, pair, width):
    if pair > 0:
        first, second = blocks[2 * pair - 1][:, :width], blocks[2 * pair][:, :width]
    else:
        passed, own, crossed = blocks[0], blocks[-2], blocks[-1]
        first, second = jnp.where(at_home(), own[...], passed[...]), crossed[...]
    return first.astype(jnp.float32) + second.astype(jnp.float32)


def rotated(vector, cosine, sine):
    return vector * cosine + pltpu.roll(vector, HEAD_DIM // 2, 1) * sine


def rope(lengths, rows):
    slot = lax.broadcasted_iota(jnp.int32, (rows, HEAD_DIM), 0)
    length_of = jnp.zeros((rows, HEAD_DIM), jnp.int32)
    for i in range(rows):
        length_of = jnp.where(slot == i, lengths[i], length_of)
    lane = lax.broadcasted_iota(jnp.int32, (rows, HEAD_DIM), 1)
    half = HEAD_DIM // 2
    step = lax.rem(lane, half).astype(jnp.float32)
    phases = length_of.astype(jnp.float32) * jnp.exp(-math.log(THETA) * step / half)
    sine = jnp.sin(phases)
    return jnp.cos(phases), jnp.where(lane < half, -sine, sine), length_of


def attend_all(count, parts, cosine, sine, lengths, *refs):
    pairs = (count - 1) // 2
    blocks, (sums, keys, values), refs = refs[:count], refs[count : count + 3], refs[count + 3 :]
    outs, (scores_of, probs_of) = refs[:parts], refs[parts:]
    rows, cache = keys.shape[:2]
    low = lax.rem(lax.axis_index("col"), pairs)
    width = GROUP_WIDTH
    other_sums = jnp.where(at_home(), blocks[1][:, width:], blocks[2][:, width:])
    squares = sums[...].astype(jnp.float32) + other_sums.astype(jnp.float32)
    scale = lax.rsqrt(jnp.sum(squares, axis=1, keepdims=True) / D + EPSILON)
    factor = HEAD_DIM ** (-0.5)
    cosines, sines, length_of = cosine[...], sine[...], lengths[:, :1]
    lane = lax.broadcasted_iota(jnp.int32, (SLOTS, SLOTS * cache), 1)
    slot = lax.broadcasted_iota(jnp.int32, (SLOTS, SLOTS * cache), 0)
    position = lane - slot * cache
    runs = [slice(start, start + SLOTS) for start in range(0, rows, SLOTS)]
    filled = [(position >= 0) & (position < length_of[part]) for part in runs]
    own, new_values, own_probs = [], [], []
    for pair in range(pairs):
        total = total_of(blocks, pair, width)
        total = (total * scale).astype(jnp.bfloat16).astype(jnp.float32)
        heads = [total[:, h * HEAD_DIM : (h + 1) * HEAD_DIM] for h in range(GROUP + 2)]
        queries = [
            rotated(head, cosines, sines).astype(jnp.bfloat16).astype(jnp.float32)
            for head in heads[:GROUP]
        ]
        new_key = rotated(heads[GROUP], cosines, sines).astype(jnp.bfloat16).astype(jnp.float32)
        new_values.append(heads[GROUP + 1])
        own.append([jnp.sum(query * new_key, axis=1, keepdims=True) * factor for query in queries])
        lanes = pl.ds(pl.multiple_of((low ^ pair) * HEAD_DIM, HEAD_DIM), HEAD_DIM)
        for run, part in enumerate(runs):
            query = jnp.concatenate([head[part] for head in queries], axis=0)
            key = keys[part, :, lanes].reshape(SLOTS * cache, HEAD_DIM)
            scores_of[pair, run] = lax.dot_general(
                query.astype(jnp.bfloat16),
                key,
                (((1,), (1,)), ((), ())),
                preferred_element_type=jnp.float32,
            )
    for pair in range(pairs):
        for run, part in enumerate(runs):
            scores = (scores_of[pair, run] * factor).reshape(GROUP, SLOTS, SLOTS * cache)
            scores = jnp.where(filled[run][None], scores, -1e30)
            own_score = jnp.concatenate([head[part] for head in own[pair]], axis=0).reshape(
                GROUP, SLOTS, 1
            )
            highest = jnp.maximum(jnp.max(scores, axis=2, keepdims=True), own_score)
            weights = jnp.exp(scores - highest)
            own_weight = jnp.exp(own_score - highest)
            inverse = 1.0 / (jnp.sum(weights, axis=2, keepdims=True) + own_weight)
            probs = (weights * inverse).astype(jnp.bfloat16)
            probs_of[pair, run] = probs.reshape(GROUP * SLOTS, SLOTS * cache)
            own_probs.append((own_weight * inverse).astype(jnp.bfloat16).astype(jnp.float32))
    for pair in range(pairs):
        lanes = pl.ds(pl.multiple_of((low ^ pair) * HEAD_DIM, HEAD_DIM), HEAD_DIM)
        results = []
        for run, part in enumerate(runs):
            value = values[part, :, lanes].reshape(SLOTS * cache, HEAD_DIM)
            mixed = jnp.dot(probs_of[pair, run], value, preferred_element_type=jnp.float32)
            own_prob = own_probs[pair * len(runs) + run]
            results.append(
                mixed.reshape(GROUP, SLOTS, HEAD_DIM) + own_prob * new_values[pair][part][None]
            )
        for head in range(GROUP):
            at = pl.multiple_of((low ^ pair) * OUT_WIDTH + head * HEAD_DIM, HEAD_DIM)
            size = len(results) // parts
            for i, out in enumerate(outs):
                joined = jnp.concatenate(
                    [result[head] for result in results[i * size : (i + 1) * size]], axis=0
                )
                out[:, pl.ds(at, HEAD_DIM)] = joined.astype(jnp.bfloat16)


def sum_kernel(count, parts, hidden, *refs):
    attended, blocks, (keep, send) = refs[:parts], refs[parts : parts + count], refs[-2:]
    rows, width = blocks[0].shape
    pairs = keep.shape[1] // width
    side = lax.axis_index("side")
    low = lax.rem(lax.axis_index("col"), pairs)
    for pair in range(pairs):
        column = low ^ pair
        total = total_of(blocks, pair, width)
        at = pl.ds(pl.multiple_of((2 * column + side) * width, width), width)
        hidden_out = (hidden[:, at].astype(jnp.float32) + total).astype(jnp.bfloat16)
        at = pl.ds(pl.multiple_of(column * width, width), width)
        attention = jnp.concatenate([part[:, at] for part in attended], axis=0)
        keep[:, at] = jnp.where(side == 0, hidden_out, attention)
        send[:, at] = jnp.where(side == 0, attention, hidden_out)


def join_kernel(keep, received, out, sems):
    side = lax.axis_index("side")
    width = OUT_WIDTH
    copies = []
    for j in range(keep.shape[1] // width):
        part = slice(j * width, (j + 1) * width)
        for ref, core in ((keep, side), (received, 1 - side)):
            at = pl.ds(pl.multiple_of((2 * j + core) * width, width), width)
            copies.append((ref.at[:, part], out.at[0, :, at]))
    run_copies(copies, sems)


def paired_plan(
    hidden_in, norm_gain, qkv_weight, out_weight, key_cache, value_cache, cache_lengths, slot_request
):
    col_count, row_count = lax.axis_size("col"), lax.axis_size("row")
    pairs = col_count // row_count
    side = lax.axis_index("side")
    rows, depth = hidden_in.shape
    half = depth // 2
    cache = key_cache.shape[1]
    parts = 2
    piece = rows // parts

    own_part = lax.dynamic_slice_in_dim(hidden_in, side * half, half, 1)
    gain = norm_gain.reshape(depth // HEAD_DIM, HEAD_DIM)
    half_in, half_out = qkv_weight.shape[1] // 2, out_weight.shape[1] // 2
    total = rows * col_count
    square = (total, total)
    give_in, own_in, chosen_in = call(
        functools.partial(stage_in_kernel, col_count),
        [pltpu.VMEM((half, half_in), jnp.bfloat16)] * 2 + [struct(square)],
        [HBM, HBM],
        [VMEM] * 3,
        0,
        half * half_in * 4,
        [
            pltpu.VMEM(square, jnp.float32),
            pltpu.VMEM((total,), jnp.int32),
            pltpu.SemaphoreType.DMA((3,)),
        ],
    )(in_hbm(qkv_weight), in_hbm(slot_request))
    blocks = gathered(
        [own_part[i * piece : (i + 1) * piece] for i in range(parts)], "col"
    )
    products, sums = project(in_kernel, chosen_in, blocks, [gain], [give_in, own_in], HEAD_DIM)
    products = spread(products)

    table = struct((rows, HEAD_DIM), jnp.float32)
    give_out, key_part, value_part, *tables, chosen_out = call(
        functools.partial(stage_rest_kernel, col_count),
        [pltpu.VMEM((half, half_out), jnp.bfloat16)]
        + [pltpu.VMEM((rows, cache, pairs * HEAD_DIM), jnp.bfloat16)] * 2
        + [table, table, struct((rows, HEAD_DIM), jnp.int32), struct(square)],
        [SMEM, HBM, HBM, HBM, VMEM],
        [VMEM] * 7,
        0,
        half * half_out * 2 + 4 * rows * cache * pairs * HEAD_DIM,
        [pltpu.VMEM(square, jnp.float32), pltpu.SemaphoreType.DMA((3 * pairs,))],
    )(cache_lengths, in_hbm(out_weight), in_hbm(key_cache), in_hbm(value_cache), slot_request)
    runs = (pairs, rows // SLOTS, GROUP * SLOTS, SLOTS * cache)
    attended = call(
        functools.partial(attend_all, len(products), parts),
        [struct((piece, half))] * parts,
        [VMEM] * (len(products) + 6),
        [VMEM] * parts,
        4 * rows * half * cache,
        0,
        [pltpu.VMEM(runs, jnp.float32), pltpu.VMEM(runs, jnp.bfloat16)],
    )(*tables, *products, *sums, in_vmem(key_part), in_vmem(value_part))

    own_out = call(
        stage_out_kernel,
        pltpu.VMEM((half, half_out), jnp.bfloat16),
        [HBM, HBM],
        VMEM,
        0,
        half * half_out * 2,
        [pltpu.SemaphoreType.DMA((pairs,))],
    )(in_hbm(out_weight), attended[-1])
    products, _ = project(
        out_kernel, chosen_out, gathered(attended, "col"), [], [give_out, own_out], 0
    )
    products = spread(products)
    keep, send = call(
        functools.partial(sum_kernel, len(products), parts),
        [struct((rows, half)), struct((rows, half))],
        [VMEM] * (1 + parts + len(products)),
        [VMEM, VMEM],
        rows * depth * 4,
        rows * depth * 8,
    )(hidden_in, *attended, *products)
    return call(
        join_kernel,
        struct((1, rows, depth)),
        [VMEM, VMEM],
        HBM,
        0,
        rows * depth * 4,
        [pltpu.SemaphoreType.DMA((2 * pairs,))],
    )(keep, moved(send, "side", 1))


def per_device(*args):
    hidden_in, _, qkv_weight, out_weight, key_cache = args[:5]
    col_count, row_count = lax.axis_size("col"), lax.axis_size("row")
    fits = (
        lax.axis_size("side") == 2
        and qkv_weight.shape[1] == 2 * GROUP_WIDTH
        and row_count == 2
        and col_count > row_count
        and col_count & (col_count - 1) == 0
        and hidden_in.shape[0] % 32 == 0
        and key_cache.shape[1] % 16 == 0
        and hidden_in.shape[1] == 2 * OUT_WIDTH * (col_count // row_count)
    )
    return paired_plan(*args) if fits else general_plan(*args)


def solution(mesh):
    placed = (
        P(("groups", "col"), "row"),
        P("row"),
        P("row", "col"),
        P("row", "col"),
        P(("groups", "col"), None, "row"),
        P(("groups", "col"), None, "row"),
        P(("groups", "col")),
        P("groups"),
    )
    return jax.shard_map(
        per_device,
        mesh=mesh,
        in_specs=placed,
        out_specs=P("side", ("groups", "col"), "row"),
        check_vma=False,
    )
```

```python
import functools
import math

import jax
import jax.numpy as jnp
from jax import lax
from jax.experimental import pallas as pl
from jax.experimental.pallas import tpu as pltpu
from jax.sharding import PartitionSpec as P

D = 8192
HEADS = 64
KV_HEADS = 8
HEAD_DIM = 128
QKV = 10240


EPSILON = 1e-05
THETA = 500000.0


def swapped(value, axis, bit):
    mask = 2**bit
    pairs = [(source, source ^ mask) for source in range(lax.axis_size(axis))]
    return lax.ppermute(value, axis, pairs)


def rope_tables(lengths, head_dim):
    half_dim = head_dim // 2
    inv_freq = jnp.exp(
        -jnp.log(jnp.float32(THETA)) * jnp.arange(half_dim, dtype=jnp.float32) / half_dim
    )
    phases = lengths.astype(jnp.float32)[:, None] * inv_freq[None, :]
    return (jnp.cos(phases), jnp.sin(phases))


def rotate(vector, cos_vals, sine_vals):
    half_dim = vector.shape[-1] // 2
    front_half = vector[..., :half_dim]
    back_half = vector[..., half_dim:]
    return jnp.concatenate(
        [
            front_half * cos_vals - back_half * sine_vals,
            back_half * cos_vals + front_half * sine_vals,
        ],
        axis=-1,
    )


def attend(packed, key_block, value_block, lengths):
    slot_count = packed.shape[0]
    cache_size = key_block.shape[1]
    groups = key_block.shape[2] // HEAD_DIM
    per_group = HEADS // KV_HEADS
    grouped = packed.reshape(slot_count, groups, per_group + 2, HEAD_DIM)
    cos_vals, sine_vals = rope_tables(lengths, HEAD_DIM)
    queries = rotate(
        grouped[:, :, :per_group].astype(jnp.float32),
        cos_vals[:, None, None, :],
        sine_vals[:, None, None, :],
    ).astype(jnp.bfloat16)
    new_keys = rotate(
        grouped[:, :, per_group].astype(jnp.float32), cos_vals[:, None, :], sine_vals[:, None, :]
    ).astype(jnp.bfloat16)
    new_values = grouped[:, :, per_group + 1]
    cache_keys = key_block.reshape(slot_count, cache_size, groups, HEAD_DIM)
    cache_values = value_block.reshape(slot_count, cache_size, groups, HEAD_DIM)
    factor = HEAD_DIM ** (-0.5)
    cache_scores = (
        jnp.einsum("sghd,slgd->sghl", queries, cache_keys, preferred_element_type=jnp.float32)
        * factor
    )
    own_scores = (
        jnp.einsum("sghd,sgd->sgh", queries, new_keys, preferred_element_type=jnp.float32) * factor
    )
    in_cache = lax.broadcasted_iota(jnp.int32, (slot_count, cache_size), 1) < lengths[:, None]
    cache_scores = jnp.where(in_cache[:, None, None, :], cache_scores, -1e30)
    row_max = jnp.maximum(jnp.max(cache_scores, axis=-1), own_scores)
    cache_exp = jnp.exp(cache_scores - row_max[..., None])
    own_exp = jnp.exp(own_scores - row_max)
    denominator = jnp.sum(cache_exp, axis=-1) + own_exp
    cache_weight = (cache_exp / denominator[..., None]).astype(jnp.bfloat16)
    own_weight = (own_exp / denominator).astype(jnp.bfloat16)
    combined = jnp.einsum(
        "sghl,slgd->sghd", cache_weight, cache_values, preferred_element_type=jnp.float32
    )
    combined = (
        combined
        + own_weight.astype(jnp.float32)[..., None] * new_values.astype(jnp.float32)[:, :, None, :]
    )
    return combined.astype(jnp.bfloat16).reshape(slot_count, groups * per_group * HEAD_DIM)


def general_plan(
    hidden_in,
    norm_gain,
    qkv_weight,
    out_weight,
    key_cache,
    value_cache,
    cache_lengths,
    slot_request,
):
    side_index = lax.axis_index("side")
    is_weight = side_index == 0
    col_count = lax.axis_size("col")
    row_count = lax.axis_size("row")
    group_cols = col_count // row_count
    in_half = qkv_weight.shape[1] // 2
    out_half = out_weight.shape[1] // 2
    residual = hidden_in.astype(jnp.float32)
    square_sums = lax.psum(jnp.sum(residual * residual, axis=1), "row")
    normed = (
        residual
        * lax.rsqrt(square_sums[:, None] / D + EPSILON)
        * norm_gain.astype(jnp.float32)[None, :]
    ).astype(jnp.bfloat16)
    in_weight = lax.dynamic_slice_in_dim(qkv_weight, side_index * in_half, in_half, 1)
    partial_in = jnp.dot(
        lax.all_gather(normed, "col", axis=0, tiled=True),
        in_weight,
        preferred_element_type=jnp.float32,
    )
    in_slots = jnp.take(partial_in, slot_request, axis=0)
    own_width = QKV // row_count
    summed = lax.psum(in_slots.astype(jnp.bfloat16), "row")
    spread = lax.all_to_all(summed, "col", split_axis=0, concat_axis=1, tiled=True)
    own_columns = lax.dynamic_slice_in_dim(
        spread.reshape(spread.shape[0], col_count, in_half),
        lax.axis_index("row") * group_cols,
        group_cols,
        1,
    )
    slot_half = key_cache.shape[0] // 2
    halves = lax.all_to_all(
        own_columns[:, :, None, :], "side", split_axis=0, concat_axis=2, tiled=True
    )
    arrived = halves.reshape(slot_half, own_width)
    first_slot = side_index * slot_half
    key_part = lax.dynamic_slice_in_dim(key_cache, first_slot, slot_half, 0)
    value_part = lax.dynamic_slice_in_dim(value_cache, first_slot, slot_half, 0)
    length_part = lax.dynamic_slice_in_dim(cache_lengths, first_slot, slot_half, 0)
    attended = attend(arrived, key_part, value_part, length_part)
    out_cols = lax.dynamic_slice_in_dim(out_weight, side_index * out_half, out_half, 1)
    collected = lax.all_gather(attended, ("col", "side"), axis=0, tiled=True)
    out_slots = jnp.dot(collected, out_cols, preferred_element_type=jnp.float32)
    inverse = jnp.argsort(slot_request)
    out_requests = jnp.take(out_slots, inverse, axis=0)
    spread_out = lax.all_to_all(
        out_requests.astype(jnp.bfloat16), "col", split_axis=0, concat_axis=1, tiled=True
    ).astype(out_requests.dtype)
    out_view = spread_out.reshape(spread_out.shape[0], col_count, out_half)
    summed_out = lax.psum_scatter(
        out_view.astype(jnp.bfloat16), "row", scatter_dimension=1, tiled=True
    ).astype(jnp.float32)
    req_rows = hidden_in.shape[0]
    residual_view = residual.reshape(req_rows, group_cols, 2, out_half)
    residual_half = lax.dynamic_index_in_dim(residual_view, side_index, 2, keepdims=False)
    own_hidden = (residual_half + summed_out).astype(jnp.bfloat16)
    payload = jnp.where(is_weight, attended, own_hidden.reshape(attended.shape))
    received = swapped(payload, "side", 0)
    hidden = jnp.stack([own_hidden, received.reshape(own_hidden.shape)], axis=2).reshape(
        req_rows, residual.shape[1]
    )
    attention_rows = jnp.concatenate([received, attended], axis=0)
    result = jnp.where(is_weight, hidden, attention_rows)
    return result[None]


GROUP = HEADS // KV_HEADS
GROUP_WIDTH = (GROUP + 2) * HEAD_DIM
OUT_WIDTH = GROUP * HEAD_DIM
SLOTS = 8
VMEM = pl.BlockSpec(memory_space=pltpu.VMEM)
SMEM = pl.BlockSpec(memory_space=pltpu.SMEM)
HBM = pl.BlockSpec(memory_space=pl.ANY)
MIB = 2**20


def call(kernel, out_shape, in_specs, out_specs, flops, size, scratch=(), limit=16):
    return pl.pallas_call(
        kernel,
        out_shape=out_shape,
        in_specs=in_specs,
        out_specs=out_specs,
        scratch_shapes=list(scratch),
        compiler_params=pltpu.CompilerParams(vmem_limit_bytes=limit * MIB),
        cost_estimate=pl.CostEstimate(flops=flops, bytes_accessed=size, transcendentals=0),
    )


def in_vmem(value):
    return pltpu.with_memory_space_constraint(value, pltpu.VMEM)


def in_hbm(value):
    return pltpu.with_memory_space_constraint(value, pltpu.HBM)


def struct(shape, dtype=jnp.bfloat16):
    return jax.ShapeDtypeStruct(shape, dtype)


def moved(value, axis, mask):
    pairs = [(source, source ^ mask) for source in range(lax.axis_size(axis))]
    return lax.ppermute(value, axis, pairs)


def started(copies, sems):
    copies = [
        pltpu.make_async_copy(source, target, sems.at[i])
        for i, (source, target) in enumerate(copies)
    ]
    for copy in copies:
        copy.start()
    return copies


def run_copies(copies, sems):
    for copy in started(copies, sems):
        copy.wait()


def position():
    return lax.axis_index("side"), lax.axis_index("col")


def rows_copy(weight, target, half):
    depth, width = target.shape
    rows = pl.ds(pl.multiple_of(lax.axis_index("side") * depth, depth), depth)
    columns = pl.ds(pl.multiple_of(half * width, width), width)
    return weight.at[rows, columns], target


def stage_in_kernel(blocks, weight, slots, give_part, own_part, chosen, scratch, slot_part, sems):
    side, col = position()
    slots_copy, *copies = started(
        [
            (slots, slot_part),
            rows_copy(weight, give_part, 1 - side),
            rows_copy(weight, own_part, side),
        ],
        sems,
    )
    slots_copy.wait()
    chosen[...] = one_hot(slot_part, scratch, blocks, col, col).astype(jnp.bfloat16)
    for copy in copies:
        copy.wait()


def head_copies(weight, target, half):
    width = target.shape[1]
    columns = pl.ds(pl.multiple_of(half * width, width), width)
    copies = []
    for j in range(target.shape[0] // OUT_WIDTH):
        row = pl.multiple_of((2 * j + lax.axis_index("side")) * OUT_WIDTH, OUT_WIDTH)
        copies.append(
            (
                weight.at[pl.ds(row, OUT_WIDTH), columns],
                target.at[pl.ds(j * OUT_WIDTH, OUT_WIDTH), :],
            )
        )
    return copies


def stage_cache_kernel(blocks, lengths, keys, values, slots, *refs):
    key_part, value_part, cosine, sine, length_of, chosen, scratch, sems = refs
    side, col = position()
    copies = []
    for j in range(key_part.shape[2] // HEAD_DIM):
        lane = pl.multiple_of((2 * j + side) * HEAD_DIM, HEAD_DIM)
        for cache, part in ((keys, key_part), (values, value_part)):
            copies.append(
                (
                    cache.at[:, :, pl.ds(lane, HEAD_DIM)],
                    part.at[:, :, pl.ds(j * HEAD_DIM, HEAD_DIM)],
                )
            )
    copies = started(copies, sems)
    cosine[...], sine[...], length_of[...] = rope(lengths, cosine.shape[0])
    chosen[...] = one_hot(slots, scratch, blocks, col, col).T.astype(jnp.bfloat16)
    for copy in copies:
        copy.wait()


def stage_give_kernel(weight, give_part, sems):
    run_copies(head_copies(weight, give_part, 1 - lax.axis_index("side")), sems)


def stage_out_kernel(weight, attended, own_part, sems):
    run_copies(head_copies(weight, own_part, lax.axis_index("side")), sems)


def one_hot(slots, scratch, blocks, slot_base, request_base):
    total = slots.shape[0]
    rows = total // blocks
    index = lax.broadcasted_iota(jnp.int32, (total, total), 0)
    request = (lax.div(index, rows) ^ request_base) * rows + lax.rem(index, rows)
    scratch[...] = jnp.where(slots[...].reshape(1, total) == request, 1.0, 0.0).T
    parts = [
        scratch[pl.ds(pl.multiple_of((slot_base ^ i) * rows, rows), rows), :]
        for i in range(blocks)
    ]
    return jnp.concatenate(parts, axis=0)


def pieces(sums):
    high = sums.astype(jnp.bfloat16).astype(jnp.float32)
    middle = (sums - high).astype(jnp.bfloat16).astype(jnp.float32)
    low = sums - high - middle
    lane = lax.broadcasted_iota(jnp.int32, (sums.shape[0], HEAD_DIM), 1)
    parts = jnp.where(lane == 0, high, jnp.where(lane == 1, middle, low))
    return jnp.where(lane < 3, parts, 0.0).astype(jnp.bfloat16)


def dot_columns(rows, weight, out):
    size, width = weight.shape[1], 512
    for start in range(0, size, width):
        part = slice(start, min(start + width, size))
        product = jnp.dot(rows, weight[:, part], preferred_element_type=jnp.float32)
        out[:, part] = product.astype(out.dtype)


def in_kernel(count, chosen, *refs):
    pieces_in, (_, gain, weight, give, permuted) = refs[:count], refs[count:]
    depth = pieces_in[0].shape[1]
    half = weight.shape[1]
    runs = depth // HEAD_DIM
    first = pl.multiple_of(lax.axis_index("side") * runs, runs)
    gains = gain[pl.ds(first, runs), :].astype(jnp.float32)
    values = jnp.concatenate([piece[...].astype(jnp.float32) for piece in pieces_in], axis=0)
    scaled = jnp.concatenate(
        [
            values[:, i * HEAD_DIM : (i + 1) * HEAD_DIM] * gains[i : i + 1, :]
            for i in range(runs)
        ],
        axis=1,
    )
    sums = pieces(jnp.sum(values * values, axis=1, keepdims=True))
    order = jnp.dot(
        chosen[...], scaled.astype(jnp.bfloat16), preferred_element_type=jnp.float32
    ).astype(jnp.bfloat16)
    permuted[...] = order
    own_sums = jnp.dot(chosen[...], sums, preferred_element_type=jnp.float32)
    give[:, half:] = own_sums.astype(jnp.bfloat16)
    dot_columns(order, weight, give)


def out_kernel(count, chosen, *refs):
    pieces_in, (_, weight, give, permuted) = refs[:count], refs[count:]
    values = jnp.concatenate([piece[...] for piece in pieces_in], axis=0)
    order = jnp.dot(chosen[...], values, preferred_element_type=jnp.float32).astype(jnp.bfloat16)
    permuted[...] = order
    dot_columns(order, weight, give)


def at_home():
    pairs = lax.axis_size("col") // lax.axis_size("row")
    return lax.axis_index("row") == lax.div(lax.axis_index("col"), pairs)


def merge_kernel(count, own, given, received, *outs):
    rows = outs[0].shape[0]
    half = own.shape[1]
    more = given.shape[1] - half
    pairs = count // 2

    def write(out, first):
        first = first if isinstance(first, int) else pl.multiple_of(first, rows)
        part = pl.ds(first, rows)
        total = own[part, :] + received[part, :half].astype(jnp.float32)
        out[:, :half] = total.astype(jnp.bfloat16)
        if out.shape[1] > half:
            out[:, half:] = squares(part)

    def squares(part):
        lanes = slice(half, half + more // 2)
        return jnp.concatenate([given[part, lanes], received[part, lanes]], axis=1)

    write(outs[0], 0)
    write(outs[1], pairs * rows)
    home = at_home()
    for pair in range(1, pairs):
        write(outs[2 * pair], jnp.where(home, pairs + pair, pair) * rows)
        write(outs[2 * pair + 1], jnp.where(home, pair, pairs + pair) * rows)
    for out in outs[count:]:
        out[...] = squares(pl.ds(0, rows))


def own_kernel(permuted, weight, own):
    dot_columns(permuted[...], weight, own)


def project(kernel, chosen, pieces_in, extra, weights, more):
    count = lax.axis_size("col")
    parts = len(pieces_in)
    depth = pieces_in[0].shape[1]
    rows = sum(part.shape[0] for part in pieces_in)
    half = weights[0].shape[1]
    flops = 2 * rows * depth * half
    give, permuted = call(
        functools.partial(kernel, parts),
        [struct((rows, half + more)), struct((rows, depth))],
        [VMEM] * (parts + len(extra) + 3),
        [VMEM, VMEM],
        flops,
        depth * half * 2,
    )(chosen, *pieces_in, in_vmem(weights[1]), *extra, in_vmem(weights[0]))
    received = moved(give, "side", 1)
    own = call(
        own_kernel,
        struct((rows, half), jnp.float32),
        [VMEM, VMEM],
        VMEM,
        flops,
        depth * half * 2,
    )(permuted, in_vmem(weights[1]))
    outs = [struct((rows // count, half + (more if i > 1 else 0))) for i in range(count)]
    if more:
        outs = outs + [struct((rows // count, more))]
    merged = call(
        functools.partial(merge_kernel, count),
        outs,
        [VMEM] * 3,
        [VMEM] * len(outs),
        rows * half,
        rows * half * 8,
    )(own, give, received)
    return merged[:count], merged[count:]


def gathered(parts, axis, whole=None):
    blocks = {0: parts}
    mask = lax.axis_size(axis) // 2
    while mask:
        blocks |= {
            known | mask: [
                moved(part, axis, mask)
                for part in ([whole] if mask == 1 and known == 0 and whole is not None else block)
            ]
            for known, block in blocks.items()
        }
        mask //= 2
    if whole is not None:
        blocks[0] = [whole]
    return [part for i in sorted(blocks) for part in blocks[i]]


def choose_kernel(own, passed, *refs):
    out = refs[-1]
    out[...] = jnp.where(at_home(), passed[...], own[...])


def direct(value, far, pair):
    pairs = lax.axis_size("col") // 2
    moves = []
    for col in range(2 * pairs):
        for row in range(2):
            home = row == col // pairs
            target = col ^ pair ^ (pairs if home == far else 0)
            moves.append((2 * col + row, 2 * target + (row if home else 1 - row)))
    return lax.ppermute(value, ("col", "row"), moves)


def spread(products, ready):
    own, passed, *rest = products
    pairs = len(products) // 2
    passed = moved(passed, "col", pairs)
    blocks = []
    for pair in range(1, pairs):
        blocks += [
            direct(rest[2 * pair - 2], True, pair),
            direct(rest[2 * pair - 1], False, pair),
        ]
    crossing = call(
        choose_kernel,
        struct(own.shape),
        [VMEM] * 2 + [HBM] * len(ready),
        VMEM,
        0,
        own.size * 4,
    )(own, passed, *ready)
    return [passed, *blocks, own, moved(crossing, "row", 1)]


def total_of(blocks, pair, width):
    if pair > 0:
        first, second = blocks[2 * pair - 1][:, :width], blocks[2 * pair][:, :width]
    else:
        passed, own, crossed = blocks[0], blocks[-2], blocks[-1]
        first, second = jnp.where(at_home(), own[...], passed[...]), crossed[...]
    return first.astype(jnp.float32) + second.astype(jnp.float32)


def rotated(vector, cosine, sine):
    return vector * cosine + pltpu.roll(vector, HEAD_DIM // 2, 1) * sine


def rope(lengths, rows):
    slot = lax.broadcasted_iota(jnp.int32, (rows, HEAD_DIM), 0)
    length_of = jnp.zeros((rows, HEAD_DIM), jnp.int32)
    for i in range(rows):
        length_of = jnp.where(slot == i, lengths[i], length_of)
    lane = lax.broadcasted_iota(jnp.int32, (rows, HEAD_DIM), 1)
    half = HEAD_DIM // 2
    step = lax.rem(lane, half).astype(jnp.float32)
    phases = length_of.astype(jnp.float32) * jnp.exp(-math.log(THETA) * step / half)
    sine = jnp.sin(phases)
    return jnp.cos(phases), jnp.where(lane < half, -sine, sine), length_of


def attend_all(count, parts, ready, cosine, sine, lengths, *refs):
    pairs = (count - 1) // 2
    blocks, (sums, keys, values), refs = refs[:count], refs[count : count + 3], refs[count + 3 :]
    whole, outs, (scores_of, probs_of) = refs[0], refs[1 : parts + 1], refs[parts + 1 :]
    rows, cache = keys.shape[:2]
    low = lax.rem(lax.axis_index("col"), pairs)
    width = GROUP_WIDTH
    other_sums = jnp.where(at_home(), blocks[1][:, width:], blocks[2][:, width:])
    squares = sums[...].astype(jnp.float32) + other_sums.astype(jnp.float32)
    scale = lax.rsqrt(jnp.sum(squares, axis=1, keepdims=True) / D + EPSILON)
    factor = HEAD_DIM ** (-0.5)
    cosines, sines, length_of = cosine[...], sine[...], lengths[:, :1]
    lane = lax.broadcasted_iota(jnp.int32, (SLOTS, SLOTS * cache), 1)
    slot = lax.broadcasted_iota(jnp.int32, (SLOTS, SLOTS * cache), 0)
    position = lane - slot * cache
    runs = [slice(start, start + SLOTS) for start in range(0, rows, SLOTS)]
    filled = [(position >= 0) & (position < length_of[part]) for part in runs]
    own, new_values, own_probs = [], [], []
    for pair in range(pairs):
        total = total_of(blocks, pair, width)
        total = (total * scale).astype(jnp.bfloat16).astype(jnp.float32)
        heads = [total[:, h * HEAD_DIM : (h + 1) * HEAD_DIM] for h in range(GROUP + 2)]
        queries = [
            rotated(head, cosines, sines).astype(jnp.bfloat16).astype(jnp.float32)
            for head in heads[:GROUP]
        ]
        new_key = rotated(heads[GROUP], cosines, sines).astype(jnp.bfloat16).astype(jnp.float32)
        new_values.append(heads[GROUP + 1])
        own.append([jnp.sum(query * new_key, axis=1, keepdims=True) * factor for query in queries])
        lanes = pl.ds(pl.multiple_of((low ^ pair) * HEAD_DIM, HEAD_DIM), HEAD_DIM)
        for run, part in enumerate(runs):
            query = jnp.concatenate([head[part] for head in queries], axis=0)
            key = keys[part, :, lanes].reshape(SLOTS * cache, HEAD_DIM)
            scores_of[pair, run] = lax.dot_general(
                query.astype(jnp.bfloat16),
                key,
                (((1,), (1,)), ((), ())),
                preferred_element_type=jnp.float32,
            )
    for pair in range(pairs):
        for run, part in enumerate(runs):
            scores = (scores_of[pair, run] * factor).reshape(GROUP, SLOTS, SLOTS * cache)
            scores = jnp.where(filled[run][None], scores, -1e30)
            own_score = jnp.concatenate([head[part] for head in own[pair]], axis=0).reshape(
                GROUP, SLOTS, 1
            )
            highest = jnp.maximum(jnp.max(scores, axis=2, keepdims=True), own_score)
            weights = jnp.exp(scores - highest)
            own_weight = jnp.exp(own_score - highest)
            inverse = 1.0 / (jnp.sum(weights, axis=2, keepdims=True) + own_weight)
            probs = (weights * inverse).astype(jnp.bfloat16)
            probs_of[pair, run] = probs.reshape(GROUP * SLOTS, SLOTS * cache)
            own_probs.append((own_weight * inverse).astype(jnp.bfloat16).astype(jnp.float32))
    for pair in range(pairs):
        lanes = pl.ds(pl.multiple_of((low ^ pair) * HEAD_DIM, HEAD_DIM), HEAD_DIM)
        results = []
        for run, part in enumerate(runs):
            value = values[part, :, lanes].reshape(SLOTS * cache, HEAD_DIM)
            mixed = jnp.dot(probs_of[pair, run], value, preferred_element_type=jnp.float32)
            own_prob = own_probs[pair * len(runs) + run]
            results.append(
                mixed.reshape(GROUP, SLOTS, HEAD_DIM) + own_prob * new_values[pair][part][None]
            )
        for head in range(GROUP):
            at = pl.multiple_of((low ^ pair) * OUT_WIDTH + head * HEAD_DIM, HEAD_DIM)
            size = len(results) // parts
            for i, out in enumerate(outs):
                joined = jnp.concatenate(
                    [result[head] for result in results[i * size : (i + 1) * size]], axis=0
                )
                joined = joined.astype(jnp.bfloat16)
                out[:, pl.ds(at, HEAD_DIM)] = joined
                run = slice(i * joined.shape[0], (i + 1) * joined.shape[0])
                whole[run, pl.ds(at, HEAD_DIM)] = joined


def sum_kernel(count, hidden, attended, *refs):
    blocks, (keep, send) = refs[:count], refs[count:]
    rows, width = blocks[0].shape
    pairs = keep.shape[1] // width
    side = lax.axis_index("side")
    low = lax.rem(lax.axis_index("col"), pairs)
    for pair in range(pairs):
        column = low ^ pair
        total = total_of(blocks, pair, width)
        at = pl.ds(pl.multiple_of((2 * column + side) * width, width), width)
        hidden_out = (hidden[:, at].astype(jnp.float32) + total).astype(jnp.bfloat16)
        at = pl.ds(pl.multiple_of(column * width, width), width)
        attention = attended[:, at]
        keep[:, at] = jnp.where(side == 0, hidden_out, attention)
        send[:, at] = jnp.where(side == 0, attention, hidden_out)


def join_kernel(keep, received, out, sems):
    side = lax.axis_index("side")
    width = OUT_WIDTH
    copies = []
    for j in range(keep.shape[1] // width):
        part = slice(j * width, (j + 1) * width)
        for ref, core in ((keep, side), (received, 1 - side)):
            at = pl.ds(pl.multiple_of((2 * j + core) * width, width), width)
            copies.append((ref.at[:, part], out.at[0, :, at]))
    run_copies(copies, sems)


def paired_plan(
    hidden_in, norm_gain, qkv_weight, out_weight, key_cache, value_cache, cache_lengths, slot_request
):
    col_count, row_count = lax.axis_size("col"), lax.axis_size("row")
    pairs = col_count // row_count
    side = lax.axis_index("side")
    rows, depth = hidden_in.shape
    half = depth // 2
    cache = key_cache.shape[1]
    parts = 2
    piece = rows // parts

    own_part = lax.dynamic_slice_in_dim(hidden_in, side * half, half, 1)
    gain = norm_gain.reshape(depth // HEAD_DIM, HEAD_DIM)
    half_in, half_out = qkv_weight.shape[1] // 2, out_weight.shape[1] // 2
    total = rows * col_count
    square = (total, total)
    give_in, own_in, chosen_in = call(
        functools.partial(stage_in_kernel, col_count),
        [pltpu.VMEM((half, half_in), jnp.bfloat16)] * 2 + [struct(square)],
        [HBM, HBM],
        [VMEM] * 3,
        0,
        half * half_in * 4,
        [
            pltpu.VMEM(square, jnp.float32),
            pltpu.VMEM((total,), jnp.int32),
            pltpu.SemaphoreType.DMA((3,)),
        ],
    )(in_hbm(qkv_weight), in_hbm(slot_request))
    blocks = gathered(
        [own_part[i * piece : (i + 1) * piece] for i in range(parts)], "col"
    )
    table = struct((rows, HEAD_DIM), jnp.float32)
    key_part, value_part, *tables, chosen_out = call(
        functools.partial(stage_cache_kernel, col_count),
        [pltpu.VMEM((rows, cache, pairs * HEAD_DIM), jnp.bfloat16)] * 2
        + [table, table, struct((rows, HEAD_DIM), jnp.int32), struct(square)],
        [SMEM, HBM, HBM, VMEM],
        [VMEM] * 6,
        0,
        4 * rows * cache * pairs * HEAD_DIM,
        [pltpu.VMEM(square, jnp.float32), pltpu.SemaphoreType.DMA((2 * pairs,))],
    )(cache_lengths, in_hbm(key_cache), in_hbm(value_cache), slot_request)
    products, sums = project(in_kernel, chosen_in, blocks, [gain], [give_in, own_in], HEAD_DIM)
    products = spread(products, [chosen_out])

    give_out = call(
        stage_give_kernel,
        pltpu.VMEM((half, half_out), jnp.bfloat16),
        [HBM],
        VMEM,
        0,
        half * half_out * 2,
        [pltpu.SemaphoreType.DMA((pairs,))],
    )(in_hbm(out_weight))
    runs = (pairs, rows // SLOTS, GROUP * SLOTS, SLOTS * cache)
    attended, *attended_parts = call(
        functools.partial(attend_all, len(products), parts),
        [struct((rows, half))] + [struct((piece, half))] * parts,
        [HBM] + [VMEM] * (len(products) + 6),
        [VMEM] * (parts + 1),
        4 * rows * half * cache,
        0,
        [pltpu.VMEM(runs, jnp.float32), pltpu.VMEM(runs, jnp.bfloat16)],
    )(give_out, *tables, *products, *sums, in_vmem(key_part), in_vmem(value_part))

    own_out = call(
        stage_out_kernel,
        pltpu.VMEM((half, half_out), jnp.bfloat16),
        [HBM, HBM],
        VMEM,
        0,
        half * half_out * 2,
        [pltpu.SemaphoreType.DMA((pairs,))],
    )(in_hbm(out_weight), attended)
    products, _ = project(
        out_kernel, chosen_out, gathered(attended_parts, "col", attended), [], [give_out, own_out], 0
    )
    products = spread(products, [])
    keep, send = call(
        functools.partial(sum_kernel, len(products)),
        [struct((rows, half)), struct((rows, half))],
        [VMEM] * (2 + len(products)),
        [VMEM, VMEM],
        rows * depth * 4,
        rows * depth * 8,
    )(hidden_in, attended, *products)
    return call(
        join_kernel,
        struct((1, rows, depth)),
        [VMEM, VMEM],
        HBM,
        0,
        rows * depth * 4,
        [pltpu.SemaphoreType.DMA((2 * pairs,))],
    )(keep, moved(send, "side", 1))


def per_device(*args):
    hidden_in, _, qkv_weight, out_weight, key_cache = args[:5]
    col_count, row_count = lax.axis_size("col"), lax.axis_size("row")
    fits = (
        lax.axis_size("side") == 2
        and qkv_weight.shape[1] == 2 * GROUP_WIDTH
        and row_count == 2
        and col_count > row_count
        and col_count & (col_count - 1) == 0
        and hidden_in.shape[0] % 32 == 0
        and key_cache.shape[1] % 16 == 0
        and hidden_in.shape[1] == 2 * OUT_WIDTH * (col_count // row_count)
    )
    return paired_plan(*args) if fits else general_plan(*args)


def solution(mesh):
    placed = (
        P(("groups", "col"), "row"),
        P("row"),
        P("row", "col"),
        P("row", "col"),
        P(("groups", "col"), None, "row"),
        P(("groups", "col"), None, "row"),
        P(("groups", "col")),
        P("groups"),
    )
    return jax.shard_map(
        per_device,
        mesh=mesh,
        in_specs=placed,
        out_specs=P("side", ("groups", "col"), "row"),
        check_vma=False,
    )
```

```python
import functools
import math

import jax
import jax.numpy as jnp
from jax import lax
from jax.experimental import pallas as pl
from jax.experimental.pallas import tpu as pltpu
from jax.sharding import PartitionSpec as P

D = 8192
HEADS = 64
KV_HEADS = 8
HEAD_DIM = 128
QKV = 10240


EPSILON = 1e-05
THETA = 500000.0


def swapped(value, axis, bit):
    mask = 2**bit
    pairs = [(source, source ^ mask) for source in range(lax.axis_size(axis))]
    return lax.ppermute(value, axis, pairs)


def rope_tables(lengths, head_dim):
    half_dim = head_dim // 2
    inv_freq = jnp.exp(
        -jnp.log(jnp.float32(THETA)) * jnp.arange(half_dim, dtype=jnp.float32) / half_dim
    )
    phases = lengths.astype(jnp.float32)[:, None] * inv_freq[None, :]
    return (jnp.cos(phases), jnp.sin(phases))


def rotate(vector, cos_vals, sine_vals):
    half_dim = vector.shape[-1] // 2
    front_half = vector[..., :half_dim]
    back_half = vector[..., half_dim:]
    return jnp.concatenate(
        [
            front_half * cos_vals - back_half * sine_vals,
            back_half * cos_vals + front_half * sine_vals,
        ],
        axis=-1,
    )


def attend(packed, key_block, value_block, lengths):
    slot_count = packed.shape[0]
    cache_size = key_block.shape[1]
    groups = key_block.shape[2] // HEAD_DIM
    per_group = HEADS // KV_HEADS
    grouped = packed.reshape(slot_count, groups, per_group + 2, HEAD_DIM)
    cos_vals, sine_vals = rope_tables(lengths, HEAD_DIM)
    queries = rotate(
        grouped[:, :, :per_group].astype(jnp.float32),
        cos_vals[:, None, None, :],
        sine_vals[:, None, None, :],
    ).astype(jnp.bfloat16)
    new_keys = rotate(
        grouped[:, :, per_group].astype(jnp.float32), cos_vals[:, None, :], sine_vals[:, None, :]
    ).astype(jnp.bfloat16)
    new_values = grouped[:, :, per_group + 1]
    cache_keys = key_block.reshape(slot_count, cache_size, groups, HEAD_DIM)
    cache_values = value_block.reshape(slot_count, cache_size, groups, HEAD_DIM)
    factor = HEAD_DIM ** (-0.5)
    cache_scores = (
        jnp.einsum("sghd,slgd->sghl", queries, cache_keys, preferred_element_type=jnp.float32)
        * factor
    )
    own_scores = (
        jnp.einsum("sghd,sgd->sgh", queries, new_keys, preferred_element_type=jnp.float32) * factor
    )
    in_cache = lax.broadcasted_iota(jnp.int32, (slot_count, cache_size), 1) < lengths[:, None]
    cache_scores = jnp.where(in_cache[:, None, None, :], cache_scores, -1e30)
    row_max = jnp.maximum(jnp.max(cache_scores, axis=-1), own_scores)
    cache_exp = jnp.exp(cache_scores - row_max[..., None])
    own_exp = jnp.exp(own_scores - row_max)
    denominator = jnp.sum(cache_exp, axis=-1) + own_exp
    cache_weight = (cache_exp / denominator[..., None]).astype(jnp.bfloat16)
    own_weight = (own_exp / denominator).astype(jnp.bfloat16)
    combined = jnp.einsum(
        "sghl,slgd->sghd", cache_weight, cache_values, preferred_element_type=jnp.float32
    )
    combined = (
        combined
        + own_weight.astype(jnp.float32)[..., None] * new_values.astype(jnp.float32)[:, :, None, :]
    )
    return combined.astype(jnp.bfloat16).reshape(slot_count, groups * per_group * HEAD_DIM)


def general_plan(
    hidden_in,
    norm_gain,
    qkv_weight,
    out_weight,
    key_cache,
    value_cache,
    cache_lengths,
    slot_request,
):
    side_index = lax.axis_index("side")
    is_weight = side_index == 0
    col_count = lax.axis_size("col")
    row_count = lax.axis_size("row")
    group_cols = col_count // row_count
    in_half = qkv_weight.shape[1] // 2
    out_half = out_weight.shape[1] // 2
    residual = hidden_in.astype(jnp.float32)
    square_sums = lax.psum(jnp.sum(residual * residual, axis=1), "row")
    normed = (
        residual
        * lax.rsqrt(square_sums[:, None] / D + EPSILON)
        * norm_gain.astype(jnp.float32)[None, :]
    ).astype(jnp.bfloat16)
    in_weight = lax.dynamic_slice_in_dim(qkv_weight, side_index * in_half, in_half, 1)
    partial_in = jnp.dot(
        lax.all_gather(normed, "col", axis=0, tiled=True),
        in_weight,
        preferred_element_type=jnp.float32,
    )
    in_slots = jnp.take(partial_in, slot_request, axis=0)
    own_width = QKV // row_count
    summed = lax.psum(in_slots.astype(jnp.bfloat16), "row")
    spread = lax.all_to_all(summed, "col", split_axis=0, concat_axis=1, tiled=True)
    own_columns = lax.dynamic_slice_in_dim(
        spread.reshape(spread.shape[0], col_count, in_half),
        lax.axis_index("row") * group_cols,
        group_cols,
        1,
    )
    slot_half = key_cache.shape[0] // 2
    halves = lax.all_to_all(
        own_columns[:, :, None, :], "side", split_axis=0, concat_axis=2, tiled=True
    )
    arrived = halves.reshape(slot_half, own_width)
    first_slot = side_index * slot_half
    key_part = lax.dynamic_slice_in_dim(key_cache, first_slot, slot_half, 0)
    value_part = lax.dynamic_slice_in_dim(value_cache, first_slot, slot_half, 0)
    length_part = lax.dynamic_slice_in_dim(cache_lengths, first_slot, slot_half, 0)
    attended = attend(arrived, key_part, value_part, length_part)
    out_cols = lax.dynamic_slice_in_dim(out_weight, side_index * out_half, out_half, 1)
    collected = lax.all_gather(attended, ("col", "side"), axis=0, tiled=True)
    out_slots = jnp.dot(collected, out_cols, preferred_element_type=jnp.float32)
    inverse = jnp.argsort(slot_request)
    out_requests = jnp.take(out_slots, inverse, axis=0)
    spread_out = lax.all_to_all(
        out_requests.astype(jnp.bfloat16), "col", split_axis=0, concat_axis=1, tiled=True
    ).astype(out_requests.dtype)
    out_view = spread_out.reshape(spread_out.shape[0], col_count, out_half)
    summed_out = lax.psum_scatter(
        out_view.astype(jnp.bfloat16), "row", scatter_dimension=1, tiled=True
    ).astype(jnp.float32)
    req_rows = hidden_in.shape[0]
    residual_view = residual.reshape(req_rows, group_cols, 2, out_half)
    residual_half = lax.dynamic_index_in_dim(residual_view, side_index, 2, keepdims=False)
    own_hidden = (residual_half + summed_out).astype(jnp.bfloat16)
    payload = jnp.where(is_weight, attended, own_hidden.reshape(attended.shape))
    received = swapped(payload, "side", 0)
    hidden = jnp.stack([own_hidden, received.reshape(own_hidden.shape)], axis=2).reshape(
        req_rows, residual.shape[1]
    )
    attention_rows = jnp.concatenate([received, attended], axis=0)
    result = jnp.where(is_weight, hidden, attention_rows)
    return result[None]


GROUP = HEADS // KV_HEADS
GROUP_WIDTH = (GROUP + 2) * HEAD_DIM
OUT_WIDTH = GROUP * HEAD_DIM
SLOTS = 8
VMEM = pl.BlockSpec(memory_space=pltpu.VMEM)
SMEM = pl.BlockSpec(memory_space=pltpu.SMEM)
HBM = pl.BlockSpec(memory_space=pl.ANY)
MIB = 2**20


def call(kernel, out_shape, in_specs, out_specs, flops, size, scratch=(), limit=16):
    return pl.pallas_call(
        kernel,
        out_shape=out_shape,
        in_specs=in_specs,
        out_specs=out_specs,
        scratch_shapes=list(scratch),
        compiler_params=pltpu.CompilerParams(vmem_limit_bytes=limit * MIB),
        cost_estimate=pl.CostEstimate(flops=flops, bytes_accessed=size, transcendentals=0),
    )


def in_vmem(value):
    return pltpu.with_memory_space_constraint(value, pltpu.VMEM)


def in_hbm(value):
    return pltpu.with_memory_space_constraint(value, pltpu.HBM)


def struct(shape, dtype=jnp.bfloat16):
    return jax.ShapeDtypeStruct(shape, dtype)


def moved(value, axis, mask):
    pairs = [(source, source ^ mask) for source in range(lax.axis_size(axis))]
    return lax.ppermute(value, axis, pairs)


def started(copies, sems):
    copies = [
        pltpu.make_async_copy(source, target, sems.at[i])
        for i, (source, target) in enumerate(copies)
    ]
    for copy in copies:
        copy.start()
    return copies


def run_copies(copies, sems):
    for copy in started(copies, sems):
        copy.wait()


def position():
    return lax.axis_index("side"), lax.axis_index("col")


def rows_copy(weight, target, half):
    depth, width = target.shape
    rows = pl.ds(pl.multiple_of(lax.axis_index("side") * depth, depth), depth)
    columns = pl.ds(pl.multiple_of(half * width, width), width)
    return weight.at[rows, columns], target


def stage_in_kernel(blocks, weight, slots, give_part, own_part, chosen, scratch, slot_part, sems):
    side, col = position()
    slots_copy, *copies = started(
        [
            (slots, slot_part),
            rows_copy(weight, give_part, 1 - side),
            rows_copy(weight, own_part, side),
        ],
        sems,
    )
    slots_copy.wait()
    chosen[...] = one_hot(slot_part, scratch, blocks, col, col).astype(jnp.bfloat16)
    for copy in copies:
        copy.wait()


def head_copies(weight, target, half):
    width = target.shape[1]
    columns = pl.ds(pl.multiple_of(half * width, width), width)
    copies = []
    for j in range(target.shape[0] // OUT_WIDTH):
        row = pl.multiple_of((2 * j + lax.axis_index("side")) * OUT_WIDTH, OUT_WIDTH)
        copies.append(
            (
                weight.at[pl.ds(row, OUT_WIDTH), columns],
                target.at[pl.ds(j * OUT_WIDTH, OUT_WIDTH), :],
            )
        )
    return copies


def stage_rest_kernel(blocks, lengths, weight, keys, values, slots, *refs):
    target, key_part, value_part, cosine, sine, length_of, chosen, scratch, sems = refs
    side, col = position()
    copies = []
    for j in range(key_part.shape[2] // HEAD_DIM):
        lane = pl.multiple_of((2 * j + side) * HEAD_DIM, HEAD_DIM)
        for cache, part in ((keys, key_part), (values, value_part)):
            copies.append(
                (
                    cache.at[:, :, pl.ds(lane, HEAD_DIM)],
                    part.at[:, :, pl.ds(j * HEAD_DIM, HEAD_DIM)],
                )
            )
    copies = started(copies + head_copies(weight, target, 1 - side), sems)
    cosine[...], sine[...], length_of[...] = rope(lengths, cosine.shape[0])
    chosen[...] = one_hot(slots, scratch, blocks, col, col).T.astype(jnp.bfloat16)
    for copy in copies:
        copy.wait()


def stage_out_kernel(weight, attended, own_part, sems):
    run_copies(head_copies(weight, own_part, lax.axis_index("side")), sems)


def one_hot(slots, scratch, blocks, slot_base, request_base):
    total = slots.shape[0]
    rows = total // blocks
    index = lax.broadcasted_iota(jnp.int32, (total, total), 0)
    request = (lax.div(index, rows) ^ request_base) * rows + lax.rem(index, rows)
    scratch[...] = jnp.where(slots[...].reshape(1, total) == request, 1.0, 0.0).T
    parts = [
        scratch[pl.ds(pl.multiple_of((slot_base ^ i) * rows, rows), rows), :]
        for i in range(blocks)
    ]
    return jnp.concatenate(parts, axis=0)


def pieces(sums):
    high = sums.astype(jnp.bfloat16).astype(jnp.float32)
    middle = (sums - high).astype(jnp.bfloat16).astype(jnp.float32)
    low = sums - high - middle
    lane = lax.broadcasted_iota(jnp.int32, (sums.shape[0], HEAD_DIM), 1)
    parts = jnp.where(lane == 0, high, jnp.where(lane == 1, middle, low))
    return jnp.where(lane < 3, parts, 0.0).astype(jnp.bfloat16)


def dot_columns(rows, weight, out):
    size, width = weight.shape[1], 512
    for start in range(0, size, width):
        part = slice(start, min(start + width, size))
        product = jnp.dot(rows, weight[:, part], preferred_element_type=jnp.float32)
        out[:, part] = product.astype(out.dtype)


def in_kernel(count, chosen, *refs):
    pieces_in, (_, gain, weight, give, permuted) = refs[:count], refs[count:]
    depth = pieces_in[0].shape[1]
    half = weight.shape[1]
    runs = depth // HEAD_DIM
    first = pl.multiple_of(lax.axis_index("side") * runs, runs)
    gains = gain[pl.ds(first, runs), :].astype(jnp.float32)
    values = jnp.concatenate([piece[...].astype(jnp.float32) for piece in pieces_in], axis=0)
    scaled = jnp.concatenate(
        [
            values[:, i * HEAD_DIM : (i + 1) * HEAD_DIM] * gains[i : i + 1, :]
            for i in range(runs)
        ],
        axis=1,
    )
    sums = pieces(jnp.sum(values * values, axis=1, keepdims=True))
    order = jnp.dot(
        chosen[...], scaled.astype(jnp.bfloat16), preferred_element_type=jnp.float32
    ).astype(jnp.bfloat16)
    permuted[...] = order
    own_sums = jnp.dot(chosen[...], sums, preferred_element_type=jnp.float32)
    give[:, half:] = own_sums.astype(jnp.bfloat16)
    dot_columns(order, weight, give)


def out_kernel(count, chosen, *refs):
    pieces_in, (_, weight, give, permuted) = refs[:count], refs[count:]
    values = jnp.concatenate([piece[...] for piece in pieces_in], axis=0)
    order = jnp.dot(chosen[...], values, preferred_element_type=jnp.float32).astype(jnp.bfloat16)
    permuted[...] = order
    dot_columns(order, weight, give)


def at_home():
    pairs = lax.axis_size("col") // lax.axis_size("row")
    return lax.axis_index("row") == lax.div(lax.axis_index("col"), pairs)


def merge_kernel(count, own, given, received, *outs):
    rows = outs[0].shape[0]
    half = own.shape[1]
    more = given.shape[1] - half
    pairs = count // 2

    def write(out, first):
        first = first if isinstance(first, int) else pl.multiple_of(first, rows)
        part = pl.ds(first, rows)
        total = own[part, :] + received[part, :half].astype(jnp.float32)
        out[...] = total.astype(jnp.bfloat16)

    write(outs[0], 0)
    write(outs[1], pairs * rows)
    home = at_home()
    for pair in range(1, pairs):
        write(outs[2 * pair], jnp.where(home, pairs + pair, pair) * rows)
        write(outs[2 * pair + 1], jnp.where(home, pair, pairs + pair) * rows)
    for out in outs[count:]:
        lanes = slice(half, half + more // 2)
        out[...] = jnp.concatenate([given[:rows, lanes], received[:rows, lanes]], axis=1)


def own_kernel(permuted, weight, own):
    dot_columns(permuted[...], weight, own)


def project(kernel, chosen, pieces_in, extra, weights, more):
    count = lax.axis_size("col")
    parts = len(pieces_in)
    depth = pieces_in[0].shape[1]
    rows = sum(part.shape[0] for part in pieces_in)
    half = weights[0].shape[1]
    flops = 2 * rows * depth * half
    give, permuted = call(
        functools.partial(kernel, parts),
        [struct((rows, half + more)), struct((rows, depth))],
        [VMEM] * (parts + len(extra) + 3),
        [VMEM, VMEM],
        flops,
        depth * half * 2,
    )(chosen, *pieces_in, in_vmem(weights[1]), *extra, in_vmem(weights[0]))
    received = moved(give, "side", 1)
    own = call(
        own_kernel,
        struct((rows, half), jnp.float32),
        [VMEM, VMEM],
        VMEM,
        flops,
        depth * half * 2,
    )(permuted, in_vmem(weights[1]))
    outs = [struct((rows // count, half))] * count
    if more:
        outs = outs + [struct((rows // count, more))]
    merged = call(
        functools.partial(merge_kernel, count),
        outs,
        [VMEM] * 3,
        [VMEM] * len(outs),
        rows * half,
        rows * half * 8,
    )(own, give, received)
    return merged[:count], merged[count:]


def gathered(parts, axis, whole=None):
    blocks = {0: parts}
    mask = lax.axis_size(axis) // 2
    while mask:
        blocks |= {
            known | mask: [
                moved(part, axis, mask)
                for part in ([whole] if mask == 1 and known == 0 and whole is not None else block)
            ]
            for known, block in blocks.items()
        }
        mask //= 2
    if whole is not None:
        blocks[0] = [whole]
    return [part for i in sorted(blocks) for part in blocks[i]]


def choose_kernel(own, passed, *refs):
    out = refs[-1]
    out[...] = jnp.where(at_home(), passed[...], own[...])


def direct(value, far, pair):
    pairs = lax.axis_size("col") // 2
    moves = []
    for col in range(2 * pairs):
        for row in range(2):
            home = row == col // pairs
            target = col ^ pair ^ (pairs if home == far else 0)
            moves.append((2 * col + row, 2 * target + (row if home else 1 - row)))
    return lax.ppermute(value, ("col", "row"), moves)


def spread(products, ready):
    own, passed, *rest = products
    pairs = len(products) // 2
    passed = moved(passed, "col", pairs)
    blocks = []
    for pair in range(1, pairs):
        blocks += [
            direct(rest[2 * pair - 2], True, pair),
            direct(rest[2 * pair - 1], False, pair),
        ]
    crossing = call(
        choose_kernel,
        struct(own.shape),
        [VMEM] * 2 + [HBM] * len(ready),
        VMEM,
        0,
        own.size * 4,
    )(own, passed, *ready)
    return [passed, *blocks, own, moved(crossing, "row", 1)]


def total_of(blocks, pair):
    if pair > 0:
        first, second = blocks[2 * pair - 1][...], blocks[2 * pair][...]
    else:
        passed, own, crossed = blocks[0], blocks[-2], blocks[-1]
        first, second = jnp.where(at_home(), own[...], passed[...]), crossed[...]
    return first.astype(jnp.float32) + second.astype(jnp.float32)


def rotated(vector, cosine, sine):
    return vector * cosine + pltpu.roll(vector, HEAD_DIM // 2, 1) * sine


def rope(lengths, rows):
    slot = lax.broadcasted_iota(jnp.int32, (rows, HEAD_DIM), 0)
    length_of = jnp.zeros((rows, HEAD_DIM), jnp.int32)
    for i in range(rows):
        length_of = jnp.where(slot == i, lengths[i], length_of)
    lane = lax.broadcasted_iota(jnp.int32, (rows, HEAD_DIM), 1)
    half = HEAD_DIM // 2
    step = lax.rem(lane, half).astype(jnp.float32)
    phases = length_of.astype(jnp.float32) * jnp.exp(-math.log(THETA) * step / half)
    sine = jnp.sin(phases)
    return jnp.cos(phases), jnp.where(lane < half, -sine, sine), length_of


def attend_all(count, parts, cosine, sine, lengths, *refs):
    pairs = (count - 1) // 2
    blocks, (sums, other_sums, keys, values) = refs[:count], refs[count : count + 4]
    refs = refs[count + 4 :]
    whole, outs, (scores_of, probs_of) = refs[0], refs[1 : parts + 1], refs[parts + 1 :]
    rows, cache = keys.shape[:2]
    low = lax.rem(lax.axis_index("col"), pairs)
    width = GROUP_WIDTH
    squares = sums[...].astype(jnp.float32) + other_sums[...].astype(jnp.float32)
    scale = lax.rsqrt(jnp.sum(squares, axis=1, keepdims=True) / D + EPSILON)
    factor = HEAD_DIM ** (-0.5)
    cosines, sines, length_of = cosine[...], sine[...], lengths[:, :1]
    lane = lax.broadcasted_iota(jnp.int32, (SLOTS, SLOTS * cache), 1)
    slot = lax.broadcasted_iota(jnp.int32, (SLOTS, SLOTS * cache), 0)
    position = lane - slot * cache
    runs = [slice(start, start + SLOTS) for start in range(0, rows, SLOTS)]
    filled = [(position >= 0) & (position < length_of[part]) for part in runs]
    own, new_values, own_probs = [], [], []
    for pair in range(pairs):
        total = total_of(blocks, pair)
        total = (total * scale).astype(jnp.bfloat16).astype(jnp.float32)
        heads = [total[:, h * HEAD_DIM : (h + 1) * HEAD_DIM] for h in range(GROUP + 2)]
        queries = [
            rotated(head, cosines, sines).astype(jnp.bfloat16).astype(jnp.float32)
            for head in heads[:GROUP]
        ]
        new_key = rotated(heads[GROUP], cosines, sines).astype(jnp.bfloat16).astype(jnp.float32)
        new_values.append(heads[GROUP + 1])
        own.append([jnp.sum(query * new_key, axis=1, keepdims=True) * factor for query in queries])
        lanes = pl.ds(pl.multiple_of((low ^ pair) * HEAD_DIM, HEAD_DIM), HEAD_DIM)
        for run, part in enumerate(runs):
            query = jnp.concatenate([head[part] for head in queries], axis=0)
            key = keys[part, :, lanes].reshape(SLOTS * cache, HEAD_DIM)
            scores_of[pair, run] = lax.dot_general(
                query.astype(jnp.bfloat16),
                key,
                (((1,), (1,)), ((), ())),
                preferred_element_type=jnp.float32,
            )
    for pair in range(pairs):
        for run, part in enumerate(runs):
            scores = (scores_of[pair, run] * factor).reshape(GROUP, SLOTS, SLOTS * cache)
            scores = jnp.where(filled[run][None], scores, -1e30)
            own_score = jnp.concatenate([head[part] for head in own[pair]], axis=0).reshape(
                GROUP, SLOTS, 1
            )
            highest = jnp.maximum(jnp.max(scores, axis=2, keepdims=True), own_score)
            weights = jnp.exp(scores - highest)
            own_weight = jnp.exp(own_score - highest)
            inverse = 1.0 / (jnp.sum(weights, axis=2, keepdims=True) + own_weight)
            probs = (weights * inverse).astype(jnp.bfloat16)
            probs_of[pair, run] = probs.reshape(GROUP * SLOTS, SLOTS * cache)
            own_probs.append((own_weight * inverse).astype(jnp.bfloat16).astype(jnp.float32))
    for pair in range(pairs):
        lanes = pl.ds(pl.multiple_of((low ^ pair) * HEAD_DIM, HEAD_DIM), HEAD_DIM)
        results = []
        for run, part in enumerate(runs):
            value = values[part, :, lanes].reshape(SLOTS * cache, HEAD_DIM)
            mixed = jnp.dot(probs_of[pair, run], value, preferred_element_type=jnp.float32)
            own_prob = own_probs[pair * len(runs) + run]
            results.append(
                mixed.reshape(GROUP, SLOTS, HEAD_DIM) + own_prob * new_values[pair][part][None]
            )
        for head in range(GROUP):
            at = pl.multiple_of((low ^ pair) * OUT_WIDTH + head * HEAD_DIM, HEAD_DIM)
            size = len(results) // parts
            for i, out in enumerate(outs):
                joined = jnp.concatenate(
                    [result[head] for result in results[i * size : (i + 1) * size]], axis=0
                )
                joined = joined.astype(jnp.bfloat16)
                out[:, pl.ds(at, HEAD_DIM)] = joined
                run = slice(i * joined.shape[0], (i + 1) * joined.shape[0])
                whole[run, pl.ds(at, HEAD_DIM)] = joined


def sum_kernel(count, hidden, attended, *refs):
    blocks, (keep, send) = refs[:count], refs[count:]
    rows, width = blocks[0].shape
    pairs = keep.shape[1] // width
    side = lax.axis_index("side")
    low = lax.rem(lax.axis_index("col"), pairs)
    for pair in range(pairs):
        column = low ^ pair
        total = total_of(blocks, pair)
        at = pl.ds(pl.multiple_of((2 * column + side) * width, width), width)
        hidden_out = (hidden[:, at].astype(jnp.float32) + total).astype(jnp.bfloat16)
        at = pl.ds(pl.multiple_of(column * width, width), width)
        attention = attended[:, at]
        keep[:, at] = jnp.where(side == 0, hidden_out, attention)
        send[:, at] = jnp.where(side == 0, attention, hidden_out)


def join_kernel(keep, received, out, sems):
    side = lax.axis_index("side")
    width = OUT_WIDTH
    copies = []
    for j in range(keep.shape[1] // width):
        part = slice(j * width, (j + 1) * width)
        for ref, core in ((keep, side), (received, 1 - side)):
            at = pl.ds(pl.multiple_of((2 * j + core) * width, width), width)
            copies.append((ref.at[:, part], out.at[0, :, at]))
    run_copies(copies, sems)


def paired_plan(
    hidden_in, norm_gain, qkv_weight, out_weight, key_cache, value_cache, cache_lengths, slot_request
):
    col_count, row_count = lax.axis_size("col"), lax.axis_size("row")
    pairs = col_count // row_count
    side = lax.axis_index("side")
    rows, depth = hidden_in.shape
    half = depth // 2
    cache = key_cache.shape[1]
    parts = 2
    piece = rows // parts

    own_part = lax.dynamic_slice_in_dim(hidden_in, side * half, half, 1)
    gain = norm_gain.reshape(depth // HEAD_DIM, HEAD_DIM)
    half_in, half_out = qkv_weight.shape[1] // 2, out_weight.shape[1] // 2
    total = rows * col_count
    square = (total, total)
    give_in, own_in, chosen_in = call(
        functools.partial(stage_in_kernel, col_count),
        [pltpu.VMEM((half, half_in), jnp.bfloat16)] * 2 + [struct(square)],
        [HBM, HBM],
        [VMEM] * 3,
        0,
        half * half_in * 4,
        [
            pltpu.VMEM(square, jnp.float32),
            pltpu.VMEM((total,), jnp.int32),
            pltpu.SemaphoreType.DMA((3,)),
        ],
    )(in_hbm(qkv_weight), in_hbm(slot_request))
    blocks = gathered(
        [own_part[i * piece : (i + 1) * piece] for i in range(parts)], "col"
    )
    table = struct((rows, HEAD_DIM), jnp.float32)
    give_out, key_part, value_part, *tables, chosen_out = call(
        functools.partial(stage_rest_kernel, col_count),
        [pltpu.VMEM((half, half_out), jnp.bfloat16)]
        + [pltpu.VMEM((rows, cache, pairs * HEAD_DIM), jnp.bfloat16)] * 2
        + [table, table, struct((rows, HEAD_DIM), jnp.int32), struct(square)],
        [SMEM, HBM, HBM, HBM, VMEM],
        [VMEM] * 7,
        0,
        half * half_out * 2 + 4 * rows * cache * pairs * HEAD_DIM,
        [pltpu.VMEM(square, jnp.float32), pltpu.SemaphoreType.DMA((3 * pairs,))],
    )(cache_lengths, in_hbm(out_weight), in_hbm(key_cache), in_hbm(value_cache), slot_request)
    products, sums = project(in_kernel, chosen_in, blocks, [gain], [give_in, own_in], HEAD_DIM)
    other_sums = moved(sums[0], "row", 1)
    products = spread(products, [other_sums])

    runs = (pairs, rows // SLOTS, GROUP * SLOTS, SLOTS * cache)
    attended, *attended_parts = call(
        functools.partial(attend_all, len(products), parts),
        [struct((rows, half))] + [struct((piece, half))] * parts,
        [VMEM] * (len(products) + 7),
        [VMEM] * (parts + 1),
        4 * rows * half * cache,
        0,
        [pltpu.VMEM(runs, jnp.float32), pltpu.VMEM(runs, jnp.bfloat16)],
    )(
        *tables,
        *products,
        *sums,
        other_sums,
        in_vmem(key_part),
        in_vmem(value_part),
    )

    own_out = call(
        stage_out_kernel,
        pltpu.VMEM((half, half_out), jnp.bfloat16),
        [HBM, HBM],
        VMEM,
        0,
        half * half_out * 2,
        [pltpu.SemaphoreType.DMA((pairs,))],
    )(in_hbm(out_weight), attended)
    products, _ = project(
        out_kernel, chosen_out, gathered(attended_parts, "col", attended), [], [give_out, own_out], 0
    )
    products = spread(products, [])
    keep, send = call(
        functools.partial(sum_kernel, len(products)),
        [struct((rows, half)), struct((rows, half))],
        [VMEM] * (2 + len(products)),
        [VMEM, VMEM],
        rows * depth * 4,
        rows * depth * 8,
    )(hidden_in, attended, *products)
    return call(
        join_kernel,
        struct((1, rows, depth)),
        [VMEM, VMEM],
        HBM,
        0,
        rows * depth * 4,
        [pltpu.SemaphoreType.DMA((2 * pairs,))],
    )(keep, moved(send, "side", 1))


def per_device(*args):
    hidden_in, _, qkv_weight, out_weight, key_cache = args[:5]
    col_count, row_count = lax.axis_size("col"), lax.axis_size("row")
    fits = (
        lax.axis_size("side") == 2
        and qkv_weight.shape[1] == 2 * GROUP_WIDTH
        and row_count == 2
        and col_count > row_count
        and col_count & (col_count - 1) == 0
        and hidden_in.shape[0] % 32 == 0
        and key_cache.shape[1] % 16 == 0
        and hidden_in.shape[1] == 2 * OUT_WIDTH * (col_count // row_count)
    )
    return paired_plan(*args) if fits else general_plan(*args)


def solution(mesh):
    placed = (
        P(("groups", "col"), "row"),
        P("row"),
        P("row", "col"),
        P("row", "col"),
        P(("groups", "col"), None, "row"),
        P(("groups", "col"), None, "row"),
        P(("groups", "col")),
        P("groups"),
    )
    return jax.shard_map(
        per_device,
        mesh=mesh,
        in_specs=placed,
        out_specs=P("side", ("groups", "col"), "row"),
        check_vma=False,
    )
```

```python
import functools
import math

import jax
import jax.numpy as jnp
from jax import lax
from jax.experimental import pallas as pl
from jax.experimental.pallas import tpu as pltpu
from jax.sharding import PartitionSpec as P

D = 8192
HEADS = 64
KV_HEADS = 8
HEAD_DIM = 128
QKV = 10240


EPSILON = 1e-05
THETA = 500000.0


def swapped(value, axis, bit):
    mask = 2**bit
    pairs = [(source, source ^ mask) for source in range(lax.axis_size(axis))]
    return lax.ppermute(value, axis, pairs)


def rope_tables(lengths, head_dim):
    half_dim = head_dim // 2
    inv_freq = jnp.exp(
        -jnp.log(jnp.float32(THETA)) * jnp.arange(half_dim, dtype=jnp.float32) / half_dim
    )
    phases = lengths.astype(jnp.float32)[:, None] * inv_freq[None, :]
    return (jnp.cos(phases), jnp.sin(phases))


def rotate(vector, cos_vals, sine_vals):
    half_dim = vector.shape[-1] // 2
    front_half = vector[..., :half_dim]
    back_half = vector[..., half_dim:]
    return jnp.concatenate(
        [
            front_half * cos_vals - back_half * sine_vals,
            back_half * cos_vals + front_half * sine_vals,
        ],
        axis=-1,
    )


def attend(packed, key_block, value_block, lengths):
    slot_count = packed.shape[0]
    cache_size = key_block.shape[1]
    groups = key_block.shape[2] // HEAD_DIM
    per_group = HEADS // KV_HEADS
    grouped = packed.reshape(slot_count, groups, per_group + 2, HEAD_DIM)
    cos_vals, sine_vals = rope_tables(lengths, HEAD_DIM)
    queries = rotate(
        grouped[:, :, :per_group].astype(jnp.float32),
        cos_vals[:, None, None, :],
        sine_vals[:, None, None, :],
    ).astype(jnp.bfloat16)
    new_keys = rotate(
        grouped[:, :, per_group].astype(jnp.float32), cos_vals[:, None, :], sine_vals[:, None, :]
    ).astype(jnp.bfloat16)
    new_values = grouped[:, :, per_group + 1]
    cache_keys = key_block.reshape(slot_count, cache_size, groups, HEAD_DIM)
    cache_values = value_block.reshape(slot_count, cache_size, groups, HEAD_DIM)
    factor = HEAD_DIM ** (-0.5)
    cache_scores = (
        jnp.einsum("sghd,slgd->sghl", queries, cache_keys, preferred_element_type=jnp.float32)
        * factor
    )
    own_scores = (
        jnp.einsum("sghd,sgd->sgh", queries, new_keys, preferred_element_type=jnp.float32) * factor
    )
    in_cache = lax.broadcasted_iota(jnp.int32, (slot_count, cache_size), 1) < lengths[:, None]
    cache_scores = jnp.where(in_cache[:, None, None, :], cache_scores, -1e30)
    row_max = jnp.maximum(jnp.max(cache_scores, axis=-1), own_scores)
    cache_exp = jnp.exp(cache_scores - row_max[..., None])
    own_exp = jnp.exp(own_scores - row_max)
    denominator = jnp.sum(cache_exp, axis=-1) + own_exp
    cache_weight = (cache_exp / denominator[..., None]).astype(jnp.bfloat16)
    own_weight = (own_exp / denominator).astype(jnp.bfloat16)
    combined = jnp.einsum(
        "sghl,slgd->sghd", cache_weight, cache_values, preferred_element_type=jnp.float32
    )
    combined = (
        combined
        + own_weight.astype(jnp.float32)[..., None] * new_values.astype(jnp.float32)[:, :, None, :]
    )
    return combined.astype(jnp.bfloat16).reshape(slot_count, groups * per_group * HEAD_DIM)


def general_plan(
    hidden_in,
    norm_gain,
    qkv_weight,
    out_weight,
    key_cache,
    value_cache,
    cache_lengths,
    slot_request,
):
    side_index = lax.axis_index("side")
    is_weight = side_index == 0
    col_count = lax.axis_size("col")
    row_count = lax.axis_size("row")
    group_cols = col_count // row_count
    in_half = qkv_weight.shape[1] // 2
    out_half = out_weight.shape[1] // 2
    residual = hidden_in.astype(jnp.float32)
    square_sums = lax.psum(jnp.sum(residual * residual, axis=1), "row")
    normed = (
        residual
        * lax.rsqrt(square_sums[:, None] / D + EPSILON)
        * norm_gain.astype(jnp.float32)[None, :]
    ).astype(jnp.bfloat16)
    in_weight = lax.dynamic_slice_in_dim(qkv_weight, side_index * in_half, in_half, 1)
    partial_in = jnp.dot(
        lax.all_gather(normed, "col", axis=0, tiled=True),
        in_weight,
        preferred_element_type=jnp.float32,
    )
    in_slots = jnp.take(partial_in, slot_request, axis=0)
    own_width = QKV // row_count
    summed = lax.psum(in_slots.astype(jnp.bfloat16), "row")
    spread = lax.all_to_all(summed, "col", split_axis=0, concat_axis=1, tiled=True)
    own_columns = lax.dynamic_slice_in_dim(
        spread.reshape(spread.shape[0], col_count, in_half),
        lax.axis_index("row") * group_cols,
        group_cols,
        1,
    )
    slot_half = key_cache.shape[0] // 2
    halves = lax.all_to_all(
        own_columns[:, :, None, :], "side", split_axis=0, concat_axis=2, tiled=True
    )
    arrived = halves.reshape(slot_half, own_width)
    first_slot = side_index * slot_half
    key_part = lax.dynamic_slice_in_dim(key_cache, first_slot, slot_half, 0)
    value_part = lax.dynamic_slice_in_dim(value_cache, first_slot, slot_half, 0)
    length_part = lax.dynamic_slice_in_dim(cache_lengths, first_slot, slot_half, 0)
    attended = attend(arrived, key_part, value_part, length_part)
    out_cols = lax.dynamic_slice_in_dim(out_weight, side_index * out_half, out_half, 1)
    collected = lax.all_gather(attended, ("col", "side"), axis=0, tiled=True)
    out_slots = jnp.dot(collected, out_cols, preferred_element_type=jnp.float32)
    inverse = jnp.argsort(slot_request)
    out_requests = jnp.take(out_slots, inverse, axis=0)
    spread_out = lax.all_to_all(
        out_requests.astype(jnp.bfloat16), "col", split_axis=0, concat_axis=1, tiled=True
    ).astype(out_requests.dtype)
    out_view = spread_out.reshape(spread_out.shape[0], col_count, out_half)
    summed_out = lax.psum_scatter(
        out_view.astype(jnp.bfloat16), "row", scatter_dimension=1, tiled=True
    ).astype(jnp.float32)
    req_rows = hidden_in.shape[0]
    residual_view = residual.reshape(req_rows, group_cols, 2, out_half)
    residual_half = lax.dynamic_index_in_dim(residual_view, side_index, 2, keepdims=False)
    own_hidden = (residual_half + summed_out).astype(jnp.bfloat16)
    payload = jnp.where(is_weight, attended, own_hidden.reshape(attended.shape))
    received = swapped(payload, "side", 0)
    hidden = jnp.stack([own_hidden, received.reshape(own_hidden.shape)], axis=2).reshape(
        req_rows, residual.shape[1]
    )
    attention_rows = jnp.concatenate([received, attended], axis=0)
    result = jnp.where(is_weight, hidden, attention_rows)
    return result[None]


GROUP = HEADS // KV_HEADS
GROUP_WIDTH = (GROUP + 2) * HEAD_DIM
OUT_WIDTH = GROUP * HEAD_DIM
SLOTS = 8
VMEM = pl.BlockSpec(memory_space=pltpu.VMEM)
SMEM = pl.BlockSpec(memory_space=pltpu.SMEM)
HBM = pl.BlockSpec(memory_space=pl.ANY)
MIB = 2**20


def call(kernel, out_shape, in_specs, out_specs, flops, size, scratch=(), limit=16):
    return pl.pallas_call(
        kernel,
        out_shape=out_shape,
        in_specs=in_specs,
        out_specs=out_specs,
        scratch_shapes=list(scratch),
        compiler_params=pltpu.CompilerParams(vmem_limit_bytes=limit * MIB),
        cost_estimate=pl.CostEstimate(flops=flops, bytes_accessed=size, transcendentals=0),
    )


def in_vmem(value):
    return pltpu.with_memory_space_constraint(value, pltpu.VMEM)


def in_hbm(value):
    return pltpu.with_memory_space_constraint(value, pltpu.HBM)


def struct(shape, dtype=jnp.bfloat16):
    return jax.ShapeDtypeStruct(shape, dtype)


def moved(value, axis, mask):
    pairs = [(source, source ^ mask) for source in range(lax.axis_size(axis))]
    return lax.ppermute(value, axis, pairs)


def started(copies, sems):
    copies = [
        pltpu.make_async_copy(source, target, sems.at[i])
        for i, (source, target) in enumerate(copies)
    ]
    for copy in copies:
        copy.start()
    return copies


def run_copies(copies, sems):
    for copy in started(copies, sems):
        copy.wait()


def position():
    return lax.axis_index("side"), lax.axis_index("col")


def rows_copy(weight, target, half):
    depth, width = target.shape
    rows = pl.ds(pl.multiple_of(lax.axis_index("side") * depth, depth), depth)
    columns = pl.ds(pl.multiple_of(half * width, width), width)
    return weight.at[rows, columns], target


def stage_in_kernel(blocks, weight, slots, give_part, chosen, scratch, slot_part, sems):
    side, col = position()
    slots_copy, copy = started(
        [(slots, slot_part), rows_copy(weight, give_part, 1 - side)], sems
    )
    slots_copy.wait()
    chosen[...] = one_hot(slot_part, scratch, blocks, col, col).astype(jnp.bfloat16)
    copy.wait()


def head_copies(weight, target, half):
    width = target.shape[1]
    columns = pl.ds(pl.multiple_of(half * width, width), width)
    copies = []
    for j in range(target.shape[0] // OUT_WIDTH):
        row = pl.multiple_of((2 * j + lax.axis_index("side")) * OUT_WIDTH, OUT_WIDTH)
        copies.append(
            (
                weight.at[pl.ds(row, OUT_WIDTH), columns],
                target.at[pl.ds(j * OUT_WIDTH, OUT_WIDTH), :],
            )
        )
    return copies


def stage_rest_kernel(blocks, lengths, weight, keys, values, slots, *refs):
    target, key_part, value_part, cosine, sine, length_of, chosen, scratch, sems = refs
    side, col = position()
    copies = []
    for j in range(key_part.shape[2] // HEAD_DIM):
        lane = pl.multiple_of((2 * j + side) * HEAD_DIM, HEAD_DIM)
        for cache, part in ((keys, key_part), (values, value_part)):
            copies.append(
                (
                    cache.at[:, :, pl.ds(lane, HEAD_DIM)],
                    part.at[:, :, pl.ds(j * HEAD_DIM, HEAD_DIM)],
                )
            )
    copies = started(copies + head_copies(weight, target, 1 - side), sems)
    cosine[...], sine[...], length_of[...] = rope(lengths, cosine.shape[0])
    chosen[...] = one_hot(slots, scratch, blocks, col, col).T.astype(jnp.bfloat16)
    for copy in copies:
        copy.wait()


def stage_out_kernel(weight, attended, own_part, sems):
    run_copies(head_copies(weight, own_part, lax.axis_index("side")), sems)


def one_hot(slots, scratch, blocks, slot_base, request_base):
    total = slots.shape[0]
    rows = total // blocks
    index = lax.broadcasted_iota(jnp.int32, (total, total), 0)
    request = (lax.div(index, rows) ^ request_base) * rows + lax.rem(index, rows)
    scratch[...] = jnp.where(slots[...].reshape(1, total) == request, 1.0, 0.0).T
    parts = [
        scratch[pl.ds(pl.multiple_of((slot_base ^ i) * rows, rows), rows), :]
        for i in range(blocks)
    ]
    return jnp.concatenate(parts, axis=0)


def pieces(sums):
    high = sums.astype(jnp.bfloat16).astype(jnp.float32)
    middle = (sums - high).astype(jnp.bfloat16).astype(jnp.float32)
    low = sums - high - middle
    lane = lax.broadcasted_iota(jnp.int32, (sums.shape[0], HEAD_DIM), 1)
    parts = jnp.where(lane == 0, high, jnp.where(lane == 1, middle, low))
    return jnp.where(lane < 3, parts, 0.0).astype(jnp.bfloat16)


def dot_columns(rows, weight, out):
    size, width = weight.shape[1], 512
    for start in range(0, size, width):
        part = slice(start, min(start + width, size))
        product = jnp.dot(rows, weight[:, part], preferred_element_type=jnp.float32)
        out[:, part] = product.astype(out.dtype)


def in_kernel(count, chosen, *refs):
    pieces_in, (gain, weight, give, permuted) = refs[:count], refs[count:]
    depth = pieces_in[0].shape[1]
    half = weight.shape[1]
    runs = depth // HEAD_DIM
    first = pl.multiple_of(lax.axis_index("side") * runs, runs)
    gains = gain[pl.ds(first, runs), :].astype(jnp.float32)
    values = jnp.concatenate([piece[...].astype(jnp.float32) for piece in pieces_in], axis=0)
    scaled = jnp.concatenate(
        [
            values[:, i * HEAD_DIM : (i + 1) * HEAD_DIM] * gains[i : i + 1, :]
            for i in range(runs)
        ],
        axis=1,
    )
    sums = pieces(jnp.sum(values * values, axis=1, keepdims=True))
    order = jnp.dot(
        chosen[...], scaled.astype(jnp.bfloat16), preferred_element_type=jnp.float32
    ).astype(jnp.bfloat16)
    permuted[...] = order
    own_sums = jnp.dot(chosen[...], sums, preferred_element_type=jnp.float32)
    give[:, half:] = own_sums.astype(jnp.bfloat16)
    dot_columns(order, weight, give)


def out_kernel(count, chosen, *refs):
    pieces_in, (_, weight, give, permuted) = refs[:count], refs[count:]
    values = jnp.concatenate([piece[...] for piece in pieces_in], axis=0)
    order = jnp.dot(chosen[...], values, preferred_element_type=jnp.float32).astype(jnp.bfloat16)
    permuted[...] = order
    dot_columns(order, weight, give)


def at_home():
    pairs = lax.axis_size("col") // lax.axis_size("row")
    return lax.axis_index("row") == lax.div(lax.axis_index("col"), pairs)


def merge_kernel(count, own, given, received, *outs):
    rows = outs[0].shape[0]
    half = own.shape[1]
    more = given.shape[1] - half
    pairs = count // 2

    def write(out, first):
        first = first if isinstance(first, int) else pl.multiple_of(first, rows)
        part = pl.ds(first, rows)
        total = own[part, :] + received[part, :half].astype(jnp.float32)
        out[...] = total.astype(jnp.bfloat16)

    write(outs[0], 0)
    write(outs[1], pairs * rows)
    home = at_home()
    for pair in range(1, pairs):
        write(outs[2 * pair], jnp.where(home, pairs + pair, pair) * rows)
        write(outs[2 * pair + 1], jnp.where(home, pair, pairs + pair) * rows)
    for out in outs[count:]:
        lanes = slice(half, half + more // 2)
        out[...] = jnp.concatenate([given[:rows, lanes], received[:rows, lanes]], axis=1)


def own_stream_kernel(permuted, weight, own, chunks, sems):
    count, depth, width = chunks.shape
    side = lax.axis_index("side")
    rows = pl.ds(pl.multiple_of(side * depth, depth), depth)
    copies = []
    for i in range(count):
        first = pl.multiple_of((side * count + i) * width, width)
        copies.append((weight.at[rows, pl.ds(first, width)], chunks.at[i]))
    for i, copy in enumerate(started(copies, sems)):
        copy.wait()
        own[:, i * width : (i + 1) * width] = jnp.dot(
            permuted[...], chunks[i], preferred_element_type=jnp.float32
        )


def own_kernel(permuted, weight, own):
    dot_columns(permuted[...], weight, own)


def project(kernel, chosen, pieces_in, extra, give_weight, own_weight, more):
    count = lax.axis_size("col")
    parts = len(pieces_in)
    depth = pieces_in[0].shape[1]
    rows = sum(part.shape[0] for part in pieces_in)
    half = give_weight.shape[1]
    flops = 2 * rows * depth * half
    give, permuted = call(
        functools.partial(kernel, parts),
        [struct((rows, half + more)), struct((rows, depth))],
        [VMEM] * (parts + len(extra) + 2),
        [VMEM, VMEM],
        flops,
        depth * half * 2,
    )(chosen, *pieces_in, *extra, in_vmem(give_weight))
    received = moved(give, "side", 1)
    staged = own_weight.shape == give_weight.shape
    width = 256
    own = call(
        own_kernel if staged else own_stream_kernel,
        struct((rows, half), jnp.float32),
        [VMEM, VMEM if staged else HBM],
        VMEM,
        flops,
        depth * half * 2,
        []
        if staged
        else [
            pltpu.VMEM((half // width, depth, width), jnp.bfloat16),
            pltpu.SemaphoreType.DMA((half // width,)),
        ],
    )(permuted, in_vmem(own_weight) if staged else in_hbm(own_weight))
    outs = [struct((rows // count, half))] * count
    if more:
        outs = outs + [struct((rows // count, more))]
    merged = call(
        functools.partial(merge_kernel, count),
        outs,
        [VMEM] * 3,
        [VMEM] * len(outs),
        rows * half,
        rows * half * 8,
    )(own, give, received)
    return merged[:count], merged[count:]


def gathered(parts, axis, whole=None):
    blocks = {0: parts}
    mask = lax.axis_size(axis) // 2
    while mask:
        blocks |= {
            known | mask: [
                moved(part, axis, mask)
                for part in ([whole] if mask == 1 and known == 0 and whole is not None else block)
            ]
            for known, block in blocks.items()
        }
        mask //= 2
    if whole is not None:
        blocks[0] = [whole]
    return [part for i in sorted(blocks) for part in blocks[i]]


def choose_kernel(own, passed, *refs):
    out = refs[-1]
    out[...] = jnp.where(at_home(), passed[...], own[...])


def direct(value, far, pair):
    pairs = lax.axis_size("col") // 2
    moves = []
    for col in range(2 * pairs):
        for row in range(2):
            home = row == col // pairs
            target = col ^ pair ^ (pairs if home == far else 0)
            moves.append((2 * col + row, 2 * target + (row if home else 1 - row)))
    return lax.ppermute(value, ("col", "row"), moves)


def spread(products, ready):
    own, passed, *rest = products
    pairs = len(products) // 2
    passed = moved(passed, "col", pairs)
    blocks = []
    for pair in range(1, pairs):
        blocks += [
            direct(rest[2 * pair - 2], True, pair),
            direct(rest[2 * pair - 1], False, pair),
        ]
    crossing = call(
        choose_kernel,
        struct(own.shape),
        [VMEM] * 2 + [HBM] * len(ready),
        VMEM,
        0,
        own.size * 4,
    )(own, passed, *ready)
    return [passed, *blocks, own, moved(crossing, "row", 1)]


def total_of(blocks, pair):
    if pair > 0:
        first, second = blocks[2 * pair - 1][...], blocks[2 * pair][...]
    else:
        passed, own, crossed = blocks[0], blocks[-2], blocks[-1]
        first, second = jnp.where(at_home(), own[...], passed[...]), crossed[...]
    return first.astype(jnp.float32) + second.astype(jnp.float32)


def rotated(vector, cosine, sine):
    return vector * cosine + pltpu.roll(vector, HEAD_DIM // 2, 1) * sine


def rope(lengths, rows):
    slot = lax.broadcasted_iota(jnp.int32, (rows, HEAD_DIM), 0)
    length_of = jnp.zeros((rows, HEAD_DIM), jnp.int32)
    for i in range(rows):
        length_of = jnp.where(slot == i, lengths[i], length_of)
    lane = lax.broadcasted_iota(jnp.int32, (rows, HEAD_DIM), 1)
    half = HEAD_DIM // 2
    step = lax.rem(lane, half).astype(jnp.float32)
    phases = length_of.astype(jnp.float32) * jnp.exp(-math.log(THETA) * step / half)
    sine = jnp.sin(phases)
    return jnp.cos(phases), jnp.where(lane < half, -sine, sine), length_of


def attend_all(count, parts, cosine, sine, lengths, *refs):
    pairs = (count - 1) // 2
    blocks, (sums, other_sums, keys, values) = refs[:count], refs[count : count + 4]
    refs = refs[count + 4 :]
    whole, outs, (scores_of, probs_of) = refs[0], refs[1 : parts + 1], refs[parts + 1 :]
    rows, cache = keys.shape[:2]
    low = lax.rem(lax.axis_index("col"), pairs)
    width = GROUP_WIDTH
    squares = sums[...].astype(jnp.float32) + other_sums[...].astype(jnp.float32)
    scale = lax.rsqrt(jnp.sum(squares, axis=1, keepdims=True) / D + EPSILON)
    factor = HEAD_DIM ** (-0.5)
    cosines, sines, length_of = cosine[...], sine[...], lengths[:, :1]
    lane = lax.broadcasted_iota(jnp.int32, (SLOTS, SLOTS * cache), 1)
    slot = lax.broadcasted_iota(jnp.int32, (SLOTS, SLOTS * cache), 0)
    position = lane - slot * cache
    runs = [slice(start, start + SLOTS) for start in range(0, rows, SLOTS)]
    filled = [(position >= 0) & (position < length_of[part]) for part in runs]
    own, new_values, own_probs = [], [], []
    for pair in range(pairs):
        total = total_of(blocks, pair)
        total = (total * scale).astype(jnp.bfloat16).astype(jnp.float32)
        heads = [total[:, h * HEAD_DIM : (h + 1) * HEAD_DIM] for h in range(GROUP + 2)]
        queries = [
            rotated(head, cosines, sines).astype(jnp.bfloat16).astype(jnp.float32)
            for head in heads[:GROUP]
        ]
        new_key = rotated(heads[GROUP], cosines, sines).astype(jnp.bfloat16).astype(jnp.float32)
        new_values.append(heads[GROUP + 1])
        own.append([jnp.sum(query * new_key, axis=1, keepdims=True) * factor for query in queries])
        lanes = pl.ds(pl.multiple_of((low ^ pair) * HEAD_DIM, HEAD_DIM), HEAD_DIM)
        for run, part in enumerate(runs):
            query = jnp.concatenate([head[part] for head in queries], axis=0)
            key = keys[part, :, lanes].reshape(SLOTS * cache, HEAD_DIM)
            scores_of[pair, run] = lax.dot_general(
                query.astype(jnp.bfloat16),
                key,
                (((1,), (1,)), ((), ())),
                preferred_element_type=jnp.float32,
            )
    for pair in range(pairs):
        for run, part in enumerate(runs):
            scores = (scores_of[pair, run] * factor).reshape(GROUP, SLOTS, SLOTS * cache)
            scores = jnp.where(filled[run][None], scores, -1e30)
            own_score = jnp.concatenate([head[part] for head in own[pair]], axis=0).reshape(
                GROUP, SLOTS, 1
            )
            highest = jnp.maximum(jnp.max(scores, axis=2, keepdims=True), own_score)
            weights = jnp.exp(scores - highest)
            own_weight = jnp.exp(own_score - highest)
            inverse = 1.0 / (jnp.sum(weights, axis=2, keepdims=True) + own_weight)
            probs = (weights * inverse).astype(jnp.bfloat16)
            probs_of[pair, run] = probs.reshape(GROUP * SLOTS, SLOTS * cache)
            own_probs.append((own_weight * inverse).astype(jnp.bfloat16).astype(jnp.float32))
    for pair in range(pairs):
        lanes = pl.ds(pl.multiple_of((low ^ pair) * HEAD_DIM, HEAD_DIM), HEAD_DIM)
        results = []
        for run, part in enumerate(runs):
            value = values[part, :, lanes].reshape(SLOTS * cache, HEAD_DIM)
            mixed = jnp.dot(probs_of[pair, run], value, preferred_element_type=jnp.float32)
            own_prob = own_probs[pair * len(runs) + run]
            results.append(
                mixed.reshape(GROUP, SLOTS, HEAD_DIM) + own_prob * new_values[pair][part][None]
            )
        for head in range(GROUP):
            at = pl.multiple_of((low ^ pair) * OUT_WIDTH + head * HEAD_DIM, HEAD_DIM)
            size = len(results) // parts
            for i, out in enumerate(outs):
                joined = jnp.concatenate(
                    [result[head] for result in results[i * size : (i + 1) * size]], axis=0
                )
                joined = joined.astype(jnp.bfloat16)
                out[:, pl.ds(at, HEAD_DIM)] = joined
                run = slice(i * joined.shape[0], (i + 1) * joined.shape[0])
                whole[run, pl.ds(at, HEAD_DIM)] = joined


def sum_kernel(count, hidden, attended, *refs):
    blocks, (keep, send) = refs[:count], refs[count:]
    rows, width = blocks[0].shape
    pairs = keep.shape[1] // width
    side = lax.axis_index("side")
    low = lax.rem(lax.axis_index("col"), pairs)
    for pair in range(pairs):
        column = low ^ pair
        total = total_of(blocks, pair)
        at = pl.ds(pl.multiple_of((2 * column + side) * width, width), width)
        hidden_out = (hidden[:, at].astype(jnp.float32) + total).astype(jnp.bfloat16)
        at = pl.ds(pl.multiple_of(column * width, width), width)
        attention = attended[:, at]
        keep[:, at] = jnp.where(side == 0, hidden_out, attention)
        send[:, at] = jnp.where(side == 0, attention, hidden_out)


def join_kernel(keep, received, out, sems):
    side = lax.axis_index("side")
    width = OUT_WIDTH
    copies = []
    for j in range(keep.shape[1] // width):
        part = slice(j * width, (j + 1) * width)
        for ref, core in ((keep, side), (received, 1 - side)):
            at = pl.ds(pl.multiple_of((2 * j + core) * width, width), width)
            copies.append((ref.at[:, part], out.at[0, :, at]))
    run_copies(copies, sems)


def paired_plan(
    hidden_in, norm_gain, qkv_weight, out_weight, key_cache, value_cache, cache_lengths, slot_request
):
    col_count, row_count = lax.axis_size("col"), lax.axis_size("row")
    pairs = col_count // row_count
    side = lax.axis_index("side")
    rows, depth = hidden_in.shape
    half = depth // 2
    cache = key_cache.shape[1]
    parts = 2
    piece = rows // parts

    own_part = lax.dynamic_slice_in_dim(hidden_in, side * half, half, 1)
    gain = norm_gain.reshape(depth // HEAD_DIM, HEAD_DIM)
    half_in, half_out = qkv_weight.shape[1] // 2, out_weight.shape[1] // 2
    total = rows * col_count
    square = (total, total)
    give_in, chosen_in = call(
        functools.partial(stage_in_kernel, col_count),
        [pltpu.VMEM((half, half_in), jnp.bfloat16), struct(square)],
        [HBM, HBM],
        [VMEM] * 2,
        0,
        half * half_in * 2,
        [
            pltpu.VMEM(square, jnp.float32),
            pltpu.VMEM((total,), jnp.int32),
            pltpu.SemaphoreType.DMA((2,)),
        ],
    )(in_hbm(qkv_weight), in_hbm(slot_request))
    blocks = gathered(
        [own_part[i * piece : (i + 1) * piece] for i in range(parts)], "col"
    )
    table = struct((rows, HEAD_DIM), jnp.float32)
    give_out, key_part, value_part, *tables, chosen_out = call(
        functools.partial(stage_rest_kernel, col_count),
        [pltpu.VMEM((half, half_out), jnp.bfloat16)]
        + [pltpu.VMEM((rows, cache, pairs * HEAD_DIM), jnp.bfloat16)] * 2
        + [table, table, struct((rows, HEAD_DIM), jnp.int32), struct(square)],
        [SMEM, HBM, HBM, HBM, VMEM],
        [VMEM] * 7,
        0,
        half * half_out * 2 + 4 * rows * cache * pairs * HEAD_DIM,
        [pltpu.VMEM(square, jnp.float32), pltpu.SemaphoreType.DMA((3 * pairs,))],
    )(cache_lengths, in_hbm(out_weight), in_hbm(key_cache), in_hbm(value_cache), slot_request)
    products, sums = project(in_kernel, chosen_in, blocks, [gain], give_in, qkv_weight, HEAD_DIM)
    other_sums = moved(sums[0], "row", 1)
    products = spread(products, [other_sums])

    runs = (pairs, rows // SLOTS, GROUP * SLOTS, SLOTS * cache)
    attended, *attended_parts = call(
        functools.partial(attend_all, len(products), parts),
        [struct((rows, half))] + [struct((piece, half))] * parts,
        [VMEM] * (len(products) + 7),
        [VMEM] * (parts + 1),
        4 * rows * half * cache,
        0,
        [pltpu.VMEM(runs, jnp.float32), pltpu.VMEM(runs, jnp.bfloat16)],
    )(
        *tables,
        *products,
        *sums,
        other_sums,
        in_vmem(key_part),
        in_vmem(value_part),
    )

    own_out = call(
        stage_out_kernel,
        pltpu.VMEM((half, half_out), jnp.bfloat16),
        [HBM, HBM],
        VMEM,
        0,
        half * half_out * 2,
        [pltpu.SemaphoreType.DMA((pairs,))],
    )(in_hbm(out_weight), attended)
    products, _ = project(
        out_kernel, chosen_out, gathered(attended_parts, "col", attended), [in_vmem(own_out)], give_out, own_out, 0
    )
    products = spread(products, [])
    keep, send = call(
        functools.partial(sum_kernel, len(products)),
        [struct((rows, half)), struct((rows, half))],
        [VMEM] * (2 + len(products)),
        [VMEM, VMEM],
        rows * depth * 4,
        rows * depth * 8,
    )(hidden_in, attended, *products)
    return call(
        join_kernel,
        struct((1, rows, depth)),
        [VMEM, VMEM],
        HBM,
        0,
        rows * depth * 4,
        [pltpu.SemaphoreType.DMA((2 * pairs,))],
    )(keep, moved(send, "side", 1))


def per_device(*args):
    hidden_in, _, qkv_weight, out_weight, key_cache = args[:5]
    col_count, row_count = lax.axis_size("col"), lax.axis_size("row")
    fits = (
        lax.axis_size("side") == 2
        and qkv_weight.shape[1] == 2 * GROUP_WIDTH
        and row_count == 2
        and col_count > row_count
        and col_count & (col_count - 1) == 0
        and hidden_in.shape[0] % 32 == 0
        and GROUP_WIDTH % 256 == 0
        and key_cache.shape[1] % 16 == 0
        and hidden_in.shape[1] == 2 * OUT_WIDTH * (col_count // row_count)
    )
    return paired_plan(*args) if fits else general_plan(*args)


def solution(mesh):
    placed = (
        P(("groups", "col"), "row"),
        P("row"),
        P("row", "col"),
        P("row", "col"),
        P(("groups", "col"), None, "row"),
        P(("groups", "col"), None, "row"),
        P(("groups", "col")),
        P("groups"),
    )
    return jax.shard_map(
        per_device,
        mesh=mesh,
        in_specs=placed,
        out_specs=P("side", ("groups", "col"), "row"),
        check_vma=False,
    )
```

```python
import functools
import math

import jax
import jax.numpy as jnp
from jax import lax
from jax.experimental import pallas as pl
from jax.experimental.pallas import tpu as pltpu
from jax.sharding import PartitionSpec as P

D = 8192
HEADS = 64
KV_HEADS = 8
HEAD_DIM = 128
QKV = 10240


EPSILON = 1e-05
THETA = 500000.0


def swapped(value, axis, bit):
    mask = 2**bit
    pairs = [(source, source ^ mask) for source in range(lax.axis_size(axis))]
    return lax.ppermute(value, axis, pairs)


def rope_tables(lengths, head_dim):
    half_dim = head_dim // 2
    inv_freq = jnp.exp(
        -jnp.log(jnp.float32(THETA)) * jnp.arange(half_dim, dtype=jnp.float32) / half_dim
    )
    phases = lengths.astype(jnp.float32)[:, None] * inv_freq[None, :]
    return (jnp.cos(phases), jnp.sin(phases))


def rotate(vector, cos_vals, sine_vals):
    half_dim = vector.shape[-1] // 2
    front_half = vector[..., :half_dim]
    back_half = vector[..., half_dim:]
    return jnp.concatenate(
        [
            front_half * cos_vals - back_half * sine_vals,
            back_half * cos_vals + front_half * sine_vals,
        ],
        axis=-1,
    )


def attend(packed, key_block, value_block, lengths):
    slot_count = packed.shape[0]
    cache_size = key_block.shape[1]
    groups = key_block.shape[2] // HEAD_DIM
    per_group = HEADS // KV_HEADS
    grouped = packed.reshape(slot_count, groups, per_group + 2, HEAD_DIM)
    cos_vals, sine_vals = rope_tables(lengths, HEAD_DIM)
    queries = rotate(
        grouped[:, :, :per_group].astype(jnp.float32),
        cos_vals[:, None, None, :],
        sine_vals[:, None, None, :],
    ).astype(jnp.bfloat16)
    new_keys = rotate(
        grouped[:, :, per_group].astype(jnp.float32), cos_vals[:, None, :], sine_vals[:, None, :]
    ).astype(jnp.bfloat16)
    new_values = grouped[:, :, per_group + 1]
    cache_keys = key_block.reshape(slot_count, cache_size, groups, HEAD_DIM)
    cache_values = value_block.reshape(slot_count, cache_size, groups, HEAD_DIM)
    factor = HEAD_DIM ** (-0.5)
    cache_scores = (
        jnp.einsum("sghd,slgd->sghl", queries, cache_keys, preferred_element_type=jnp.float32)
        * factor
    )
    own_scores = (
        jnp.einsum("sghd,sgd->sgh", queries, new_keys, preferred_element_type=jnp.float32) * factor
    )
    in_cache = lax.broadcasted_iota(jnp.int32, (slot_count, cache_size), 1) < lengths[:, None]
    cache_scores = jnp.where(in_cache[:, None, None, :], cache_scores, -1e30)
    row_max = jnp.maximum(jnp.max(cache_scores, axis=-1), own_scores)
    cache_exp = jnp.exp(cache_scores - row_max[..., None])
    own_exp = jnp.exp(own_scores - row_max)
    denominator = jnp.sum(cache_exp, axis=-1) + own_exp
    cache_weight = (cache_exp / denominator[..., None]).astype(jnp.bfloat16)
    own_weight = (own_exp / denominator).astype(jnp.bfloat16)
    combined = jnp.einsum(
        "sghl,slgd->sghd", cache_weight, cache_values, preferred_element_type=jnp.float32
    )
    combined = (
        combined
        + own_weight.astype(jnp.float32)[..., None] * new_values.astype(jnp.float32)[:, :, None, :]
    )
    return combined.astype(jnp.bfloat16).reshape(slot_count, groups * per_group * HEAD_DIM)


def general_plan(
    hidden_in,
    norm_gain,
    qkv_weight,
    out_weight,
    key_cache,
    value_cache,
    cache_lengths,
    slot_request,
):
    side_index = lax.axis_index("side")
    is_weight = side_index == 0
    col_count = lax.axis_size("col")
    row_count = lax.axis_size("row")
    group_cols = col_count // row_count
    in_half = qkv_weight.shape[1] // 2
    out_half = out_weight.shape[1] // 2
    residual = hidden_in.astype(jnp.float32)
    square_sums = lax.psum(jnp.sum(residual * residual, axis=1), "row")
    normed = (
        residual
        * lax.rsqrt(square_sums[:, None] / D + EPSILON)
        * norm_gain.astype(jnp.float32)[None, :]
    ).astype(jnp.bfloat16)
    in_weight = lax.dynamic_slice_in_dim(qkv_weight, side_index * in_half, in_half, 1)
    partial_in = jnp.dot(
        lax.all_gather(normed, "col", axis=0, tiled=True),
        in_weight,
        preferred_element_type=jnp.float32,
    )
    in_slots = jnp.take(partial_in, slot_request, axis=0)
    own_width = QKV // row_count
    summed = lax.psum(in_slots.astype(jnp.bfloat16), "row")
    spread = lax.all_to_all(summed, "col", split_axis=0, concat_axis=1, tiled=True)
    own_columns = lax.dynamic_slice_in_dim(
        spread.reshape(spread.shape[0], col_count, in_half),
        lax.axis_index("row") * group_cols,
        group_cols,
        1,
    )
    slot_half = key_cache.shape[0] // 2
    halves = lax.all_to_all(
        own_columns[:, :, None, :], "side", split_axis=0, concat_axis=2, tiled=True
    )
    arrived = halves.reshape(slot_half, own_width)
    first_slot = side_index * slot_half
    key_part = lax.dynamic_slice_in_dim(key_cache, first_slot, slot_half, 0)
    value_part = lax.dynamic_slice_in_dim(value_cache, first_slot, slot_half, 0)
    length_part = lax.dynamic_slice_in_dim(cache_lengths, first_slot, slot_half, 0)
    attended = attend(arrived, key_part, value_part, length_part)
    out_cols = lax.dynamic_slice_in_dim(out_weight, side_index * out_half, out_half, 1)
    collected = lax.all_gather(attended, ("col", "side"), axis=0, tiled=True)
    out_slots = jnp.dot(collected, out_cols, preferred_element_type=jnp.float32)
    inverse = jnp.argsort(slot_request)
    out_requests = jnp.take(out_slots, inverse, axis=0)
    spread_out = lax.all_to_all(
        out_requests.astype(jnp.bfloat16), "col", split_axis=0, concat_axis=1, tiled=True
    ).astype(out_requests.dtype)
    out_view = spread_out.reshape(spread_out.shape[0], col_count, out_half)
    summed_out = lax.psum_scatter(
        out_view.astype(jnp.bfloat16), "row", scatter_dimension=1, tiled=True
    ).astype(jnp.float32)
    req_rows = hidden_in.shape[0]
    residual_view = residual.reshape(req_rows, group_cols, 2, out_half)
    residual_half = lax.dynamic_index_in_dim(residual_view, side_index, 2, keepdims=False)
    own_hidden = (residual_half + summed_out).astype(jnp.bfloat16)
    payload = jnp.where(is_weight, attended, own_hidden.reshape(attended.shape))
    received = swapped(payload, "side", 0)
    hidden = jnp.stack([own_hidden, received.reshape(own_hidden.shape)], axis=2).reshape(
        req_rows, residual.shape[1]
    )
    attention_rows = jnp.concatenate([received, attended], axis=0)
    result = jnp.where(is_weight, hidden, attention_rows)
    return result[None]


GROUP = HEADS // KV_HEADS
GROUP_WIDTH = (GROUP + 2) * HEAD_DIM
OUT_WIDTH = GROUP * HEAD_DIM
SLOTS = 8
VMEM = pl.BlockSpec(memory_space=pltpu.VMEM)
HBM = pl.BlockSpec(memory_space=pl.ANY)
MIB = 2**20


def call(kernel, out_shape, in_specs, out_specs, flops, size, scratch=(), limit=16):
    return pl.pallas_call(
        kernel,
        out_shape=out_shape,
        in_specs=in_specs,
        out_specs=out_specs,
        scratch_shapes=list(scratch),
        compiler_params=pltpu.CompilerParams(vmem_limit_bytes=limit * MIB),
        cost_estimate=pl.CostEstimate(flops=flops, bytes_accessed=size, transcendentals=0),
    )


def in_vmem(value):
    return pltpu.with_memory_space_constraint(value, pltpu.VMEM)


def in_hbm(value):
    return pltpu.with_memory_space_constraint(value, pltpu.HBM)


def struct(shape, dtype=jnp.bfloat16):
    return jax.ShapeDtypeStruct(shape, dtype)


def moved(value, axis, mask):
    pairs = [(source, source ^ mask) for source in range(lax.axis_size(axis))]
    return lax.ppermute(value, axis, pairs)


def started(copies, sems):
    copies = [
        pltpu.make_async_copy(source, target, sems.at[i])
        for i, (source, target) in enumerate(copies)
    ]
    for copy in copies:
        copy.start()
    return copies


def run_copies(copies, sems):
    for copy in started(copies, sems):
        copy.wait()


def position():
    return lax.axis_index("side"), lax.axis_index("col")


def rows_copy(weight, target, half):
    depth, width = target.shape
    rows = pl.ds(pl.multiple_of(lax.axis_index("side") * depth, depth), depth)
    columns = pl.ds(pl.multiple_of(half * width, width), width)
    return weight.at[rows, columns], target


def stage_in_kernel(blocks, weight, slots, give_part, own_part, chosen, scratch, slot_part, sems):
    side, col = position()
    slots_copy, *copies = started(
        [
            (slots, slot_part),
            rows_copy(weight, give_part, 1 - side),
            rows_copy(weight, own_part, side),
        ],
        sems,
    )
    slots_copy.wait()
    chosen[...] = one_hot(slot_part, scratch, blocks, col, col).astype(jnp.bfloat16)
    for copy in copies:
        copy.wait()


def head_copies(weight, target, half):
    width = target.shape[1]
    columns = pl.ds(pl.multiple_of(half * width, width), width)
    copies = []
    for j in range(target.shape[0] // OUT_WIDTH):
        row = pl.multiple_of((2 * j + lax.axis_index("side")) * OUT_WIDTH, OUT_WIDTH)
        copies.append(
            (
                weight.at[pl.ds(row, OUT_WIDTH), columns],
                target.at[pl.ds(j * OUT_WIDTH, OUT_WIDTH), :],
            )
        )
    return copies


def stage_rest_kernel(blocks, lengths, weight, keys, values, slots, *refs):
    target, key_part, value_part, cosine, sine, length_of, chosen, scratch, sems = refs
    side, col = position()
    copies = []
    for j in range(key_part.shape[2] // HEAD_DIM):
        lane = pl.multiple_of((2 * j + side) * HEAD_DIM, HEAD_DIM)
        for cache, part in ((keys, key_part), (values, value_part)):
            copies.append(
                (
                    cache.at[:, :, pl.ds(lane, HEAD_DIM)],
                    part.at[:, :, pl.ds(j * HEAD_DIM, HEAD_DIM)],
                )
            )
    copies = started(copies + head_copies(weight, target, 1 - side), sems)
    cosine[...], sine[...], length_of[...] = rope(lengths, cosine.shape[0])
    chosen[...] = one_hot(slots, scratch, blocks, col, col).T.astype(jnp.bfloat16)
    for copy in copies:
        copy.wait()


def stage_out_kernel(weight, attended, own_part, sems):
    run_copies(head_copies(weight, own_part, lax.axis_index("side")), sems)


def one_hot(slots, scratch, blocks, slot_base, request_base):
    total = slots.shape[0]
    rows = total // blocks
    index = lax.broadcasted_iota(jnp.int32, (total, total), 0)
    request = (lax.div(index, rows) ^ request_base) * rows + lax.rem(index, rows)
    scratch[...] = jnp.where(slots[...].reshape(1, total) == request, 1.0, 0.0).T
    parts = [
        scratch[pl.ds(pl.multiple_of((slot_base ^ i) * rows, rows), rows), :]
        for i in range(blocks)
    ]
    return jnp.concatenate(parts, axis=0)


def pieces(sums):
    high = sums.astype(jnp.bfloat16).astype(jnp.float32)
    middle = (sums - high).astype(jnp.bfloat16).astype(jnp.float32)
    low = sums - high - middle
    lane = lax.broadcasted_iota(jnp.int32, (sums.shape[0], HEAD_DIM), 1)
    parts = jnp.where(lane == 0, high, jnp.where(lane == 1, middle, low))
    return jnp.where(lane < 3, parts, 0.0).astype(jnp.bfloat16)


def dot_columns(rows, weight, out):
    size, width = weight.shape[1], 512
    for start in range(0, size, width):
        part = slice(start, min(start + width, size))
        product = jnp.dot(rows, weight[:, part], preferred_element_type=jnp.float32)
        out[:, part] = product.astype(out.dtype)


def in_kernel(count, chosen, *refs):
    pieces_in, (_, gain, weight, give, permuted) = refs[:count], refs[count:]
    depth = pieces_in[0].shape[1]
    half = weight.shape[1]
    runs = depth // HEAD_DIM
    first = pl.multiple_of(lax.axis_index("side") * runs, runs)
    gains = gain[pl.ds(first, runs), :].astype(jnp.float32)
    values = jnp.concatenate([piece[...].astype(jnp.float32) for piece in pieces_in], axis=0)
    scaled = jnp.concatenate(
        [
            values[:, i * HEAD_DIM : (i + 1) * HEAD_DIM] * gains[i : i + 1, :]
            for i in range(runs)
        ],
        axis=1,
    )
    sums = pieces(jnp.sum(values * values, axis=1, keepdims=True))
    order = jnp.dot(
        chosen[...], scaled.astype(jnp.bfloat16), preferred_element_type=jnp.float32
    ).astype(jnp.bfloat16)
    permuted[...] = order
    own_sums = jnp.dot(chosen[...], sums, preferred_element_type=jnp.float32)
    give[:, half:] = own_sums.astype(jnp.bfloat16)
    dot_columns(order, weight, give)


def out_kernel(count, chosen, *refs):
    pieces_in, (_, weight, give, permuted) = refs[:count], refs[count:]
    values = jnp.concatenate([piece[...] for piece in pieces_in], axis=0)
    order = jnp.dot(chosen[...], values, preferred_element_type=jnp.float32).astype(jnp.bfloat16)
    permuted[...] = order
    dot_columns(order, weight, give)


def at_home():
    pairs = lax.axis_size("col") // lax.axis_size("row")
    return lax.axis_index("row") == lax.div(lax.axis_index("col"), pairs)


def merge_kernel(count, own, given, received, *outs):
    rows = outs[0].shape[0]
    half = own.shape[1]
    more = given.shape[1] - half
    pairs = count // 2

    def write(out, first):
        first = first if isinstance(first, int) else pl.multiple_of(first, rows)
        part = pl.ds(first, rows)
        total = own[part, :] + received[part, :half].astype(jnp.float32)
        out[...] = total.astype(jnp.bfloat16)

    write(outs[0], 0)
    write(outs[1], pairs * rows)
    home = at_home()
    for pair in range(1, pairs):
        write(outs[2 * pair], jnp.where(home, pairs + pair, pair) * rows)
        write(outs[2 * pair + 1], jnp.where(home, pair, pairs + pair) * rows)
    for out in outs[count:]:
        lanes = slice(half, half + more // 2)
        out[...] = jnp.concatenate([given[:rows, lanes], received[:rows, lanes]], axis=1)


def own_kernel(permuted, weight, own):
    dot_columns(permuted[...], weight, own)


def project(kernel, chosen, pieces_in, extra, weights, more):
    count = lax.axis_size("col")
    parts = len(pieces_in)
    depth = pieces_in[0].shape[1]
    rows = sum(part.shape[0] for part in pieces_in)
    half = weights[0].shape[1]
    flops = 2 * rows * depth * half
    give, permuted = call(
        functools.partial(kernel, parts),
        [struct((rows, half + more)), struct((rows, depth))],
        [VMEM] * (parts + len(extra) + 3),
        [VMEM, VMEM],
        flops,
        depth * half * 2,
    )(chosen, *pieces_in, in_vmem(weights[1]), *extra, in_vmem(weights[0]))
    received = moved(give, "side", 1)
    own = call(
        own_kernel,
        struct((rows, half), jnp.float32),
        [VMEM, VMEM],
        VMEM,
        flops,
        depth * half * 2,
    )(permuted, in_vmem(weights[1]))
    outs = [struct((rows // count, half))] * count
    if more:
        outs = outs + [struct((rows // count, more))]
    merged = call(
        functools.partial(merge_kernel, count),
        outs,
        [VMEM] * 3,
        [VMEM] * len(outs),
        rows * half,
        rows * half * 8,
    )(own, give, received)
    return merged[:count], merged[count:]


def gathered(parts, axis, whole=None):
    blocks = {0: parts}
    mask = lax.axis_size(axis) // 2
    while mask:
        blocks |= {
            known | mask: [
                moved(part, axis, mask)
                for part in ([whole] if mask == 1 and known == 0 and whole is not None else block)
            ]
            for known, block in blocks.items()
        }
        mask //= 2
    if whole is not None:
        blocks[0] = [whole]
    return [part for i in sorted(blocks) for part in blocks[i]]


def choose_kernel(own, passed, *refs):
    out = refs[-1]
    out[...] = jnp.where(at_home(), passed[...], own[...])


def direct(value, far, pair):
    pairs = lax.axis_size("col") // 2
    moves = []
    for col in range(2 * pairs):
        for row in range(2):
            home = row == col // pairs
            target = col ^ pair ^ (pairs if home == far else 0)
            moves.append((2 * col + row, 2 * target + (row if home else 1 - row)))
    return lax.ppermute(value, ("col", "row"), moves)


def spread(products, ready):
    own, passed, *rest = products
    pairs = len(products) // 2
    passed = moved(passed, "col", pairs)
    blocks = []
    for pair in range(1, pairs):
        blocks += [
            direct(rest[2 * pair - 2], True, pair),
            direct(rest[2 * pair - 1], False, pair),
        ]
    crossing = call(
        choose_kernel,
        struct(own.shape),
        [VMEM] * 2 + [HBM] * len(ready),
        VMEM,
        0,
        own.size * 4,
    )(own, passed, *ready)
    return [passed, *blocks, own, moved(crossing, "row", 1)]


def total_of(blocks, pair):
    if pair > 0:
        first, second = blocks[2 * pair - 1][...], blocks[2 * pair][...]
    else:
        passed, own, crossed = blocks[0], blocks[-2], blocks[-1]
        first, second = jnp.where(at_home(), own[...], passed[...]), crossed[...]
    return first.astype(jnp.float32) + second.astype(jnp.float32)


def rotated(vector, cosine, sine):
    return vector * cosine + pltpu.roll(vector, HEAD_DIM // 2, 1) * sine


def rope(lengths, rows):
    row = lax.broadcasted_iota(jnp.int32, (rows, rows), 0)
    slot = lax.broadcasted_iota(jnp.int32, (rows, rows), 1)
    own = jnp.where(row == slot, lengths[...].reshape(1, rows), 0)
    column = jnp.sum(own.astype(jnp.float32), axis=1, keepdims=True).astype(jnp.int32)
    length_of = jnp.broadcast_to(column, (rows, HEAD_DIM))
    lane = lax.broadcasted_iota(jnp.int32, (rows, HEAD_DIM), 1)
    half = HEAD_DIM // 2
    step = lax.rem(lane, half).astype(jnp.float32)
    phases = length_of.astype(jnp.float32) * jnp.exp(-math.log(THETA) * step / half)
    sine = jnp.sin(phases)
    return jnp.cos(phases), jnp.where(lane < half, -sine, sine), length_of


def attend_all(count, parts, cosine, sine, lengths, *refs):
    pairs = (count - 1) // 2
    blocks, (sums, other_sums, keys, values) = refs[:count], refs[count : count + 4]
    refs = refs[count + 4 :]
    whole, outs, (scores_of, probs_of) = refs[0], refs[1 : parts + 1], refs[parts + 1 :]
    rows, cache = keys.shape[:2]
    low = lax.rem(lax.axis_index("col"), pairs)
    width = GROUP_WIDTH
    squares = sums[...].astype(jnp.float32) + other_sums[...].astype(jnp.float32)
    scale = lax.rsqrt(jnp.sum(squares, axis=1, keepdims=True) / D + EPSILON)
    factor = HEAD_DIM ** (-0.5)
    cosines, sines, length_of = cosine[...], sine[...], lengths[:, :1]
    lane = lax.broadcasted_iota(jnp.int32, (SLOTS, SLOTS * cache), 1)
    slot = lax.broadcasted_iota(jnp.int32, (SLOTS, SLOTS * cache), 0)
    position = lane - slot * cache
    runs = [slice(start, start + SLOTS) for start in range(0, rows, SLOTS)]
    filled = [(position >= 0) & (position < length_of[part]) for part in runs]
    own, new_values, own_probs = [], [], []
    for pair in range(pairs):
        total = total_of(blocks, pair)
        total = (total * scale).astype(jnp.bfloat16).astype(jnp.float32)
        heads = [total[:, h * HEAD_DIM : (h + 1) * HEAD_DIM] for h in range(GROUP + 2)]
        queries = [
            rotated(head, cosines, sines).astype(jnp.bfloat16).astype(jnp.float32)
            for head in heads[:GROUP]
        ]
        new_key = rotated(heads[GROUP], cosines, sines).astype(jnp.bfloat16).astype(jnp.float32)
        new_values.append(heads[GROUP + 1])
        own.append([jnp.sum(query * new_key, axis=1, keepdims=True) * factor for query in queries])
        lanes = pl.ds(pl.multiple_of((low ^ pair) * HEAD_DIM, HEAD_DIM), HEAD_DIM)
        for run, part in enumerate(runs):
            query = jnp.concatenate([head[part] for head in queries], axis=0)
            key = keys[part, :, lanes].reshape(SLOTS * cache, HEAD_DIM)
            scores_of[pair, run] = lax.dot_general(
                query.astype(jnp.bfloat16),
                key,
                (((1,), (1,)), ((), ())),
                preferred_element_type=jnp.float32,
            )
    for pair in range(pairs):
        for run, part in enumerate(runs):
            scores = (scores_of[pair, run] * factor).reshape(GROUP, SLOTS, SLOTS * cache)
            scores = jnp.where(filled[run][None], scores, -1e30)
            own_score = jnp.concatenate([head[part] for head in own[pair]], axis=0).reshape(
                GROUP, SLOTS, 1
            )
            highest = jnp.maximum(jnp.max(scores, axis=2, keepdims=True), own_score)
            weights = jnp.exp(scores - highest)
            own_weight = jnp.exp(own_score - highest)
            inverse = 1.0 / (jnp.sum(weights, axis=2, keepdims=True) + own_weight)
            probs_of[pair, run] = weights.astype(jnp.bfloat16).reshape(
                GROUP * SLOTS, SLOTS * cache
            )
            own_probs.append((own_weight, inverse))
    for pair in range(pairs):
        lanes = pl.ds(pl.multiple_of((low ^ pair) * HEAD_DIM, HEAD_DIM), HEAD_DIM)
        results = []
        for run, part in enumerate(runs):
            value = values[part, :, lanes].reshape(SLOTS * cache, HEAD_DIM)
            mixed = jnp.dot(probs_of[pair, run], value, preferred_element_type=jnp.float32)
            own_weight, inverse = own_probs[pair * len(runs) + run]
            mixed = mixed.reshape(GROUP, SLOTS, HEAD_DIM) + own_weight * new_values[pair][part][None]
            results.append(mixed * inverse)
        for head in range(GROUP):
            at = pl.multiple_of((low ^ pair) * OUT_WIDTH + head * HEAD_DIM, HEAD_DIM)
            size = len(results) // parts
            for i, out in enumerate(outs):
                joined = jnp.concatenate(
                    [result[head] for result in results[i * size : (i + 1) * size]], axis=0
                )
                joined = joined.astype(jnp.bfloat16)
                out[:, pl.ds(at, HEAD_DIM)] = joined
                run = slice(i * joined.shape[0], (i + 1) * joined.shape[0])
                whole[run, pl.ds(at, HEAD_DIM)] = joined


def sum_kernel(count, hidden, attended, *refs):
    blocks, (keep, send) = refs[:count], refs[count:]
    rows, width = blocks[0].shape
    pairs = keep.shape[1] // width
    side = lax.axis_index("side")
    low = lax.rem(lax.axis_index("col"), pairs)
    for pair in range(pairs):
        column = low ^ pair
        total = total_of(blocks, pair)
        at = pl.ds(pl.multiple_of((2 * column + side) * width, width), width)
        hidden_out = (hidden[:, at].astype(jnp.float32) + total).astype(jnp.bfloat16)
        at = pl.ds(pl.multiple_of(column * width, width), width)
        attention = attended[:, at]
        keep[:, at] = jnp.where(side == 0, hidden_out, attention)
        send[:, at] = jnp.where(side == 0, attention, hidden_out)


def join_kernel(keep, received, out, sems):
    side = lax.axis_index("side")
    width = OUT_WIDTH
    copies = []
    for j in range(keep.shape[1] // width):
        part = slice(j * width, (j + 1) * width)
        for ref, core in ((keep, side), (received, 1 - side)):
            at = pl.ds(pl.multiple_of((2 * j + core) * width, width), width)
            copies.append((ref.at[:, part], out.at[0, :, at]))
    run_copies(copies, sems)


def paired_plan(
    hidden_in, norm_gain, qkv_weight, out_weight, key_cache, value_cache, cache_lengths, slot_request
):
    col_count, row_count = lax.axis_size("col"), lax.axis_size("row")
    pairs = col_count // row_count
    side = lax.axis_index("side")
    rows, depth = hidden_in.shape
    half = depth // 2
    cache = key_cache.shape[1]
    parts = 2
    piece = rows // parts

    own_part = lax.dynamic_slice_in_dim(hidden_in, side * half, half, 1)
    gain = norm_gain.reshape(depth // HEAD_DIM, HEAD_DIM)
    half_in, half_out = qkv_weight.shape[1] // 2, out_weight.shape[1] // 2
    total = rows * col_count
    square = (total, total)
    give_in, own_in, chosen_in = call(
        functools.partial(stage_in_kernel, col_count),
        [pltpu.VMEM((half, half_in), jnp.bfloat16)] * 2 + [struct(square)],
        [HBM, HBM],
        [VMEM] * 3,
        0,
        half * half_in * 4,
        [
            pltpu.VMEM(square, jnp.float32),
            pltpu.VMEM((total,), jnp.int32),
            pltpu.SemaphoreType.DMA((3,)),
        ],
    )(in_hbm(qkv_weight), in_hbm(slot_request))
    blocks = gathered(
        [own_part[i * piece : (i + 1) * piece] for i in range(parts)], "col"
    )
    table = struct((rows, HEAD_DIM), jnp.float32)
    give_out, key_part, value_part, *tables, chosen_out = call(
        functools.partial(stage_rest_kernel, col_count),
        [pltpu.VMEM((half, half_out), jnp.bfloat16)]
        + [pltpu.VMEM((rows, cache, pairs * HEAD_DIM), jnp.bfloat16)] * 2
        + [table, table, struct((rows, HEAD_DIM), jnp.int32), struct(square)],
        [VMEM, HBM, HBM, HBM, VMEM],
        [VMEM] * 7,
        0,
        half * half_out * 2 + 4 * rows * cache * pairs * HEAD_DIM,
        [pltpu.VMEM(square, jnp.float32), pltpu.SemaphoreType.DMA((3 * pairs,))],
    )(cache_lengths, in_hbm(out_weight), in_hbm(key_cache), in_hbm(value_cache), slot_request)
    products, sums = project(in_kernel, chosen_in, blocks, [gain], [give_in, own_in], HEAD_DIM)
    other_sums = moved(sums[0], "row", 1)
    products = spread(products, [other_sums])

    runs = (pairs, rows // SLOTS, GROUP * SLOTS, SLOTS * cache)
    attended, *attended_parts = call(
        functools.partial(attend_all, len(products), parts),
        [struct((rows, half))] + [struct((piece, half))] * parts,
        [VMEM] * (len(products) + 7),
        [VMEM] * (parts + 1),
        4 * rows * half * cache,
        0,
        [pltpu.VMEM(runs, jnp.float32), pltpu.VMEM(runs, jnp.bfloat16)],
    )(
        *tables,
        *products,
        *sums,
        other_sums,
        in_vmem(key_part),
        in_vmem(value_part),
    )

    own_out = call(
        stage_out_kernel,
        pltpu.VMEM((half, half_out), jnp.bfloat16),
        [HBM, HBM],
        VMEM,
        0,
        half * half_out * 2,
        [pltpu.SemaphoreType.DMA((pairs,))],
    )(in_hbm(out_weight), attended)
    products, _ = project(
        out_kernel, chosen_out, gathered(attended_parts, "col", attended), [], [give_out, own_out], 0
    )
    products = spread(products, [])
    keep, send = call(
        functools.partial(sum_kernel, len(products)),
        [struct((rows, half)), struct((rows, half))],
        [VMEM] * (2 + len(products)),
        [VMEM, VMEM],
        rows * depth * 4,
        rows * depth * 8,
    )(hidden_in, attended, *products)
    return call(
        join_kernel,
        struct((1, rows, depth)),
        [VMEM, VMEM],
        HBM,
        0,
        rows * depth * 4,
        [pltpu.SemaphoreType.DMA((2 * pairs,))],
    )(keep, moved(send, "side", 1))


def per_device(*args):
    hidden_in, _, qkv_weight, out_weight, key_cache = args[:5]
    col_count, row_count = lax.axis_size("col"), lax.axis_size("row")
    fits = (
        lax.axis_size("side") == 2
        and qkv_weight.shape[1] == 2 * GROUP_WIDTH
        and row_count == 2
        and col_count > row_count
        and col_count & (col_count - 1) == 0
        and hidden_in.shape[0] % 32 == 0
        and key_cache.shape[1] % 16 == 0
        and hidden_in.shape[1] == 2 * OUT_WIDTH * (col_count // row_count)
    )
    return paired_plan(*args) if fits else general_plan(*args)


def solution(mesh):
    placed = (
        P(("groups", "col"), "row"),
        P("row"),
        P("row", "col"),
        P("row", "col"),
        P(("groups", "col"), None, "row"),
        P(("groups", "col"), None, "row"),
        P(("groups", "col")),
        P("groups"),
    )
    return jax.shard_map(
        per_device,
        mesh=mesh,
        in_specs=placed,
        out_specs=P("side", ("groups", "col"), "row"),
        check_vma=False,
    )
```

```python
import functools
import math

import jax
import jax.numpy as jnp
from jax import lax
from jax.experimental import pallas as pl
from jax.experimental.pallas import tpu as pltpu
from jax.sharding import PartitionSpec as P

D = 8192
HEADS = 64
KV_HEADS = 8
HEAD_DIM = 128
QKV = 10240


EPSILON = 1e-05
THETA = 500000.0


def swapped(value, axis, bit):
    mask = 2**bit
    pairs = [(source, source ^ mask) for source in range(lax.axis_size(axis))]
    return lax.ppermute(value, axis, pairs)


def rope_tables(lengths, head_dim):
    half_dim = head_dim // 2
    inv_freq = jnp.exp(
        -jnp.log(jnp.float32(THETA)) * jnp.arange(half_dim, dtype=jnp.float32) / half_dim
    )
    phases = lengths.astype(jnp.float32)[:, None] * inv_freq[None, :]
    return (jnp.cos(phases), jnp.sin(phases))


def rotate(vector, cos_vals, sine_vals):
    half_dim = vector.shape[-1] // 2
    front_half = vector[..., :half_dim]
    back_half = vector[..., half_dim:]
    return jnp.concatenate(
        [
            front_half * cos_vals - back_half * sine_vals,
            back_half * cos_vals + front_half * sine_vals,
        ],
        axis=-1,
    )


def attend(packed, key_block, value_block, lengths):
    slot_count = packed.shape[0]
    cache_size = key_block.shape[1]
    groups = key_block.shape[2] // HEAD_DIM
    per_group = HEADS // KV_HEADS
    grouped = packed.reshape(slot_count, groups, per_group + 2, HEAD_DIM)
    cos_vals, sine_vals = rope_tables(lengths, HEAD_DIM)
    queries = rotate(
        grouped[:, :, :per_group].astype(jnp.float32),
        cos_vals[:, None, None, :],
        sine_vals[:, None, None, :],
    ).astype(jnp.bfloat16)
    new_keys = rotate(
        grouped[:, :, per_group].astype(jnp.float32), cos_vals[:, None, :], sine_vals[:, None, :]
    ).astype(jnp.bfloat16)
    new_values = grouped[:, :, per_group + 1]
    cache_keys = key_block.reshape(slot_count, cache_size, groups, HEAD_DIM)
    cache_values = value_block.reshape(slot_count, cache_size, groups, HEAD_DIM)
    factor = HEAD_DIM ** (-0.5)
    cache_scores = (
        jnp.einsum("sghd,slgd->sghl", queries, cache_keys, preferred_element_type=jnp.float32)
        * factor
    )
    own_scores = (
        jnp.einsum("sghd,sgd->sgh", queries, new_keys, preferred_element_type=jnp.float32) * factor
    )
    in_cache = lax.broadcasted_iota(jnp.int32, (slot_count, cache_size), 1) < lengths[:, None]
    cache_scores = jnp.where(in_cache[:, None, None, :], cache_scores, -1e30)
    row_max = jnp.maximum(jnp.max(cache_scores, axis=-1), own_scores)
    cache_exp = jnp.exp(cache_scores - row_max[..., None])
    own_exp = jnp.exp(own_scores - row_max)
    denominator = jnp.sum(cache_exp, axis=-1) + own_exp
    cache_weight = (cache_exp / denominator[..., None]).astype(jnp.bfloat16)
    own_weight = (own_exp / denominator).astype(jnp.bfloat16)
    combined = jnp.einsum(
        "sghl,slgd->sghd", cache_weight, cache_values, preferred_element_type=jnp.float32
    )
    combined = (
        combined
        + own_weight.astype(jnp.float32)[..., None] * new_values.astype(jnp.float32)[:, :, None, :]
    )
    return combined.astype(jnp.bfloat16).reshape(slot_count, groups * per_group * HEAD_DIM)


def general_plan(
    hidden_in,
    norm_gain,
    qkv_weight,
    out_weight,
    key_cache,
    value_cache,
    cache_lengths,
    slot_request,
):
    side_index = lax.axis_index("side")
    is_weight = side_index == 0
    col_count = lax.axis_size("col")
    row_count = lax.axis_size("row")
    group_cols = col_count // row_count
    in_half = qkv_weight.shape[1] // 2
    out_half = out_weight.shape[1] // 2
    residual = hidden_in.astype(jnp.float32)
    square_sums = lax.psum(jnp.sum(residual * residual, axis=1), "row")
    normed = (
        residual
        * lax.rsqrt(square_sums[:, None] / D + EPSILON)
        * norm_gain.astype(jnp.float32)[None, :]
    ).astype(jnp.bfloat16)
    in_weight = lax.dynamic_slice_in_dim(qkv_weight, side_index * in_half, in_half, 1)
    partial_in = jnp.dot(
        lax.all_gather(normed, "col", axis=0, tiled=True),
        in_weight,
        preferred_element_type=jnp.float32,
    )
    in_slots = jnp.take(partial_in, slot_request, axis=0)
    own_width = QKV // row_count
    summed = lax.psum(in_slots.astype(jnp.bfloat16), "row")
    spread = lax.all_to_all(summed, "col", split_axis=0, concat_axis=1, tiled=True)
    own_columns = lax.dynamic_slice_in_dim(
        spread.reshape(spread.shape[0], col_count, in_half),
        lax.axis_index("row") * group_cols,
        group_cols,
        1,
    )
    slot_half = key_cache.shape[0] // 2
    halves = lax.all_to_all(
        own_columns[:, :, None, :], "side", split_axis=0, concat_axis=2, tiled=True
    )
    arrived = halves.reshape(slot_half, own_width)
    first_slot = side_index * slot_half
    key_part = lax.dynamic_slice_in_dim(key_cache, first_slot, slot_half, 0)
    value_part = lax.dynamic_slice_in_dim(value_cache, first_slot, slot_half, 0)
    length_part = lax.dynamic_slice_in_dim(cache_lengths, first_slot, slot_half, 0)
    attended = attend(arrived, key_part, value_part, length_part)
    out_cols = lax.dynamic_slice_in_dim(out_weight, side_index * out_half, out_half, 1)
    collected = lax.all_gather(attended, ("col", "side"), axis=0, tiled=True)
    out_slots = jnp.dot(collected, out_cols, preferred_element_type=jnp.float32)
    inverse = jnp.argsort(slot_request)
    out_requests = jnp.take(out_slots, inverse, axis=0)
    spread_out = lax.all_to_all(
        out_requests.astype(jnp.bfloat16), "col", split_axis=0, concat_axis=1, tiled=True
    ).astype(out_requests.dtype)
    out_view = spread_out.reshape(spread_out.shape[0], col_count, out_half)
    summed_out = lax.psum_scatter(
        out_view.astype(jnp.bfloat16), "row", scatter_dimension=1, tiled=True
    ).astype(jnp.float32)
    req_rows = hidden_in.shape[0]
    residual_view = residual.reshape(req_rows, group_cols, 2, out_half)
    residual_half = lax.dynamic_index_in_dim(residual_view, side_index, 2, keepdims=False)
    own_hidden = (residual_half + summed_out).astype(jnp.bfloat16)
    payload = jnp.where(is_weight, attended, own_hidden.reshape(attended.shape))
    received = swapped(payload, "side", 0)
    hidden = jnp.stack([own_hidden, received.reshape(own_hidden.shape)], axis=2).reshape(
        req_rows, residual.shape[1]
    )
    attention_rows = jnp.concatenate([received, attended], axis=0)
    result = jnp.where(is_weight, hidden, attention_rows)
    return result[None]


GROUP = HEADS // KV_HEADS
GROUP_WIDTH = (GROUP + 2) * HEAD_DIM
OUT_WIDTH = GROUP * HEAD_DIM
SLOTS = 8
VMEM = pl.BlockSpec(memory_space=pltpu.VMEM)
HBM = pl.BlockSpec(memory_space=pl.ANY)
MIB = 2**20


def call(kernel, out_shape, in_specs, out_specs, flops, size, scratch=(), limit=16):
    return pl.pallas_call(
        kernel,
        out_shape=out_shape,
        in_specs=in_specs,
        out_specs=out_specs,
        scratch_shapes=list(scratch),
        compiler_params=pltpu.CompilerParams(vmem_limit_bytes=limit * MIB),
        cost_estimate=pl.CostEstimate(flops=flops, bytes_accessed=size, transcendentals=0),
    )


def in_vmem(value):
    return pltpu.with_memory_space_constraint(value, pltpu.VMEM)


def in_hbm(value):
    return pltpu.with_memory_space_constraint(value, pltpu.HBM)


def struct(shape, dtype=jnp.bfloat16):
    return jax.ShapeDtypeStruct(shape, dtype)


def moved(value, axis, mask):
    pairs = [(source, source ^ mask) for source in range(lax.axis_size(axis))]
    return lax.ppermute(value, axis, pairs)


def started(copies, sems):
    copies = [
        pltpu.make_async_copy(source, target, sems.at[i])
        for i, (source, target) in enumerate(copies)
    ]
    for copy in copies:
        copy.start()
    return copies


def run_copies(copies, sems):
    for copy in started(copies, sems):
        copy.wait()


def position():
    return lax.axis_index("side"), lax.axis_index("col")


def rows_copy(weight, target, half):
    depth, width = target.shape
    rows = pl.ds(pl.multiple_of(lax.axis_index("side") * depth, depth), depth)
    columns = pl.ds(pl.multiple_of(half * width, width), width)
    return weight.at[rows, columns], target


def stage_in_kernel(blocks, weight, slots, give_part, own_part, chosen, scratch, slot_part, sems):
    side, col = position()
    slots_copy, *copies = started(
        [
            (slots, slot_part),
            rows_copy(weight, give_part, 1 - side),
            rows_copy(weight, own_part, side),
        ],
        sems,
    )
    slots_copy.wait()
    chosen[...] = one_hot(slot_part, scratch, blocks, col, col).astype(jnp.bfloat16)
    for copy in copies:
        copy.wait()


def head_copies(weight, target, half):
    width = target.shape[1]
    columns = pl.ds(pl.multiple_of(half * width, width), width)
    copies = []
    for j in range(target.shape[0] // OUT_WIDTH):
        row = pl.multiple_of((2 * j + lax.axis_index("side")) * OUT_WIDTH, OUT_WIDTH)
        copies.append(
            (
                weight.at[pl.ds(row, OUT_WIDTH), columns],
                target.at[pl.ds(j * OUT_WIDTH, OUT_WIDTH), :],
            )
        )
    return copies


def stage_rest_kernel(blocks, lengths, weight, keys, values, slots, *refs):
    target, key_part, value_part, cosine, sine, length_of, chosen, scratch, sems = refs
    side, col = position()
    copies = []
    for j in range(key_part.shape[2] // HEAD_DIM):
        lane = pl.multiple_of((2 * j + side) * HEAD_DIM, HEAD_DIM)
        for cache, part in ((keys, key_part), (values, value_part)):
            copies.append(
                (
                    cache.at[:, :, pl.ds(lane, HEAD_DIM)],
                    part.at[:, :, pl.ds(j * HEAD_DIM, HEAD_DIM)],
                )
            )
    copies = started(copies + head_copies(weight, target, 1 - side), sems)
    cosine[...], sine[...], length_of[...] = rope(lengths, cosine.shape[0])
    chosen[...] = one_hot(slots, scratch, blocks, col, col).T.astype(jnp.bfloat16)
    for copy in copies:
        copy.wait()


def stage_out_kernel(weight, attended, own_part, sems):
    run_copies(head_copies(weight, own_part, lax.axis_index("side")), sems)


def one_hot(slots, scratch, blocks, slot_base, request_base):
    total = slots.shape[0]
    rows = total // blocks
    index = lax.broadcasted_iota(jnp.int32, (total, total), 0)
    request = (lax.div(index, rows) ^ request_base) * rows + lax.rem(index, rows)
    scratch[...] = jnp.where(slots[...].reshape(1, total) == request, 1.0, 0.0).T
    parts = [
        scratch[pl.ds(pl.multiple_of((slot_base ^ i) * rows, rows), rows), :]
        for i in range(blocks)
    ]
    return jnp.concatenate(parts, axis=0)


def pieces(sums):
    high = sums.astype(jnp.bfloat16).astype(jnp.float32)
    middle = (sums - high).astype(jnp.bfloat16).astype(jnp.float32)
    low = sums - high - middle
    lane = lax.broadcasted_iota(jnp.int32, (sums.shape[0], HEAD_DIM), 1)
    parts = jnp.where(lane == 0, high, jnp.where(lane == 1, middle, low))
    return jnp.where(lane < 3, parts, 0.0).astype(jnp.bfloat16)


def dot_columns(rows, weight, out):
    size, width = weight.shape[1], 512
    for start in range(0, size, width):
        part = slice(start, min(start + width, size))
        product = jnp.dot(rows, weight[:, part], preferred_element_type=jnp.float32)
        out[:, part] = product.astype(out.dtype)


def in_kernel(count, chosen, *refs):
    pieces_in, (_, gain, weight, give, permuted) = refs[:count], refs[count:]
    depth = pieces_in[0].shape[1]
    half = weight.shape[1]
    runs = depth // HEAD_DIM
    first = pl.multiple_of(lax.axis_index("side") * runs, runs)
    gains = gain[pl.ds(first, runs), :].astype(jnp.float32)
    values = jnp.concatenate([piece[...].astype(jnp.float32) for piece in pieces_in], axis=0)
    scaled = jnp.concatenate(
        [
            values[:, i * HEAD_DIM : (i + 1) * HEAD_DIM] * gains[i : i + 1, :]
            for i in range(runs)
        ],
        axis=1,
    )
    sums = pieces(jnp.sum(values * values, axis=1, keepdims=True))
    order = jnp.dot(
        chosen[...], scaled.astype(jnp.bfloat16), preferred_element_type=jnp.float32
    ).astype(jnp.bfloat16)
    permuted[...] = order
    own_sums = jnp.dot(chosen[...], sums, preferred_element_type=jnp.float32)
    give[:, half:] = own_sums.astype(jnp.bfloat16)
    dot_columns(order, weight, give)


def out_kernel(count, chosen, *refs):
    pieces_in, (_, weight, give, permuted) = refs[:count], refs[count:]
    values = jnp.concatenate([piece[...] for piece in pieces_in], axis=0)
    order = jnp.dot(chosen[...], values, preferred_element_type=jnp.float32).astype(jnp.bfloat16)
    permuted[...] = order
    dot_columns(order, weight, give)


def at_home():
    pairs = lax.axis_size("col") // lax.axis_size("row")
    return lax.axis_index("row") == lax.div(lax.axis_index("col"), pairs)


def merge_kernel(count, own, given, received, *outs):
    rows = outs[0].shape[0]
    half = own.shape[1]
    more = given.shape[1] - half
    pairs = count // 2

    def write(out, first):
        first = first if isinstance(first, int) else pl.multiple_of(first, rows)
        part = pl.ds(first, rows)
        total = own[part, :] + received[part, :half].astype(jnp.float32)
        out[...] = total.astype(jnp.bfloat16)

    write(outs[0], 0)
    write(outs[1], pairs * rows)
    home = at_home()
    for pair in range(1, pairs):
        write(outs[2 * pair], jnp.where(home, pairs + pair, pair) * rows)
        write(outs[2 * pair + 1], jnp.where(home, pair, pairs + pair) * rows)
    for out in outs[count:]:
        lanes = slice(half, half + more // 2)
        out[...] = jnp.concatenate([given[:rows, lanes], received[:rows, lanes]], axis=1)


def own_kernel(permuted, weight, own):
    dot_columns(permuted[...], weight, own)


def project(kernel, chosen, pieces_in, extra, weights, more):
    count = lax.axis_size("col")
    parts = len(pieces_in)
    depth = pieces_in[0].shape[1]
    rows = sum(part.shape[0] for part in pieces_in)
    half = weights[0].shape[1]
    flops = 2 * rows * depth * half
    give, permuted = call(
        functools.partial(kernel, parts),
        [struct((rows, half + more)), struct((rows, depth))],
        [VMEM] * (parts + len(extra) + 3),
        [VMEM, VMEM],
        flops,
        depth * half * 2,
    )(chosen, *pieces_in, in_vmem(weights[1]), *extra, in_vmem(weights[0]))
    received = moved(give, "side", 1)
    own = call(
        own_kernel,
        struct((rows, half), jnp.float32),
        [VMEM, VMEM],
        VMEM,
        flops,
        depth * half * 2,
    )(permuted, in_vmem(weights[1]))
    outs = [struct((rows // count, half))] * count
    if more:
        outs = outs + [struct((rows // count, more))]
    merged = call(
        functools.partial(merge_kernel, count),
        outs,
        [VMEM] * 3,
        [VMEM] * len(outs),
        rows * half,
        rows * half * 8,
    )(own, give, received)
    return merged[:count], merged[count:]


def gathered(parts, axis, whole=None):
    blocks = {0: parts}
    mask = lax.axis_size(axis) // 2
    while mask:
        blocks |= {
            known | mask: [
                moved(part, axis, mask)
                for part in ([whole] if mask == 1 and known == 0 and whole is not None else block)
            ]
            for known, block in blocks.items()
        }
        mask //= 2
    if whole is not None:
        blocks[0] = [whole]
    return [part for i in sorted(blocks) for part in blocks[i]]


def choose_kernel(own, passed, *refs):
    out = refs[-1]
    out[...] = jnp.where(at_home(), passed[...], own[...])


def direct(value, far, pair):
    pairs = lax.axis_size("col") // 2
    moves = []
    for col in range(2 * pairs):
        for row in range(2):
            home = row == col // pairs
            target = col ^ pair ^ (pairs if home == far else 0)
            moves.append((2 * col + row, 2 * target + (row if home else 1 - row)))
    return lax.ppermute(value, ("col", "row"), moves)


def spread(products, ready):
    own, passed, *rest = products
    pairs = len(products) // 2
    passed = moved(passed, "col", pairs)
    blocks = []
    for pair in range(1, pairs):
        blocks += [
            direct(rest[2 * pair - 2], True, pair),
            direct(rest[2 * pair - 1], False, pair),
        ]
    crossing = call(
        choose_kernel,
        struct(own.shape),
        [VMEM] * 2 + [HBM] * len(ready),
        VMEM,
        0,
        own.size * 4,
    )(own, passed, *ready)
    return [passed, *blocks, own, moved(crossing, "row", 1)]


def total_of(blocks, pair):
    if pair > 0:
        first, second = blocks[2 * pair - 1][...], blocks[2 * pair][...]
    else:
        passed, own, crossed = blocks[0], blocks[-2], blocks[-1]
        first, second = jnp.where(at_home(), own[...], passed[...]), crossed[...]
    return first.astype(jnp.float32) + second.astype(jnp.float32)


def rotated(vector, cosine, sine):
    return vector * cosine + pltpu.roll(vector, HEAD_DIM // 2, 1) * sine


def rope(lengths, rows):
    row = lax.broadcasted_iota(jnp.int32, (rows, rows), 0)
    slot = lax.broadcasted_iota(jnp.int32, (rows, rows), 1)
    own = jnp.where(row == slot, lengths[...].reshape(1, rows), 0)
    column = jnp.sum(own.astype(jnp.float32), axis=1, keepdims=True).astype(jnp.int32)
    length_of = jnp.broadcast_to(column, (rows, HEAD_DIM))
    lane = lax.broadcasted_iota(jnp.int32, (rows, HEAD_DIM), 1)
    half = HEAD_DIM // 2
    step = lax.rem(lane, half).astype(jnp.float32)
    phases = length_of.astype(jnp.float32) * jnp.exp(-math.log(THETA) * step / half)
    sine = jnp.sin(phases)
    return jnp.cos(phases), jnp.where(lane < half, -sine, sine), length_of


def attend_all(count, parts, cosine, sine, lengths, *refs):
    pairs = (count - 1) // 2
    blocks, (sums, other_sums, keys, values) = refs[:count], refs[count : count + 4]
    refs = refs[count + 4 :]
    whole, outs, (scores_of, probs_of) = refs[0], refs[1 : parts + 1], refs[parts + 1 :]
    rows, cache = keys.shape[:2]
    low = lax.rem(lax.axis_index("col"), pairs)
    width = GROUP_WIDTH
    squares = sums[...].astype(jnp.float32) + other_sums[...].astype(jnp.float32)
    scale = lax.rsqrt(jnp.sum(squares, axis=1, keepdims=True) / D + EPSILON)
    factor = HEAD_DIM ** (-0.5)
    cosines, sines, length_of = cosine[...], sine[...], lengths[:, :1]
    lane = lax.broadcasted_iota(jnp.int32, (SLOTS, SLOTS * cache), 1)
    slot = lax.broadcasted_iota(jnp.int32, (SLOTS, SLOTS * cache), 0)
    position = lane - slot * cache
    runs = [slice(start, start + SLOTS) for start in range(0, rows, SLOTS)]
    filled = [(position >= 0) & (position < length_of[part]) for part in runs]
    own, new_values, own_probs = [], [], []
    for pair in range(pairs):
        total = total_of(blocks, pair)
        total = (total * scale).astype(jnp.bfloat16).astype(jnp.float32)
        heads = [total[:, h * HEAD_DIM : (h + 1) * HEAD_DIM] for h in range(GROUP + 2)]
        queries = [
            rotated(head, cosines, sines).astype(jnp.bfloat16).astype(jnp.float32)
            for head in heads[:GROUP]
        ]
        new_key = rotated(heads[GROUP], cosines, sines).astype(jnp.bfloat16).astype(jnp.float32)
        new_values.append(heads[GROUP + 1])
        own.append([jnp.sum(query * new_key, axis=1, keepdims=True) * factor for query in queries])
        lanes = pl.ds(pl.multiple_of((low ^ pair) * HEAD_DIM, HEAD_DIM), HEAD_DIM)
        for run, part in enumerate(runs):
            query = jnp.concatenate([head[part] for head in queries], axis=0)
            key = keys[part, :, lanes].reshape(SLOTS * cache, HEAD_DIM)
            scores_of[pair, run] = lax.dot_general(
                query.astype(jnp.bfloat16),
                key,
                (((1,), (1,)), ((), ())),
                preferred_element_type=jnp.float32,
            )
    for pair in range(pairs):
        for run, part in enumerate(runs):
            scores = (scores_of[pair, run] * factor).reshape(GROUP, SLOTS, SLOTS * cache)
            scores = jnp.where(filled[run][None], scores, -1e30)
            own_score = jnp.concatenate([head[part] for head in own[pair]], axis=0).reshape(
                GROUP, SLOTS, 1
            )
            highest = jnp.maximum(jnp.max(scores, axis=2, keepdims=True), own_score)
            weights = jnp.exp(scores - highest)
            own_weight = jnp.exp(own_score - highest)
            inverse = 1.0 / (jnp.sum(weights, axis=2, keepdims=True) + own_weight)
            probs = (weights * inverse).astype(jnp.bfloat16)
            probs_of[pair, run] = probs.reshape(GROUP * SLOTS, SLOTS * cache)
            own_probs.append((own_weight * inverse).astype(jnp.bfloat16).astype(jnp.float32))
    for pair in range(pairs):
        lanes = pl.ds(pl.multiple_of((low ^ pair) * HEAD_DIM, HEAD_DIM), HEAD_DIM)
        results = []
        for run, part in enumerate(runs):
            value = values[part, :, lanes].reshape(SLOTS * cache, HEAD_DIM)
            mixed = jnp.dot(probs_of[pair, run], value, preferred_element_type=jnp.float32)
            own_prob = own_probs[pair * len(runs) + run]
            results.append(
                mixed.reshape(GROUP, SLOTS, HEAD_DIM) + own_prob * new_values[pair][part][None]
            )
        for head in range(GROUP):
            at = pl.multiple_of((low ^ pair) * OUT_WIDTH + head * HEAD_DIM, HEAD_DIM)
            size = len(results) // parts
            for i, out in enumerate(outs):
                joined = jnp.concatenate(
                    [result[head] for result in results[i * size : (i + 1) * size]], axis=0
                )
                joined = joined.astype(jnp.bfloat16)
                out[:, pl.ds(at, HEAD_DIM)] = joined
                run = slice(i * joined.shape[0], (i + 1) * joined.shape[0])
                whole[run, pl.ds(at, HEAD_DIM)] = joined


def sum_kernel(count, hidden, attended, *refs):
    blocks, (keep, send) = refs[:count], refs[count:]
    rows, width = blocks[0].shape
    pairs = keep.shape[1] // width
    side = lax.axis_index("side")
    low = lax.rem(lax.axis_index("col"), pairs)
    for pair in range(pairs):
        column = low ^ pair
        total = total_of(blocks, pair)
        at = pl.ds(pl.multiple_of((2 * column + side) * width, width), width)
        hidden_out = (hidden[:, at].astype(jnp.float32) + total).astype(jnp.bfloat16)
        at = pl.ds(pl.multiple_of(column * width, width), width)
        attention = attended[:, at]
        keep[:, at] = jnp.where(side == 0, hidden_out, attention)
        send[:, at] = jnp.where(side == 0, attention, hidden_out)


def join_kernel(keep, received, out, sems):
    side = lax.axis_index("side")
    width = OUT_WIDTH
    copies = []
    for j in range(keep.shape[1] // width):
        part = slice(j * width, (j + 1) * width)
        for ref, core in ((keep, side), (received, 1 - side)):
            at = pl.ds(pl.multiple_of((2 * j + core) * width, width), width)
            copies.append((ref.at[:, part], out.at[0, :, at]))
    run_copies(copies, sems)


def paired_plan(
    hidden_in, norm_gain, qkv_weight, out_weight, key_cache, value_cache, cache_lengths, slot_request
):
    col_count, row_count = lax.axis_size("col"), lax.axis_size("row")
    pairs = col_count // row_count
    side = lax.axis_index("side")
    rows, depth = hidden_in.shape
    half = depth // 2
    cache = key_cache.shape[1]
    parts = 2
    piece = rows // parts

    own_part = lax.dynamic_slice_in_dim(hidden_in, side * half, half, 1)
    gain = norm_gain.reshape(depth // HEAD_DIM, HEAD_DIM)
    half_in, half_out = qkv_weight.shape[1] // 2, out_weight.shape[1] // 2
    total = rows * col_count
    square = (total, total)
    give_in, own_in, chosen_in = call(
        functools.partial(stage_in_kernel, col_count),
        [pltpu.VMEM((half, half_in), jnp.bfloat16)] * 2 + [struct(square)],
        [HBM, HBM],
        [VMEM] * 3,
        0,
        half * half_in * 4,
        [
            pltpu.VMEM(square, jnp.float32),
            pltpu.VMEM((total,), jnp.int32),
            pltpu.SemaphoreType.DMA((3,)),
        ],
    )(in_hbm(qkv_weight), in_hbm(slot_request))
    blocks = gathered(
        [own_part[i * piece : (i + 1) * piece] for i in range(parts)], "col"
    )
    table = struct((rows, HEAD_DIM), jnp.float32)
    give_out, key_part, value_part, *tables, chosen_out = call(
        functools.partial(stage_rest_kernel, col_count),
        [pltpu.VMEM((half, half_out), jnp.bfloat16)]
        + [pltpu.VMEM((rows, cache, pairs * HEAD_DIM), jnp.bfloat16)] * 2
        + [table, table, struct((rows, HEAD_DIM), jnp.int32), struct(square)],
        [VMEM, HBM, HBM, HBM, VMEM],
        [VMEM] * 7,
        0,
        half * half_out * 2 + 4 * rows * cache * pairs * HEAD_DIM,
        [pltpu.VMEM(square, jnp.float32), pltpu.SemaphoreType.DMA((3 * pairs,))],
    )(cache_lengths, in_hbm(out_weight), in_hbm(key_cache), in_hbm(value_cache), slot_request)
    products, sums = project(in_kernel, chosen_in, blocks, [gain], [give_in, own_in], HEAD_DIM)
    other_sums = moved(sums[0], "row", 1)
    products = spread(products, [other_sums])

    runs = (pairs, rows // SLOTS, GROUP * SLOTS, SLOTS * cache)
    attended, *attended_parts = call(
        functools.partial(attend_all, len(products), parts),
        [struct((rows, half))] + [struct((piece, half))] * parts,
        [VMEM] * (len(products) + 7),
        [VMEM] * (parts + 1),
        4 * rows * half * cache,
        0,
        [pltpu.VMEM(runs, jnp.float32), pltpu.VMEM(runs, jnp.bfloat16)],
    )(
        *tables,
        *products,
        *sums,
        other_sums,
        in_vmem(key_part),
        in_vmem(value_part),
    )

    own_out = call(
        stage_out_kernel,
        pltpu.VMEM((half, half_out), jnp.bfloat16),
        [HBM, HBM],
        VMEM,
        0,
        half * half_out * 2,
        [pltpu.SemaphoreType.DMA((pairs,))],
    )(in_hbm(out_weight), attended)
    products, _ = project(
        out_kernel, chosen_out, gathered(attended_parts, "col", attended), [], [give_out, own_out], 0
    )
    products = spread(products, [])
    keep, send = call(
        functools.partial(sum_kernel, len(products)),
        [struct((rows, half)), struct((rows, half))],
        [VMEM] * (2 + len(products)),
        [VMEM, VMEM],
        rows * depth * 4,
        rows * depth * 8,
    )(hidden_in, attended, *products)
    return call(
        join_kernel,
        struct((1, rows, depth)),
        [VMEM, VMEM],
        HBM,
        0,
        rows * depth * 4,
        [pltpu.SemaphoreType.DMA((2 * pairs,))],
    )(keep, moved(send, "side", 1))


def per_device(*args):
    hidden_in, _, qkv_weight, out_weight, key_cache = args[:5]
    col_count, row_count = lax.axis_size("col"), lax.axis_size("row")
    fits = (
        lax.axis_size("side") == 2
        and qkv_weight.shape[1] == 2 * GROUP_WIDTH
        and row_count == 2
        and col_count > row_count
        and col_count & (col_count - 1) == 0
        and hidden_in.shape[0] % 32 == 0
        and key_cache.shape[1] % 16 == 0
        and hidden_in.shape[1] == 2 * OUT_WIDTH * (col_count // row_count)
    )
    return paired_plan(*args) if fits else general_plan(*args)


def solution(mesh):
    placed = (
        P(("groups", "col"), "row"),
        P("row"),
        P("row", "col"),
        P("row", "col"),
        P(("groups", "col"), None, "row"),
        P(("groups", "col"), None, "row"),
        P(("groups", "col")),
        P("groups"),
    )
    return jax.shard_map(
        per_device,
        mesh=mesh,
        in_specs=placed,
        out_specs=P("side", ("groups", "col"), "row"),
        check_vma=False,
    )
```

```python
import functools
import math

import jax
import jax.numpy as jnp
from jax import lax
from jax.experimental import pallas as pl
from jax.experimental.pallas import tpu as pltpu
from jax.sharding import PartitionSpec as P

D = 8192
HEADS = 64
KV_HEADS = 8
HEAD_DIM = 128
QKV = 10240


EPSILON = 1e-05
THETA = 500000.0


def swapped(value, axis, bit):
    mask = 2**bit
    pairs = [(source, source ^ mask) for source in range(lax.axis_size(axis))]
    return lax.ppermute(value, axis, pairs)


def rope_tables(lengths, head_dim):
    half_dim = head_dim // 2
    inv_freq = jnp.exp(
        -jnp.log(jnp.float32(THETA)) * jnp.arange(half_dim, dtype=jnp.float32) / half_dim
    )
    phases = lengths.astype(jnp.float32)[:, None] * inv_freq[None, :]
    return (jnp.cos(phases), jnp.sin(phases))


def rotate(vector, cos_vals, sine_vals):
    half_dim = vector.shape[-1] // 2
    front_half = vector[..., :half_dim]
    back_half = vector[..., half_dim:]
    return jnp.concatenate(
        [
            front_half * cos_vals - back_half * sine_vals,
            back_half * cos_vals + front_half * sine_vals,
        ],
        axis=-1,
    )


def attend(packed, key_block, value_block, lengths):
    slot_count = packed.shape[0]
    cache_size = key_block.shape[1]
    groups = key_block.shape[2] // HEAD_DIM
    per_group = HEADS // KV_HEADS
    grouped = packed.reshape(slot_count, groups, per_group + 2, HEAD_DIM)
    cos_vals, sine_vals = rope_tables(lengths, HEAD_DIM)
    queries = rotate(
        grouped[:, :, :per_group].astype(jnp.float32),
        cos_vals[:, None, None, :],
        sine_vals[:, None, None, :],
    ).astype(jnp.bfloat16)
    new_keys = rotate(
        grouped[:, :, per_group].astype(jnp.float32), cos_vals[:, None, :], sine_vals[:, None, :]
    ).astype(jnp.bfloat16)
    new_values = grouped[:, :, per_group + 1]
    cache_keys = key_block.reshape(slot_count, cache_size, groups, HEAD_DIM)
    cache_values = value_block.reshape(slot_count, cache_size, groups, HEAD_DIM)
    factor = HEAD_DIM ** (-0.5)
    cache_scores = (
        jnp.einsum("sghd,slgd->sghl", queries, cache_keys, preferred_element_type=jnp.float32)
        * factor
    )
    own_scores = (
        jnp.einsum("sghd,sgd->sgh", queries, new_keys, preferred_element_type=jnp.float32) * factor
    )
    in_cache = lax.broadcasted_iota(jnp.int32, (slot_count, cache_size), 1) < lengths[:, None]
    cache_scores = jnp.where(in_cache[:, None, None, :], cache_scores, -1e30)
    row_max = jnp.maximum(jnp.max(cache_scores, axis=-1), own_scores)
    cache_exp = jnp.exp(cache_scores - row_max[..., None])
    own_exp = jnp.exp(own_scores - row_max)
    denominator = jnp.sum(cache_exp, axis=-1) + own_exp
    cache_weight = (cache_exp / denominator[..., None]).astype(jnp.bfloat16)
    own_weight = (own_exp / denominator).astype(jnp.bfloat16)
    combined = jnp.einsum(
        "sghl,slgd->sghd", cache_weight, cache_values, preferred_element_type=jnp.float32
    )
    combined = (
        combined
        + own_weight.astype(jnp.float32)[..., None] * new_values.astype(jnp.float32)[:, :, None, :]
    )
    return combined.astype(jnp.bfloat16).reshape(slot_count, groups * per_group * HEAD_DIM)


def general_plan(
    hidden_in,
    norm_gain,
    qkv_weight,
    out_weight,
    key_cache,
    value_cache,
    cache_lengths,
    slot_request,
):
    side_index = lax.axis_index("side")
    is_weight = side_index == 0
    col_count = lax.axis_size("col")
    row_count = lax.axis_size("row")
    group_cols = col_count // row_count
    in_half = qkv_weight.shape[1] // 2
    out_half = out_weight.shape[1] // 2
    residual = hidden_in.astype(jnp.float32)
    square_sums = lax.psum(jnp.sum(residual * residual, axis=1), "row")
    normed = (
        residual
        * lax.rsqrt(square_sums[:, None] / D + EPSILON)
        * norm_gain.astype(jnp.float32)[None, :]
    ).astype(jnp.bfloat16)
    in_weight = lax.dynamic_slice_in_dim(qkv_weight, side_index * in_half, in_half, 1)
    partial_in = jnp.dot(
        lax.all_gather(normed, "col", axis=0, tiled=True),
        in_weight,
        preferred_element_type=jnp.float32,
    )
    in_slots = jnp.take(partial_in, slot_request, axis=0)
    own_width = QKV // row_count
    summed = lax.psum(in_slots.astype(jnp.bfloat16), "row")
    spread = lax.all_to_all(summed, "col", split_axis=0, concat_axis=1, tiled=True)
    own_columns = lax.dynamic_slice_in_dim(
        spread.reshape(spread.shape[0], col_count, in_half),
        lax.axis_index("row") * group_cols,
        group_cols,
        1,
    )
    slot_half = key_cache.shape[0] // 2
    halves = lax.all_to_all(
        own_columns[:, :, None, :], "side", split_axis=0, concat_axis=2, tiled=True
    )
    arrived = halves.reshape(slot_half, own_width)
    first_slot = side_index * slot_half
    key_part = lax.dynamic_slice_in_dim(key_cache, first_slot, slot_half, 0)
    value_part = lax.dynamic_slice_in_dim(value_cache, first_slot, slot_half, 0)
    length_part = lax.dynamic_slice_in_dim(cache_lengths, first_slot, slot_half, 0)
    attended = attend(arrived, key_part, value_part, length_part)
    out_cols = lax.dynamic_slice_in_dim(out_weight, side_index * out_half, out_half, 1)
    collected = lax.all_gather(attended, ("col", "side"), axis=0, tiled=True)
    out_slots = jnp.dot(collected, out_cols, preferred_element_type=jnp.float32)
    inverse = jnp.argsort(slot_request)
    out_requests = jnp.take(out_slots, inverse, axis=0)
    spread_out = lax.all_to_all(
        out_requests.astype(jnp.bfloat16), "col", split_axis=0, concat_axis=1, tiled=True
    ).astype(out_requests.dtype)
    out_view = spread_out.reshape(spread_out.shape[0], col_count, out_half)
    summed_out = lax.psum_scatter(
        out_view.astype(jnp.bfloat16), "row", scatter_dimension=1, tiled=True
    ).astype(jnp.float32)
    req_rows = hidden_in.shape[0]
    residual_view = residual.reshape(req_rows, group_cols, 2, out_half)
    residual_half = lax.dynamic_index_in_dim(residual_view, side_index, 2, keepdims=False)
    own_hidden = (residual_half + summed_out).astype(jnp.bfloat16)
    payload = jnp.where(is_weight, attended, own_hidden.reshape(attended.shape))
    received = swapped(payload, "side", 0)
    hidden = jnp.stack([own_hidden, received.reshape(own_hidden.shape)], axis=2).reshape(
        req_rows, residual.shape[1]
    )
    attention_rows = jnp.concatenate([received, attended], axis=0)
    result = jnp.where(is_weight, hidden, attention_rows)
    return result[None]


GROUP = HEADS // KV_HEADS
GROUP_WIDTH = (GROUP + 2) * HEAD_DIM
OUT_WIDTH = GROUP * HEAD_DIM
SLOTS = 8
VMEM = pl.BlockSpec(memory_space=pltpu.VMEM)
SMEM = pl.BlockSpec(memory_space=pltpu.SMEM)
HBM = pl.BlockSpec(memory_space=pl.ANY)
MIB = 2**20


def call(kernel, out_shape, in_specs, out_specs, flops, size, scratch=(), limit=16):
    return pl.pallas_call(
        kernel,
        out_shape=out_shape,
        in_specs=in_specs,
        out_specs=out_specs,
        scratch_shapes=list(scratch),
        compiler_params=pltpu.CompilerParams(vmem_limit_bytes=limit * MIB),
        cost_estimate=pl.CostEstimate(flops=flops, bytes_accessed=size, transcendentals=0),
    )


def in_vmem(value):
    return pltpu.with_memory_space_constraint(value, pltpu.VMEM)


def in_hbm(value):
    return pltpu.with_memory_space_constraint(value, pltpu.HBM)


def struct(shape, dtype=jnp.bfloat16):
    return jax.ShapeDtypeStruct(shape, dtype)


def moved(value, axis, mask):
    pairs = [(source, source ^ mask) for source in range(lax.axis_size(axis))]
    return lax.ppermute(value, axis, pairs)


def started(copies, sems):
    copies = [
        pltpu.make_async_copy(source, target, sems.at[i])
        for i, (source, target) in enumerate(copies)
    ]
    for copy in copies:
        copy.start()
    return copies


def run_copies(copies, sems):
    for copy in started(copies, sems):
        copy.wait()


def position():
    return lax.axis_index("side"), lax.axis_index("col")


def rows_copy(weight, target, half):
    depth, width = target.shape
    rows = pl.ds(pl.multiple_of(lax.axis_index("side") * depth, depth), depth)
    columns = pl.ds(pl.multiple_of(half * width, width), width)
    return weight.at[rows, columns], target


def stage_in_kernel(blocks, weight, slots, give_part, own_part, chosen, scratch, slot_part, sems):
    side, col = position()
    slots_copy, *copies = started(
        [
            (slots, slot_part),
            rows_copy(weight, give_part, 1 - side),
            rows_copy(weight, own_part, side),
        ],
        sems,
    )
    slots_copy.wait()
    chosen[...] = one_hot(slot_part, scratch, blocks, col, col).astype(jnp.bfloat16)
    for copy in copies:
        copy.wait()


def head_copies(weight, target, half):
    width = target.shape[1]
    columns = pl.ds(pl.multiple_of(half * width, width), width)
    copies = []
    for j in range(target.shape[0] // OUT_WIDTH):
        row = pl.multiple_of((2 * j + lax.axis_index("side")) * OUT_WIDTH, OUT_WIDTH)
        copies.append(
            (
                weight.at[pl.ds(row, OUT_WIDTH), columns],
                target.at[pl.ds(j * OUT_WIDTH, OUT_WIDTH), :],
            )
        )
    return copies


def stage_rest_kernel(blocks, lengths, weight, keys, values, slots, *refs):
    target, key_part, value_part, cosine, sine, length_of, chosen, scratch, sems = refs
    side, col = position()
    copies = []
    for j in range(key_part.shape[2] // HEAD_DIM):
        lane = pl.multiple_of((2 * j + side) * HEAD_DIM, HEAD_DIM)
        for cache, part in ((keys, key_part), (values, value_part)):
            copies.append(
                (
                    cache.at[:, :, pl.ds(lane, HEAD_DIM)],
                    part.at[:, :, pl.ds(j * HEAD_DIM, HEAD_DIM)],
                )
            )
    copies = started(copies + head_copies(weight, target, 1 - side), sems)
    cosine[...], sine[...], length_of[...] = rope(lengths, cosine.shape[0])
    chosen[...] = one_hot(slots, scratch, blocks, col, col).T.astype(jnp.bfloat16)
    for copy in copies:
        copy.wait()


def stage_out_kernel(weight, attended, own_part, sems):
    run_copies(head_copies(weight, own_part, lax.axis_index("side")), sems)


def one_hot(slots, scratch, blocks, slot_base, request_base):
    total = slots.shape[0]
    rows = total // blocks
    index = lax.broadcasted_iota(jnp.int32, (total, total), 0)
    request = (lax.div(index, rows) ^ request_base) * rows + lax.rem(index, rows)
    scratch[...] = jnp.where(slots[...].reshape(1, total) == request, 1.0, 0.0).T
    parts = [
        scratch[pl.ds(pl.multiple_of((slot_base ^ i) * rows, rows), rows), :]
        for i in range(blocks)
    ]
    return jnp.concatenate(parts, axis=0)


def pieces(sums):
    high = sums.astype(jnp.bfloat16).astype(jnp.float32)
    middle = (sums - high).astype(jnp.bfloat16).astype(jnp.float32)
    low = sums - high - middle
    lane = lax.broadcasted_iota(jnp.int32, (sums.shape[0], HEAD_DIM), 1)
    parts = jnp.where(lane == 0, high, jnp.where(lane == 1, middle, low))
    return jnp.where(lane < 3, parts, 0.0).astype(jnp.bfloat16)


def dot_columns(rows, weight, out):
    size, width = weight.shape[1], 512
    for start in range(0, size, width):
        part = slice(start, min(start + width, size))
        product = jnp.dot(rows, weight[:, part], preferred_element_type=jnp.float32)
        out[:, part] = product.astype(out.dtype)


def in_kernel(count, chosen, *refs):
    pieces_in, (_, gain, weight, give, permuted) = refs[:count], refs[count:]
    depth = pieces_in[0].shape[1]
    half = weight.shape[1]
    runs = depth // HEAD_DIM
    first = pl.multiple_of(lax.axis_index("side") * runs, runs)
    gains = gain[pl.ds(first, runs), :].astype(jnp.float32)
    values = jnp.concatenate([piece[...].astype(jnp.float32) for piece in pieces_in], axis=0)
    scaled = jnp.concatenate(
        [
            values[:, i * HEAD_DIM : (i + 1) * HEAD_DIM] * gains[i : i + 1, :]
            for i in range(runs)
        ],
        axis=1,
    )
    sums = pieces(jnp.sum(values * values, axis=1, keepdims=True))
    order = jnp.dot(
        chosen[...], scaled.astype(jnp.bfloat16), preferred_element_type=jnp.float32
    ).astype(jnp.bfloat16)
    permuted[...] = order
    own_sums = jnp.dot(chosen[...], sums, preferred_element_type=jnp.float32)
    give[:, half:] = own_sums.astype(jnp.bfloat16)
    dot_columns(order, weight, give)


def out_kernel(count, chosen, *refs):
    pieces_in, (_, weight, give, permuted) = refs[:count], refs[count:]
    values = jnp.concatenate([piece[...] for piece in pieces_in], axis=0)
    order = jnp.dot(chosen[...], values, preferred_element_type=jnp.float32).astype(jnp.bfloat16)
    permuted[...] = order
    dot_columns(order, weight, give)


def at_home():
    pairs = lax.axis_size("col") // lax.axis_size("row")
    return lax.axis_index("row") == lax.div(lax.axis_index("col"), pairs)


def merge_kernel(count, own, given, received, *outs):
    rows = outs[0].shape[0]
    half = own.shape[1]
    more = given.shape[1] - half
    pairs = count // 2

    def write(out, first):
        first = first if isinstance(first, int) else pl.multiple_of(first, rows)
        part = pl.ds(first, rows)
        total = own[part, :] + received[part, :half].astype(jnp.float32)
        out[...] = total.astype(jnp.bfloat16)

    write(outs[0], 0)
    write(outs[1], pairs * rows)
    home = at_home()
    for pair in range(1, pairs):
        write(outs[2 * pair], jnp.where(home, pairs + pair, pair) * rows)
        write(outs[2 * pair + 1], jnp.where(home, pair, pairs + pair) * rows)
    for out in outs[count:]:
        lanes = slice(half, half + more // 2)
        out[...] = jnp.concatenate([given[:rows, lanes], received[:rows, lanes]], axis=1)


def own_kernel(permuted, weight, own):
    dot_columns(permuted[...], weight, own)


def project(kernel, chosen, pieces_in, extra, weights, more):
    count = lax.axis_size("col")
    parts = len(pieces_in)
    depth = pieces_in[0].shape[1]
    rows = sum(part.shape[0] for part in pieces_in)
    half = weights[0].shape[1]
    flops = 2 * rows * depth * half
    give, permuted = call(
        functools.partial(kernel, parts),
        [struct((rows, half + more)), struct((rows, depth))],
        [VMEM] * (parts + len(extra) + 3),
        [VMEM, VMEM],
        flops,
        depth * half * 2,
    )(chosen, *pieces_in, in_vmem(weights[1]), *extra, in_vmem(weights[0]))
    received = moved(give, "side", 1)
    own = call(
        own_kernel,
        struct((rows, half), jnp.float32),
        [VMEM, VMEM],
        VMEM,
        flops,
        depth * half * 2,
    )(permuted, in_vmem(weights[1]))
    outs = [struct((rows // count, half))] * count
    if more:
        outs = outs + [struct((rows // count, more))]
    merged = call(
        functools.partial(merge_kernel, count),
        outs,
        [VMEM] * 3,
        [VMEM] * len(outs),
        rows * half,
        rows * half * 8,
    )(own, give, received)
    return merged[:count], merged[count:]


def gathered(parts, axis, whole=None):
    blocks = {0: parts}
    mask = lax.axis_size(axis) // 2
    while mask:
        blocks |= {
            known | mask: [
                moved(part, axis, mask)
                for part in ([whole] if mask == 1 and known == 0 and whole is not None else block)
            ]
            for known, block in blocks.items()
        }
        mask //= 2
    if whole is not None:
        blocks[0] = [whole]
    return [part for i in sorted(blocks) for part in blocks[i]]


def choose_kernel(own, passed, *refs):
    out = refs[-1]
    out[...] = jnp.where(at_home(), passed[...], own[...])


def direct(value, far, pair):
    pairs = lax.axis_size("col") // 2
    moves = []
    for col in range(2 * pairs):
        for row in range(2):
            home = row == col // pairs
            target = col ^ pair ^ (pairs if home == far else 0)
            moves.append((2 * col + row, 2 * target + (row if home else 1 - row)))
    return lax.ppermute(value, ("col", "row"), moves)


def spread(products, ready):
    own, passed, *rest = products
    pairs = len(products) // 2
    passed = moved(passed, "col", pairs)
    blocks = []
    for pair in range(1, pairs):
        blocks += [
            direct(rest[2 * pair - 1], False, pair),
            direct(rest[2 * pair - 2], True, pair),
        ]
    crossing = call(
        choose_kernel,
        struct(own.shape),
        [VMEM] * 2 + [HBM] * len(ready),
        VMEM,
        0,
        own.size * 4,
    )(own, passed, *ready)
    return [passed, *blocks, own, moved(crossing, "row", 1)]


def total_of(blocks, pair):
    if pair > 0:
        first, second = blocks[2 * pair - 1][...], blocks[2 * pair][...]
    else:
        passed, own, crossed = blocks[0], blocks[-2], blocks[-1]
        first, second = jnp.where(at_home(), own[...], passed[...]), crossed[...]
    return first.astype(jnp.float32) + second.astype(jnp.float32)


def rotated(vector, cosine, sine):
    return vector * cosine + pltpu.roll(vector, HEAD_DIM // 2, 1) * sine


def rope(lengths, rows):
    slot = lax.broadcasted_iota(jnp.int32, (rows, HEAD_DIM), 0)
    length_of = jnp.zeros((rows, HEAD_DIM), jnp.int32)
    for i in range(rows):
        length_of = jnp.where(slot == i, lengths[i], length_of)
    lane = lax.broadcasted_iota(jnp.int32, (rows, HEAD_DIM), 1)
    half = HEAD_DIM // 2
    step = lax.rem(lane, half).astype(jnp.float32)
    phases = length_of.astype(jnp.float32) * jnp.exp(-math.log(THETA) * step / half)
    sine = jnp.sin(phases)
    return jnp.cos(phases), jnp.where(lane < half, -sine, sine), length_of


def attend_all(count, parts, cosine, sine, lengths, *refs):
    pairs = (count - 1) // 2
    blocks, (sums, other_sums, keys, values) = refs[:count], refs[count : count + 4]
    refs = refs[count + 4 :]
    whole, outs, (scores_of, probs_of) = refs[0], refs[1 : parts + 1], refs[parts + 1 :]
    rows, cache = keys.shape[:2]
    low = lax.rem(lax.axis_index("col"), pairs)
    width = GROUP_WIDTH
    squares = sums[...].astype(jnp.float32) + other_sums[...].astype(jnp.float32)
    scale = lax.rsqrt(jnp.sum(squares, axis=1, keepdims=True) / D + EPSILON)
    factor = HEAD_DIM ** (-0.5)
    cosines, sines, length_of = cosine[...], sine[...], lengths[:, :1]
    lane = lax.broadcasted_iota(jnp.int32, (SLOTS, SLOTS * cache), 1)
    slot = lax.broadcasted_iota(jnp.int32, (SLOTS, SLOTS * cache), 0)
    position = lane - slot * cache
    runs = [slice(start, start + SLOTS) for start in range(0, rows, SLOTS)]
    filled = [(position >= 0) & (position < length_of[part]) for part in runs]
    own, new_values, own_probs = [], [], []
    for pair in range(pairs):
        total = total_of(blocks, pair)
        total = (total * scale).astype(jnp.bfloat16).astype(jnp.float32)
        heads = [total[:, h * HEAD_DIM : (h + 1) * HEAD_DIM] for h in range(GROUP + 2)]
        queries = [
            rotated(head, cosines, sines).astype(jnp.bfloat16).astype(jnp.float32)
            for head in heads[:GROUP]
        ]
        new_key = rotated(heads[GROUP], cosines, sines).astype(jnp.bfloat16).astype(jnp.float32)
        new_values.append(heads[GROUP + 1])
        own.append([jnp.sum(query * new_key, axis=1, keepdims=True) * factor for query in queries])
        lanes = pl.ds(pl.multiple_of((low ^ pair) * HEAD_DIM, HEAD_DIM), HEAD_DIM)
        for run, part in enumerate(runs):
            query = jnp.concatenate([head[part] for head in queries], axis=0)
            key = keys[part, :, lanes].reshape(SLOTS * cache, HEAD_DIM)
            scores_of[pair, run] = lax.dot_general(
                query.astype(jnp.bfloat16),
                key,
                (((1,), (1,)), ((), ())),
                preferred_element_type=jnp.float32,
            )
    for pair in range(pairs):
        for run, part in enumerate(runs):
            scores = (scores_of[pair, run] * factor).reshape(GROUP, SLOTS, SLOTS * cache)
            scores = jnp.where(filled[run][None], scores, -1e30)
            own_score = jnp.concatenate([head[part] for head in own[pair]], axis=0).reshape(
                GROUP, SLOTS, 1
            )
            highest = jnp.maximum(jnp.max(scores, axis=2, keepdims=True), own_score)
            weights = jnp.exp(scores - highest)
            own_weight = jnp.exp(own_score - highest)
            inverse = 1.0 / (jnp.sum(weights, axis=2, keepdims=True) + own_weight)
            probs = (weights * inverse).astype(jnp.bfloat16)
            probs_of[pair, run] = probs.reshape(GROUP * SLOTS, SLOTS * cache)
            own_probs.append((own_weight * inverse).astype(jnp.bfloat16).astype(jnp.float32))
    for pair in range(pairs):
        lanes = pl.ds(pl.multiple_of((low ^ pair) * HEAD_DIM, HEAD_DIM), HEAD_DIM)
        results = []
        for run, part in enumerate(runs):
            value = values[part, :, lanes].reshape(SLOTS * cache, HEAD_DIM)
            mixed = jnp.dot(probs_of[pair, run], value, preferred_element_type=jnp.float32)
            own_prob = own_probs[pair * len(runs) + run]
            results.append(
                mixed.reshape(GROUP, SLOTS, HEAD_DIM) + own_prob * new_values[pair][part][None]
            )
        for head in range(GROUP):
            at = pl.multiple_of((low ^ pair) * OUT_WIDTH + head * HEAD_DIM, HEAD_DIM)
            size = len(results) // parts
            for i, out in enumerate(outs):
                joined = jnp.concatenate(
                    [result[head] for result in results[i * size : (i + 1) * size]], axis=0
                )
                joined = joined.astype(jnp.bfloat16)
                out[:, pl.ds(at, HEAD_DIM)] = joined
                run = slice(i * joined.shape[0], (i + 1) * joined.shape[0])
                whole[run, pl.ds(at, HEAD_DIM)] = joined


def sum_kernel(count, hidden, attended, *refs):
    blocks, (keep, send) = refs[:count], refs[count:]
    rows, width = blocks[0].shape
    pairs = keep.shape[1] // width
    side = lax.axis_index("side")
    low = lax.rem(lax.axis_index("col"), pairs)
    for pair in range(pairs):
        column = low ^ pair
        total = total_of(blocks, pair)
        at = pl.ds(pl.multiple_of((2 * column + side) * width, width), width)
        hidden_out = (hidden[:, at].astype(jnp.float32) + total).astype(jnp.bfloat16)
        at = pl.ds(pl.multiple_of(column * width, width), width)
        attention = attended[:, at]
        keep[:, at] = jnp.where(side == 0, hidden_out, attention)
        send[:, at] = jnp.where(side == 0, attention, hidden_out)


def join_kernel(keep, received, out, sems):
    side = lax.axis_index("side")
    width = OUT_WIDTH
    copies = []
    for j in range(keep.shape[1] // width):
        part = slice(j * width, (j + 1) * width)
        for ref, core in ((keep, side), (received, 1 - side)):
            at = pl.ds(pl.multiple_of((2 * j + core) * width, width), width)
            copies.append((ref.at[:, part], out.at[0, :, at]))
    run_copies(copies, sems)


def paired_plan(
    hidden_in, norm_gain, qkv_weight, out_weight, key_cache, value_cache, cache_lengths, slot_request
):
    col_count, row_count = lax.axis_size("col"), lax.axis_size("row")
    pairs = col_count // row_count
    side = lax.axis_index("side")
    rows, depth = hidden_in.shape
    half = depth // 2
    cache = key_cache.shape[1]
    parts = 2
    piece = rows // parts

    own_part = lax.dynamic_slice_in_dim(hidden_in, side * half, half, 1)
    gain = norm_gain.reshape(depth // HEAD_DIM, HEAD_DIM)
    half_in, half_out = qkv_weight.shape[1] // 2, out_weight.shape[1] // 2
    total = rows * col_count
    square = (total, total)
    give_in, own_in, chosen_in = call(
        functools.partial(stage_in_kernel, col_count),
        [pltpu.VMEM((half, half_in), jnp.bfloat16)] * 2 + [struct(square)],
        [HBM, HBM],
        [VMEM] * 3,
        0,
        half * half_in * 4,
        [
            pltpu.VMEM(square, jnp.float32),
            pltpu.VMEM((total,), jnp.int32),
            pltpu.SemaphoreType.DMA((3,)),
        ],
    )(in_hbm(qkv_weight), in_hbm(slot_request))
    blocks = gathered(
        [own_part[i * piece : (i + 1) * piece] for i in range(parts)], "col"
    )
    table = struct((rows, HEAD_DIM), jnp.float32)
    give_out, key_part, value_part, *tables, chosen_out = call(
        functools.partial(stage_rest_kernel, col_count),
        [pltpu.VMEM((half, half_out), jnp.bfloat16)]
        + [pltpu.VMEM((rows, cache, pairs * HEAD_DIM), jnp.bfloat16)] * 2
        + [table, table, struct((rows, HEAD_DIM), jnp.int32), struct(square)],
        [SMEM, HBM, HBM, HBM, VMEM],
        [VMEM] * 7,
        0,
        half * half_out * 2 + 4 * rows * cache * pairs * HEAD_DIM,
        [pltpu.VMEM(square, jnp.float32), pltpu.SemaphoreType.DMA((3 * pairs,))],
    )(cache_lengths, in_hbm(out_weight), in_hbm(key_cache), in_hbm(value_cache), slot_request)
    products, sums = project(in_kernel, chosen_in, blocks, [gain], [give_in, own_in], HEAD_DIM)
    other_sums = moved(sums[0], "row", 1)
    products = spread(products, [other_sums])

    runs = (pairs, rows // SLOTS, GROUP * SLOTS, SLOTS * cache)
    attended, *attended_parts = call(
        functools.partial(attend_all, len(products), parts),
        [struct((rows, half))] + [struct((piece, half))] * parts,
        [VMEM] * (len(products) + 7),
        [VMEM] * (parts + 1),
        4 * rows * half * cache,
        0,
        [pltpu.VMEM(runs, jnp.float32), pltpu.VMEM(runs, jnp.bfloat16)],
    )(
        *tables,
        *products,
        *sums,
        other_sums,
        in_vmem(key_part),
        in_vmem(value_part),
    )

    own_out = call(
        stage_out_kernel,
        pltpu.VMEM((half, half_out), jnp.bfloat16),
        [HBM, HBM],
        VMEM,
        0,
        half * half_out * 2,
        [pltpu.SemaphoreType.DMA((pairs,))],
    )(in_hbm(out_weight), attended)
    products, _ = project(
        out_kernel, chosen_out, gathered(attended_parts, "col", attended), [], [give_out, own_out], 0
    )
    products = spread(products, [])
    keep, send = call(
        functools.partial(sum_kernel, len(products)),
        [struct((rows, half)), struct((rows, half))],
        [VMEM] * (2 + len(products)),
        [VMEM, VMEM],
        rows * depth * 4,
        rows * depth * 8,
    )(hidden_in, attended, *products)
    return call(
        join_kernel,
        struct((1, rows, depth)),
        [VMEM, VMEM],
        HBM,
        0,
        rows * depth * 4,
        [pltpu.SemaphoreType.DMA((2 * pairs,))],
    )(keep, moved(send, "side", 1))


def per_device(*args):
    hidden_in, _, qkv_weight, out_weight, key_cache = args[:5]
    col_count, row_count = lax.axis_size("col"), lax.axis_size("row")
    fits = (
        lax.axis_size("side") == 2
        and qkv_weight.shape[1] == 2 * GROUP_WIDTH
        and row_count == 2
        and col_count > row_count
        and col_count & (col_count - 1) == 0
        and hidden_in.shape[0] % 32 == 0
        and key_cache.shape[1] % 16 == 0
        and hidden_in.shape[1] == 2 * OUT_WIDTH * (col_count // row_count)
    )
    return paired_plan(*args) if fits else general_plan(*args)


def solution(mesh):
    placed = (
        P(("groups", "col"), "row"),
        P("row"),
        P("row", "col"),
        P("row", "col"),
        P(("groups", "col"), None, "row"),
        P(("groups", "col"), None, "row"),
        P(("groups", "col")),
        P("groups"),
    )
    return jax.shard_map(
        per_device,
        mesh=mesh,
        in_specs=placed,
        out_specs=P("side", ("groups", "col"), "row"),
        check_vma=False,
    )
```

```python
import functools
import math

import jax
import jax.numpy as jnp
from jax import lax
from jax.experimental import pallas as pl
from jax.experimental.pallas import tpu as pltpu
from jax.sharding import PartitionSpec as P

D = 8192
HEADS = 64
KV_HEADS = 8
HEAD_DIM = 128
QKV = 10240


EPSILON = 1e-05
THETA = 500000.0


def swapped(value, axis, bit):
    mask = 2**bit
    pairs = [(source, source ^ mask) for source in range(lax.axis_size(axis))]
    return lax.ppermute(value, axis, pairs)


def rope_tables(lengths, head_dim):
    half_dim = head_dim // 2
    inv_freq = jnp.exp(
        -jnp.log(jnp.float32(THETA)) * jnp.arange(half_dim, dtype=jnp.float32) / half_dim
    )
    phases = lengths.astype(jnp.float32)[:, None] * inv_freq[None, :]
    return (jnp.cos(phases), jnp.sin(phases))


def rotate(vector, cos_vals, sine_vals):
    half_dim = vector.shape[-1] // 2
    front_half = vector[..., :half_dim]
    back_half = vector[..., half_dim:]
    return jnp.concatenate(
        [
            front_half * cos_vals - back_half * sine_vals,
            back_half * cos_vals + front_half * sine_vals,
        ],
        axis=-1,
    )


def attend(packed, key_block, value_block, lengths):
    slot_count = packed.shape[0]
    cache_size = key_block.shape[1]
    groups = key_block.shape[2] // HEAD_DIM
    per_group = HEADS // KV_HEADS
    grouped = packed.reshape(slot_count, groups, per_group + 2, HEAD_DIM)
    cos_vals, sine_vals = rope_tables(lengths, HEAD_DIM)
    queries = rotate(
        grouped[:, :, :per_group].astype(jnp.float32),
        cos_vals[:, None, None, :],
        sine_vals[:, None, None, :],
    ).astype(jnp.bfloat16)
    new_keys = rotate(
        grouped[:, :, per_group].astype(jnp.float32), cos_vals[:, None, :], sine_vals[:, None, :]
    ).astype(jnp.bfloat16)
    new_values = grouped[:, :, per_group + 1]
    cache_keys = key_block.reshape(slot_count, cache_size, groups, HEAD_DIM)
    cache_values = value_block.reshape(slot_count, cache_size, groups, HEAD_DIM)
    factor = HEAD_DIM ** (-0.5)
    cache_scores = (
        jnp.einsum("sghd,slgd->sghl", queries, cache_keys, preferred_element_type=jnp.float32)
        * factor
    )
    own_scores = (
        jnp.einsum("sghd,sgd->sgh", queries, new_keys, preferred_element_type=jnp.float32) * factor
    )
    in_cache = lax.broadcasted_iota(jnp.int32, (slot_count, cache_size), 1) < lengths[:, None]
    cache_scores = jnp.where(in_cache[:, None, None, :], cache_scores, -1e30)
    row_max = jnp.maximum(jnp.max(cache_scores, axis=-1), own_scores)
    cache_exp = jnp.exp(cache_scores - row_max[..., None])
    own_exp = jnp.exp(own_scores - row_max)
    denominator = jnp.sum(cache_exp, axis=-1) + own_exp
    cache_weight = (cache_exp / denominator[..., None]).astype(jnp.bfloat16)
    own_weight = (own_exp / denominator).astype(jnp.bfloat16)
    combined = jnp.einsum(
        "sghl,slgd->sghd", cache_weight, cache_values, preferred_element_type=jnp.float32
    )
    combined = (
        combined
        + own_weight.astype(jnp.float32)[..., None] * new_values.astype(jnp.float32)[:, :, None, :]
    )
    return combined.astype(jnp.bfloat16).reshape(slot_count, groups * per_group * HEAD_DIM)


def general_plan(
    hidden_in,
    norm_gain,
    qkv_weight,
    out_weight,
    key_cache,
    value_cache,
    cache_lengths,
    slot_request,
):
    side_index = lax.axis_index("side")
    is_weight = side_index == 0
    col_count = lax.axis_size("col")
    row_count = lax.axis_size("row")
    group_cols = col_count // row_count
    in_half = qkv_weight.shape[1] // 2
    out_half = out_weight.shape[1] // 2
    residual = hidden_in.astype(jnp.float32)
    square_sums = lax.psum(jnp.sum(residual * residual, axis=1), "row")
    normed = (
        residual
        * lax.rsqrt(square_sums[:, None] / D + EPSILON)
        * norm_gain.astype(jnp.float32)[None, :]
    ).astype(jnp.bfloat16)
    in_weight = lax.dynamic_slice_in_dim(qkv_weight, side_index * in_half, in_half, 1)
    partial_in = jnp.dot(
        lax.all_gather(normed, "col", axis=0, tiled=True),
        in_weight,
        preferred_element_type=jnp.float32,
    )
    in_slots = jnp.take(partial_in, slot_request, axis=0)
    own_width = QKV // row_count
    summed = lax.psum(in_slots.astype(jnp.bfloat16), "row")
    spread = lax.all_to_all(summed, "col", split_axis=0, concat_axis=1, tiled=True)
    own_columns = lax.dynamic_slice_in_dim(
        spread.reshape(spread.shape[0], col_count, in_half),
        lax.axis_index("row") * group_cols,
        group_cols,
        1,
    )
    slot_half = key_cache.shape[0] // 2
    halves = lax.all_to_all(
        own_columns[:, :, None, :], "side", split_axis=0, concat_axis=2, tiled=True
    )
    arrived = halves.reshape(slot_half, own_width)
    first_slot = side_index * slot_half
    key_part = lax.dynamic_slice_in_dim(key_cache, first_slot, slot_half, 0)
    value_part = lax.dynamic_slice_in_dim(value_cache, first_slot, slot_half, 0)
    length_part = lax.dynamic_slice_in_dim(cache_lengths, first_slot, slot_half, 0)
    attended = attend(arrived, key_part, value_part, length_part)
    out_cols = lax.dynamic_slice_in_dim(out_weight, side_index * out_half, out_half, 1)
    collected = lax.all_gather(attended, ("col", "side"), axis=0, tiled=True)
    out_slots = jnp.dot(collected, out_cols, preferred_element_type=jnp.float32)
    inverse = jnp.argsort(slot_request)
    out_requests = jnp.take(out_slots, inverse, axis=0)
    spread_out = lax.all_to_all(
        out_requests.astype(jnp.bfloat16), "col", split_axis=0, concat_axis=1, tiled=True
    ).astype(out_requests.dtype)
    out_view = spread_out.reshape(spread_out.shape[0], col_count, out_half)
    summed_out = lax.psum_scatter(
        out_view.astype(jnp.bfloat16), "row", scatter_dimension=1, tiled=True
    ).astype(jnp.float32)
    req_rows = hidden_in.shape[0]
    residual_view = residual.reshape(req_rows, group_cols, 2, out_half)
    residual_half = lax.dynamic_index_in_dim(residual_view, side_index, 2, keepdims=False)
    own_hidden = (residual_half + summed_out).astype(jnp.bfloat16)
    payload = jnp.where(is_weight, attended, own_hidden.reshape(attended.shape))
    received = swapped(payload, "side", 0)
    hidden = jnp.stack([own_hidden, received.reshape(own_hidden.shape)], axis=2).reshape(
        req_rows, residual.shape[1]
    )
    attention_rows = jnp.concatenate([received, attended], axis=0)
    result = jnp.where(is_weight, hidden, attention_rows)
    return result[None]


GROUP = HEADS // KV_HEADS
GROUP_WIDTH = (GROUP + 2) * HEAD_DIM
OUT_WIDTH = GROUP * HEAD_DIM
SLOTS = 8
VMEM = pl.BlockSpec(memory_space=pltpu.VMEM)
SMEM = pl.BlockSpec(memory_space=pltpu.SMEM)
HBM = pl.BlockSpec(memory_space=pl.ANY)
MIB = 2**20


def call(kernel, out_shape, in_specs, out_specs, flops, size, scratch=(), limit=16):
    return pl.pallas_call(
        kernel,
        out_shape=out_shape,
        in_specs=in_specs,
        out_specs=out_specs,
        scratch_shapes=list(scratch),
        compiler_params=pltpu.CompilerParams(vmem_limit_bytes=limit * MIB),
        cost_estimate=pl.CostEstimate(flops=flops, bytes_accessed=size, transcendentals=0),
    )


def in_vmem(value):
    return pltpu.with_memory_space_constraint(value, pltpu.VMEM)


def in_hbm(value):
    return pltpu.with_memory_space_constraint(value, pltpu.HBM)


def struct(shape, dtype=jnp.bfloat16):
    return jax.ShapeDtypeStruct(shape, dtype)


def moved(value, axis, mask):
    pairs = [(source, source ^ mask) for source in range(lax.axis_size(axis))]
    return lax.ppermute(value, axis, pairs)


def started(copies, sems):
    copies = [
        pltpu.make_async_copy(source, target, sems.at[i])
        for i, (source, target) in enumerate(copies)
    ]
    for copy in copies:
        copy.start()
    return copies


def run_copies(copies, sems):
    for copy in started(copies, sems):
        copy.wait()


def position():
    return lax.axis_index("side"), lax.axis_index("col")


def rows_copy(weight, target, half):
    depth, width = target.shape
    rows = pl.ds(pl.multiple_of(lax.axis_index("side") * depth, depth), depth)
    columns = pl.ds(pl.multiple_of(half * width, width), width)
    return weight.at[rows, columns], target


def stage_in_kernel(blocks, weight, slots, give_part, own_part, chosen, scratch, slot_part, sems):
    side, col = position()
    slots_copy, *copies = started(
        [
            (slots, slot_part),
            rows_copy(weight, give_part, 1 - side),
            rows_copy(weight, own_part, side),
        ],
        sems,
    )
    slots_copy.wait()
    chosen[...] = one_hot(slot_part, scratch, blocks, col, col).astype(jnp.bfloat16)
    for copy in copies:
        copy.wait()


def head_copies(weight, target, half):
    width = target.shape[1]
    columns = pl.ds(pl.multiple_of(half * width, width), width)
    copies = []
    for j in range(target.shape[0] // OUT_WIDTH):
        row = pl.multiple_of((2 * j + lax.axis_index("side")) * OUT_WIDTH, OUT_WIDTH)
        copies.append(
            (
                weight.at[pl.ds(row, OUT_WIDTH), columns],
                target.at[pl.ds(j * OUT_WIDTH, OUT_WIDTH), :],
            )
        )
    return copies


def stage_rest_kernel(blocks, lengths, weight, keys, values, slots, *refs):
    target, key_part, value_part, cosine, sine, length_of, chosen, scratch, sems = refs
    side, col = position()
    copies = []
    for j in range(key_part.shape[2] // HEAD_DIM):
        lane = pl.multiple_of((2 * j + side) * HEAD_DIM, HEAD_DIM)
        for cache, part in ((keys, key_part), (values, value_part)):
            copies.append(
                (
                    cache.at[:, :, pl.ds(lane, HEAD_DIM)],
                    part.at[:, :, pl.ds(j * HEAD_DIM, HEAD_DIM)],
                )
            )
    copies = started(copies + head_copies(weight, target, 1 - side), sems)
    cosine[...], sine[...], length_of[...] = rope(lengths, cosine.shape[0])
    chosen[...] = one_hot(slots, scratch, blocks, col, col).T.astype(jnp.bfloat16)
    for copy in copies:
        copy.wait()


def stage_out_kernel(weight, attended, own_part, sems):
    run_copies(head_copies(weight, own_part, lax.axis_index("side")), sems)


def one_hot(slots, scratch, blocks, slot_base, request_base):
    total = slots.shape[0]
    rows = total // blocks
    index = lax.broadcasted_iota(jnp.int32, (total, total), 0)
    request = (lax.div(index, rows) ^ request_base) * rows + lax.rem(index, rows)
    scratch[...] = jnp.where(slots[...].reshape(1, total) == request, 1.0, 0.0).T
    parts = [
        scratch[pl.ds(pl.multiple_of((slot_base ^ i) * rows, rows), rows), :]
        for i in range(blocks)
    ]
    return jnp.concatenate(parts, axis=0)


def pieces(sums):
    high = sums.astype(jnp.bfloat16).astype(jnp.float32)
    middle = (sums - high).astype(jnp.bfloat16).astype(jnp.float32)
    low = sums - high - middle
    lane = lax.broadcasted_iota(jnp.int32, (sums.shape[0], HEAD_DIM), 1)
    parts = jnp.where(lane == 0, high, jnp.where(lane == 1, middle, low))
    return jnp.where(lane < 3, parts, 0.0).astype(jnp.bfloat16)


def dot_columns(rows, weight, out):
    size, width = weight.shape[1], 512
    for start in range(0, size, width):
        part = slice(start, min(start + width, size))
        product = jnp.dot(rows, weight[:, part], preferred_element_type=jnp.float32)
        out[:, part] = product.astype(out.dtype)


def in_kernel(count, chosen, *refs):
    pieces_in, (_, gain, weight, give, permuted) = refs[:count], refs[count:]
    depth = pieces_in[0].shape[1]
    half = weight.shape[1]
    runs = depth // HEAD_DIM
    first = pl.multiple_of(lax.axis_index("side") * runs, runs)
    gains = gain[pl.ds(first, runs), :].astype(jnp.float32)
    values = jnp.concatenate([piece[...].astype(jnp.float32) for piece in pieces_in], axis=0)
    scaled = jnp.concatenate(
        [
            values[:, i * HEAD_DIM : (i + 1) * HEAD_DIM] * gains[i : i + 1, :]
            for i in range(runs)
        ],
        axis=1,
    )
    sums = pieces(jnp.sum(values * values, axis=1, keepdims=True))
    order = jnp.dot(
        chosen[...], scaled.astype(jnp.bfloat16), preferred_element_type=jnp.float32
    ).astype(jnp.bfloat16)
    permuted[...] = order
    own_sums = jnp.dot(chosen[...], sums, preferred_element_type=jnp.float32)
    give[:, half:] = own_sums.astype(jnp.bfloat16)
    dot_columns(order, weight, give)


def out_kernel(count, chosen, *refs):
    pieces_in, (_, weight, give, permuted) = refs[:count], refs[count:]
    values = jnp.concatenate([piece[...] for piece in pieces_in], axis=0)
    order = jnp.dot(chosen[...], values, preferred_element_type=jnp.float32).astype(jnp.bfloat16)
    permuted[...] = order
    dot_columns(order, weight, give)


def at_home():
    pairs = lax.axis_size("col") // lax.axis_size("row")
    return lax.axis_index("row") == lax.div(lax.axis_index("col"), pairs)


def merge_kernel(count, own, given, received, *outs):
    rows = outs[0].shape[0]
    half = own.shape[1]
    more = given.shape[1] - half
    pairs = count // 2

    def write(out, first):
        first = first if isinstance(first, int) else pl.multiple_of(first, rows)
        part = pl.ds(first, rows)
        total = own[part, :] + received[part, :half].astype(jnp.float32)
        out[...] = total.astype(jnp.bfloat16)

    write(outs[0], 0)
    write(outs[1], pairs * rows)
    home = at_home()
    for pair in range(1, pairs):
        write(outs[2 * pair], jnp.where(home, pairs + pair, pair) * rows)
        write(outs[2 * pair + 1], jnp.where(home, pair, pairs + pair) * rows)
    for out in outs[count:]:
        lanes = slice(half, half + more // 2)
        out[...] = jnp.concatenate([given[:rows, lanes], received[:rows, lanes]], axis=1)


def own_kernel(permuted, weight, own):
    dot_columns(permuted[...], weight, own)


def project(kernel, chosen, pieces_in, extra, weights, more):
    count = lax.axis_size("col")
    parts = len(pieces_in)
    depth = pieces_in[0].shape[1]
    rows = sum(part.shape[0] for part in pieces_in)
    half = weights[0].shape[1]
    flops = 2 * rows * depth * half
    give, permuted = call(
        functools.partial(kernel, parts),
        [struct((rows, half + more)), struct((rows, depth))],
        [VMEM] * (parts + len(extra) + 3),
        [VMEM, VMEM],
        flops,
        depth * half * 2,
    )(chosen, *pieces_in, in_vmem(weights[1]), *extra, in_vmem(weights[0]))
    received = moved(give, "side", 1)
    own = call(
        own_kernel,
        struct((rows, half), jnp.float32),
        [VMEM, VMEM],
        VMEM,
        flops,
        depth * half * 2,
    )(permuted, in_vmem(weights[1]))
    outs = [struct((rows // count, half))] * count
    if more:
        outs = outs + [struct((rows // count, more))]
    merged = call(
        functools.partial(merge_kernel, count),
        outs,
        [VMEM] * 3,
        [VMEM] * len(outs),
        rows * half,
        rows * half * 8,
    )(own, give, received)
    return merged[:count], merged[count:]


def gathered(parts, axis, whole=None):
    blocks = {0: parts}
    mask = lax.axis_size(axis) // 2
    while mask:
        blocks |= {
            known | mask: [
                moved(part, axis, mask)
                for part in ([whole] if mask == 1 and known == 0 and whole is not None else block)
            ]
            for known, block in blocks.items()
        }
        mask //= 2
    if whole is not None:
        blocks[0] = [whole]
    return [part for i in sorted(blocks) for part in blocks[i]]


def choose_kernel(own, passed, *refs):
    out = refs[-1]
    out[...] = jnp.where(at_home(), passed[...], own[...])


def direct(value, far, pair):
    pairs = lax.axis_size("col") // 2
    moves = []
    for col in range(2 * pairs):
        for row in range(2):
            home = row == col // pairs
            target = col ^ pair ^ (pairs if home == far else 0)
            moves.append((2 * col + row, 2 * target + (row if home else 1 - row)))
    return lax.ppermute(value, ("col", "row"), moves)


def spread(products, ready):
    own, passed, *rest = products
    pairs = len(products) // 2
    passed = moved(passed, "col", pairs)
    blocks = []
    for pair in range(1, pairs):
        blocks += [
            direct(rest[2 * pair - 2], True, pair),
            direct(rest[2 * pair - 1], False, pair),
        ]
    crossing = call(
        choose_kernel,
        struct(own.shape),
        [VMEM] * 2 + [HBM] * len(ready),
        VMEM,
        0,
        own.size * 4,
    )(own, passed, *ready)
    return [passed, *blocks, own, moved(crossing, "row", 1)]


def total_of(blocks, pair):
    if pair > 0:
        first, second = blocks[2 * pair - 1][...], blocks[2 * pair][...]
    else:
        passed, own, crossed = blocks[0], blocks[-2], blocks[-1]
        first, second = jnp.where(at_home(), own[...], passed[...]), crossed[...]
    return first.astype(jnp.float32) + second.astype(jnp.float32)


def rotated(vector, cosine, sine):
    return vector * cosine + pltpu.roll(vector, HEAD_DIM // 2, 1) * sine


def rope(lengths, rows):
    slot = lax.broadcasted_iota(jnp.int32, (rows, HEAD_DIM), 0)
    length_of = jnp.zeros((rows, HEAD_DIM), jnp.int32)
    for i in range(rows):
        length_of = jnp.where(slot == i, lengths[i], length_of)
    lane = lax.broadcasted_iota(jnp.int32, (rows, HEAD_DIM), 1)
    half = HEAD_DIM // 2
    step = lax.rem(lane, half).astype(jnp.float32)
    phases = length_of.astype(jnp.float32) * jnp.exp(-math.log(THETA) * step / half)
    sine = jnp.sin(phases)
    return jnp.cos(phases), jnp.where(lane < half, -sine, sine), length_of


def attend_all(count, parts, cosine, sine, lengths, *refs):
    pairs = (count - 1) // 2
    blocks, (sums, other_sums, keys, values) = refs[:count], refs[count : count + 4]
    refs = refs[count + 4 :]
    whole, outs, (scores_of, probs_of) = refs[0], refs[1 : parts + 1], refs[parts + 1 :]
    rows, cache = keys.shape[:2]
    low = lax.rem(lax.axis_index("col"), pairs)
    width = GROUP_WIDTH
    squares = sums[...].astype(jnp.float32) + other_sums[...].astype(jnp.float32)
    scale = lax.rsqrt(jnp.sum(squares, axis=1, keepdims=True) / D + EPSILON)
    factor = HEAD_DIM ** (-0.5)
    cosines, sines, length_of = cosine[...], sine[...], lengths[:, :1]
    lane = lax.broadcasted_iota(jnp.int32, (SLOTS, SLOTS * cache), 1)
    slot = lax.broadcasted_iota(jnp.int32, (SLOTS, SLOTS * cache), 0)
    position = lane - slot * cache
    runs = [slice(start, start + SLOTS) for start in range(0, rows, SLOTS)]
    filled = [(position >= 0) & (position < length_of[part]) for part in runs]
    own, new_values, own_probs = [], [], []
    for pair in range(pairs):
        total = total_of(blocks, pair)
        total = (total * scale).astype(jnp.bfloat16).astype(jnp.float32)
        heads = [total[:, h * HEAD_DIM : (h + 1) * HEAD_DIM] for h in range(GROUP + 2)]
        queries = [
            rotated(head, cosines, sines).astype(jnp.bfloat16).astype(jnp.float32)
            for head in heads[:GROUP]
        ]
        new_key = rotated(heads[GROUP], cosines, sines).astype(jnp.bfloat16).astype(jnp.float32)
        new_values.append(heads[GROUP + 1])
        own.append([jnp.sum(query * new_key, axis=1, keepdims=True) * factor for query in queries])
        lanes = pl.ds(pl.multiple_of((low ^ pair) * HEAD_DIM, HEAD_DIM), HEAD_DIM)
        for run, part in enumerate(runs):
            query = jnp.concatenate([head[part] for head in queries], axis=0)
            key = keys[part, :, lanes].reshape(SLOTS * cache, HEAD_DIM)
            scores_of[pair, run] = lax.dot_general(
                query.astype(jnp.bfloat16),
                key,
                (((1,), (1,)), ((), ())),
                preferred_element_type=jnp.float32,
            )
    for pair in range(pairs):
        for run, part in enumerate(runs):
            scores = (scores_of[pair, run] * factor).reshape(GROUP, SLOTS, SLOTS * cache)
            scores = jnp.where(filled[run][None], scores, -1e30)
            own_score = jnp.concatenate([head[part] for head in own[pair]], axis=0).reshape(
                GROUP, SLOTS, 1
            )
            highest = jnp.maximum(jnp.max(scores, axis=2, keepdims=True), own_score)
            weights = jnp.exp(scores - highest)
            own_weight = jnp.exp(own_score - highest)
            inverse = 1.0 / (jnp.sum(weights, axis=2, keepdims=True) + own_weight)
            probs = (weights * inverse).astype(jnp.bfloat16)
            probs_of[pair, run] = probs.reshape(GROUP * SLOTS, SLOTS * cache)
            own_probs.append((own_weight * inverse).astype(jnp.bfloat16).astype(jnp.float32))
    for pair in range(pairs):
        lanes = pl.ds(pl.multiple_of((low ^ pair) * HEAD_DIM, HEAD_DIM), HEAD_DIM)
        results = []
        for run, part in enumerate(runs):
            value = values[part, :, lanes].reshape(SLOTS * cache, HEAD_DIM)
            mixed = jnp.dot(probs_of[pair, run], value, preferred_element_type=jnp.float32)
            own_prob = own_probs[pair * len(runs) + run]
            results.append(
                mixed.reshape(GROUP, SLOTS, HEAD_DIM) + own_prob * new_values[pair][part][None]
            )
        for head in range(GROUP):
            at = pl.multiple_of((low ^ pair) * OUT_WIDTH + head * HEAD_DIM, HEAD_DIM)
            size = len(results) // parts
            for i, out in enumerate(outs):
                joined = jnp.concatenate(
                    [result[head] for result in results[i * size : (i + 1) * size]], axis=0
                )
                joined = joined.astype(jnp.bfloat16)
                out[:, pl.ds(at, HEAD_DIM)] = joined
                run = slice(i * joined.shape[0], (i + 1) * joined.shape[0])
                whole[run, pl.ds(at, HEAD_DIM)] = joined


def sum_kernel(count, hidden, attended, *refs):
    blocks, (keep, send) = refs[:count], refs[count:]
    rows, width = blocks[0].shape
    pairs = keep.shape[1] // width
    side = lax.axis_index("side")
    low = lax.rem(lax.axis_index("col"), pairs)
    for pair in range(pairs):
        column = low ^ pair
        total = total_of(blocks, pair)
        at = pl.ds(pl.multiple_of((2 * column + side) * width, width), width)
        hidden_out = (hidden[:, at].astype(jnp.float32) + total).astype(jnp.bfloat16)
        at = pl.ds(pl.multiple_of(column * width, width), width)
        attention = attended[:, at]
        keep[:, at] = jnp.where(side == 0, hidden_out, attention)
        send[:, at] = jnp.where(side == 0, attention, hidden_out)


def join_kernel(keep, received, out, sems):
    side = lax.axis_index("side")
    width = OUT_WIDTH
    copies = []
    for j in range(keep.shape[1] // width):
        part = slice(j * width, (j + 1) * width)
        for ref, core in ((keep, side), (received, 1 - side)):
            at = pl.ds(pl.multiple_of((2 * j + core) * width, width), width)
            copies.append((ref.at[:, part], out.at[0, :, at]))
    run_copies(copies, sems)


def paired_plan(
    hidden_in, norm_gain, qkv_weight, out_weight, key_cache, value_cache, cache_lengths, slot_request
):
    col_count, row_count = lax.axis_size("col"), lax.axis_size("row")
    pairs = col_count // row_count
    side = lax.axis_index("side")
    rows, depth = hidden_in.shape
    half = depth // 2
    cache = key_cache.shape[1]
    parts = 2
    piece = rows // parts

    own_part = lax.dynamic_slice_in_dim(hidden_in, side * half, half, 1)
    gain = norm_gain.reshape(depth // HEAD_DIM, HEAD_DIM)
    half_in, half_out = qkv_weight.shape[1] // 2, out_weight.shape[1] // 2
    total = rows * col_count
    square = (total, total)
    give_in, own_in, chosen_in = call(
        functools.partial(stage_in_kernel, col_count),
        [pltpu.VMEM((half, half_in), jnp.bfloat16)] * 2 + [struct(square)],
        [HBM, HBM],
        [VMEM] * 3,
        0,
        half * half_in * 4,
        [
            pltpu.VMEM(square, jnp.float32),
            pltpu.VMEM((total,), jnp.int32),
            pltpu.SemaphoreType.DMA((3,)),
        ],
    )(in_hbm(qkv_weight), in_hbm(slot_request))
    blocks = gathered(
        [own_part[i * piece : (i + 1) * piece] for i in range(parts)], "col"
    )
    table = struct((rows, HEAD_DIM), jnp.float32)
    give_out, key_part, value_part, *tables, chosen_out = call(
        functools.partial(stage_rest_kernel, col_count),
        [pltpu.VMEM((half, half_out), jnp.bfloat16)]
        + [pltpu.VMEM((rows, cache, pairs * HEAD_DIM), jnp.bfloat16)] * 2
        + [table, table, struct((rows, HEAD_DIM), jnp.int32), struct(square)],
        [SMEM, HBM, HBM, HBM, VMEM],
        [VMEM] * 7,
        0,
        half * half_out * 2 + 4 * rows * cache * pairs * HEAD_DIM,
        [pltpu.VMEM(square, jnp.float32), pltpu.SemaphoreType.DMA((3 * pairs,))],
    )(cache_lengths, in_hbm(out_weight), in_hbm(key_cache), in_hbm(value_cache), slot_request)
    products, sums = project(in_kernel, chosen_in, blocks, [gain], [give_in, own_in], HEAD_DIM)
    other_sums = moved(sums[0], "row", 1)
    products = spread(products, [other_sums])

    runs = (pairs, rows // SLOTS, GROUP * SLOTS, SLOTS * cache)
    attended, *attended_parts = call(
        functools.partial(attend_all, len(products), parts),
        [struct((rows, half))] + [struct((piece, half))] * parts,
        [VMEM] * (len(products) + 7),
        [VMEM] * (parts + 1),
        4 * rows * half * cache,
        0,
        [pltpu.VMEM(runs, jnp.float32), pltpu.VMEM(runs, jnp.bfloat16)],
    )(
        *tables,
        *products,
        *sums,
        other_sums,
        in_vmem(key_part),
        in_vmem(value_part),
    )

    own_out = call(
        stage_out_kernel,
        pltpu.VMEM((half, half_out), jnp.bfloat16),
        [HBM, HBM],
        VMEM,
        0,
        half * half_out * 2,
        [pltpu.SemaphoreType.DMA((pairs,))],
    )(in_hbm(out_weight), attended)
    products, _ = project(
        out_kernel, chosen_out, gathered(attended_parts, "col"), [], [give_out, own_out], 0
    )
    products = spread(products, [])
    keep, send = call(
        functools.partial(sum_kernel, len(products)),
        [struct((rows, half)), struct((rows, half))],
        [VMEM] * (2 + len(products)),
        [VMEM, VMEM],
        rows * depth * 4,
        rows * depth * 8,
    )(hidden_in, attended, *products)
    return call(
        join_kernel,
        struct((1, rows, depth)),
        [VMEM, VMEM],
        HBM,
        0,
        rows * depth * 4,
        [pltpu.SemaphoreType.DMA((2 * pairs,))],
    )(keep, moved(send, "side", 1))


def per_device(*args):
    hidden_in, _, qkv_weight, out_weight, key_cache = args[:5]
    col_count, row_count = lax.axis_size("col"), lax.axis_size("row")
    fits = (
        lax.axis_size("side") == 2
        and qkv_weight.shape[1] == 2 * GROUP_WIDTH
        and row_count == 2
        and col_count > row_count
        and col_count & (col_count - 1) == 0
        and hidden_in.shape[0] % 32 == 0
        and key_cache.shape[1] % 16 == 0
        and hidden_in.shape[1] == 2 * OUT_WIDTH * (col_count // row_count)
    )
    return paired_plan(*args) if fits else general_plan(*args)


def solution(mesh):
    placed = (
        P(("groups", "col"), "row"),
        P("row"),
        P("row", "col"),
        P("row", "col"),
        P(("groups", "col"), None, "row"),
        P(("groups", "col"), None, "row"),
        P(("groups", "col")),
        P("groups"),
    )
    return jax.shard_map(
        per_device,
        mesh=mesh,
        in_specs=placed,
        out_specs=P("side", ("groups", "col"), "row"),
        check_vma=False,
    )
```

```python
import functools
import math

import jax
import jax.numpy as jnp
from jax import lax
from jax.experimental import pallas as pl
from jax.experimental.pallas import tpu as pltpu
from jax.sharding import PartitionSpec as P

D = 8192
HEADS = 64
KV_HEADS = 8
HEAD_DIM = 128
QKV = 10240


EPSILON = 1e-05
THETA = 500000.0


def swapped(value, axis, bit):
    mask = 2**bit
    pairs = [(source, source ^ mask) for source in range(lax.axis_size(axis))]
    return lax.ppermute(value, axis, pairs)


def rope_tables(lengths, head_dim):
    half_dim = head_dim // 2
    inv_freq = jnp.exp(
        -jnp.log(jnp.float32(THETA)) * jnp.arange(half_dim, dtype=jnp.float32) / half_dim
    )
    phases = lengths.astype(jnp.float32)[:, None] * inv_freq[None, :]
    return (jnp.cos(phases), jnp.sin(phases))


def rotate(vector, cos_vals, sine_vals):
    half_dim = vector.shape[-1] // 2
    front_half = vector[..., :half_dim]
    back_half = vector[..., half_dim:]
    return jnp.concatenate(
        [
            front_half * cos_vals - back_half * sine_vals,
            back_half * cos_vals + front_half * sine_vals,
        ],
        axis=-1,
    )


def attend(packed, key_block, value_block, lengths):
    slot_count = packed.shape[0]
    cache_size = key_block.shape[1]
    groups = key_block.shape[2] // HEAD_DIM
    per_group = HEADS // KV_HEADS
    grouped = packed.reshape(slot_count, groups, per_group + 2, HEAD_DIM)
    cos_vals, sine_vals = rope_tables(lengths, HEAD_DIM)
    queries = rotate(
        grouped[:, :, :per_group].astype(jnp.float32),
        cos_vals[:, None, None, :],
        sine_vals[:, None, None, :],
    ).astype(jnp.bfloat16)
    new_keys = rotate(
        grouped[:, :, per_group].astype(jnp.float32), cos_vals[:, None, :], sine_vals[:, None, :]
    ).astype(jnp.bfloat16)
    new_values = grouped[:, :, per_group + 1]
    cache_keys = key_block.reshape(slot_count, cache_size, groups, HEAD_DIM)
    cache_values = value_block.reshape(slot_count, cache_size, groups, HEAD_DIM)
    factor = HEAD_DIM ** (-0.5)
    cache_scores = (
        jnp.einsum("sghd,slgd->sghl", queries, cache_keys, preferred_element_type=jnp.float32)
        * factor
    )
    own_scores = (
        jnp.einsum("sghd,sgd->sgh", queries, new_keys, preferred_element_type=jnp.float32) * factor
    )
    in_cache = lax.broadcasted_iota(jnp.int32, (slot_count, cache_size), 1) < lengths[:, None]
    cache_scores = jnp.where(in_cache[:, None, None, :], cache_scores, -1e30)
    row_max = jnp.maximum(jnp.max(cache_scores, axis=-1), own_scores)
    cache_exp = jnp.exp(cache_scores - row_max[..., None])
    own_exp = jnp.exp(own_scores - row_max)
    denominator = jnp.sum(cache_exp, axis=-1) + own_exp
    cache_weight = (cache_exp / denominator[..., None]).astype(jnp.bfloat16)
    own_weight = (own_exp / denominator).astype(jnp.bfloat16)
    combined = jnp.einsum(
        "sghl,slgd->sghd", cache_weight, cache_values, preferred_element_type=jnp.float32
    )
    combined = (
        combined
        + own_weight.astype(jnp.float32)[..., None] * new_values.astype(jnp.float32)[:, :, None, :]
    )
    return combined.astype(jnp.bfloat16).reshape(slot_count, groups * per_group * HEAD_DIM)


def general_plan(
    hidden_in,
    norm_gain,
    qkv_weight,
    out_weight,
    key_cache,
    value_cache,
    cache_lengths,
    slot_request,
):
    side_index = lax.axis_index("side")
    is_weight = side_index == 0
    col_count = lax.axis_size("col")
    row_count = lax.axis_size("row")
    group_cols = col_count // row_count
    in_half = qkv_weight.shape[1] // 2
    out_half = out_weight.shape[1] // 2
    residual = hidden_in.astype(jnp.float32)
    square_sums = lax.psum(jnp.sum(residual * residual, axis=1), "row")
    normed = (
        residual
        * lax.rsqrt(square_sums[:, None] / D + EPSILON)
        * norm_gain.astype(jnp.float32)[None, :]
    ).astype(jnp.bfloat16)
    in_weight = lax.dynamic_slice_in_dim(qkv_weight, side_index * in_half, in_half, 1)
    partial_in = jnp.dot(
        lax.all_gather(normed, "col", axis=0, tiled=True),
        in_weight,
        preferred_element_type=jnp.float32,
    )
    in_slots = jnp.take(partial_in, slot_request, axis=0)
    own_width = QKV // row_count
    summed = lax.psum(in_slots.astype(jnp.bfloat16), "row")
    spread = lax.all_to_all(summed, "col", split_axis=0, concat_axis=1, tiled=True)
    own_columns = lax.dynamic_slice_in_dim(
        spread.reshape(spread.shape[0], col_count, in_half),
        lax.axis_index("row") * group_cols,
        group_cols,
        1,
    )
    slot_half = key_cache.shape[0] // 2
    halves = lax.all_to_all(
        own_columns[:, :, None, :], "side", split_axis=0, concat_axis=2, tiled=True
    )
    arrived = halves.reshape(slot_half, own_width)
    first_slot = side_index * slot_half
    key_part = lax.dynamic_slice_in_dim(key_cache, first_slot, slot_half, 0)
    value_part = lax.dynamic_slice_in_dim(value_cache, first_slot, slot_half, 0)
    length_part = lax.dynamic_slice_in_dim(cache_lengths, first_slot, slot_half, 0)
    attended = attend(arrived, key_part, value_part, length_part)
    out_cols = lax.dynamic_slice_in_dim(out_weight, side_index * out_half, out_half, 1)
    collected = lax.all_gather(attended, ("col", "side"), axis=0, tiled=True)
    out_slots = jnp.dot(collected, out_cols, preferred_element_type=jnp.float32)
    inverse = jnp.argsort(slot_request)
    out_requests = jnp.take(out_slots, inverse, axis=0)
    spread_out = lax.all_to_all(
        out_requests.astype(jnp.bfloat16), "col", split_axis=0, concat_axis=1, tiled=True
    ).astype(out_requests.dtype)
    out_view = spread_out.reshape(spread_out.shape[0], col_count, out_half)
    summed_out = lax.psum_scatter(
        out_view.astype(jnp.bfloat16), "row", scatter_dimension=1, tiled=True
    ).astype(jnp.float32)
    req_rows = hidden_in.shape[0]
    residual_view = residual.reshape(req_rows, group_cols, 2, out_half)
    residual_half = lax.dynamic_index_in_dim(residual_view, side_index, 2, keepdims=False)
    own_hidden = (residual_half + summed_out).astype(jnp.bfloat16)
    payload = jnp.where(is_weight, attended, own_hidden.reshape(attended.shape))
    received = swapped(payload, "side", 0)
    hidden = jnp.stack([own_hidden, received.reshape(own_hidden.shape)], axis=2).reshape(
        req_rows, residual.shape[1]
    )
    attention_rows = jnp.concatenate([received, attended], axis=0)
    result = jnp.where(is_weight, hidden, attention_rows)
    return result[None]


GROUP = HEADS // KV_HEADS
GROUP_WIDTH = (GROUP + 2) * HEAD_DIM
OUT_WIDTH = GROUP * HEAD_DIM
SLOTS = 8
VMEM = pl.BlockSpec(memory_space=pltpu.VMEM)
SMEM = pl.BlockSpec(memory_space=pltpu.SMEM)
HBM = pl.BlockSpec(memory_space=pl.ANY)
MIB = 2**20


def call(kernel, out_shape, in_specs, out_specs, flops, size, scratch=(), limit=16):
    return pl.pallas_call(
        kernel,
        out_shape=out_shape,
        in_specs=in_specs,
        out_specs=out_specs,
        scratch_shapes=list(scratch),
        compiler_params=pltpu.CompilerParams(vmem_limit_bytes=limit * MIB),
        cost_estimate=pl.CostEstimate(flops=flops, bytes_accessed=size, transcendentals=0),
    )


def in_vmem(value):
    return pltpu.with_memory_space_constraint(value, pltpu.VMEM)


def in_hbm(value):
    return pltpu.with_memory_space_constraint(value, pltpu.HBM)


def struct(shape, dtype=jnp.bfloat16):
    return jax.ShapeDtypeStruct(shape, dtype)


def moved(value, axis, mask):
    pairs = [(source, source ^ mask) for source in range(lax.axis_size(axis))]
    return lax.ppermute(value, axis, pairs)


def started(copies, sems):
    copies = [
        pltpu.make_async_copy(source, target, sems.at[i])
        for i, (source, target) in enumerate(copies)
    ]
    for copy in copies:
        copy.start()
    return copies


def run_copies(copies, sems):
    for copy in started(copies, sems):
        copy.wait()


def position():
    return lax.axis_index("side"), lax.axis_index("col")


def rows_copy(weight, target, half):
    depth, width = target.shape
    rows = pl.ds(pl.multiple_of(lax.axis_index("side") * depth, depth), depth)
    columns = pl.ds(pl.multiple_of(half * width, width), width)
    return weight.at[rows, columns], target


def stage_in_kernel(blocks, weight, slots, give_part, own_part, chosen, scratch, slot_part, sems):
    side, col = position()
    slots_copy, *copies = started(
        [
            (slots, slot_part),
            rows_copy(weight, give_part, 1 - side),
            rows_copy(weight, own_part, side),
        ],
        sems,
    )
    slots_copy.wait()
    chosen[...] = one_hot(slot_part, scratch, blocks, col, col).astype(jnp.bfloat16)
    for copy in copies:
        copy.wait()


def head_copies(weight, target, half):
    width = target.shape[1]
    columns = pl.ds(pl.multiple_of(half * width, width), width)
    copies = []
    for j in range(target.shape[0] // OUT_WIDTH):
        row = pl.multiple_of((2 * j + lax.axis_index("side")) * OUT_WIDTH, OUT_WIDTH)
        copies.append(
            (
                weight.at[pl.ds(row, OUT_WIDTH), columns],
                target.at[pl.ds(j * OUT_WIDTH, OUT_WIDTH), :],
            )
        )
    return copies


def stage_rest_kernel(blocks, lengths, weight, keys, values, slots, *refs):
    target, key_part, value_part, cosine, sine, length_of, chosen, scratch, sems = refs
    side, col = position()
    copies = []
    for j in range(key_part.shape[2] // HEAD_DIM):
        lane = pl.multiple_of((2 * j + side) * HEAD_DIM, HEAD_DIM)
        for cache, part in ((keys, key_part), (values, value_part)):
            copies.append(
                (
                    cache.at[:, :, pl.ds(lane, HEAD_DIM)],
                    part.at[:, :, pl.ds(j * HEAD_DIM, HEAD_DIM)],
                )
            )
    copies = started(copies + head_copies(weight, target, 1 - side), sems)
    cosine[...], sine[...], length_of[...] = rope(lengths, cosine.shape[0])
    chosen[...] = one_hot(slots, scratch, blocks, col, col).T.astype(jnp.bfloat16)
    for copy in copies:
        copy.wait()


def stage_out_kernel(weight, attended, own_part, sems):
    run_copies(head_copies(weight, own_part, lax.axis_index("side")), sems)


def one_hot(slots, scratch, blocks, slot_base, request_base):
    total = slots.shape[0]
    rows = total // blocks
    index = lax.broadcasted_iota(jnp.int32, (total, total), 0)
    request = (lax.div(index, rows) ^ request_base) * rows + lax.rem(index, rows)
    scratch[...] = jnp.where(slots[...].reshape(1, total) == request, 1.0, 0.0).T
    parts = [
        scratch[pl.ds(pl.multiple_of((slot_base ^ i) * rows, rows), rows), :]
        for i in range(blocks)
    ]
    return jnp.concatenate(parts, axis=0)


def pieces(sums):
    high = sums.astype(jnp.bfloat16).astype(jnp.float32)
    middle = (sums - high).astype(jnp.bfloat16).astype(jnp.float32)
    low = sums - high - middle
    lane = lax.broadcasted_iota(jnp.int32, (sums.shape[0], HEAD_DIM), 1)
    parts = jnp.where(lane == 0, high, jnp.where(lane == 1, middle, low))
    return jnp.where(lane < 3, parts, 0.0).astype(jnp.bfloat16)


def dot_columns(rows, weight, out):
    size, width = weight.shape[1], 1024
    for start in range(0, size, width):
        part = slice(start, min(start + width, size))
        product = jnp.dot(rows, weight[:, part], preferred_element_type=jnp.float32)
        out[:, part] = product.astype(out.dtype)


def in_kernel(count, chosen, *refs):
    pieces_in, (_, gain, weight, give, permuted) = refs[:count], refs[count:]
    depth = pieces_in[0].shape[1]
    half = weight.shape[1]
    runs = depth // HEAD_DIM
    first = pl.multiple_of(lax.axis_index("side") * runs, runs)
    gains = gain[pl.ds(first, runs), :].astype(jnp.float32)
    values = jnp.concatenate([piece[...].astype(jnp.float32) for piece in pieces_in], axis=0)
    scaled = jnp.concatenate(
        [
            values[:, i * HEAD_DIM : (i + 1) * HEAD_DIM] * gains[i : i + 1, :]
            for i in range(runs)
        ],
        axis=1,
    )
    sums = pieces(jnp.sum(values * values, axis=1, keepdims=True))
    order = jnp.dot(
        chosen[...], scaled.astype(jnp.bfloat16), preferred_element_type=jnp.float32
    ).astype(jnp.bfloat16)
    permuted[...] = order
    own_sums = jnp.dot(chosen[...], sums, preferred_element_type=jnp.float32)
    give[:, half:] = own_sums.astype(jnp.bfloat16)
    dot_columns(order, weight, give)


def out_kernel(count, chosen, *refs):
    pieces_in, (_, weight, give, permuted) = refs[:count], refs[count:]
    values = jnp.concatenate([piece[...] for piece in pieces_in], axis=0)
    order = jnp.dot(chosen[...], values, preferred_element_type=jnp.float32).astype(jnp.bfloat16)
    permuted[...] = order
    dot_columns(order, weight, give)


def at_home():
    pairs = lax.axis_size("col") // lax.axis_size("row")
    return lax.axis_index("row") == lax.div(lax.axis_index("col"), pairs)


def merge_kernel(count, own, given, received, *outs):
    rows = outs[0].shape[0]
    half = own.shape[1]
    more = given.shape[1] - half
    pairs = count // 2

    def write(out, first):
        first = first if isinstance(first, int) else pl.multiple_of(first, rows)
        part = pl.ds(first, rows)
        total = own[part, :] + received[part, :half].astype(jnp.float32)
        out[...] = total.astype(jnp.bfloat16)

    write(outs[0], 0)
    write(outs[1], pairs * rows)
    home = at_home()
    for pair in range(1, pairs):
        write(outs[2 * pair], jnp.where(home, pairs + pair, pair) * rows)
        write(outs[2 * pair + 1], jnp.where(home, pair, pairs + pair) * rows)
    for out in outs[count:]:
        lanes = slice(half, half + more // 2)
        out[...] = jnp.concatenate([given[:rows, lanes], received[:rows, lanes]], axis=1)


def own_kernel(permuted, weight, own):
    dot_columns(permuted[...], weight, own)


def project(kernel, chosen, pieces_in, extra, weights, more):
    count = lax.axis_size("col")
    parts = len(pieces_in)
    depth = pieces_in[0].shape[1]
    rows = sum(part.shape[0] for part in pieces_in)
    half = weights[0].shape[1]
    flops = 2 * rows * depth * half
    give, permuted = call(
        functools.partial(kernel, parts),
        [struct((rows, half + more)), struct((rows, depth))],
        [VMEM] * (parts + len(extra) + 3),
        [VMEM, VMEM],
        flops,
        depth * half * 2,
    )(chosen, *pieces_in, in_vmem(weights[1]), *extra, in_vmem(weights[0]))
    received = moved(give, "side", 1)
    own = call(
        own_kernel,
        struct((rows, half), jnp.float32),
        [VMEM, VMEM],
        VMEM,
        flops,
        depth * half * 2,
    )(permuted, in_vmem(weights[1]))
    outs = [struct((rows // count, half))] * count
    if more:
        outs = outs + [struct((rows // count, more))]
    merged = call(
        functools.partial(merge_kernel, count),
        outs,
        [VMEM] * 3,
        [VMEM] * len(outs),
        rows * half,
        rows * half * 8,
    )(own, give, received)
    return merged[:count], merged[count:]


def gathered(parts, axis, whole=None):
    blocks = {0: parts}
    mask = lax.axis_size(axis) // 2
    while mask:
        blocks |= {
            known | mask: [
                moved(part, axis, mask)
                for part in ([whole] if mask == 1 and known == 0 and whole is not None else block)
            ]
            for known, block in blocks.items()
        }
        mask //= 2
    if whole is not None:
        blocks[0] = [whole]
    return [part for i in sorted(blocks) for part in blocks[i]]


def choose_kernel(own, passed, *refs):
    out = refs[-1]
    out[...] = jnp.where(at_home(), passed[...], own[...])


def direct(value, far, pair):
    pairs = lax.axis_size("col") // 2
    moves = []
    for col in range(2 * pairs):
        for row in range(2):
            home = row == col // pairs
            target = col ^ pair ^ (pairs if home == far else 0)
            moves.append((2 * col + row, 2 * target + (row if home else 1 - row)))
    return lax.ppermute(value, ("col", "row"), moves)


def spread(products, ready):
    own, passed, *rest = products
    pairs = len(products) // 2
    passed = moved(passed, "col", pairs)
    blocks = []
    for pair in range(1, pairs):
        blocks += [
            direct(rest[2 * pair - 2], True, pair),
            direct(rest[2 * pair - 1], False, pair),
        ]
    crossing = call(
        choose_kernel,
        struct(own.shape),
        [VMEM] * 2 + [HBM] * len(ready),
        VMEM,
        0,
        own.size * 4,
    )(own, passed, *ready)
    return [passed, *blocks, own, moved(crossing, "row", 1)]


def total_of(blocks, pair):
    if pair > 0:
        first, second = blocks[2 * pair - 1][...], blocks[2 * pair][...]
    else:
        passed, own, crossed = blocks[0], blocks[-2], blocks[-1]
        first, second = jnp.where(at_home(), own[...], passed[...]), crossed[...]
    return first.astype(jnp.float32) + second.astype(jnp.float32)


def rotated(vector, cosine, sine):
    return vector * cosine + pltpu.roll(vector, HEAD_DIM // 2, 1) * sine


def rope(lengths, rows):
    slot = lax.broadcasted_iota(jnp.int32, (rows, HEAD_DIM), 0)
    length_of = jnp.zeros((rows, HEAD_DIM), jnp.int32)
    for i in range(rows):
        length_of = jnp.where(slot == i, lengths[i], length_of)
    lane = lax.broadcasted_iota(jnp.int32, (rows, HEAD_DIM), 1)
    half = HEAD_DIM // 2
    step = lax.rem(lane, half).astype(jnp.float32)
    phases = length_of.astype(jnp.float32) * jnp.exp(-math.log(THETA) * step / half)
    sine = jnp.sin(phases)
    return jnp.cos(phases), jnp.where(lane < half, -sine, sine), length_of


def attend_all(count, parts, cosine, sine, lengths, *refs):
    pairs = (count - 1) // 2
    blocks, (sums, other_sums, keys, values) = refs[:count], refs[count : count + 4]
    refs = refs[count + 4 :]
    whole, outs, (scores_of, probs_of) = refs[0], refs[1 : parts + 1], refs[parts + 1 :]
    rows, cache = keys.shape[:2]
    low = lax.rem(lax.axis_index("col"), pairs)
    width = GROUP_WIDTH
    squares = sums[...].astype(jnp.float32) + other_sums[...].astype(jnp.float32)
    scale = lax.rsqrt(jnp.sum(squares, axis=1, keepdims=True) / D + EPSILON)
    factor = HEAD_DIM ** (-0.5)
    cosines, sines, length_of = cosine[...], sine[...], lengths[:, :1]
    lane = lax.broadcasted_iota(jnp.int32, (SLOTS, SLOTS * cache), 1)
    slot = lax.broadcasted_iota(jnp.int32, (SLOTS, SLOTS * cache), 0)
    position = lane - slot * cache
    runs = [slice(start, start + SLOTS) for start in range(0, rows, SLOTS)]
    filled = [(position >= 0) & (position < length_of[part]) for part in runs]
    own, new_values, own_probs = [], [], []
    for pair in range(pairs):
        total = total_of(blocks, pair)
        total = (total * scale).astype(jnp.bfloat16).astype(jnp.float32)
        heads = [total[:, h * HEAD_DIM : (h + 1) * HEAD_DIM] for h in range(GROUP + 2)]
        queries = [
            rotated(head, cosines, sines).astype(jnp.bfloat16).astype(jnp.float32)
            for head in heads[:GROUP]
        ]
        new_key = rotated(heads[GROUP], cosines, sines).astype(jnp.bfloat16).astype(jnp.float32)
        new_values.append(heads[GROUP + 1])
        own.append([jnp.sum(query * new_key, axis=1, keepdims=True) * factor for query in queries])
        lanes = pl.ds(pl.multiple_of((low ^ pair) * HEAD_DIM, HEAD_DIM), HEAD_DIM)
        for run, part in enumerate(runs):
            query = jnp.concatenate([head[part] for head in queries], axis=0)
            key = keys[part, :, lanes].reshape(SLOTS * cache, HEAD_DIM)
            scores_of[pair, run] = lax.dot_general(
                query.astype(jnp.bfloat16),
                key,
                (((1,), (1,)), ((), ())),
                preferred_element_type=jnp.float32,
            )
    for pair in range(pairs):
        for run, part in enumerate(runs):
            scores = (scores_of[pair, run] * factor).reshape(GROUP, SLOTS, SLOTS * cache)
            scores = jnp.where(filled[run][None], scores, -1e30)
            own_score = jnp.concatenate([head[part] for head in own[pair]], axis=0).reshape(
                GROUP, SLOTS, 1
            )
            highest = jnp.maximum(jnp.max(scores, axis=2, keepdims=True), own_score)
            weights = jnp.exp(scores - highest)
            own_weight = jnp.exp(own_score - highest)
            inverse = 1.0 / (jnp.sum(weights, axis=2, keepdims=True) + own_weight)
            probs = (weights * inverse).astype(jnp.bfloat16)
            probs_of[pair, run] = probs.reshape(GROUP * SLOTS, SLOTS * cache)
            own_probs.append((own_weight * inverse).astype(jnp.bfloat16).astype(jnp.float32))
    for pair in range(pairs):
        lanes = pl.ds(pl.multiple_of((low ^ pair) * HEAD_DIM, HEAD_DIM), HEAD_DIM)
        results = []
        for run, part in enumerate(runs):
            value = values[part, :, lanes].reshape(SLOTS * cache, HEAD_DIM)
            mixed = jnp.dot(probs_of[pair, run], value, preferred_element_type=jnp.float32)
            own_prob = own_probs[pair * len(runs) + run]
            results.append(
                mixed.reshape(GROUP, SLOTS, HEAD_DIM) + own_prob * new_values[pair][part][None]
            )
        for head in range(GROUP):
            at = pl.multiple_of((low ^ pair) * OUT_WIDTH + head * HEAD_DIM, HEAD_DIM)
            size = len(results) // parts
            for i, out in enumerate(outs):
                joined = jnp.concatenate(
                    [result[head] for result in results[i * size : (i + 1) * size]], axis=0
                )
                joined = joined.astype(jnp.bfloat16)
                out[:, pl.ds(at, HEAD_DIM)] = joined
                run = slice(i * joined.shape[0], (i + 1) * joined.shape[0])
                whole[run, pl.ds(at, HEAD_DIM)] = joined


def sum_kernel(count, hidden, attended, *refs):
    blocks, (keep, send) = refs[:count], refs[count:]
    rows, width = blocks[0].shape
    pairs = keep.shape[1] // width
    side = lax.axis_index("side")
    low = lax.rem(lax.axis_index("col"), pairs)
    for pair in range(pairs):
        column = low ^ pair
        total = total_of(blocks, pair)
        at = pl.ds(pl.multiple_of((2 * column + side) * width, width), width)
        hidden_out = (hidden[:, at].astype(jnp.float32) + total).astype(jnp.bfloat16)
        at = pl.ds(pl.multiple_of(column * width, width), width)
        attention = attended[:, at]
        keep[:, at] = jnp.where(side == 0, hidden_out, attention)
        send[:, at] = jnp.where(side == 0, attention, hidden_out)


def join_kernel(keep, received, out, sems):
    side = lax.axis_index("side")
    width = OUT_WIDTH
    copies = []
    for j in range(keep.shape[1] // width):
        part = slice(j * width, (j + 1) * width)
        for ref, core in ((keep, side), (received, 1 - side)):
            at = pl.ds(pl.multiple_of((2 * j + core) * width, width), width)
            copies.append((ref.at[:, part], out.at[0, :, at]))
    run_copies(copies, sems)


def paired_plan(
    hidden_in, norm_gain, qkv_weight, out_weight, key_cache, value_cache, cache_lengths, slot_request
):
    col_count, row_count = lax.axis_size("col"), lax.axis_size("row")
    pairs = col_count // row_count
    side = lax.axis_index("side")
    rows, depth = hidden_in.shape
    half = depth // 2
    cache = key_cache.shape[1]
    parts = 2
    piece = rows // parts

    own_part = lax.dynamic_slice_in_dim(hidden_in, side * half, half, 1)
    gain = norm_gain.reshape(depth // HEAD_DIM, HEAD_DIM)
    half_in, half_out = qkv_weight.shape[1] // 2, out_weight.shape[1] // 2
    total = rows * col_count
    square = (total, total)
    give_in, own_in, chosen_in = call(
        functools.partial(stage_in_kernel, col_count),
        [pltpu.VMEM((half, half_in), jnp.bfloat16)] * 2 + [struct(square)],
        [HBM, HBM],
        [VMEM] * 3,
        0,
        half * half_in * 4,
        [
            pltpu.VMEM(square, jnp.float32),
            pltpu.VMEM((total,), jnp.int32),
            pltpu.SemaphoreType.DMA((3,)),
        ],
    )(in_hbm(qkv_weight), in_hbm(slot_request))
    blocks = gathered(
        [own_part[i * piece : (i + 1) * piece] for i in range(parts)], "col"
    )
    table = struct((rows, HEAD_DIM), jnp.float32)
    give_out, key_part, value_part, *tables, chosen_out = call(
        functools.partial(stage_rest_kernel, col_count),
        [pltpu.VMEM((half, half_out), jnp.bfloat16)]
        + [pltpu.VMEM((rows, cache, pairs * HEAD_DIM), jnp.bfloat16)] * 2
        + [table, table, struct((rows, HEAD_DIM), jnp.int32), struct(square)],
        [SMEM, HBM, HBM, HBM, VMEM],
        [VMEM] * 7,
        0,
        half * half_out * 2 + 4 * rows * cache * pairs * HEAD_DIM,
        [pltpu.VMEM(square, jnp.float32), pltpu.SemaphoreType.DMA((3 * pairs,))],
    )(cache_lengths, in_hbm(out_weight), in_hbm(key_cache), in_hbm(value_cache), slot_request)
    products, sums = project(in_kernel, chosen_in, blocks, [gain], [give_in, own_in], HEAD_DIM)
    other_sums = moved(sums[0], "row", 1)
    products = spread(products, [other_sums])

    runs = (pairs, rows // SLOTS, GROUP * SLOTS, SLOTS * cache)
    attended, *attended_parts = call(
        functools.partial(attend_all, len(products), parts),
        [struct((rows, half))] + [struct((piece, half))] * parts,
        [VMEM] * (len(products) + 7),
        [VMEM] * (parts + 1),
        4 * rows * half * cache,
        0,
        [pltpu.VMEM(runs, jnp.float32), pltpu.VMEM(runs, jnp.bfloat16)],
    )(
        *tables,
        *products,
        *sums,
        other_sums,
        in_vmem(key_part),
        in_vmem(value_part),
    )

    own_out = call(
        stage_out_kernel,
        pltpu.VMEM((half, half_out), jnp.bfloat16),
        [HBM, HBM],
        VMEM,
        0,
        half * half_out * 2,
        [pltpu.SemaphoreType.DMA((pairs,))],
    )(in_hbm(out_weight), attended)
    products, _ = project(
        out_kernel, chosen_out, gathered(attended_parts, "col"), [], [give_out, own_out], 0
    )
    products = spread(products, [])
    keep, send = call(
        functools.partial(sum_kernel, len(products)),
        [struct((rows, half)), struct((rows, half))],
        [VMEM] * (2 + len(products)),
        [VMEM, VMEM],
        rows * depth * 4,
        rows * depth * 8,
    )(hidden_in, attended, *products)
    return call(
        join_kernel,
        struct((1, rows, depth)),
        [VMEM, VMEM],
        HBM,
        0,
        rows * depth * 4,
        [pltpu.SemaphoreType.DMA((2 * pairs,))],
    )(keep, moved(send, "side", 1))


def per_device(*args):
    hidden_in, _, qkv_weight, out_weight, key_cache = args[:5]
    col_count, row_count = lax.axis_size("col"), lax.axis_size("row")
    fits = (
        lax.axis_size("side") == 2
        and qkv_weight.shape[1] == 2 * GROUP_WIDTH
        and row_count == 2
        and col_count > row_count
        and col_count & (col_count - 1) == 0
        and hidden_in.shape[0] % 32 == 0
        and key_cache.shape[1] % 16 == 0
        and hidden_in.shape[1] == 2 * OUT_WIDTH * (col_count // row_count)
    )
    return paired_plan(*args) if fits else general_plan(*args)


def solution(mesh):
    placed = (
        P(("groups", "col"), "row"),
        P("row"),
        P("row", "col"),
        P("row", "col"),
        P(("groups", "col"), None, "row"),
        P(("groups", "col"), None, "row"),
        P(("groups", "col")),
        P("groups"),
    )
    return jax.shard_map(
        per_device,
        mesh=mesh,
        in_specs=placed,
        out_specs=P("side", ("groups", "col"), "row"),
        check_vma=False,
    )
```
